32 devices in a mesh: section: 2 (over x), space: 8 (over z, y), dp: 2 (over core).
Axes of the slice: x: 2, y: 2, z: 4, core: 2. Of those that a mesh axis runs over, the one named last changes fastest.
Arguments:
- features: bfloat16 [2, 2, 4, 512, 256], P(None, 'dp', None, 'space'), may hold values from -6 to 6
- coords: float32 [2, 2, 3, 512], P(None, 'dp', None, 'space'), as said below
- neighbours: int32 [2, 2, 32, 512], P(None, 'dp', None, 'space'), may hold values from 0 to 95, as said below
- counts: int32 [2, 2, 512], P(None, 'dp', 'space'), may hold values from 1 to 32, as said below
- shifts: int32 [2, 2, 2, 32, 512], P(None, 'dp', None, None, 'space'), may hold values from -1 to 1
- norm_gain: bfloat16 [2, 256], P('section'), may hold values from 0.25 to 1.75
- norm_bias: bfloat16 [2, 256], P('section'), may hold values from -3 to 3
- qkv_weight: bfloat16 [2, 256, 1280], P('section'), may hold values from -0.375 to 0.375
- vector_weight: bfloat16 [2, 256, 768], P('section'), may hold values from -0.375 to 0.375
- filter_weight: bfloat16 [2, 32, 1024], P('section'), may hold values from -3 to 3
- out_weight: bfloat16 [2, 256, 768], P('section'), may hold values from -0.75 to 0.75
- cotangent: bfloat16 [2, 2, 4, 512, 256], P(None, 'dp', None, 'space'), may hold values from -6 to 6
Outputs:
- layer_outputs: bfloat16 [2, 2, 2, 4, 512, 256], P('section', None, 'dp', None, 'space')
- input_grads: float32 [2, 2, 2, 4, 512, 256], P('section', None, 'dp', None, 'space')
- gain_grad: float32 [2, 256], P('section', 'space')
- bias_grad: float32 [2, 256], P('section', 'space')
- qkv_grad: float32 [2, 256, 1280], P('section', None, 'space')
- vector_weight_gradient: float32 [2, 256, 768], P('section', None, 'space')
- filter_grad: float32 [2, 32, 1024], P('section', None, 'space')
- out_grad: float32 [2, 256, 768], P('section', None, 'space')
- coords_grad: float32 [2, 2, 3, 512], P(None, 'dp', None, 'space')
The draws below stay inside these ranges and needn't reach their ends.
Inputs may be any that keep to these rules, and one draw needn't show every extreme that they name: `neighbours`: slot n of the atom in row r of its slab (r = i mod 64) holds r + 16 + o with 1 <= |o| <= 16; the 32 offsets o of an atom are distinct. Every slab of 64 atoms of every box holds an atom with 32 live slots; the slabs' mean counts differ. `coords`: component 0 of atom i lies within 1.8 / 16 of 4 i / 16; components 1 and 2 lie in [0, 2.5).
All inputs are finite; a program needn't handle non-finite values.
Results may differ from the reference program's by a relative error of at most 0.015.
The reference program's roundings to bfloat16 on the way count: a program that leaves them out, or rounds other values in their place, can miss the bound.
Values may be sent and summed in bfloat16 or wider, within the bound.
No kernel may reach another device: no remote copies, remote signals or barrier semaphores. Data moves between devices by JAX's collectives and lax.ppermute only.
A program may use at most 256 MiB of HBM per device.

```python
import math
import jax
import jax.numpy as jnp
from jax import lax

F = 256
HEADS = 8
RBF = 32
K = 32
A_DEV = 64
MB = 2
BORDER_ROWS = 16
BOX = 512
GROUPS = 2
N_SPACE = 8


def draw_coords(key, part):
    key = jax.random.fold_in(key, 11)
    first_key, second_key = jax.random.split(key, 2)
    along = jnp.arange(BOX, dtype=jnp.float32)
    jitter = jax.random.uniform(first_key, (MB, GROUPS, 1, BOX), jnp.float32, -0.45, 0.45)
    leading = (along + jitter) * (4.0 / BORDER_ROWS)
    across = jax.random.uniform(second_key, (MB, GROUPS, 2, BOX), jnp.float32, 0.0, 2.5)
    return jnp.concatenate([leading, across], axis=2)


def draw_neighbours(key, part):
    key = jax.random.fold_in(key, 12)
    score_values = jax.random.randint(key, (MB, GROUPS, BOX, 2 * BORDER_ROWS), 0, 1 << 20) * (2 * BORDER_ROWS) + jnp.arange(2 * BORDER_ROWS, dtype=jnp.int32)
    slab_row = jnp.arange(BOX, dtype=jnp.int32) % A_DEV
    candidate = jnp.arange(2 * BORDER_ROWS, dtype=jnp.int32)
    lowest_selection = (slab_row[:, None] == 0) & (candidate[None, :] == 0)
    highest_selection = (slab_row[:, None] == A_DEV - 1) & (candidate[None, :] == 2 * BORDER_ROWS - 1)
    extra_reward = jnp.where(lowest_selection | highest_selection, (1 << 20) * (2 * BORDER_ROWS), 0).astype(jnp.int32)
    score_values = score_values + extra_reward
    picked = lax.top_k(score_values, K)[1]
    offset = jnp.where(picked < BORDER_ROWS, picked - BORDER_ROWS, picked - BORDER_ROWS + 1)
    local = offset + BORDER_ROWS + slab_row[:, None]
    return jnp.transpose(local, (0, 1, 3, 2)).astype(jnp.int32)


def draw_counts(key, part):
    key = jax.random.fold_in(key, 13)
    level_key, spread_key, full_key = jax.random.split(key, 3)
    level = jax.random.randint(level_key, (MB, GROUPS, N_SPACE, 1), 0, 5)
    lowest = K * level // 8 + 1
    spread = jax.random.randint(spread_key, (MB, GROUPS, N_SPACE, A_DEV), 0, 1 << 20)
    value = lowest + spread % (K + 1 - lowest)
    full_row = jax.random.randint(full_key, (MB, GROUPS, N_SPACE, 1), 0, A_DEV)
    value = jnp.where(jnp.arange(A_DEV, dtype=jnp.int32) == full_row, K, value)
    return value.reshape(MB, GROUPS, BOX).astype(jnp.int32)


def with_ends(entries, key, low, high):
    longest = entries.shape.index(max(entries.shape))
    spots = []
    for shift in (0, 1):
        where = [jax.random.randint(jax.random.fold_in(key, axis), (), 0, length) for axis, length in enumerate(entries.shape)]
        where[longest] = (where[longest] + shift) % entries.shape[longest]
        spots.append(tuple(where))
    return entries.at[spots[0]].set(low).at[spots[1]].set(high)


def level_of(rng, dims, cuts, least, high):
    gain = 1.0
    for axis_at, blocks in cuts:
        heights = jax.random.uniform(jax.random.fold_in(jax.random.fold_in(rng, 6), axis_at), (blocks,), jnp.float32, least / len(cuts), high / len(cuts))
        gain = gain * jnp.repeat(jnp.exp(heights), dims[axis_at] // blocks).reshape((-1,) + (1,) * (len(dims) - 1 - axis_at))
    return gain


def bell_draw(key, extent, width, most, cuts=(), kind=jnp.bfloat16):
    level = level_of(key, extent, cuts, -0.22, 0.18) if cuts else 1.0
    values = jax.random.normal(key, extent, jnp.float32) * width * level
    return jnp.minimum(jnp.maximum(values, -most), most).astype(kind)


def setup_inputs(seed: int = 0) -> dict:
    keys = jax.random.split(jax.random.key(seed), 13)
    features = bell_draw(keys[0], (MB, GROUPS, 4, BOX, F), 1.0, 6.0, ((1, 2), (3, 8)))
    coords = draw_coords(jax.random.fold_in(keys[12], 71), 0)
    neighbours = draw_neighbours(jax.random.fold_in(keys[12], 71), 0)
    counts = draw_counts(jax.random.fold_in(keys[12], 71), 0)
    shifts = with_ends(jax.random.randint(keys[4], (MB, GROUPS, 2, K, BOX), -1, 2), jax.random.fold_in(keys[4], 1), -1, 1).astype(jnp.int32)
    norm_gain = jnp.clip(1.0 + 0.15 * jax.random.normal(keys[5], (2, F), jnp.float32), 0.25, 1.75).astype(jnp.bfloat16)
    norm_bias = bell_draw(keys[6], (2, F), 0.5, 3.0, ((0, 2),))
    qkv_weight = bell_draw(keys[7], (2, F, 5 * F), F ** -0.5, 0.375, ((0, 2),))
    vector_weight = bell_draw(keys[8], (2, F, 3 * F), F ** -0.5, 0.375, ((0, 2),))
    filter_weight = bell_draw(keys[9], (2, RBF, 4 * F), 4 ** -0.5, 3.0, ((0, 2),))
    out_weight = bell_draw(keys[10], (2, F, 3 * F), (F // 4) ** -0.5, 0.75, ((0, 2),))
    cotangent = bell_draw(keys[11], (MB, GROUPS, 4, BOX, F), 1.0, 6.0, ((1, 2), (3, 8)))
    return {"features": features, "coords": coords, "neighbours": neighbours, "counts": counts, "shifts": shifts, "norm_gain": norm_gain, "norm_bias": norm_bias, "qkv_weight": qkv_weight, "vector_weight": vector_weight, "filter_weight": filter_weight, "out_weight": out_weight, "cotangent": cotangent}


@jax.custom_vjp
def low(v):
    return lax.optimization_barrier(v.astype(jnp.bfloat16)).astype(jnp.float32)

@jax.custom_vjp
def low_back(v):
    return v

def low_keep(v):
    return (low(v), None)

def low_pass(kept, grad):
    return (grad,)

def back_keep(v):
    return (v, None)

def back_low(kept, grad):
    return (low(grad),)
low.defvjp(low_keep, low_pass)
low_back.defvjp(back_keep, back_low)
CUTOFF = 5.0
LN_EPS = 1e-05
SOFTEN = 0.25
CROSS = 2.5
TOP_PRECISION = lax.Precision.HIGHEST

def layer_norm(scalars, norm_gain, norm_bias):
    centre = lax.optimization_barrier(jnp.mean(scalars, axis=-1, keepdims=True))
    centred = scalars - centre
    spread = lax.optimization_barrier(jnp.mean(centred * centred, axis=-1, keepdims=True))
    return centred * lax.rsqrt(spread + LN_EPS) * norm_gain + norm_bias

def edge_terms(separation, live_slot, basis_count):
    distance = jnp.sqrt(lax.optimization_barrier(jnp.sum(separation * separation, axis=0)) + SOFTEN)
    unit_vec = separation / distance
    inside = distance < CUTOFF
    cutoff = jnp.where(inside, 0.5 * (jnp.cos(math.pi * distance / CUTOFF) + 1.0), 0.0) * live_slot
    centres = jnp.linspace(math.exp(-CUTOFF), 1.0, basis_count, dtype=jnp.float32)
    sharpness = (2.0 / basis_count * (1.0 - math.exp(-CUTOFF))) ** (-2)
    shrink = jnp.exp(-distance)
    smearing = cutoff[None] * jnp.exp(-sharpness * (shrink[None] - centres[:, None, None]) ** 2)
    return (unit_vec, cutoff, smearing)

def edge_core(filter_pre, queries, key_value, vector_features, unit_vec, cutoff, source, head_count):
    feature_width = queries.shape[1]
    slot_count = source.shape[0]
    row_count = source.shape[1]
    head_dim = feature_width // head_count
    filters = jax.nn.silu(filter_pre).reshape(slot_count, row_count, 4 * feature_width)
    gathered = key_value[source]
    neighbour_vec = vector_features[:, source]
    product = queries[None] * gathered[..., :feature_width] * filters[..., :feature_width]
    score_values = lax.optimization_barrier(jnp.sum(product.reshape(slot_count, row_count, head_count, head_dim), axis=-1))
    attention = jax.nn.silu(score_values) * cutoff[..., None]
    values = gathered[..., feature_width:] * filters[..., feature_width:]
    scalar_msg = (values[..., :feature_width].reshape(slot_count, row_count, head_count, head_dim) * attention[..., None]).reshape(slot_count, row_count, feature_width)
    vector_msg = neighbour_vec * values[None, ..., feature_width:2 * feature_width] + values[None, ..., 2 * feature_width:] * unit_vec[..., None]
    return (lax.optimization_barrier(jnp.sum(scalar_msg, axis=0)), lax.optimization_barrier(jnp.sum(vector_msg, axis=1)))

def combine(out_proj, vector_projection, vector_agg):
    feature_width = out_proj.shape[1] // 3
    vec_dot = lax.optimization_barrier(jnp.sum(vector_projection[..., :feature_width] * vector_projection[..., feature_width:2 * feature_width], axis=0))
    scalar_delta = vec_dot * out_proj[:, feature_width:2 * feature_width] + out_proj[:, 2 * feature_width:]
    vector_delta = vector_projection[..., 2 * feature_width:] * out_proj[None, :, :feature_width] + vector_agg
    return (scalar_delta, vector_delta)

def layer_apply(weights, feats, positions, neighbour_ids, live_counts, cell_shifts):
    norm_gain, norm_bias, qkv_weight, vector_weight, filter_weight, out_weight = weights
    feature_width = feats.shape[2]
    scalars = feats[0]
    vector_features = feats[1:]
    normed = low(layer_norm(scalars, norm_gain, norm_bias))
    projected = low_back(jnp.dot(normed, qkv_weight, precision=TOP_PRECISION, preferred_element_type=jnp.float32))
    vector_projection = low_back(jnp.einsum('smv,va->sma', vector_features, vector_weight, precision=TOP_PRECISION))
    key_value = projected[:, feature_width:]
    atom_index = jnp.arange(BOX, dtype=jnp.int32)
    raw_index = (atom_index // A_DEV * A_DEV)[None, :] + neighbour_ids - BORDER_ROWS
    wrap_image = (raw_index >= BOX).astype(jnp.float32) - (raw_index < 0).astype(jnp.float32)
    source = jnp.mod(raw_index, BOX).astype(jnp.int32)
    length_x = BOX * 4.0 / BORDER_ROWS
    tile_rows = math.gcd(A_DEV, 128)
    tile_count = BOX // tile_rows

    def tile_pass(items):
        tile_source, tile_image, tile_shift, tile_count_live, tile_query, tile_coords = items
        others = positions[:, tile_source]
        offset = jnp.stack([tile_image * length_x, tile_shift[0].astype(jnp.float32) * CROSS, tile_shift[1].astype(jnp.float32) * CROSS])
        separation = others - tile_coords[:, None, :] + offset
        live_slot = (jnp.arange(K, dtype=jnp.int32)[:, None] < tile_count_live[None, :]).astype(jnp.float32)
        unit_vec, cutoff, smearing = edge_terms(separation, live_slot, RBF)
        flat = low(smearing.reshape(RBF, -1))
        filter_pre = low_back(lax.dot_general(flat, filter_weight, (((0,), (0,)), ((), ())), precision=TOP_PRECISION, preferred_element_type=jnp.float32))
        return edge_core(filter_pre, tile_query, key_value, vector_features, unit_vec, cutoff, tile_source, HEADS)
    items = (jnp.transpose(source.reshape(K, tile_count, tile_rows), (1, 0, 2)), jnp.transpose(wrap_image.reshape(K, tile_count, tile_rows), (1, 0, 2)), jnp.transpose(cell_shifts.reshape(2, K, tile_count, tile_rows), (2, 0, 1, 3)), live_counts.reshape(tile_count, tile_rows), projected[:, :feature_width].reshape(tile_count, tile_rows, feature_width), jnp.transpose(positions.reshape(3, tile_count, tile_rows), (1, 0, 2)))
    scalar_tiles, vector_tiles = lax.map(jax.checkpoint(tile_pass), items)
    scalar_agg = scalar_tiles.reshape(BOX, feature_width)
    vector_agg = jnp.transpose(vector_tiles, (1, 0, 2, 3)).reshape(3, BOX, feature_width)
    out_proj = low_back(jnp.dot(low(scalar_agg), out_weight, precision=TOP_PRECISION, preferred_element_type=jnp.float32))
    scalar_delta, vector_delta = combine(out_proj, vector_projection, vector_agg)
    return jnp.concatenate([(scalars + scalar_delta)[None], vector_features + vector_delta], axis=0)

def reference(features, coords, neighbours, counts, shifts, norm_gain, norm_bias, qkv_weight, vector_weight, filter_weight, out_weight, cotangent):
    weights = (norm_gain.astype(jnp.float32), norm_bias.astype(jnp.float32), qkv_weight.astype(jnp.float32), vector_weight.astype(jnp.float32), filter_weight.astype(jnp.float32), out_weight.astype(jnp.float32))
    feats_flat = features.reshape((-1,) + features.shape[2:]).astype(jnp.float32)
    coords_flat = coords.reshape((-1,) + coords.shape[2:])
    neighbour_flat = neighbours.reshape((-1,) + neighbours.shape[2:])
    counts_flat = counts.reshape((-1,) + counts.shape[2:])
    shifts_flat = shifts.reshape((-1,) + shifts.shape[2:])
    cotangent_flat = cotangent.reshape((-1,) + cotangent.shape[2:]).astype(jnp.float32)
    probe = jnp.zeros_like(feats_flat)

    def forward(layer_weights, feats_in, coords_in, probe_in):

        def box_pass(items):
            feat_box, coord_box, extra, neighbour_box, count_box, shift_box = items
            first_weights = tuple((stacked[0] for stacked in layer_weights))
            second_weights = tuple((stacked[1] for stacked in layer_weights))
            middle = layer_apply(first_weights, feat_box, coord_box, neighbour_box, count_box, shift_box)
            sent = low_back(low(middle)) + extra
            final = layer_apply(second_weights, sent, coord_box, neighbour_box, count_box, shift_box)
            return (middle, final)
        return lax.map(jax.checkpoint(box_pass), (feats_in, coords_in, probe_in, neighbour_flat, counts_flat, shifts_flat))
    (middle, final), pullback = jax.vjp(forward, weights, feats_flat, coords_flat, probe)
    weight_grads, feats_grad, coords_back, probe_grad = pullback((jnp.zeros_like(middle), cotangent_flat))
    full_shape = (2,) + features.shape
    layer_outputs = jnp.stack([middle, final]).astype(jnp.bfloat16).reshape(full_shape)
    input_grads = jnp.stack([feats_grad, probe_grad]).reshape(full_shape)
    return (layer_outputs, input_grads, weight_grads[0], weight_grads[1], weight_grads[2], weight_grads[3], weight_grads[4], weight_grads[5], coords_back.reshape(coords.shape))
```

```python
import math
from types import SimpleNamespace

import jax
import jax.numpy as jnp
from jax import lax
from jax.experimental import pallas as pl
from jax.experimental.pallas import tpu as pltpu
from jax.sharding import PartitionSpec as P

HEADS = 8
CUTOFF = 5.0
LN_EPS = 1e-05
SOFTEN = 0.25
CROSS = 2.5
GROUP = 4
LANES = 128
SUBLANES = 8
FIRST, SECOND = 0, 1

F32 = jnp.float32
BF16 = jnp.bfloat16
VMEM = pl.BlockSpec(memory_space=pltpu.VMEM)
SMEM = pl.BlockSpec(memory_space=pltpu.SMEM)
HBM = pl.BlockSpec(memory_space=pltpu.HBM)


def dot(left, right, left_dim=1, right_dim=0):
    return lax.dot_general(
        left, right, (((left_dim,), (right_dim,)), ((), ())), preferred_element_type=F32
    )


def iota(shape, dim):
    return lax.broadcasted_iota(jnp.int32, shape, dim)


def packed_places(parts, width):
    row = jnp.concatenate(parts, axis=1)
    high = row.astype(BF16).astype(F32)
    rest = row - high
    middle = rest.astype(BF16).astype(F32)
    rows = jnp.concatenate([high, middle, rest - middle, jnp.zeros((13, row.shape[1]), F32)], axis=0)
    return jnp.concatenate([rows, jnp.zeros((16, width - row.shape[1]), F32)], axis=1).astype(BF16)


def unpacked_places(block, c, count):
    rows = block[:, c * count : (c + 1) * count].astype(F32)
    return rows[0:1] + rows[1:2] + rows[2:3]


class Sizes:
    def __init__(self, atoms, width, basis, slots, space):
        self.atoms, self.width, self.basis, self.slots, self.space = atoms, width, basis, slots, space
        self.halo = atoms // 4
        self.rows = atoms + 2 * self.halo
        self.blocks = slots // GROUP
        self.edges = GROUP * atoms
        self.halves = width // LANES
        self.window = atoms + SUBLANES
        self.sent = 3 * self.halo
        self.widths = (5 * width // space, 3 * width // space, 3 * width // space)
        self.spare = sum(self.widths)
        self.packed = -(-(self.spare + basis) // LANES) * LANES
        self.factors = -(-(self.rows + 4 * atoms) // LANES) * LANES


def halves_of(sz):
    return [slice(cg * LANES, (cg + 1) * LANES) for cg in range(sz.halves)]


def first_row(b):
    return GROUP * b + jnp.where(b >= 4, 1, 0)


def sharpness_of(basis):
    return (2.0 / basis * (1.0 - math.exp(-CUTOFF))) ** (-2)


def write_centres(ref, basis):
    low_end = math.exp(-CUTOFF)
    step = iota(ref.shape, 0).astype(F32) / (basis - 1)
    ref[...] = low_end * (1.0 - step) + step


def edge_geometry(r, sz, m, coords, nbr, counts, shifts):
    A, H, E, EB = sz.atoms, sz.halo, sz.rows, sz.edges
    lane = iota((8, LANES), 1)
    row = iota((8, LANES), 0)
    slab, last = r.scal[1], r.scal[3]
    spot = iota((1, LANES), 1)
    length_x = (last + 1).astype(F32) * (A * 4.0 / H)
    places = []
    for c in range(3):
        places.append(
            jnp.concatenate(
                [
                    unpacked_places(r.pack_low[m, 4], c, H),
                    coords[c],
                    unpacked_places(r.pack_high[m, 4], c, H),
                    jnp.zeros((1, LANES - E), F32),
                ],
                axis=1,
            )
        )
    places.append(
        jnp.where((spot < H) & (slab == 0), -length_x, 0.0)
        + jnp.where((spot >= H + A) & (slab == last), length_x, 0.0)
    )
    near = []
    for c in range(4):
        y = jnp.broadcast_to(places[c], (8, LANES))
        for bit in range(3):
            y = jnp.where((row >> bit) & 1 == 1, pltpu.roll(y, LANES - GROUP * 2**bit, 1), y)
        y = jnp.where(row >= 4, pltpu.roll(y, LANES - 1, 1), y)
        first = jnp.where(lane < A, y, pltpu.roll(y, A - 1, 1))
        other = jnp.where(lane < A, pltpu.roll(y, LANES - 2, 1), pltpu.roll(y, A - 3, 1))
        near.append(jnp.concatenate([first, other], axis=1))
    wide_lane = iota((8, EB), 1)
    wide_row = iota((8, EB), 0)
    wanted = GROUP * wide_row + wide_lane // A + jnp.where(wide_row >= 4, 1, 0) + wide_lane % A
    alive = iota((sz.slots, A), 0) < counts[...]
    code = jnp.where(alive, 16, 0) + (shifts[0] + 1) * 4 + (shifts[1] + 1)
    code = jnp.concatenate([code] * GROUP, axis=1)
    named = jnp.concatenate([nbr[...]] * GROUP, axis=1)
    found = jnp.zeros((8, EB), jnp.int32)
    for n in range(sz.slots):
        found = found + jnp.where(named[n : n + 1, :] == wanted, code[n : n + 1, :], 0)
    live = (found >> 4).astype(F32)
    offsets = (
        near[3],
        (((found >> 2) & 3) - 1).astype(F32) * CROSS,
        ((found & 3) - 1).astype(F32) * CROSS,
    )
    sep = []
    for c in range(3):
        mine = coords[c]
        sep.append(near[c] - jnp.concatenate([mine] * GROUP, axis=1) + offsets[c])
    distance = jnp.sqrt(sep[0] * sep[0] + sep[1] * sep[1] + sep[2] * sep[2] + SOFTEN)
    inside = distance < CUTOFF
    cut = jnp.where(inside, 0.5 * (jnp.cos(math.pi * distance / CUTOFF) + 1.0), 0.0) * live
    for index, value in enumerate(
        sep + [distance, live, cut, jnp.exp(-distance)] + [part / distance for part in sep]
    ):
        r.geo[index] = value


DISTANCE, LIVE, CUT, SHRINK, UNIT = 3, 4, 5, 6, 7


def bell_of(r, sz, b):
    delta = r.geo[SHRINK, pl.ds(b, 1), :] - r.centres[...]
    return delta, jnp.exp(-sharpness_of(sz.basis) * delta * delta)


def write_edge_tables(r, sz, b, wide_kind):
    A, EB = sz.atoms, sz.edges
    cut = r.geo[CUT, pl.ds(b, 1), :]
    _, bell = bell_of(r, sz, b)
    smear = cut * bell
    if hasattr(r, "smear"):
        r.smear[b] = smear.astype(BF16)
    r.smear_t[b] = jnp.transpose(smear).astype(BF16)
    coarse = cut.astype(BF16).astype(F32)
    which = iota((16, EB), 0)
    pair = jnp.where(which == 0, coarse, jnp.where(which == 1, cut - coarse, 0.0)).astype(BF16)
    r.cut_wide[b] = dot(pair, jnp.ones((16, LANES), BF16), 0, 0).astype(wide_kind)
    for c in range(3):
        r.units[b, c * A : (c + 1) * A, :] = (
            r.diag[...] * r.geo[UNIT + c, pl.ds(b, 1), :]
        ).astype(BF16)


def write_constants(r, sz):
    A, EB, F = sz.atoms, sz.edges, sz.width
    if hasattr(r, "centres"):
        write_centres(r.centres, sz.basis)
    if hasattr(r, "diag"):
        r.diag[...] = jnp.where(iota((A, EB), 1) % A == iota((A, EB), 0), 1.0, 0.0)
    if hasattr(r, "fold"):
        r.fold[...] = jnp.where(iota((A, EB), 1) % A == iota((A, EB), 0), 1.0, 0.0).astype(BF16)
    if hasattr(r, "heads"):
        r.heads[...] = jnp.where(
            iota((F, F), 0) // (F // HEADS) == iota((F, F), 1) // (F // HEADS), 0.5, 0.0
        ).astype(BF16)


def node_part(r, sz, own, low, high, wqkv):
    A, H, E, F, CG = sz.atoms, sz.halo, sz.rows, sz.width, sz.halves
    halves = halves_of(sz)
    scalars = jnp.concatenate([low[0, 0:H], own[0], high[0, 0:H]], axis=0).astype(F32)
    centred = scalars - jnp.mean(scalars, axis=-1, keepdims=True)
    spread = jnp.mean(centred * centred, axis=-1, keepdims=True)
    scale = lax.rsqrt(spread + LN_EPS)
    normed = (centred * scale * r.norms[0:1, :] + r.norms[1:2, :]).astype(BF16)
    left = r.left
    left[0:E, :] = normed
    left[E : E + 3 * A, :] = own[1:4].reshape(3 * A, F)
    left[E + 4 * A :, :] = jnp.zeros((sz.factors - E - 4 * A, F), BF16)
    for part in range(5):
        projected = dot(normed, wqkv[:, part * F : (part + 1) * F])
        for cg in range(CG):
            if part == 0:
                r.query[cg] = projected[H : H + A, halves[cg]]
            else:
                r.kv[(part - 1) * CG + cg] = projected[:, halves[cg]]
    for c in range(3):
        for cg in range(CG):
            r.vec[c * CG + cg, 0:H, :] = low[c + 1, 0:H, halves[cg]].astype(F32)
            r.vec[c * CG + cg, H : H + A, :] = own[c + 1][:, halves[cg]].astype(F32)
            r.vec[c * CG + cg, H + A : E, :] = high[c + 1, 0:H, halves[cg]].astype(F32)
    return centred * scale, scale


def tiles(sz, first):
    A = sz.atoms
    for kk in range(GROUP):
        for cg in range(sz.halves):
            yield (
                cg,
                slice(kk * A, (kk + 1) * A),
                slice(cg * LANES, (cg + 1) * LANES),
                pl.ds(first + kk, A),
            )


def vector_dot(r, sz):
    A, F, vp = sz.atoms, sz.width, r.vproj
    return sum(
        vp[c * A : (c + 1) * A, 0:F] * vp[c * A : (c + 1) * A, F : 2 * F] for c in range(3)
    )


def write_layer_output(r, sz, own, out_proj, vec_dot, vector_agg):
    A, H, F, vp = sz.atoms, sz.halo, sz.width, r.vproj
    for index in range(4):
        if index == 0:
            fresh = vec_dot * out_proj[:, F : 2 * F] + out_proj[:, 2 * F :]
        else:
            rows = slice((index - 1) * A, index * A)
            fresh = vp[rows, 2 * F :] * out_proj[:, 0:F] + vector_agg[index - 1]
        fresh = (own[index].astype(F32) + fresh).astype(BF16)
        r.fresh[index] = fresh
        if hasattr(r, "head"):
            r.head[index, 0:H, :] = fresh[:H]
            r.tail[index, 0:H, :] = fresh[A - H :]


def first_forward(r, sz, m):
    A, H, E, F, EB = sz.atoms, sz.halo, sz.rows, sz.width, sz.edges
    CG = sz.halves
    early = [
        (r.coords.at[m], r.s_coords),
        (r.nbr.at[m, 0], r.s_nbr),
        (r.counts.at[m], r.s_counts),
        (r.shifts.at[m, 0], r.s_shifts),
        (r.features.at[m, 0], r.s_own),
        (r.wqkv.at[0], r.s_wqkv),
    ]
    late = [(r.wfilt.at[0], r.s_wfilt), (r.wvec.at[0], r.s_wvec), (r.wout.at[0], r.s_wout)]
    copies = [
        pltpu.make_async_copy(source, target, r.sems.at[i])
        for i, (source, target) in enumerate(early + late)
    ]
    for copy in copies:
        copy.start()
    write_constants(r, sz)
    r.sagg[...] = jnp.zeros_like(r.sagg)
    r.vagg[...] = jnp.zeros_like(r.vagg)
    for copy in copies[: len(early)]:
        copy.wait()
    edge_geometry(r, sz, m, r.s_coords, r.s_nbr, r.s_counts, r.s_shifts)

    def tables(b, carry):
        write_edge_tables(r, sz, b, F32)
        return carry

    lax.fori_loop(0, sz.blocks, tables, 0, unroll=2)
    own = r.s_own
    node_part(r, sz, own, r.pack_low.at[m], r.pack_high.at[m], r.s_wqkv)
    for copy in copies[len(early) :]:
        copy.wait()
    r.wh[...] = (r.s_wfilt[...].astype(F32) * 0.5).astype(BF16)
    r.vproj[...] = dot(r.left[E : E + 3 * A, :], r.s_wvec[...])

    def filter_part(b, part):
        return dot(r.smear_t[b], r.wh[:, part * F : (part + 1) * F])

    def block(b, carry):
        first = first_row(b)
        half = filter_part(b, 0)
        for cg, at, cols, near_rows in tiles(sz, first):
            h = half[at, cols]
            product = r.query[cg] * r.kv[cg, near_rows, :] * (h + h * jnp.tanh(h))
            coarse = product.astype(BF16)
            r.pack1[at, cols] = coarse
            r.pack2[at, cols] = (product - coarse.astype(F32)).astype(BF16)
        score = dot(r.pack1[...], r.heads[...]) + dot(r.pack2[...], r.heads[...])
        r.score[b] = score.astype(BF16)
        half = filter_part(b, 2)
        for cg, at, cols, near_rows in tiles(sz, first):
            h = half[at, cols]
            value = r.kv[2 * CG + cg, near_rows, :] * (h + h * jnp.tanh(h))
            for c in range(3):
                r.vagg[c * CG + cg] += r.vec[c * CG + cg, near_rows, :] * value
        half = filter_part(b, 3)
        for cg, at, cols, near_rows in tiles(sz, first):
            h = half[at, cols]
            value = r.kv[3 * CG + cg, near_rows, :] * (h + h * jnp.tanh(h))
            r.third[b, at, cols] = value.astype(BF16)
        half = filter_part(b, 1)
        for cg, at, cols, near_rows in tiles(sz, first):
            h = half[at, cols]
            s = score[at, cols]
            attention = (s + s * jnp.tanh(s)) * r.cut_wide[b, at, :]
            r.sagg[cg] += attention * (r.kv[CG + cg, near_rows, :] * (h + h * jnp.tanh(h)))
        return carry

    lax.fori_loop(0, sz.blocks, block, 0)
    third = sum(dot(r.units[b], r.third[b]) for b in range(sz.blocks))
    scalar_low = jnp.concatenate([r.sagg[cg] for cg in range(CG)], axis=1).astype(BF16)
    r.scalar_out[...] = scalar_low
    out_proj = dot(scalar_low, r.s_wout[...])
    vector_agg = [
        jnp.concatenate([r.vagg[c * CG + cg] for cg in range(CG)], axis=1)
        + third[c * A : (c + 1) * A, :]
        for c in range(3)
    ]
    write_layer_output(r, sz, own, out_proj, vector_dot(r, sz), vector_agg)


def edge_filters(r, sz, m):
    F = sz.width
    write_constants(r, sz)
    edge_geometry(r, sz, m, r.coords.at[m], r.nbr.at[m, 0], r.counts.at[m], r.shifts.at[m, 0])
    r.wh[...] = (r.wfilt[0].astype(F32) * 0.5).astype(BF16)

    def block(b, carry):
        write_edge_tables(r, sz, b, BF16)
        for part in range(4):
            cols = slice(part * F, (part + 1) * F)
            h = dot(r.smear_t[b], r.wh[:, cols])
            t = jnp.tanh(h)
            up = 1.0 + t
            f = h * up
            r.silu[b, :, cols] = f.astype(BF16)
            r.slope[b, :, cols] = (up + f * (1.0 - t)).astype(BF16)
        return carry

    lax.fori_loop(0, sz.blocks, block, 0)


def both_ways(r, sz, m, fwd):
    A, H, E, F = sz.atoms, sz.halo, sz.rows, sz.width
    EB, CG, NB, W = sz.edges, sz.halves, sz.blocks, sz.window
    lane = iota((8, LANES), 1)
    row = iota((8, LANES), 0)
    halves = halves_of(sz)
    if fwd:
        own, low, high = r.own, r.low, r.high
    else:
        own, low, high = r.features.at[m, 0], r.pack_low.at[m], r.pack_high.at[m]
    wqkv, wvec, wout = r.wqkv.at[0], r.wvec.at[0], r.wout.at[0]
    write_constants(r, sz)
    xhat, scale = node_part(r, sz, own, low, high, wqkv)
    gain = r.norms[0:1, :]
    left = r.left
    vp = r.vproj
    vp[...] = dot(left[E : E + 3 * A, :], wvec[...])
    r.wh[...] = (r.wfilt[0].astype(F32) * 0.5).astype(BF16)
    for cg in range(CG):
        r.query_low[:, halves[cg]] = r.query[cg].astype(BF16)

    if fwd:
        r.sagg[...] = jnp.zeros_like(r.sagg)
        r.vagg[...] = jnp.zeros_like(r.vagg)

        def forward_block(b, carry):
            first = first_row(b)
            for cg, at, cols, near_rows in tiles(sz, first):
                product = r.query[cg] * r.kv[cg, near_rows, :] * r.silu[b, at, cols].astype(F32)
                coarse = product.astype(BF16)
                r.pack1[at, cols] = coarse
                r.pack2[at, cols] = (product - coarse.astype(F32)).astype(BF16)
            score = dot(r.pack1[...], r.heads[...]) + dot(r.pack2[...], r.heads[...])
            for cg, at, cols, near_rows in tiles(sz, first):
                f = r.silu[b, at, slice(2 * F + cg * LANES, 2 * F + (cg + 1) * LANES)]
                value = r.kv[2 * CG + cg, near_rows, :].astype(BF16) * f
                for c in range(3):
                    r.spread[1 + c, at, cols] = (
                        r.vec[c * CG + cg, near_rows, :].astype(BF16) * value
                    )
            for cg, at, cols, near_rows in tiles(sz, first):
                f = r.silu[b, at, slice(3 * F + cg * LANES, 3 * F + (cg + 1) * LANES)]
                r.pack3[at, cols] = r.kv[3 * CG + cg, near_rows, :].astype(BF16) * f
            for cg, at, cols, near_rows in tiles(sz, first):
                f = r.silu[b, at, slice(F + cg * LANES, F + (cg + 1) * LANES)]
                s = score[at, cols].astype(BF16)
                r.score[b, at, cols] = s
                attention = s * (1.0 + jnp.tanh(s)) * r.cut_wide[b, at, :]
                r.spread[0, at, cols] = attention * (
                    r.kv[CG + cg, near_rows, :].astype(BF16) * f
                )
            r.sagg[...] += dot(r.fold[...], r.spread[0])
            for c in range(3):
                r.vagg[c] += dot(r.fold[...], r.spread[1 + c]) + dot(
                    r.units[b, c * A : (c + 1) * A, :], r.pack3[...]
                )
            return carry

        lax.fori_loop(0, NB, forward_block, 0)
        scalar_low = r.sagg[...].astype(BF16)
    else:
        scalar_low = r.scalar_in[...]
    left[E + 3 * A : E + 4 * A, :] = scalar_low
    out_proj = dot(scalar_low, wout[...])
    vec_dot = vector_dot(r, sz)
    if fwd:
        write_layer_output(r, sz, own, out_proj, vec_dot, [r.vagg[c] for c in range(3)])

    def incoming(index):
        if fwd:
            return r.cotangent[m, 0, index].astype(F32)
        gap = jnp.zeros((A - 2 * H, F), F32)
        edge = [r.inc_low[index, 0:H].astype(F32), gap, r.inc_high[index, 0:H].astype(F32)]
        value = r.inc[index].astype(F32) + jnp.concatenate(edge, axis=0)
        return value.astype(BF16).astype(F32)

    g_x = incoming(0)
    r.gx[0] = g_x
    g_first = jnp.zeros((A, F), F32)
    g_mid = g_x * out_proj[:, F : 2 * F]
    for c in range(3):
        g_vec = incoming(c + 1)
        r.gx[c + 1] = g_vec
        rows = slice(c * A, (c + 1) * A)
        r.gvlow[rows, :] = g_vec.astype(BF16)
        g_first = g_first + g_vec * vp[rows, 2 * F :]
        r.gvproj[rows, 0:F] = (g_mid * vp[rows, F : 2 * F]).astype(BF16)
        r.gvproj[rows, F : 2 * F] = (g_mid * vp[rows, 0:F]).astype(BF16)
        r.gvproj[rows, 2 * F :] = (g_vec * out_proj[:, 0:F]).astype(BF16)
    r.gout[:, 0:F] = g_first.astype(BF16)
    r.gout[:, F : 2 * F] = (g_x * vec_dot).astype(BF16)
    r.gout[:, 2 * F :] = g_x.astype(BF16)
    r.gs[...] = dot(r.gout[...], wout[...], 1, 1).astype(BF16)
    for total in (r.gnear, r.gq, r.gfilt):
        total[...] = jnp.zeros_like(total)

    def backward_block(b, carry):
        first = first_row(b)
        base = pl.multiple_of(first // SUBLANES * SUBLANES, SUBLANES)

        def filters(part, cg, at):
            cols = slice(part * F + cg * LANES, part * F + (cg + 1) * LANES)
            return r.silu[b, at, cols], r.slope[b, at, cols], cols

        for cg, at, cols, near_rows in tiles(sz, first):
            f, _, _ = filters(1, cg, at)
            value = r.kv[CG + cg, near_rows, :].astype(BF16)
            r.pack2[at, cols] = r.gs[:, cols] * (value * f)
            r.keep4[at, cols] = value
        g_att = dot(r.pack2[...], r.heads[...])
        for cg, at, cols, near_rows in tiles(sz, first):
            f, slope, part_cols = filters(2, cg, at)
            value = r.kv[2 * CG + cg, near_rows, :].astype(BF16)
            message = value * f
            for c in range(3):
                g_vec = r.gvlow[c * A : (c + 1) * A, cols]
                term = g_vec * r.vec[c * CG + cg, near_rows, :].astype(BF16)
                g_edge = term if c == 0 else g_edge + term
                r.spread[4 + c, at, cols] = g_vec * message
            r.spread[2, at, cols] = g_edge * f
            r.gpre[at, part_cols] = g_edge * (value * slope)
        g_third = dot(r.units[b], r.gvlow[...], 0, 0)
        for cg, at, cols, near_rows in tiles(sz, first):
            f, slope, part_cols = filters(3, cg, at)
            value = r.kv[3 * CG + cg, near_rows, :].astype(BF16)
            r.pack3[at, cols] = value * f
            g_edge = g_third[at, cols].astype(BF16)
            r.spread[3, at, cols] = g_edge * f
            r.gpre[at, part_cols] = g_edge * (value * slope)
        for cg, at, cols, near_rows in tiles(sz, first):
            s = r.score[b, at, cols]
            t = jnp.tanh(s)
            up = 1.0 + t
            act = s * up
            wide = r.cut_wide[b, at, :]
            ga = g_att[at, cols].astype(BF16)
            r.pack1[at, cols] = ga * act
            g_score = ga * wide * (up + act * (1.0 - t))
            g_edge = r.gs[:, cols] * (act * wide)
            f, slope, part_cols = filters(0, cg, at)
            key = r.kv[cg, near_rows, :].astype(BF16)
            middle = g_score * f
            steep = g_score * slope
            r.spread[7, at, cols] = middle * key
            r.spread[0, at, cols] = middle * r.query_low[:, cols]
            r.gpre[at, part_cols] = steep * (key * r.query_low[:, cols])
            f, slope, part_cols = filters(1, cg, at)
            r.spread[1, at, cols] = g_edge * f
            r.gpre[at, part_cols] = g_edge * (r.keep4[at, cols] * slope)
        lanes = iota((W, EB), 1)
        place = jnp.where(
            lanes % A + lanes // A + (first - base) == iota((W, EB), 0), 1.0, 0.0
        ).astype(BF16)
        for index in range(7):
            r.gnear[index, pl.ds(base, W), :] += dot(place, r.spread[index])
        r.gq[...] += dot(r.fold[...], r.spread[7])
        g_unit = dot(r.gvlow[...], r.pack3[...], 1, 1)
        for c in range(3):
            r.gunit[c, pl.ds(b, 1), :] = jnp.sum(
                g_unit[c * A : (c + 1) * A, :] * r.diag[...], axis=0, keepdims=True
            )
        g_cut = dot(jnp.ones((16, F), BF16), r.pack1[...], 1, 1)[0:1, :] * (2.0 * HEADS / F)
        g_smear = dot(r.wh[...], r.gpre[...], 1, 1)
        r.gfilt[...] += dot(r.smear[b], r.gpre[...])
        delta, bell = bell_of(r, sz, b)
        through = g_smear * bell
        r.gcut[pl.ds(b, 1), :] = g_cut + jnp.sum(through, axis=0, keepdims=True)
        r.gshrink[pl.ds(b, 1), :] = r.geo[CUT, pl.ds(b, 1), :] * jnp.sum(
            through * delta, axis=0, keepdims=True
        ) * (-2.0 * sharpness_of(sz.basis))
        return carry

    lax.fori_loop(0, NB, backward_block, 0)

    distance = r.geo[DISTANCE]
    g_dist = r.gcut[...] * r.geo[LIVE] * jnp.where(
        distance < CUTOFF,
        (-0.5 * math.pi / CUTOFF) * jnp.sin(math.pi * distance / CUTOFF),
        0.0,
    ) - r.gshrink[...] * r.geo[SHRINK]
    inverse = 1.0 / distance
    g_unit = [r.gunit[c] for c in range(3)]
    sep = [r.geo[c] for c in range(3)]
    along = g_unit[0] * sep[0] + g_unit[1] * sep[1] + g_unit[2] * sep[2]
    radial = (g_dist - along * inverse * inverse) * inverse
    r.gplaces[...] = jnp.zeros_like(r.gplaces)
    for c in range(3):
        g_sep = g_unit[c] * inverse + radial * sep[c]
        first, other = g_sep[:, :LANES], g_sep[:, LANES:]
        z = (
            jnp.where(lane < A, first, 0.0)
            + pltpu.roll(jnp.where(lane < A, 0.0, first), A + 1, 1)
            + pltpu.roll(jnp.where(lane < A, other, 0.0), 2, 1)
            + pltpu.roll(jnp.where(lane < A, 0.0, other), A + 3, 1)
        )
        for bit in range(3):
            z = jnp.where((row >> bit) & 1 == 1, pltpu.roll(z, GROUP * 2**bit, 1), z)
        z = jnp.where(row >= 4, pltpu.roll(z, 1, 1), z)
        total = jnp.sum(g_sep, axis=0, keepdims=True)
        mine = total[:, 0:A] + total[:, A : 2 * A] + total[:, 2 * A : 3 * A] + total[:, 3 * A :]
        mine = jnp.concatenate(
            [jnp.zeros((1, H), F32), mine, jnp.zeros((1, LANES - H - A), F32)], axis=1
        )
        r.gplaces[c : c + 1, :] = jnp.sum(z, axis=0, keepdims=True) - mine

    gproj = r.gproj
    gproj[:, 0:F] = jnp.zeros((E, F), BF16)
    gproj[H : H + A, 0:F] = r.gq[...].astype(BF16)
    for part in range(4):
        gproj[:, (part + 1) * F : (part + 2) * F] = r.gnear[part].astype(BF16)
    g_normed = dot(gproj[...], wqkv[...], 1, 1)
    u = gain * g_normed
    g_scalars = scale * (
        u
        - jnp.mean(u, axis=-1, keepdims=True)
        - xhat * jnp.mean(u * xhat, axis=-1, keepdims=True)
    )
    r.gnorm[...] = jnp.zeros_like(r.gnorm)
    r.gnorm[0:1, :] = jnp.sum(g_normed * xhat, axis=0, keepdims=True)
    r.gnorm[1:2, :] = jnp.sum(g_normed, axis=0, keepdims=True)
    vec_back = dot(r.gvproj[...], wvec[...], 1, 1)
    for index in range(4):
        if index == 0:
            whole = g_scalars
            middle = whole[H : H + A] + r.gx[0]
        else:
            c = index - 1
            whole = r.gnear[4 + c]
            middle = whole[H : H + A] + r.gx[index] + vec_back[c * A : (c + 1) * A, :]
        r.back[index] = middle
        r.back_low[index] = middle.astype(BF16)
        r.rim_low[index] = whole[0:H].astype(BF16)
        r.rim_high[index] = whole[H + A :].astype(BF16)


FACTORS = ("left", "gproj", "gvproj", "gout", "gfilt", "gnorm", "rim_low", "rim_high", "gplaces")


def call(body, arrays, outs, scratch, role=None, grant_mb=24):
    arrays, outs = vars(arrays), vars(outs)
    names = list(arrays) + list(outs) + list(scratch)

    def kernel(*args):
        refs = SimpleNamespace(**dict(zip(names, args, strict=True)))
        if role is None:
            body(refs)
        else:
            pl.when(refs.scal[0] == role)(lambda: body(refs))

    results = pl.pallas_call(
        kernel,
        out_shape=list(outs.values()),
        in_specs=[spec for _, spec in arrays.values()],
        out_specs=[VMEM for _ in outs],
        scratch_shapes=[
            pltpu.VMEM(*s) if isinstance(s, tuple) else s for s in scratch.values()
        ],
        compiler_params=pltpu.CompilerParams(vmem_limit_bytes=grant_mb * 2**20),
    )(*[array for array, _ in arrays.values()])
    return SimpleNamespace(**dict(zip(outs, results, strict=True)))


def first_call(sz, m, arrays):
    A, H, E, F = sz.atoms, sz.halo, sz.rows, sz.width
    EB, CG, NB = sz.edges, sz.halves, sz.blocks
    shape = jax.ShapeDtypeStruct
    outs = SimpleNamespace(
        fresh=shape((4, A, F), BF16),
        head=shape((4, sz.sent, F), BF16),
        tail=shape((4, sz.sent, F), BF16),
        scalar_out=shape((A, F), BF16),
        score=shape((NB, EB, F), BF16),
    )
    scratch = dict(
        s_own=((4, A, F), BF16),
        s_coords=((3, 1, A), F32),
        s_nbr=((sz.slots, A), jnp.int32),
        s_counts=((1, A), jnp.int32),
        s_shifts=((2, sz.slots, A), jnp.int32),
        s_wqkv=((F, 5 * F), BF16),
        s_wvec=((F, 3 * F), BF16),
        s_wfilt=((sz.basis, 4 * F), BF16),
        s_wout=((F, 3 * F), BF16),
        sems=pltpu.SemaphoreType.DMA((9,)),
        left=((sz.factors, F), BF16),
        query=((CG, A, LANES), F32),
        kv=((4 * CG, E, LANES), F32),
        vec=((3 * CG, E, LANES), F32),
        vproj=((3 * A, 3 * F), F32),
        wh=((sz.basis, 4 * F), BF16),
        heads=((F, F), BF16),
        diag=((A, EB), F32),
        geo=((10, 8, EB), F32),
        centres=((sz.basis, EB), F32),
        smear_t=((NB, EB, sz.basis), BF16),
        cut_wide=((NB, EB, LANES), F32),
        units=((NB, 3 * A, EB), BF16),
        pack1=((EB, F), BF16),
        pack2=((EB, F), BF16),
        sagg=((CG, A, LANES), F32),
        vagg=((3 * CG, A, LANES), F32),
        third=((NB, EB, F), BF16),
    )
    return call(lambda r: first_forward(r, sz, m), arrays, outs, scratch, FIRST, grant_mb=54)


def filter_call(sz, m, arrays):
    A, F = sz.atoms, sz.width
    EB, NB = sz.edges, sz.blocks
    shape = jax.ShapeDtypeStruct
    outs = SimpleNamespace(
        geo=shape((10, 8, EB), F32),
        smear=shape((NB, sz.basis, EB), BF16),
        cut_wide=shape((NB, EB, LANES), BF16),
        units=shape((NB, 3 * A, EB), BF16),
        silu=shape((NB, EB, 4 * F), BF16),
        slope=shape((NB, EB, 4 * F), BF16),
    )
    scratch = dict(
        wh=((sz.basis, 4 * F), BF16),
        diag=((A, EB), F32),
        centres=((sz.basis, EB), F32),
        smear_t=((NB, EB, sz.basis), BF16),
    )
    return call(lambda r: edge_filters(r, sz, m), arrays, outs, scratch)


def both_call(sz, m, fwd, arrays):
    A, H, E, F = sz.atoms, sz.halo, sz.rows, sz.width
    EB, CG, NB = sz.edges, sz.halves, sz.blocks
    shape = jax.ShapeDtypeStruct
    outs = SimpleNamespace(
        back=shape((4, A, F), F32),
        back_low=shape((4, A, F), BF16),
        rim_low=shape((4, H, F), BF16),
        rim_high=shape((4, H, F), BF16),
        gplaces=shape((8, LANES), F32),
        left=shape((sz.factors, F), BF16),
        gproj=shape((E, 5 * F), BF16),
        gvproj=shape((3 * A, 3 * F), BF16),
        gout=shape((A, 3 * F), BF16),
        gfilt=shape((sz.basis, 4 * F), F32),
        gnorm=shape((8, F), F32),
    )
    scratch = dict(
        query=((CG, A, LANES), F32),
        query_low=((A, F), BF16),
        kv=((4 * CG, E, LANES), F32),
        vec=((3 * CG, E, LANES), F32),
        vproj=((3 * A, 3 * F), F32),
        wh=((sz.basis, 4 * F), BF16),
        heads=((F, F), BF16),
        diag=((A, EB), F32),
        fold=((A, EB), BF16),
        centres=((sz.basis, EB), F32),
        pack1=((EB, F), BF16),
        pack2=((EB, F), BF16),
        pack3=((EB, F), BF16),
        keep4=((EB, F), BF16),
        gx=((4, A, F), F32),
        gvlow=((3 * A, F), BF16),
        gs=((A, F), BF16),
        spread=((8, EB, F), BF16),
        gpre=((EB, 4 * F), BF16),
        gq=((A, F), F32),
        gnear=((7, E, F), F32),
        gunit=((3, 8, EB), F32),
        gcut=((8, EB), F32),
        gshrink=((8, EB), F32),
    )
    if fwd:
        outs.fresh = shape((4, A, F), BF16)
        scratch.update(
            score=((NB, EB, F), BF16), sagg=((A, F), F32), vagg=((3, A, F), F32)
        )
    role = SECOND if fwd else FIRST
    return call(lambda r: both_ways(r, sz, m, fwd), arrays, outs, scratch, role)


def border_call(sz, features, coords):
    A, H, F = sz.atoms, sz.halo, sz.width
    count = features.shape[0]

    def body(r):
        copies = [pltpu.make_async_copy(r.coords, r.s_coords, r.sems.at[2 * count])]
        for m in range(count):
            copies.append(
                pltpu.make_async_copy(
                    r.features.at[m, 0, :, A - H : A, :], r.up.at[m, 0:4], r.sems.at[2 * m]
                )
            )
            copies.append(
                pltpu.make_async_copy(
                    r.features.at[m, 0, :, 0:H, :], r.down.at[m, 0:4], r.sems.at[2 * m + 1]
                )
            )
        for copy in copies:
            copy.start()
        copies[0].wait()
        for m in range(count):
            r.up[m, 4] = packed_places([r.s_coords[m, c][:, A - H :] for c in range(3)], F)
            r.down[m, 4] = packed_places([r.s_coords[m, c][:, :H] for c in range(3)], F)
        for copy in copies[1:]:
            copy.wait()

    shape = jax.ShapeDtypeStruct((count, 5, H, F), BF16)
    return call(
        body,
        SimpleNamespace(features=(features, HBM), coords=(coords, HBM)),
        SimpleNamespace(up=shape, down=shape),
        dict(s_coords=(coords.shape, F32), sems=pltpu.SemaphoreType.DMA((2 * count + 1,))),
        grant_mb=54,
    )


def gradient_call(sz, scal, sets):
    A, H, E, F = sz.atoms, sz.halo, sz.rows, sz.width
    count = len(sets[0])
    K = sz.factors
    w1, w2, w3 = sz.widths
    w4, w5 = 4 * F // sz.space, F // sz.space
    half = F // 2
    arrays = SimpleNamespace(scal=(scal, SMEM))
    for role in (FIRST, SECOND):
        for m in range(count):
            for name in FACTORS:
                setattr(arrays, f"{name}_{role}_{m}", (getattr(sets[role][m], name), VMEM))

    def body(r, role):
        def get(name, m):
            return getattr(r, f"{name}_{role}_{m}")

        for m in range(count):
            r.up[m, 0:4] = get("rim_high", m)[...]
            r.down[m, 0:4] = get("rim_low", m)[...]
            places = get("gplaces", m)
            r.up[m, 4] = packed_places([places[c : c + 1, H + A : E] for c in range(3)], F)
            r.down[m, 4] = packed_places([places[c : c + 1, 0:H] for c in range(3)], F)
            for c in range(3):
                r.mine[m, c] = places[c : c + 1, H : H + A]
            r.left[:, m * K : (m + 1) * K] = jnp.transpose(get("left", m)[...])
        filt = jnp.transpose(sum(get("gfilt", m)[...] for m in range(count)) * 0.5)
        norm = sum(get("gnorm", m)[...] for m in range(count))
        r.right[...] = jnp.zeros_like(r.right)
        core = r.scal[2]
        for k in range(sz.space):
            for m in range(count):
                at = m * K
                r.right[at : at + E, 0:w1] = get("gproj", m)[:, k * w1 : (k + 1) * w1]
                at += E
                r.right[at : at + 3 * A, w1 : w1 + w2] = get("gvproj", m)[:, k * w2 : (k + 1) * w2]
                at += 3 * A
                r.right[at : at + A, w1 + w2 : sz.spare] = get("gout", m)[:, k * w3 : (k + 1) * w3]
            r.packed[...] = dot(r.left[...], r.right[...])
            spare = slice(sz.spare, sz.spare + sz.basis)
            r.packed[0:w4, spare] = filt[k * w4 : (k + 1) * w4, :]
            narrow = slice(sz.spare, sz.spare + w5)
            r.packed[half : half + 1, narrow] = norm[0:1, k * w5 : (k + 1) * w5]
            r.packed[half + 8 : half + 9, narrow] = norm[1:2, k * w5 : (k + 1) * w5]
            r.send[k] = r.packed[pl.ds(pl.multiple_of((1 - core) * half, half), half), :].astype(BF16)
            r.stay[k] = r.packed[pl.ds(pl.multiple_of(core * half, half), half), :]

    def both(r):
        for role in (FIRST, SECOND):
            pl.when(r.scal[0] == role)(lambda role=role: body(r, role))

    shape = jax.ShapeDtypeStruct
    return call(
        both,
        arrays,
        SimpleNamespace(
            up=shape((count, 5, H, F), BF16),
            down=shape((count, 5, H, F), BF16),
            mine=shape((count, 3, 1, A), F32),
            send=shape((sz.space, half, sz.packed), BF16),
            stay=shape((sz.space, half, sz.packed), F32),
        ),
        dict(
            left=((F, count * K), BF16),
            right=((count * K, sz.packed), BF16),
            packed=((F, sz.packed), F32),
        ),
    )


def result_call(sz, scal, fresh, back, from_low, from_high, mine):
    A, H, F = sz.atoms, sz.halo, sz.width
    count = len(back[0])
    arrays = SimpleNamespace(
        scal=(scal, SMEM), low=(from_low, VMEM), high=(from_high, VMEM), mine=(mine, VMEM)
    )
    for role in (FIRST, SECOND):
        for m in range(count):
            setattr(arrays, f"fresh_{role}_{m}", (fresh[role][m], VMEM))
            setattr(arrays, f"back_{role}_{m}", (back[role][m], VMEM))

    def body(r, role):
        for m in range(count):
            r.outputs[0, m, 0] = getattr(r, f"fresh_{role}_{m}")[...]
            whole = getattr(r, f"back_{role}_{m}")
            r.grads[0, m, 0, :, 0:H, :] = whole[:, 0:H, :] + r.low[m, 0:4].astype(F32)
            r.grads[0, m, 0, :, H : A - H, :] = whole[:, H : A - H, :]
            r.grads[0, m, 0, :, A - H :, :] = whole[:, A - H :, :] + r.high[m, 0:4].astype(F32)
            for c in range(3):
                edge = [
                    unpacked_places(r.low[m, 4], c, H),
                    jnp.zeros((1, A - 2 * H), F32),
                    unpacked_places(r.high[m, 4], c, H),
                ]
                r.places[m, c] = r.mine[m, c] + jnp.concatenate(edge, axis=1)

    def both(r):
        for role in (FIRST, SECOND):
            pl.when(r.scal[0] == role)(lambda role=role: body(r, role))

    shape = jax.ShapeDtypeStruct
    return call(
        both,
        arrays,
        SimpleNamespace(
            outputs=shape((1, count, 1, 4, A, F), BF16),
            grads=shape((1, count, 1, 4, A, F), F32),
            places=shape((count, 3, 1, A), F32),
        ),
        {},
    )


def share_call(sz, scal, total, other):
    F = sz.width
    w1, w2, w3 = sz.widths
    w4, w5 = 4 * F // sz.space, F // sz.space
    half = F // 2

    def body(r, first, second):
        for at, part in ((0, first), (half, second)):
            r.qkv[0, at : at + half, :] = part[:, :w1]
            r.vector[0, at : at + half, :] = part[:, w1 : w1 + w2]
            r.out[0, at : at + half, :] = part[:, w1 + w2 : sz.spare]
        r.filt[0] = jnp.transpose(first[:w4, sz.spare : sz.spare + sz.basis])
        r.gain[...] = second[0:1, sz.spare : sz.spare + w5]
        r.bias[...] = second[8:9, sz.spare : sz.spare + w5]

    def both(r):
        pl.when(r.scal[2] == 0)(lambda: body(r, r.total, r.other))
        pl.when(r.scal[2] == 1)(lambda: body(r, r.other, r.total))

    shape = jax.ShapeDtypeStruct
    return call(
        both,
        SimpleNamespace(scal=(scal, SMEM), total=(total, VMEM), other=(other, VMEM)),
        SimpleNamespace(
            gain=shape((1, w5), F32),
            bias=shape((1, w5), F32),
            qkv=shape((1, F, w1), F32),
            vector=shape((1, F, w2), F32),
            filt=shape((1, sz.basis, w4), F32),
            out=shape((1, F, w3), F32),
        ),
        {},
    )


def on_device(
    features,
    coords,
    neighbours,
    counts,
    shifts,
    norm_gain,
    norm_bias,
    qkv_weight,
    vector_weight,
    filter_weight,
    out_weight,
    cotangent,
):
    micro_count = features.shape[0]
    space = lax.axis_size("space")
    section = lax.axis_index("section")
    slab = lax.axis_index("space")
    core = lax.axis_index("dp")
    sz = Sizes(features.shape[3], features.shape[4], filter_weight.shape[1], neighbours.shape[2], space)
    up = [(i, (i + 1) % space) for i in range(space)]
    down = [((i + 1) % space, i) for i in range(space)]

    scal = jnp.stack([section, slab, core, space - 1]).astype(jnp.int32)
    places = jnp.transpose(coords, (0, 2, 1, 3))
    norms = jnp.concatenate([norm_gain, norm_bias], axis=0).astype(F32)
    borders = border_call(sz, features, places)
    pack_low = lax.ppermute(borders.up, "space", up)
    pack_high = lax.ppermute(borders.down, "space", down)
    both = ("section", "space")
    forth = [(k, space + k) for k in range(space)]
    forth_up = [(k, space + (k + 1) % space) for k in range(space)]
    forth_down = [((k + 1) % space, space + k) for k in range(space)]
    back = [(space + k, k) for k in range(space)]
    back_up = [(space + k, (k + 1) % space) for k in range(space)]
    back_down = [(space + (k + 1) % space, k) for k in range(space)]

    def geometry_inputs(place):
        return SimpleNamespace(
            scal=(scal, SMEM),
            pack_low=(pack_low, VMEM),
            pack_high=(pack_high, VMEM),
            coords=(places, place),
            nbr=(neighbours, place),
            counts=(counts, place),
            shifts=(shifts, place),
            wfilt=(filter_weight, place),
        )

    firsts, sent = [], []
    for m in range(micro_count):
        arrays = geometry_inputs(HBM)
        arrays.features = (features, HBM)
        arrays.norms = (norms, VMEM)
        arrays.wqkv, arrays.wvec, arrays.wout = (
            (qkv_weight, HBM), (vector_weight, HBM), (out_weight, HBM)
        )
        first = first_call(sz, m, arrays)
        firsts.append(first)
        sent.append((
            lax.ppermute(first.fresh, both, forth),
            lax.ppermute(first.tail, both, forth_up),
            lax.ppermute(first.head, both, forth_down),
        ))
    filters = [filter_call(sz, m, geometry_inputs(VMEM)) for m in range(micro_count)]
    for made, geo in zip(filters, lax.optimization_barrier([made.geo for made in filters])):
        made.geo = geo

    def both_inputs(m):
        made = filters[m]
        return SimpleNamespace(
            scal=(scal, SMEM),
            norms=(norms, VMEM),
            wqkv=(qkv_weight, VMEM),
            wvec=(vector_weight, VMEM),
            wfilt=(filter_weight, VMEM),
            wout=(out_weight, VMEM),
            geo=(made.geo, VMEM),
            smear=(made.smear, VMEM),
            cut_wide=(made.cut_wide, VMEM),
            units=(made.units, VMEM),
            silu=(made.silu, VMEM),
            slope=(made.slope, VMEM),
        )

    seconds, returned = [], []
    for m in range(micro_count):
        arrays = both_inputs(m)
        own, low, high = sent[m]
        arrays.own, arrays.low, arrays.high = (own, VMEM), (low, VMEM), (high, VMEM)
        arrays.cotangent = (cotangent, VMEM)
        second = both_call(sz, m, True, arrays)
        seconds.append(second)
        back_low, rim_low, rim_high = second.back_low, second.rim_low, second.rim_high
        if m:
            _, inc_low, inc_high = returned[-1]
            inc_low, inc_high, back_low, rim_low, rim_high = lax.optimization_barrier(
                (inc_low, inc_high, back_low, rim_low, rim_high)
            )
            returned[-1] = (returned[-1][0], inc_low, inc_high)
        returned.append((
            lax.ppermute(back_low, both, back),
            lax.ppermute(rim_high, both, back_up),
            lax.ppermute(rim_low, both, back_down),
        ))
    thirds = []
    for m in range(micro_count):
        arrays = both_inputs(m)
        arrays.pack_low, arrays.pack_high = (pack_low, VMEM), (pack_high, VMEM)
        arrays.features = (features, VMEM)
        arrays.scalar_in = (firsts[m].scalar_out, VMEM)
        arrays.score = (firsts[m].score, VMEM)
        inc, inc_low, inc_high = returned[m]
        arrays.inc, arrays.inc_low, arrays.inc_high = (inc, VMEM), (inc_low, VMEM), (inc_high, VMEM)
        thirds.append(both_call(sz, m, False, arrays))

    shares = gradient_call(sz, scal, (thirds, seconds))
    summed = shares.stay + lax.ppermute(shares.send, "dp", [(0, 1), (1, 0)]).astype(F32)
    pieces = summed.astype(BF16)
    total = lax.dynamic_index_in_dim(summed, slab, 0, keepdims=False)
    for hop in range(1, space):
        piece = lax.dynamic_index_in_dim(pieces, (slab + hop) % space, 0, keepdims=False)
        total = total + lax.ppermute(
            piece, "space", [(i, (i + hop) % space) for i in range(space)]
        ).astype(F32)
    from_low = lax.ppermute(shares.up, "space", up)
    from_high = lax.ppermute(shares.down, "space", down)
    results = result_call(
        sz,
        scal,
        ([v.fresh for v in firsts], [v.fresh for v in seconds]),
        ([v.back for v in thirds], [v.back for v in seconds]),
        from_low,
        from_high,
        shares.mine,
    )
    places_sum = results.places + lax.ppermute(results.places, "section", [(0, 1), (1, 0)])
    other = lax.ppermute(total, "dp", [(0, 1), (1, 0)])
    share = share_call(sz, scal, total, other)
    return (
        results.outputs,
        results.grads,
        share.gain,
        share.bias,
        share.qkv,
        share.vector,
        share.filt,
        share.out,
        jnp.transpose(places_sum, (0, 2, 1, 3)),
    )


def solution(mesh):
    return jax.shard_map(
        on_device,
        mesh=mesh,
        in_specs=(
            P(None, "dp", None, "space", None),
            P(None, "dp", None, "space"),
            P(None, "dp", None, "space"),
            P(None, "dp", "space"),
            P(None, "dp", None, None, "space"),
            P("section", None),
            P("section", None),
            P("section", None, None),
            P("section", None, None),
            P("section", None, None),
            P("section", None, None),
            P(None, "dp", None, "space", None),
        ),
        out_specs=(
            P("section", None, "dp", None, "space", None),
            P("section", None, "dp", None, "space", None),
            P("section", "space"),
            P("section", "space"),
            P("section", None, "space"),
            P("section", None, "space"),
            P("section", None, "space"),
            P("section", None, "space"),
            P(None, "dp", None, "space"),
        ),
        check_vma=False,
    )
```

```python
import math
from types import SimpleNamespace

import jax
import jax.numpy as jnp
from jax import lax
from jax.experimental import pallas as pl
from jax.experimental.pallas import tpu as pltpu
from jax.sharding import PartitionSpec as P

HEADS = 8
CUTOFF = 5.0
LN_EPS = 1e-05
SOFTEN = 0.25
CROSS = 2.5
GROUP = 4
LANES = 128
SUBLANES = 8
FIRST, SECOND = 0, 1

F32 = jnp.float32
BF16 = jnp.bfloat16
VMEM = pl.BlockSpec(memory_space=pltpu.VMEM)
SMEM = pl.BlockSpec(memory_space=pltpu.SMEM)
HBM = pl.BlockSpec(memory_space=pltpu.HBM)


def dot(left, right, left_dim=1, right_dim=0):
    return lax.dot_general(
        left, right, (((left_dim,), (right_dim,)), ((), ())), preferred_element_type=F32
    )


def iota(shape, dim):
    return lax.broadcasted_iota(jnp.int32, shape, dim)


def packed_places(parts, width):
    row = jnp.concatenate(parts, axis=1)
    high = row.astype(BF16).astype(F32)
    rest = row - high
    middle = rest.astype(BF16).astype(F32)
    rows = jnp.concatenate([high, middle, rest - middle, jnp.zeros((13, row.shape[1]), F32)], axis=0)
    return jnp.concatenate([rows, jnp.zeros((16, width - row.shape[1]), F32)], axis=1).astype(BF16)


def unpacked_places(block, c, count):
    rows = block[:, c * count : (c + 1) * count].astype(F32)
    return rows[0:1] + rows[1:2] + rows[2:3]


class Sizes:
    def __init__(self, atoms, width, basis, slots, space):
        self.atoms, self.width, self.basis, self.slots, self.space = atoms, width, basis, slots, space
        self.halo = atoms // 4
        self.rows = atoms + 2 * self.halo
        self.blocks = slots // GROUP
        self.edges = GROUP * atoms
        self.halves = width // LANES
        self.window = atoms + SUBLANES
        self.sent = atoms
        self.widths = (5 * width // space, 3 * width // space, 3 * width // space)
        self.spare = sum(self.widths)
        self.packed = -(-(self.spare + basis) // 16) * 16
        self.factors = -(-(self.rows + 4 * atoms) // LANES) * LANES


def halves_of(sz):
    return [slice(cg * LANES, (cg + 1) * LANES) for cg in range(sz.halves)]


def first_row(b):
    return GROUP * b + jnp.where(b >= 4, 1, 0)


def sharpness_of(basis):
    return (2.0 / basis * (1.0 - math.exp(-CUTOFF))) ** (-2)


def write_centres(ref, basis):
    low_end = math.exp(-CUTOFF)
    step = iota(ref.shape, 0).astype(F32) / (basis - 1)
    ref[...] = low_end * (1.0 - step) + step


def edge_geometry(r, sz, m, coords, slots):
    A, H, E, EB, K = sz.atoms, sz.halo, sz.rows, sz.edges, sz.slots
    lane = iota((8, LANES), 1)
    row = iota((8, LANES), 0)
    slab, last = r.scal[1], r.scal[3]
    spot = iota((1, LANES), 1)
    length_x = (last + 1).astype(F32) * (A * 4.0 / H)
    places = []
    for c in range(3):
        places.append(
            jnp.concatenate(
                [
                    unpacked_places(r.pack_low[m, 4], c, H),
                    coords[c],
                    unpacked_places(r.pack_high[m, 4], c, H),
                    jnp.zeros((1, LANES - E), F32),
                ],
                axis=1,
            )
        )
    places.append(
        jnp.where((spot < H) & (slab == 0), -length_x, 0.0)
        + jnp.where((spot >= H + A) & (slab == last), length_x, 0.0)
    )
    near = []
    for c in range(4):
        y = jnp.broadcast_to(places[c], (8, LANES))
        for bit in range(3):
            y = jnp.where((row >> bit) & 1 == 1, pltpu.roll(y, LANES - GROUP * 2**bit, 1), y)
        y = jnp.where(row >= 4, pltpu.roll(y, LANES - 1, 1), y)
        first = jnp.where(lane < A, y, pltpu.roll(y, A - 1, 1))
        other = jnp.where(lane < A, pltpu.roll(y, LANES - 2, 1), pltpu.roll(y, A - 3, 1))
        near.append(jnp.concatenate([first, other], axis=1))
    wide_lane = iota((8, EB), 1)
    wide_row = iota((8, EB), 0)
    wanted = GROUP * wide_row + wide_lane // A + jnp.where(wide_row >= 4, 1, 0) + wide_lane % A
    alive = iota((K, A), 0) < slots[3 * K : 3 * K + 1, :]
    code = jnp.where(alive, 16, 0) + (slots[K : 2 * K, :] + 1) * 4 + (slots[2 * K : 3 * K, :] + 1)
    code = jnp.concatenate([code] * GROUP, axis=1)
    named = jnp.concatenate([slots[0:K, :]] * GROUP, axis=1)
    found = jnp.zeros((8, EB), jnp.int32)
    for n in range(K):
        found = found + jnp.where(named[n : n + 1, :] == wanted, code[n : n + 1, :], 0)
    live = (found >> 4).astype(F32)
    offsets = (
        near[3],
        (((found >> 2) & 3) - 1).astype(F32) * CROSS,
        ((found & 3) - 1).astype(F32) * CROSS,
    )
    sep = []
    for c in range(3):
        mine = coords[c]
        sep.append(near[c] - jnp.concatenate([mine] * GROUP, axis=1) + offsets[c])
    distance = jnp.sqrt(sep[0] * sep[0] + sep[1] * sep[1] + sep[2] * sep[2] + SOFTEN)
    inside = distance < CUTOFF
    cut = jnp.where(inside, 0.5 * (jnp.cos(math.pi * distance / CUTOFF) + 1.0), 0.0) * live
    for index, value in enumerate(
        sep + [distance, live, cut, jnp.exp(-distance)] + [part / distance for part in sep]
    ):
        r.geo[index] = value


DISTANCE, LIVE, CUT, SHRINK, UNIT = 3, 4, 5, 6, 7


def bell_of(r, sz, b):
    delta = r.geo[SHRINK, pl.ds(b, 1), :] - r.centres[...]
    return delta, jnp.exp(-sharpness_of(sz.basis) * delta * delta)


def write_edge_tables(r, sz, b, wide_kind):
    A, EB = sz.atoms, sz.edges
    cut = r.geo[CUT, pl.ds(b, 1), :]
    _, bell = bell_of(r, sz, b)
    smear = cut * bell
    if hasattr(r, "smear"):
        r.smear[b] = smear.astype(BF16)
    r.smear_t[b] = jnp.transpose(smear).astype(BF16)
    coarse = cut.astype(BF16).astype(F32)
    which = iota((16, EB), 0)
    pair = jnp.where(which == 0, coarse, jnp.where(which == 1, cut - coarse, 0.0)).astype(BF16)
    r.cut_wide[b] = dot(pair, jnp.ones((16, LANES), BF16), 0, 0).astype(wide_kind)
    for c in range(3):
        r.units[b, c * A : (c + 1) * A, :] = (
            r.diag[...] * r.geo[UNIT + c, pl.ds(b, 1), :]
        ).astype(BF16)


def write_constants(r, sz):
    A, EB, F = sz.atoms, sz.edges, sz.width
    if hasattr(r, "centres"):
        write_centres(r.centres, sz.basis)
    if hasattr(r, "diag"):
        r.diag[...] = jnp.where(iota((A, EB), 1) % A == iota((A, EB), 0), 1.0, 0.0)
    if hasattr(r, "fold"):
        r.fold[...] = jnp.where(iota((A, EB), 1) % A == iota((A, EB), 0), 1.0, 0.0).astype(BF16)
    if hasattr(r, "heads"):
        r.heads[...] = jnp.where(
            iota((F, F), 0) // (F // HEADS) == iota((F, F), 1) // (F // HEADS), 0.5, 0.0
        ).astype(BF16)


def node_part(r, sz, own, low, high, wqkv):
    A, H, E, F, CG = sz.atoms, sz.halo, sz.rows, sz.width, sz.halves
    halves = halves_of(sz)
    scalars = jnp.concatenate([low[0, 0:H], own[0], high[0, 0:H]], axis=0).astype(F32)
    centred = scalars - jnp.mean(scalars, axis=-1, keepdims=True)
    spread = jnp.mean(centred * centred, axis=-1, keepdims=True)
    scale = lax.rsqrt(spread + LN_EPS)
    normed = (centred * scale * r.norms[0:1, :] + r.norms[1:2, :]).astype(BF16)
    left = r.left
    left[0:E, :] = normed
    left[E : E + 3 * A, :] = own[1:4].reshape(3 * A, F)
    left[E + 4 * A :, :] = jnp.zeros((sz.factors - E - 4 * A, F), BF16)
    for part in range(5):
        projected = dot(normed, wqkv[:, part * F : (part + 1) * F])
        for cg in range(CG):
            if part == 0:
                r.query[cg] = projected[H : H + A, halves[cg]]
            else:
                r.kv[(part - 1) * CG + cg] = projected[:, halves[cg]]
    for c in range(3):
        for cg in range(CG):
            r.vec[c * CG + cg, 0:H, :] = low[c + 1, 0:H, halves[cg]].astype(F32)
            r.vec[c * CG + cg, H : H + A, :] = own[c + 1][:, halves[cg]].astype(F32)
            r.vec[c * CG + cg, H + A : E, :] = high[c + 1, 0:H, halves[cg]].astype(F32)
    return centred * scale, scale


def buffers(r, sz, which):
    end = str(which)
    return SimpleNamespace(**{k[:-1]: v for k, v in vars(r).items() if k.endswith(end)})


def tiles(sz, first):
    A = sz.atoms
    for kk in range(GROUP):
        for cg in range(sz.halves):
            yield (
                cg,
                slice(kk * A, (kk + 1) * A),
                slice(cg * LANES, (cg + 1) * LANES),
                pl.ds(first + kk, A),
            )


def stacked(sz, first, tile):
    made = [tile(*where) for where in tiles(sz, first)]
    CG = sz.halves
    wholes = []
    for index in range(len(made[0])):
        lines = [
            jnp.concatenate([made[kk * CG + cg][index] for cg in range(CG)], axis=1)
            for kk in range(GROUP)
        ]
        wholes.append(jnp.concatenate(lines, axis=0))
    return wholes


def vector_dot(r, sz):
    A, F, vp = sz.atoms, sz.width, r.vproj
    return sum(
        vp[c * A : (c + 1) * A, 0:F] * vp[c * A : (c + 1) * A, F : 2 * F] for c in range(3)
    )


def write_layer_output(r, sz, own, out_proj, vec_dot, vector_agg):
    A, H, F, vp = sz.atoms, sz.halo, sz.width, r.vproj
    for index in range(4):
        if index == 0:
            fresh = vec_dot * out_proj[:, F : 2 * F] + out_proj[:, 2 * F :]
        else:
            rows = slice((index - 1) * A, index * A)
            fresh = vp[rows, 2 * F :] * out_proj[:, 0:F] + vector_agg[index - 1]
        fresh = (own[index].astype(F32) + fresh).astype(BF16)
        r.fresh[index] = fresh
        if hasattr(r, "head"):
            r.head[index, 0:H, :] = fresh[:H]
            r.tail[index, 0:H, :] = fresh[A - H :]


def first_forward(r, sz, m, fetch):
    A, H, E, F, EB = sz.atoms, sz.halo, sz.rows, sz.width, sz.edges
    CG = sz.halves
    moves = [
        (r.coords.at[m], "s_coords"),
        (r.slots.at[m], "s_slots"),
        (r.features.at[m, 0], "s_own"),
        (r.wqkv.at[0], "s_wqkv"),
        (r.wh, "s_wh"),
        (r.wvec.at[0], "s_wvec"),
        (r.wout.at[0], "s_wout"),
    ]
    early = moves[:4]
    copies = []
    for i, (source, name) in enumerate(moves):
        if fetch:
            copies.append(pltpu.make_async_copy(source, getattr(r, name), r.sems.at[i]))
            copies[-1].start()
        else:
            setattr(r, name, source)
    write_constants(r, sz)
    r.sagg[...] = jnp.zeros_like(r.sagg)
    r.vagg[...] = jnp.zeros_like(r.vagg)
    for copy in copies[: len(early)]:
        copy.wait()
    edge_geometry(r, sz, m, r.s_coords, r.s_slots)

    def tables(b, carry):
        write_edge_tables(r, sz, b, F32)
        return carry

    lax.fori_loop(0, sz.blocks, tables, 0, unroll=2)
    own = r.s_own
    node_part(r, sz, own, r.pack_low.at[m], r.pack_high.at[m], r.s_wqkv)
    for copy in copies[len(early) :]:
        copy.wait()
    r.vproj[...] = dot(r.left[E : E + 3 * A, :], r.s_wvec[...])

    def filter_part(b, part):
        return dot(r.smear_t[b], r.s_wh[:, part * F : (part + 1) * F])

    def block(b, w):
        first = first_row(b)
        half = filter_part(b, 0)
        for cg, at, cols, near_rows in tiles(sz, first):
            h = half[at, cols]
            product = r.query[cg] * r.kv[cg, near_rows, :] * (h + h * jnp.tanh(h))
            coarse = product.astype(BF16)
            w.pack1[at, cols] = coarse
            w.pack2[at, cols] = (product - coarse.astype(F32)).astype(BF16)
        score = dot(w.pack1[...], r.heads[...]) + dot(w.pack2[...], r.heads[...])
        for cg in range(CG):
            r.score[b, cg] = score[:, cg * LANES : (cg + 1) * LANES].astype(BF16)
        half = filter_part(b, 2)
        for cg, at, cols, near_rows in tiles(sz, first):
            h = half[at, cols]
            value = r.kv[2 * CG + cg, near_rows, :] * (h + h * jnp.tanh(h))
            for c in range(3):
                r.vagg[c * CG + cg] += r.vec[c * CG + cg, near_rows, :] * value
        half = filter_part(b, 3)
        for cg, at, cols, near_rows in tiles(sz, first):
            h = half[at, cols]
            value = r.kv[3 * CG + cg, near_rows, :] * (h + h * jnp.tanh(h))
            r.third[b, at, cols] = value.astype(BF16)
        half = filter_part(b, 1)
        for cg, at, cols, near_rows in tiles(sz, first):
            h = half[at, cols]
            s = score[at, cols]
            attention = (s + s * jnp.tanh(s)) * r.cut_wide[b, at, :]
            r.sagg[cg] += attention * (r.kv[CG + cg, near_rows, :] * (h + h * jnp.tanh(h)))

    def pair(i, carry):
        for which in range(2):
            block(2 * i + which, buffers(r, sz, which))
        return carry

    lax.fori_loop(0, sz.blocks // 2, pair, 0)
    third = sum(dot(r.units[b], r.third[b]) for b in range(sz.blocks))
    scalar_low = jnp.concatenate([r.sagg[cg] for cg in range(CG)], axis=1).astype(BF16)
    r.o_scalar[...] = scalar_low
    out_proj = dot(scalar_low, r.s_wout[...])
    vector_agg = [
        jnp.concatenate([r.vagg[c * CG + cg] for cg in range(CG)], axis=1)
        + third[c * A : (c + 1) * A, :]
        for c in range(3)
    ]
    write_layer_output(r, sz, own, out_proj, vector_dot(r, sz), vector_agg)
    if not fetch:
        return
    copies = [
        pltpu.make_async_copy(source, target, r.sems.at[i])
        for i, (source, target) in enumerate([
            (r.fresh, r.out_fresh),
            (r.head, r.out_head),
            (r.tail, r.out_tail),
            (r.o_scalar, r.out_scalar),
            (r.score, r.out_score),
        ])
    ]
    for copy in copies:
        copy.start()
    for copy in copies:
        copy.wait()


def edge_filters(r, sz, which):
    F = sz.width
    write_constants(r, sz)
    for m in which:
        w = SimpleNamespace(**vars(r))
        vars(w).update(vars(buffers(r, sz, m)))
        edge_geometry(w, sz, m, r.coords.at[m], r.slots.at[m])

        def block(b, carry, w=w):
            write_edge_tables(w, sz, b, BF16)
            for part in range(4):
                cols = slice(part * F, (part + 1) * F)
                h = dot(r.smear_t[b], r.wh[:, cols])
                t = jnp.tanh(h)
                f = h + h * t
                f, t = f.astype(BF16), t.astype(BF16)
                slope = (1.0 + t) + f * (1.0 - t)
                for cg in range(sz.halves):
                    half = slice(cg * LANES, (cg + 1) * LANES)
                    w.silu[b, part * sz.halves + cg] = f[:, half]
                    w.slope[b, part * sz.halves + cg] = slope[:, half]
            return carry

        lax.fori_loop(0, sz.blocks, block, 0, unroll=2)


def both_ways(r, sz, m, fwd):
    A, H, E, F = sz.atoms, sz.halo, sz.rows, sz.width
    EB, CG, NB, W = sz.edges, sz.halves, sz.blocks, sz.window
    lane = iota((8, LANES), 1)
    row = iota((8, LANES), 0)
    halves = halves_of(sz)
    if fwd:
        own, low, high = r.own, r.low, r.high
    else:
        own, low, high = r.features.at[m, 0], r.pack_low.at[m], r.pack_high.at[m]
    wqkv, wvec, wout = r.wqkv.at[0], r.wvec.at[0], r.wout.at[0]
    write_constants(r, sz)
    xhat, scale = node_part(r, sz, own, low, high, wqkv)
    gain = r.norms[0:1, :]
    left = r.left
    vp = r.vproj
    vp[...] = dot(left[E : E + 3 * A, :], wvec[...])
    for cg in range(CG):
        r.query_low[:, halves[cg]] = r.query[cg].astype(BF16)

    if fwd:
        r.sagg[...] = jnp.zeros_like(r.sagg)
        r.vagg[...] = jnp.zeros_like(r.vagg)
        r.uagg[...] = jnp.zeros_like(r.uagg)

        def forward_block(b, carry):
            first = first_row(b)

            def filters(part, cg, at):
                return r.silu[b, part * CG + cg, at, :]

            def keys(cg, at, cols, near_rows):
                product = r.query[cg] * r.kv[cg, near_rows, :] * filters(0, cg, at).astype(F32)
                coarse = product.astype(BF16)
                return coarse, (product - coarse.astype(F32)).astype(BF16)

            coarse, fine = stacked(sz, first, keys)
            score = dot(coarse, r.heads[...]) + dot(fine, r.heads[...])
            for cg in range(CG):
                r.score[b, cg] = score[:, halves[cg]].astype(BF16)

            def vectors(cg, at, cols, near_rows):
                value = r.kv[2 * CG + cg, near_rows, :].astype(BF16) * filters(2, cg, at)
                return [
                    r.vec[c * CG + cg, near_rows, :].astype(BF16) * value for c in range(3)
                ] + [r.kv[3 * CG + cg, near_rows, :].astype(BF16) * filters(3, cg, at)]

            moved = stacked(sz, first, vectors)
            for c in range(3):
                r.vagg[c] += dot(r.fold[...], moved[c])
            r.uagg[...] += dot(r.units[b], moved[3])

            def scalars(cg, at, cols, near_rows):
                s = r.score[b, cg, at, :]
                attention = s * (1.0 + jnp.tanh(s)) * r.cut_wide[b, at, :]
                return [
                    attention * (r.kv[CG + cg, near_rows, :].astype(BF16) * filters(1, cg, at))
                ]

            r.sagg[...] += dot(r.fold[...], *stacked(sz, first, scalars))
            return carry

        lax.fori_loop(0, NB, forward_block, 0, unroll=4)
        scalar_low = r.sagg[...].astype(BF16)
    else:
        scalar_low = r.scalar_in[...]
    left[E + 3 * A : E + 4 * A, :] = scalar_low
    out_proj = dot(scalar_low, wout[...])
    vec_dot = vector_dot(r, sz)
    if fwd:
        vector_agg = [r.vagg[c] + r.uagg[c * A : (c + 1) * A, :] for c in range(3)]
        write_layer_output(r, sz, own, out_proj, vec_dot, vector_agg)

    def incoming(index):
        if fwd:
            return r.cotangent[m, 0, index].astype(F32)
        gap = jnp.zeros((A - 2 * H, F), F32)
        edge = [r.inc_low[index, 0:H].astype(F32), gap, r.inc_high[index, 0:H].astype(F32)]
        value = r.inc[index].astype(F32) + jnp.concatenate(edge, axis=0)
        return value.astype(BF16).astype(F32)

    g_x = incoming(0)
    r.gx[0] = g_x
    g_first = jnp.zeros((A, F), F32)
    g_mid = g_x * out_proj[:, F : 2 * F]
    for c in range(3):
        g_vec = incoming(c + 1)
        r.gx[c + 1] = g_vec
        rows = slice(c * A, (c + 1) * A)
        r.gvlow[rows, :] = g_vec.astype(BF16)
        g_first = g_first + g_vec * vp[rows, 2 * F :]
        r.gvproj[rows, 0:F] = (g_mid * vp[rows, F : 2 * F]).astype(BF16)
        r.gvproj[rows, F : 2 * F] = (g_mid * vp[rows, 0:F]).astype(BF16)
        r.gvproj[rows, 2 * F :] = (g_vec * out_proj[:, 0:F]).astype(BF16)
    r.gout[:, 0:F] = g_first.astype(BF16)
    r.gout[:, F : 2 * F] = (g_x * vec_dot).astype(BF16)
    r.gout[:, 2 * F :] = g_x.astype(BF16)
    r.gs[...] = dot(r.gout[...], wout[...], 1, 1).astype(BF16)
    for total in (r.gnear, r.gq, r.gfilt):
        total[...] = jnp.zeros_like(total)

    def backward_block(b, carry):
        first = first_row(b)
        base = pl.multiple_of(first // SUBLANES * SUBLANES, SUBLANES)
        lanes = iota((W, EB), 1)
        place = jnp.where(
            lanes % A + lanes // A + (first - base) == iota((W, EB), 0), 1.0, 0.0
        ).astype(BF16)

        def collect(index, terms):
            r.gnear[index, pl.ds(base, W), :] += dot(place, terms)

        def filters(part, cg, at):
            return r.silu[b, part * CG + cg, at, :], r.slope[b, part * CG + cg, at, :]

        def weights(cg, at, cols, near_rows):
            value = r.kv[CG + cg, near_rows, :].astype(BF16)
            return [r.gs[:, cols] * (value * filters(1, cg, at)[0])]

        g_att = dot(*stacked(sz, first, weights), r.heads[...])

        def vectors(cg, at, cols, near_rows):
            f, slope = filters(2, cg, at)
            value = r.kv[2 * CG + cg, near_rows, :].astype(BF16)
            message = value * f
            moved = []
            for c in range(3):
                g_vec = r.gvlow[c * A : (c + 1) * A, cols]
                term = g_vec * r.vec[c * CG + cg, near_rows, :].astype(BF16)
                g_edge = term if c == 0 else g_edge + term
                moved.append(g_vec * message)
            return moved + [g_edge * f, g_edge * (value * slope)]

        *moved, g_value, g_pre = stacked(sz, first, vectors)
        for c in range(3):
            collect(4 + c, moved[c])
        collect(2, g_value)
        pre = [None, None, g_pre, None]
        g_third = dot(r.units[b], r.gvlow[...], 0, 0)

        def units(cg, at, cols, near_rows):
            f, slope = filters(3, cg, at)
            value = r.kv[3 * CG + cg, near_rows, :].astype(BF16)
            g_edge = g_third[at, cols].astype(BF16)
            return value * f, g_edge * f, g_edge * (value * slope)

        message, g_value, pre[3] = stacked(sz, first, units)
        collect(3, g_value)
        g_unit = dot(r.gvlow[...], message, 1, 1)
        for c in range(3):
            r.gunit[c, pl.ds(b, 1), :] = jnp.sum(
                g_unit[c * A : (c + 1) * A, :] * r.diag[...], axis=0, keepdims=True
            )

        def attention(cg, at, cols, near_rows):
            s = r.score[b, cg, at, :]
            t = jnp.tanh(s)
            up = 1.0 + t
            act = s * up
            wide = r.cut_wide[b, at, :]
            ga = g_att[at, cols].astype(BF16)
            g_score = ga * wide * (up + act * (1.0 - t))
            g_edge = r.gs[:, cols] * (act * wide)
            f, slope = filters(0, cg, at)
            key = r.kv[cg, near_rows, :].astype(BF16)
            query = r.query_low[:, cols]
            middle = g_score * f
            made = [ga * act, middle * key, middle * query, (g_score * slope) * (key * query)]
            f, slope = filters(1, cg, at)
            value = r.kv[CG + cg, near_rows, :].astype(BF16)
            return made + [g_edge * f, g_edge * (value * slope)]

        g_act, g_query, g_key, pre[0], g_value, pre[1] = stacked(sz, first, attention)
        r.gq[...] += dot(r.fold[...], g_query)
        collect(0, g_key)
        collect(1, g_value)
        g_cut = dot(jnp.ones((16, F), BF16), g_act, 1, 1)[0:1, :] * (2.0 * HEADS / F)
        g_smear = jnp.zeros((sz.basis, EB), F32)
        for part in range(4):
            cols = slice(part * F, (part + 1) * F)
            g_smear = g_smear + dot(r.wh[:, cols], pre[part], 1, 1)
            r.gfilt[:, cols] += dot(r.smear[b], pre[part])
        delta, bell = bell_of(r, sz, b)
        through = g_smear * bell
        r.gcut[pl.ds(b, 1), :] = g_cut + jnp.sum(through, axis=0, keepdims=True)
        r.gshrink[pl.ds(b, 1), :] = r.geo[CUT, pl.ds(b, 1), :] * jnp.sum(
            through * delta, axis=0, keepdims=True
        ) * (-2.0 * sharpness_of(sz.basis))
        return carry

    lax.fori_loop(0, NB, backward_block, 0)

    distance = r.geo[DISTANCE]
    g_dist = r.gcut[...] * r.geo[LIVE] * jnp.where(
        distance < CUTOFF,
        (-0.5 * math.pi / CUTOFF) * jnp.sin(math.pi * distance / CUTOFF),
        0.0,
    ) - r.gshrink[...] * r.geo[SHRINK]
    inverse = 1.0 / distance
    g_unit = [r.gunit[c] for c in range(3)]
    sep = [r.geo[c] for c in range(3)]
    along = g_unit[0] * sep[0] + g_unit[1] * sep[1] + g_unit[2] * sep[2]
    radial = (g_dist - along * inverse * inverse) * inverse
    r.gplaces[...] = jnp.zeros_like(r.gplaces)
    for c in range(3):
        g_sep = g_unit[c] * inverse + radial * sep[c]
        first, other = g_sep[:, :LANES], g_sep[:, LANES:]
        z = (
            jnp.where(lane < A, first, 0.0)
            + pltpu.roll(jnp.where(lane < A, 0.0, first), A + 1, 1)
            + pltpu.roll(jnp.where(lane < A, other, 0.0), 2, 1)
            + pltpu.roll(jnp.where(lane < A, 0.0, other), A + 3, 1)
        )
        for bit in range(3):
            z = jnp.where((row >> bit) & 1 == 1, pltpu.roll(z, GROUP * 2**bit, 1), z)
        z = jnp.where(row >= 4, pltpu.roll(z, 1, 1), z)
        total = jnp.sum(g_sep, axis=0, keepdims=True)
        mine = total[:, 0:A] + total[:, A : 2 * A] + total[:, 2 * A : 3 * A] + total[:, 3 * A :]
        mine = jnp.concatenate(
            [jnp.zeros((1, H), F32), mine, jnp.zeros((1, LANES - H - A), F32)], axis=1
        )
        r.gplaces[c : c + 1, :] = jnp.sum(z, axis=0, keepdims=True) - mine

    gproj = r.gproj
    gproj[:, 0:F] = jnp.zeros((E, F), BF16)
    gproj[H : H + A, 0:F] = r.gq[...].astype(BF16)
    for part in range(4):
        gproj[:, (part + 1) * F : (part + 2) * F] = r.gnear[part].astype(BF16)
    g_normed = dot(gproj[...], wqkv[...], 1, 1)
    u = gain * g_normed
    g_scalars = scale * (
        u
        - jnp.mean(u, axis=-1, keepdims=True)
        - xhat * jnp.mean(u * xhat, axis=-1, keepdims=True)
    )
    r.gnorm[...] = jnp.zeros_like(r.gnorm)
    r.gnorm[0:1, :] = jnp.sum(g_normed * xhat, axis=0, keepdims=True)
    r.gnorm[1:2, :] = jnp.sum(g_normed, axis=0, keepdims=True)
    vec_back = dot(r.gvproj[...], wvec[...], 1, 1)
    for index in range(4):
        if index == 0:
            whole = g_scalars
            middle = whole[H : H + A] + r.gx[0]
        else:
            c = index - 1
            whole = r.gnear[4 + c]
            middle = whole[H : H + A] + r.gx[index] + vec_back[c * A : (c + 1) * A, :]
        r.back[index] = middle
        r.back_low[index] = middle.astype(BF16)
        r.rim_low[index] = whole[0:H].astype(BF16)
        r.rim_high[index] = whole[H + A :].astype(BF16)


FACTORS = ("left", "gproj", "gvproj", "gout", "gfilt", "gnorm")
BORDERS = ("rim_low", "rim_high", "gplaces")


def call(body, arrays, outs, scratch, role=None, grant_mb=16, place=VMEM):
    arrays, outs = vars(arrays), vars(outs)
    names = list(arrays) + list(outs) + list(scratch)

    def kernel(*args):
        refs = SimpleNamespace(**dict(zip(names, args, strict=True)))
        if role is None:
            body(refs)
        else:
            pl.when(refs.scal[0] == role)(lambda: body(refs))

    results = pl.pallas_call(
        kernel,
        out_shape=list(outs.values()),
        in_specs=[spec for _, spec in arrays.values()],
        out_specs=[place for _ in outs],
        scratch_shapes=[
            pltpu.VMEM(*s) if isinstance(s, tuple) else s for s in scratch.values()
        ],
        compiler_params=pltpu.CompilerParams(vmem_limit_bytes=int(grant_mb * 2**20)),
    )(*[array for array, _ in arrays.values()])
    return SimpleNamespace(**dict(zip(outs, results, strict=True)))


def first_call(sz, m, fetch, arrays):
    A, H, E, F = sz.atoms, sz.halo, sz.rows, sz.width
    EB, CG, NB = sz.edges, sz.halves, sz.blocks
    shape = jax.ShapeDtypeStruct
    results = dict(
        fresh=((4, A, F), BF16),
        head=((4, sz.sent, F), BF16),
        tail=((4, sz.sent, F), BF16),
        o_scalar=((A, F), BF16),
        score=((NB, CG, EB, LANES), BF16),
    )
    fetched = dict(
        s_own=((4, A, F), BF16),
        s_coords=((3, 1, A), F32),
        s_slots=((3 * sz.slots + 8, A), jnp.int32),
        s_wqkv=((F, 5 * F), BF16),
        s_wvec=((F, 3 * F), BF16),
        s_wh=((sz.basis, 4 * F), BF16),
        s_wout=((F, 3 * F), BF16),
        sems=pltpu.SemaphoreType.DMA((9,)),
    )
    named = dict(fresh="out_fresh", head="out_head", tail="out_tail", o_scalar="out_scalar", score="out_score")
    outs = SimpleNamespace(**{(named[k] if fetch else k): shape(*v) for k, v in results.items()})
    scratch = dict(
        left=((sz.factors, F), BF16),
        query=((CG, A, LANES), F32),
        kv=((4 * CG, E, LANES), F32),
        vec=((3 * CG, E, LANES), F32),
        vproj=((3 * A, 3 * F), F32),
        heads=((F, F), BF16),
        diag=((A, EB), F32),
        geo=((10, 8, EB), F32),
        centres=((sz.basis, EB), F32),
        smear_t=((NB, EB, sz.basis), BF16),
        cut_wide=((NB, EB, LANES), F32),
        units=((NB, 3 * A, EB), BF16),
        pack10=((EB, F), BF16),
        pack20=((EB, F), BF16),
        pack11=((EB, F), BF16),
        pack21=((EB, F), BF16),
        sagg=((CG, A, LANES), F32),
        vagg=((3 * CG, A, LANES), F32),
        third=((NB, EB, F), BF16),
    )
    if fetch:
        scratch.update(results)
        scratch.update(fetched)
    made = call(
        lambda r: first_forward(r, sz, m, fetch),
        arrays,
        outs,
        scratch,
        FIRST,
        grant_mb=54 if fetch else 20,
        place=HBM if fetch else VMEM,
    )
    return SimpleNamespace(**{k: getattr(made, named[k] if fetch else k) for k in results})


def filter_call(sz, role, which, arrays):
    A, F = sz.atoms, sz.width
    EB, CG, NB = sz.edges, sz.halves, sz.blocks
    shape = jax.ShapeDtypeStruct
    outs = dict(
        geo=shape((10, 8, EB), F32),
        smear=shape((NB, sz.basis, EB), BF16),
        cut_wide=shape((NB, EB, LANES), BF16),
        units=shape((NB, 3 * A, EB), BF16),
        silu=shape((NB, 4 * CG, EB, LANES), BF16),
        slope=shape((NB, 4 * CG, EB, LANES), BF16),
    )
    scratch = dict(
        diag=((A, EB), F32),
        centres=((sz.basis, EB), F32),
        smear_t=((NB, EB, sz.basis), BF16),
    )
    made = call(
        lambda r: edge_filters(r, sz, which),
        arrays,
        SimpleNamespace(**{f"{k}{m}": v for m in which for k, v in outs.items()}),
        scratch,
        role,
        grant_mb=6,
    )
    return {m: SimpleNamespace(**{k: getattr(made, f"{k}{m}") for k in outs}) for m in which}


def both_call(sz, m, fwd, arrays, border_sets=()):
    A, H, E, F = sz.atoms, sz.halo, sz.rows, sz.width
    EB, CG, NB = sz.edges, sz.halves, sz.blocks
    shape = jax.ShapeDtypeStruct
    outs = SimpleNamespace(
        back=shape((4, A, F), F32),
        back_low=shape((4, A, F), BF16),
        rim_low=shape((4, H, F), BF16),
        rim_high=shape((4, H, F), BF16),
        gplaces=shape((8, LANES), F32),
        left=shape((sz.factors, F), BF16),
        gproj=shape((E, 5 * F), BF16),
        gvproj=shape((3 * A, 3 * F), BF16),
        gout=shape((A, 3 * F), BF16),
        gfilt=shape((sz.basis, 4 * F), F32),
        gnorm=shape((8, F), F32),
    )
    scratch = dict(
        query=((CG, A, LANES), F32),
        query_low=((A, F), BF16),
        kv=((4 * CG, E, LANES), F32),
        vec=((3 * CG, E, LANES), F32),
        vproj=((3 * A, 3 * F), F32),
        heads=((F, F), BF16),
        diag=((A, EB), F32),
        fold=((A, EB), BF16),
        centres=((sz.basis, EB), F32),
        gx=((4, A, F), F32),
        gvlow=((3 * A, F), BF16),
        gs=((A, F), BF16),
        gq=((A, F), F32),
        gnear=((7, E, F), F32),
        gunit=((3, 8, EB), F32),
        gcut=((8, EB), F32),
        gshrink=((8, EB), F32),
    )
    if fwd:
        outs.fresh = shape((4, A, F), BF16)
        scratch.update(
            score=((NB, CG, EB, LANES), BF16), sagg=((A, F), F32), vagg=((3, A, F), F32), uagg=((3 * A, F), F32)
        )
    if not border_sets:
        role = SECOND if fwd else FIRST
        return call(lambda r: both_ways(r, sz, m, fwd), arrays, outs, scratch, role)
    count = m + 1
    outs.up, outs.down = shape((count, 4, H, F), BF16), shape((count, 4, H, F), BF16)
    outs.moved = shape((count, 8, LANES), F32)
    for role, sets in enumerate(border_sets):
        for i, made in enumerate(sets):
            for name in BORDERS:
                setattr(arrays, f"{name}_{role}_{i}", (getattr(made, name), VMEM))

    def hand_on(r, role):
        for i in range(count):
            low, high, places = (
                getattr(r, f"{name}_{role}_{i}") if i < len(border_sets[role]) else getattr(r, name)
                for name in BORDERS
            )
            r.up[i] = high[...]
            r.down[i] = low[...]
            r.moved[i] = places[...]

    def body(r):
        @pl.when(r.scal[0] == FIRST)
        def _():
            both_ways(r, sz, m, fwd)
            hand_on(r, FIRST)

        pl.when(r.scal[0] == SECOND)(lambda: hand_on(r, SECOND))

    return call(body, arrays, outs, scratch)


def border_call(sz, features, coords, neighbours, shifts, counts, gain, bias, filter_weight):
    A, H, F, K = sz.atoms, sz.halo, sz.width, sz.slots
    count = features.shape[0]

    def body(r):
        moves = [(r.coords, r.s_coords)]
        for m in range(count):
            moves += [
                (r.features.at[m, 0, :, A - H : A, :], r.up.at[m, 0:4]),
                (r.features.at[m, 0, :, 0:H, :], r.down.at[m, 0:4]),
                (r.nbr.at[m, 0], r.slots.at[m, 0:K]),
                (r.shifts.at[m, 0, 0], r.slots.at[m, K : 2 * K]),
                (r.shifts.at[m, 0, 1], r.slots.at[m, 2 * K : 3 * K]),
            ]
        copies = [
            pltpu.make_async_copy(source, target, r.sems.at[i])
            for i, (source, target) in enumerate(moves)
        ]
        for copy in copies:
            copy.start()
        r.wh[...] = (r.wfilt[0].astype(F32) * 0.5).astype(BF16)
        r.norms[0:1, :] = r.gain[...].astype(F32)
        r.norms[1:2, :] = r.bias[...].astype(F32)
        r.norms[2:, :] = jnp.zeros((6, F), F32)
        for m in range(count):
            r.slots[m, 3 * K :, :] = jnp.broadcast_to(r.counts[m], (8, A))
        copies[0].wait()
        for m in range(count):
            r.up[m, 4] = packed_places([r.s_coords[m, c][:, A - H :] for c in range(3)], F)
            r.down[m, 4] = packed_places([r.s_coords[m, c][:, :H] for c in range(3)], F)
        for copy in copies[1:]:
            copy.wait()

    shape = jax.ShapeDtypeStruct
    return call(
        body,
        SimpleNamespace(
            features=(features, HBM),
            coords=(coords, HBM),
            nbr=(neighbours, HBM),
            shifts=(shifts, HBM),
            counts=(counts, VMEM),
            gain=(gain, VMEM),
            bias=(bias, VMEM),
            wfilt=(filter_weight, VMEM),
        ),
        SimpleNamespace(
            up=shape((count, 5, H, F), BF16),
            down=shape((count, 5, H, F), BF16),
            slots=shape((count, 3 * K + 8, A), jnp.int32),
            norms=shape((8, F), F32),
            wh=shape((sz.basis, 4 * F), BF16),
        ),
        dict(s_coords=(coords.shape, F32), sems=pltpu.SemaphoreType.DMA((5 * count + 1,))),
        grant_mb=54,
    )


def gradient_call(sz, scal, sets):
    A, E, F = sz.atoms, sz.rows, sz.width
    count = len(sets[0])
    w1, w2, w3 = sz.widths
    w4, w5 = 4 * F // sz.space, F // sz.space
    half = F // 2
    arrays = SimpleNamespace(scal=(scal, SMEM))
    for role in (FIRST, SECOND):
        for m in range(count):
            for name in FACTORS:
                setattr(arrays, f"{name}_{role}_{m}", (getattr(sets[role][m], name), VMEM))

    def body(r, role):
        def get(name, m):
            return getattr(r, f"{name}_{role}_{m}")

        every = range(count)
        e, a = E, A
        r.qkv[...] = sum(dot(get("gproj", m)[...], get("left", m)[0:e, :], 0, 0) for m in every)
        r.vector[...] = sum(
            dot(get("gvproj", m)[...], get("left", m)[e : e + 3 * a, :], 0, 0) for m in every
        )
        r.out[...] = sum(
            dot(get("gout", m)[...], get("left", m)[e + 3 * a : e + 4 * a, :], 0, 0) for m in every
        )
        filt = sum(get("gfilt", m)[...] for m in every) * 0.5
        norm = sum(get("gnorm", m)[...] for m in every)
        core = r.scal[2]
        for k in range(sz.space):
            spare = [filt[:, k * w4 : (k + 1) * w4]]
            if half > w4:
                spare.append(jnp.zeros((sz.basis, half - w4), F32))
            left = jnp.concatenate(spare, axis=1)
            rows = [norm[:, k * w5 : (k + 1) * w5], jnp.zeros((8, half - w5), F32)]
            right = jnp.concatenate(rows, axis=1)
            right = jnp.concatenate(
                [right, jnp.zeros((sz.packed - sz.spare - 8, half), F32)], axis=0
            )
            if sz.packed - sz.spare > sz.basis:
                gap = jnp.zeros((sz.packed - sz.spare - sz.basis, half), F32)
                left = jnp.concatenate([left, gap], axis=0)
            parts = [
                r.qkv[k * w1 : (k + 1) * w1, :],
                r.vector[k * w2 : (k + 1) * w2, :],
                r.out[k * w3 : (k + 1) * w3, :],
            ]
            first = jnp.concatenate([part[:, :half] for part in parts] + [left], axis=0)
            second = jnp.concatenate([part[:, half:] for part in parts] + [right], axis=0)
            r.send[k] = jnp.where(core == 0, second, first).astype(BF16)
            r.stay[k] = jnp.where(core == 0, first, second)

    def both(r):
        for role in (FIRST, SECOND):
            pl.when(r.scal[0] == role)(lambda role=role: body(r, role))

    shape = jax.ShapeDtypeStruct
    return call(
        both,
        arrays,
        SimpleNamespace(
            send=shape((sz.space, sz.packed, half), BF16),
            stay=shape((sz.space, sz.packed, half), F32),
        ),
        dict(
            qkv=((5 * F, F), F32),
            vector=((3 * F, F), F32),
            out=((3 * F, F), F32),
        ),
    )


def border_rows(sz, m, index):
    start = sz.packed + (m * 5 + index) * 2 * sz.halo
    return [slice(start + i * sz.halo, start + (i + 1) * sz.halo) for i in range(2)]


def border_block(sz, ref, m, index):
    return jnp.concatenate([ref[rows, :] for rows in border_rows(sz, m, index)], axis=1)


def piece_call(sz, scal, stay, recv, up, down, moved, other):
    A, H, E, F = sz.atoms, sz.halo, sz.rows, sz.width
    count = up.shape[0]
    half = F // 2

    def body(r):
        slab, space = r.scal[1], sz.space
        for hop in range(space):
            k = lax.rem(slab + hop, space)
            total = r.stay[k] + r.recv[k].astype(F32)
            target = getattr(r, f"hop{hop}")
            target[0 : sz.packed, :] = total.astype(target.dtype)
        for m in range(count):
            places = r.moved[m] + r.other[m]
            rows = [places[c : c + 1, :] for c in range(3)]
            ends = (
                (r.hop1, r.up, [row[:, H + A : E] for row in rows]),
                (getattr(r, f"hop{space - 1}"), r.down, [row[:, 0:H] for row in rows]),
            )
            for target, border, part in ends:
                blocks = [border[m, index] for index in range(4)] + [packed_places(part, F)]
                for index, block in enumerate(blocks):
                    first, second = border_rows(sz, m, index)
                    target[first, :] = block[:, :half]
                    target[second, :] = block[:, half:]
            for c in range(3):
                r.mine[m, c] = rows[c][:, H : H + A]

    shape = jax.ShapeDtypeStruct
    outs = {
        f"hop{hop}": shape(
            (sz.packed + (10 * H * count if hop in (1, sz.space - 1) else 0), half),
            BF16 if hop else F32,
        )
        for hop in range(sz.space)
    }
    outs.update(mine=shape((count, 3, 1, A), F32))
    made = call(
        body,
        SimpleNamespace(
            scal=(scal, SMEM),
            stay=(stay, VMEM),
            recv=(recv, VMEM),
            up=(up, VMEM),
            down=(down, VMEM),
            moved=(moved, VMEM),
            other=(other, VMEM),
        ),
        SimpleNamespace(**outs),
        {},
    )
    return [getattr(made, f"hop{hop}") for hop in range(sz.space)], made.mine


def result_call(sz, scal, fresh, back, from_low, from_high, mine):
    A, H, F = sz.atoms, sz.halo, sz.width
    count = len(back[0])
    arrays = SimpleNamespace(
        scal=(scal, SMEM), low=(from_low, VMEM), high=(from_high, VMEM), mine=(mine, VMEM)
    )
    for role in (FIRST, SECOND):
        for m in range(count):
            setattr(arrays, f"fresh_{role}_{m}", (fresh[role][m], VMEM))
            setattr(arrays, f"back_{role}_{m}", (back[role][m], VMEM))

    def body(r, role):
        for m in range(count):
            r.outputs[0, m, 0] = getattr(r, f"fresh_{role}_{m}")[...]
            whole = getattr(r, f"back_{role}_{m}")
            for index in range(4):
                low = border_block(sz, r.low, m, index).astype(F32)
                high = border_block(sz, r.high, m, index).astype(F32)
                r.grads[0, m, 0, index, 0:H, :] = whole[index, 0:H, :] + low
                r.grads[0, m, 0, index, H : A - H, :] = whole[index, H : A - H, :]
                r.grads[0, m, 0, index, A - H :, :] = whole[index, A - H :, :] + high
            for c in range(3):
                edge = [
                    unpacked_places(border_block(sz, r.low, m, 4), c, H),
                    jnp.zeros((1, A - 2 * H), F32),
                    unpacked_places(border_block(sz, r.high, m, 4), c, H),
                ]
                r.places[m, c] = r.mine[m, c] + jnp.concatenate(edge, axis=1)

    def both(r):
        for role in (FIRST, SECOND):
            pl.when(r.scal[0] == role)(lambda role=role: body(r, role))

    shape = jax.ShapeDtypeStruct
    return call(
        both,
        arrays,
        SimpleNamespace(
            outputs=shape((1, count, 1, 4, A, F), BF16),
            grads=shape((1, count, 1, 4, A, F), F32),
            places=shape((count, 3, 1, A), F32),
        ),
        {},
    )


def share_call(sz, scal, total, other):
    F = sz.width
    w1, w2, w3 = sz.widths
    w4, w5 = 4 * F // sz.space, F // sz.space
    half = F // 2

    def body(r, first, second):
        for lanes, part in ((slice(0, half), first), (slice(half, F), second)):
            r.qkv[0, :, lanes] = part[0:w1, :]
            r.vector[0, :, lanes] = part[w1 : w1 + w2, :]
            r.out[0, :, lanes] = part[w1 + w2 : sz.spare, :]
        r.filt[0] = first[sz.spare : sz.spare + sz.basis, 0:w4]
        r.gain[...] = second[sz.spare : sz.spare + 1, 0:w5]
        r.bias[...] = second[sz.spare + 1 : sz.spare + 2, 0:w5]

    def both(r):
        pl.when(r.scal[2] == 0)(lambda: body(r, r.total, r.other))
        pl.when(r.scal[2] == 1)(lambda: body(r, r.other, r.total))

    shape = jax.ShapeDtypeStruct
    return call(
        both,
        SimpleNamespace(scal=(scal, SMEM), total=(total, VMEM), other=(other, VMEM)),
        SimpleNamespace(
            gain=shape((1, w5), F32),
            bias=shape((1, w5), F32),
            qkv=shape((1, w1, F), F32),
            vector=shape((1, w2, F), F32),
            filt=shape((1, sz.basis, w4), F32),
            out=shape((1, w3, F), F32),
        ),
        {},
    )


def on_device(
    features,
    coords,
    neighbours,
    counts,
    shifts,
    norm_gain,
    norm_bias,
    qkv_weight,
    vector_weight,
    filter_weight,
    out_weight,
    cotangent,
):
    micro_count = features.shape[0]
    space = lax.axis_size("space")
    section = lax.axis_index("section")
    slab = lax.axis_index("space")
    core = lax.axis_index("dp")
    sz = Sizes(features.shape[3], features.shape[4], filter_weight.shape[1], neighbours.shape[2], space)
    up = [(i, (i + 1) % space) for i in range(space)]
    down = [((i + 1) % space, i) for i in range(space)]

    scal = jnp.stack([section, slab, core, space - 1]).astype(jnp.int32)
    places = jnp.transpose(coords, (0, 2, 1, 3))
    borders = border_call(
        sz, features, places, neighbours, shifts, counts, norm_gain, norm_bias, filter_weight
    )
    slots, norms, half_filter = borders.slots, borders.norms, borders.wh
    pack_low = lax.ppermute(borders.up, "space", up)
    pack_high = lax.ppermute(borders.down, "space", down)
    both = ("section", "space")
    forth = [(k, space + k) for k in range(space)]
    forth_up = [(k, space + (k + 1) % space) for k in range(space)]
    forth_down = [((k + 1) % space, space + k) for k in range(space)]
    back = [(space + k, k) for k in range(space)]
    back_up = [(space + k, (k + 1) % space) for k in range(space)]
    back_down = [(space + (k + 1) % space, k) for k in range(space)]

    def geometry_inputs(place):
        return SimpleNamespace(
            scal=(scal, SMEM),
            pack_low=(pack_low, VMEM),
            pack_high=(pack_high, VMEM),
            coords=(places, place),
            slots=(slots, place),
            wh=(half_filter, place),
        )

    firsts, sent, filters = [], [], {}
    for m in range(micro_count):
        arrays = geometry_inputs(HBM)
        arrays.features = (features, HBM)
        arrays.norms = (norms, VMEM)
        arrays.wqkv, arrays.wvec, arrays.wout = (
            (qkv_weight, HBM), (vector_weight, HBM), (out_weight, HBM)
        )
        first = first_call(sz, m, True, arrays)
        firsts.append(first)
        if m == micro_count - 1:
            made = filters[SECOND] = filter_call(
                sz, SECOND, range(micro_count), geometry_inputs(VMEM)
            )
            first.head, made[0].geo = lax.optimization_barrier((first.head, made[0].geo))
        sent.append((
            lax.ppermute(first.fresh, both, forth),
            lax.ppermute(first.tail, both, forth_up),
            lax.ppermute(first.head, both, forth_down),
        ))
    def both_inputs(m, role):
        made = filters[role][m]
        return SimpleNamespace(
            scal=(scal, SMEM),
            norms=(norms, VMEM),
            wqkv=(qkv_weight, VMEM),
            wvec=(vector_weight, VMEM),
            wh=(half_filter, VMEM),
            wout=(out_weight, VMEM),
            geo=(made.geo, VMEM),
            smear=(made.smear, VMEM),
            cut_wide=(made.cut_wide, VMEM),
            units=(made.units, VMEM),
            silu=(made.silu, VMEM),
            slope=(made.slope, VMEM),
        )

    seconds, returned = [], []
    for m in range(micro_count):
        if m == 1:
            other = filters[FIRST][0]
            other.geo, filters[SECOND][m].geo = lax.optimization_barrier(
                (other.geo, filters[SECOND][m].geo)
            )
        arrays = both_inputs(m, SECOND)
        own, low, high = sent[m]
        arrays.own, arrays.low, arrays.high = (own, VMEM), (low, VMEM), (high, VMEM)
        arrays.cotangent = (cotangent, VMEM)
        second = both_call(sz, m, True, arrays)
        seconds.append(second)
        if m == 0:
            later = geometry_inputs(VMEM)
            held, second.gplaces = lax.optimization_barrier((slots, second.gplaces))
            later.slots = (held, VMEM)
            filters[FIRST] = filter_call(sz, FIRST, range(micro_count), later)
        back_low, rim_low, rim_high = second.back_low, second.rim_low, second.rim_high
        if m:
            returned[-1], back_low, rim_low, rim_high = lax.optimization_barrier(
                (returned[-1], back_low, rim_low, rim_high)
            )
        returned.append((
            lax.ppermute(back_low, both, back),
            lax.ppermute(rim_high, both, back_up),
            lax.ppermute(rim_low, both, back_down),
        ))
    thirds = []
    for m in range(micro_count):
        arrays = both_inputs(m, FIRST)
        arrays.pack_low, arrays.pack_high = (pack_low, VMEM), (pack_high, VMEM)
        arrays.features = (features, VMEM)
        arrays.scalar_in = (firsts[m].o_scalar, VMEM)
        arrays.score = (firsts[m].score, VMEM)
        inc, inc_low, inc_high = returned[m]
        arrays.inc, arrays.inc_low, arrays.inc_high = (inc, VMEM), (inc_low, VMEM), (inc_high, VMEM)
        sets = (thirds, seconds) if m == micro_count - 1 else ()
        thirds.append(both_call(sz, m, False, arrays, sets))

    last = thirds[-1]
    other = lax.ppermute(last.moved, "section", [(0, 1), (1, 0)])
    shares = gradient_call(sz, scal, (thirds, seconds))
    recv = lax.ppermute(shares.send, "dp", [(0, 1), (1, 0)])
    (total, *pieces), mine = piece_call(
        sz, scal, shares.stay, recv, last.up, last.down, last.moved, other
    )
    received = [
        lax.ppermute(piece, "space", [(i, (i + hop) % space) for i in range(space)])
        for hop, piece in enumerate(pieces, 1)
    ]
    for piece in received:
        total = total + piece[: sz.packed].astype(F32)
    results = result_call(
        sz,
        scal,
        ([v.fresh for v in firsts], [v.fresh for v in seconds]),
        ([v.back for v in thirds], [v.back for v in seconds]),
        received[0],
        received[-1],
        mine,
    )
    other = lax.ppermute(total, "dp", [(0, 1), (1, 0)])
    share = share_call(sz, scal, total, other)
    return (
        results.outputs,
        results.grads,
        share.gain,
        share.bias,
        jnp.transpose(share.qkv, (0, 2, 1)),
        jnp.transpose(share.vector, (0, 2, 1)),
        share.filt,
        jnp.transpose(share.out, (0, 2, 1)),
        jnp.transpose(results.places, (0, 2, 1, 3)),
    )


def solution(mesh):
    return jax.shard_map(
        on_device,
        mesh=mesh,
        in_specs=(
            P(None, "dp", None, "space", None),
            P(None, "dp", None, "space"),
            P(None, "dp", None, "space"),
            P(None, "dp", "space"),
            P(None, "dp", None, None, "space"),
            P("section", None),
            P("section", None),
            P("section", None, None),
            P("section", None, None),
            P("section", None, None),
            P("section", None, None),
            P(None, "dp", None, "space", None),
        ),
        out_specs=(
            P("section", None, "dp", None, "space", None),
            P("section", None, "dp", None, "space", None),
            P("section", "space"),
            P("section", "space"),
            P("section", None, "space"),
            P("section", None, "space"),
            P("section", None, "space"),
            P("section", None, "space"),
            P(None, "dp", None, "space"),
        ),
        check_vma=False,
    )
```

```python
import math
from types import SimpleNamespace

import jax
import jax.numpy as jnp
from jax import lax
from jax.experimental import pallas as pl
from jax.experimental.pallas import tpu as pltpu
from jax.sharding import PartitionSpec as P

HEADS = 8
CUTOFF = 5.0
LN_EPS = 1e-05
SOFTEN = 0.25
CROSS = 2.5
GROUP = 4
LANES = 128
SUBLANES = 8
FIRST, SECOND = 0, 1

F32 = jnp.float32
BF16 = jnp.bfloat16
VMEM = pl.BlockSpec(memory_space=pltpu.VMEM)
HBM = pl.BlockSpec(memory_space=pltpu.HBM)


def dot(left, right, left_dim=1, right_dim=0):
    return lax.dot_general(
        left, right, (((left_dim,), (right_dim,)), ((), ())), preferred_element_type=F32
    )


def iota(shape, dim):
    return lax.broadcasted_iota(jnp.int32, shape, dim)


def packed_places(parts, width):
    row = jnp.concatenate(parts, axis=1)
    high = row.astype(BF16).astype(F32)
    rest = row - high
    middle = rest.astype(BF16).astype(F32)
    rows = jnp.concatenate([high, middle, rest - middle, jnp.zeros((13, row.shape[1]), F32)], axis=0)
    return jnp.concatenate([rows, jnp.zeros((16, width - row.shape[1]), F32)], axis=1).astype(BF16)


def unpacked_places(block, c, count):
    rows = block[:, c * count : (c + 1) * count].astype(F32)
    return rows[0:1] + rows[1:2] + rows[2:3]


class Sizes:
    def __init__(self, atoms, width, basis, slots, space):
        self.atoms, self.width, self.basis, self.slots, self.space = atoms, width, basis, slots, space
        self.halo = atoms // 4
        self.rows = atoms + 2 * self.halo
        self.blocks = slots // GROUP
        self.edges = GROUP * atoms
        self.halves = width // LANES
        self.window = atoms + SUBLANES
        self.sent = (self.halo, atoms)
        self.widths = (5 * width // space, 3 * width // space, 3 * width // space)
        self.spare = sum(self.widths)
        self.packed = -(-(self.spare + basis) // 16) * 16
        self.factors = -(-(self.rows + 4 * atoms) // LANES) * LANES


def halves_of(sz):
    return [slice(cg * LANES, (cg + 1) * LANES) for cg in range(sz.halves)]


def first_row(b):
    return GROUP * b + jnp.where(b >= 4, 1, 0)


def sharpness_of(basis):
    return (2.0 / basis * (1.0 - math.exp(-CUTOFF))) ** (-2)


def write_centres(ref, basis):
    low_end = math.exp(-CUTOFF)
    step = iota(ref.shape, 0).astype(F32) / (basis - 1)
    ref[...] = low_end * (1.0 - step) + step


def edge_geometry(r, sz, coords, slots, low, high):
    A, H, E, EB, K = sz.atoms, sz.halo, sz.rows, sz.edges, sz.slots
    lane = iota((8, LANES), 1)
    row = iota((8, LANES), 0)
    slab, last = lax.axis_index("space"), sz.space - 1
    spot = iota((1, LANES), 1)
    length_x = sz.space * A * 4.0 / H
    places = []
    for c in range(3):
        places.append(
            jnp.concatenate(
                [
                    unpacked_places(low[4], c, H),
                    coords[c],
                    unpacked_places(high[4], c, H),
                    jnp.zeros((1, LANES - E), F32),
                ],
                axis=1,
            )
        )
    places.append(
        jnp.where((spot < H) & (slab == 0), -length_x, 0.0)
        + jnp.where((spot >= H + A) & (slab == last), length_x, 0.0)
    )
    near = []
    for c in range(4):
        y = jnp.broadcast_to(places[c], (8, LANES))
        for bit in range(3):
            y = jnp.where((row >> bit) & 1 == 1, pltpu.roll(y, LANES - GROUP * 2**bit, 1), y)
        y = jnp.where(row >= 4, pltpu.roll(y, LANES - 1, 1), y)
        first = jnp.where(lane < A, y, pltpu.roll(y, A - 1, 1))
        other = jnp.where(lane < A, pltpu.roll(y, LANES - 2, 1), pltpu.roll(y, A - 3, 1))
        near.append(jnp.concatenate([first, other], axis=1))
    wide_lane = iota((8, EB), 1)
    wide_row = iota((8, EB), 0)
    wanted = GROUP * wide_row + wide_lane // A + jnp.where(wide_row >= 4, 1, 0) + wide_lane % A
    table = slots[:, 0:A].astype(jnp.int32)
    alive = iota((K, A), 0) < table[3 * K : 3 * K + 1]
    code = jnp.where(alive, 16, 0) + (table[K : 2 * K] + 1) * 4 + (table[2 * K : 3 * K] + 1)
    code = jnp.concatenate([code] * GROUP, axis=1)
    named = jnp.concatenate([table[0:K]] * GROUP, axis=1)
    found = jnp.zeros((8, EB), jnp.int32)
    for n in range(K):
        found = found + jnp.where(named[n : n + 1, :] == wanted, code[n : n + 1, :], 0)
    live = (found >> 4).astype(F32)
    offsets = (
        near[3],
        (((found >> 2) & 3) - 1).astype(F32) * CROSS,
        ((found & 3) - 1).astype(F32) * CROSS,
    )
    sep = []
    for c in range(3):
        mine = coords[c]
        sep.append(near[c] - jnp.concatenate([mine] * GROUP, axis=1) + offsets[c])
    distance = jnp.sqrt(sep[0] * sep[0] + sep[1] * sep[1] + sep[2] * sep[2] + SOFTEN)
    inside = distance < CUTOFF
    cut = jnp.where(inside, 0.5 * (jnp.cos(math.pi * distance / CUTOFF) + 1.0), 0.0) * live
    for index, value in enumerate(
        sep + [distance, live, cut, jnp.exp(-distance)] + [part / distance for part in sep]
    ):
        r.geo[index] = value


DISTANCE, LIVE, CUT, SHRINK, UNIT = 3, 4, 5, 6, 7


def bell_of(r, sz, b):
    delta = r.geo[SHRINK, pl.ds(b, 1), :] - r.centres[...]
    return delta, jnp.exp(-sharpness_of(sz.basis) * delta * delta)


def write_edge_tables(r, sz, b, wide_kind):
    A, EB = sz.atoms, sz.edges
    cut = r.geo[CUT, pl.ds(b, 1), :]
    _, bell = bell_of(r, sz, b)
    smear = cut * bell
    if hasattr(r, "smear"):
        r.smear[b] = smear.astype(BF16)
    r.smear_t[b] = jnp.transpose(smear).astype(BF16)
    coarse = cut.astype(BF16).astype(F32)
    which = iota((16, EB), 0)
    pair = jnp.where(which == 0, coarse, jnp.where(which == 1, cut - coarse, 0.0)).astype(BF16)
    r.cut_wide[b] = dot(pair, jnp.ones((16, LANES), BF16), 0, 0).astype(wide_kind)
    for c in range(3):
        r.units[b, c * A : (c + 1) * A, :] = (
            r.diag[...] * r.geo[UNIT + c, pl.ds(b, 1), :]
        ).astype(BF16)


def write_constants(r, sz):
    A, EB, F = sz.atoms, sz.edges, sz.width
    if hasattr(r, "centres"):
        write_centres(r.centres, sz.basis)
    if hasattr(r, "diag"):
        r.diag[...] = jnp.where(iota((A, EB), 1) % A == iota((A, EB), 0), 1.0, 0.0)
    if hasattr(r, "fold"):
        r.fold[...] = jnp.where(iota((A, EB), 1) % A == iota((A, EB), 0), 1.0, 0.0).astype(BF16)
    if hasattr(r, "heads"):
        r.heads[...] = jnp.where(
            iota((F, F), 0) // (F // HEADS) == iota((F, F), 1) // (F // HEADS), 0.5, 0.0
        ).astype(BF16)


def node_part(r, sz, own, low, high, norms, wqkv):
    A, H, E, F, CG = sz.atoms, sz.halo, sz.rows, sz.width, sz.halves
    halves = halves_of(sz)
    scalars = jnp.concatenate([low[0, 0:H], own[0], high[0, 0:H]], axis=0).astype(F32)
    centred = scalars - jnp.mean(scalars, axis=-1, keepdims=True)
    spread = jnp.mean(centred * centred, axis=-1, keepdims=True)
    scale = lax.rsqrt(spread + LN_EPS)
    normed = (centred * scale * norms[0:1, :] + norms[1:2, :]).astype(BF16)
    left = r.left
    left[0:E, :] = normed
    left[E : E + 3 * A, :] = own[1:4].reshape(3 * A, F)
    left[E + 4 * A :, :] = jnp.zeros((sz.factors - E - 4 * A, F), BF16)
    for part in range(5):
        projected = dot(normed, wqkv[:, part * F : (part + 1) * F])
        for cg in range(CG):
            if part == 0:
                r.query[cg] = projected[H : H + A, halves[cg]]
            else:
                r.kv[(part - 1) * CG + cg] = projected[:, halves[cg]]
    for c in range(3):
        for cg in range(CG):
            r.vec[c * CG + cg, 0:H, :] = low[c + 1, 0:H, halves[cg]].astype(F32)
            r.vec[c * CG + cg, H : H + A, :] = own[c + 1][:, halves[cg]].astype(F32)
            r.vec[c * CG + cg, H + A : E, :] = high[c + 1, 0:H, halves[cg]].astype(F32)
    return centred * scale, scale


def buffers(r, sz, which):
    end = str(which)
    return SimpleNamespace(**{k[:-1]: v for k, v in vars(r).items() if k.endswith(end)})


def tiles(sz, first):
    A = sz.atoms
    for kk in range(GROUP):
        for cg in range(sz.halves):
            yield (
                cg,
                slice(kk * A, (kk + 1) * A),
                slice(cg * LANES, (cg + 1) * LANES),
                pl.ds(first + kk, A),
            )


def stacked(sz, first, tile):
    made = [tile(*where) for where in tiles(sz, first)]
    CG = sz.halves
    wholes = []
    for index in range(len(made[0])):
        lines = [
            jnp.concatenate([made[kk * CG + cg][index] for cg in range(CG)], axis=1)
            for kk in range(GROUP)
        ]
        wholes.append(jnp.concatenate(lines, axis=0))
    return wholes


def vector_dot(r, sz):
    A, F, vp = sz.atoms, sz.width, r.vproj
    return sum(
        vp[c * A : (c + 1) * A, 0:F] * vp[c * A : (c + 1) * A, F : 2 * F] for c in range(3)
    )


def write_layer_output(r, sz, own, out_proj, vec_dot, vector_agg):
    A, H, F, vp = sz.atoms, sz.halo, sz.width, r.vproj
    for index in range(4):
        if index == 0:
            fresh = vec_dot * out_proj[:, F : 2 * F] + out_proj[:, 2 * F :]
        else:
            rows = slice((index - 1) * A, index * A)
            fresh = vp[rows, 2 * F :] * out_proj[:, 0:F] + vector_agg[index - 1]
        fresh = (own[index].astype(F32) + fresh).astype(BF16)
        r.fresh[index] = fresh
        if hasattr(r, "head"):
            r.head[index, 0:H, :] = fresh[:H]
            r.tail[index, 0:H, :] = fresh[A - H :]


def first_forward(r, sz, m, fetch):
    A, H, E, F, EB = sz.atoms, sz.halo, sz.rows, sz.width, sz.edges
    CG = sz.halves
    r.s_low, r.s_high = r.pack_low.at[m], r.pack_high.at[m]
    copies = early = []
    if fetch:
        rooms = Rooms(sz)
        early = [
            (r.wide.at[rooms.slots, 0:LANES], r.s_slots),
            (r.wide.at[rooms.norms.start : rooms.coords.stop], r.s_norms),
            (r.room.at[rooms.wqkv], r.s_wqkv),
        ]
        for index in range(4):
            start = rooms.own.start + index * A
            early.append((r.room.at[start : start + A, 0:F], r.s_own.at[index]))
        late = [
            (r.room.at[rooms.wh, 0 : 4 * F], r.s_wh),
            (r.room.at[rooms.wvec, 0 : 3 * F], r.s_wvec),
            (r.room.at[rooms.wout, 0 : 3 * F], r.s_wout),
        ]
        copies = [
            pltpu.make_async_copy(source, target, r.sems.at[i])
            for i, (source, target) in enumerate(early + late)
        ]
        for copy in copies:
            copy.start()
    else:
        r.s_slots, r.s_norms, r.s_wh = r.slots.at[m], r.norms, r.wh
        r.s_own, r.s_wqkv = r.features.at[m, 0], r.wqkv.at[0]
        r.s_wvec, r.s_wout = r.wvec.at[0], r.wout.at[0]
    write_constants(r, sz)
    r.sagg[...] = jnp.zeros_like(r.sagg)
    r.vagg[...] = jnp.zeros_like(r.vagg)
    for copy in copies[: len(early)]:
        copy.wait()
    coords = [r.s_norms[8 + c : 9 + c, 0:A] if fetch else r.coords[m, c] for c in range(3)]
    edge_geometry(r, sz, coords, r.s_slots, r.s_low, r.s_high)

    def tables(b, carry):
        write_edge_tables(r, sz, b, F32)
        return carry

    lax.fori_loop(0, sz.blocks, tables, 0, unroll=2)
    own = r.s_own
    node_part(r, sz, own, r.s_low, r.s_high, r.s_norms, r.s_wqkv)
    for copy in copies[len(early) :]:
        copy.wait()
    r.vproj[...] = dot(r.left[E : E + 3 * A, :], r.s_wvec[...])

    def filter_part(b, part):
        return dot(r.smear_t[b], r.s_wh[:, part * F : (part + 1) * F])

    def block(b, w):
        first = first_row(b)
        half = filter_part(b, 0)
        for cg, at, cols, near_rows in tiles(sz, first):
            h = half[at, cols]
            product = r.query[cg] * r.kv[cg, near_rows, :] * (h + h * jnp.tanh(h))
            coarse = product.astype(BF16)
            w.pack1[at, cols] = coarse
            w.pack2[at, cols] = (product - coarse.astype(F32)).astype(BF16)
        score = dot(w.pack1[...], r.heads[...]) + dot(w.pack2[...], r.heads[...])
        for cg in range(CG):
            r.score[b, cg] = score[:, cg * LANES : (cg + 1) * LANES].astype(BF16)
        half = filter_part(b, 2)
        for cg, at, cols, near_rows in tiles(sz, first):
            h = half[at, cols]
            value = r.kv[2 * CG + cg, near_rows, :] * (h + h * jnp.tanh(h))
            for c in range(3):
                r.vagg[c * CG + cg] += r.vec[c * CG + cg, near_rows, :] * value
        half = filter_part(b, 3)
        for cg, at, cols, near_rows in tiles(sz, first):
            h = half[at, cols]
            value = r.kv[3 * CG + cg, near_rows, :] * (h + h * jnp.tanh(h))
            r.third[b, at, cols] = value.astype(BF16)
        half = filter_part(b, 1)
        for cg, at, cols, near_rows in tiles(sz, first):
            h = half[at, cols]
            s = score[at, cols]
            attention = (s + s * jnp.tanh(s)) * r.cut_wide[b, at, :]
            r.sagg[cg] += attention * (r.kv[CG + cg, near_rows, :] * (h + h * jnp.tanh(h)))

    def pair(i, carry):
        for which in range(2):
            block(2 * i + which, buffers(r, sz, which))
        return carry

    lax.fori_loop(0, sz.blocks // 2, pair, 0)
    third = sum(dot(r.units[b], r.third[b]) for b in range(sz.blocks))
    scalar_low = jnp.concatenate([r.sagg[cg] for cg in range(CG)], axis=1).astype(BF16)
    r.o_scalar[...] = scalar_low
    out_proj = dot(scalar_low, r.s_wout[...])
    vector_agg = [
        jnp.concatenate([r.vagg[c * CG + cg] for cg in range(CG)], axis=1)
        + third[c * A : (c + 1) * A, :]
        for c in range(3)
    ]
    write_layer_output(r, sz, own, out_proj, vector_dot(r, sz), vector_agg)


def edge_filters(r, sz, which):
    F = sz.width
    write_constants(r, sz)
    for m in which:
        w = SimpleNamespace(**vars(r))
        vars(w).update(vars(buffers(r, sz, m)))
        edge_geometry(
            w, sz, r.coords.at[m], r.slots.at[m], r.pack_low.at[m], r.pack_high.at[m]
        )

        def block(b, carry, w=w):
            write_edge_tables(w, sz, b, BF16)
            for part in range(4):
                cols = slice(part * F, (part + 1) * F)
                h = dot(r.smear_t[b], r.wh[:, cols])
                t = jnp.tanh(h)
                f = h + h * t
                f, t = f.astype(BF16), t.astype(BF16)
                slope = (1.0 + t) + f * (1.0 - t)
                for cg in range(sz.halves):
                    half = slice(cg * LANES, (cg + 1) * LANES)
                    w.silu[b, part * sz.halves + cg] = f[:, half]
                    w.slope[b, part * sz.halves + cg] = slope[:, half]
            return carry

        lax.fori_loop(0, sz.blocks, block, 0, unroll=2)


def both_ways(r, sz, m, fwd):
    A, H, E, F = sz.atoms, sz.halo, sz.rows, sz.width
    EB, CG, NB, W = sz.edges, sz.halves, sz.blocks, sz.window
    lane = iota((8, LANES), 1)
    row = iota((8, LANES), 0)
    halves = halves_of(sz)
    if fwd:
        own, low, high = r.own, r.low, r.high
    else:
        own, low, high = r.features.at[m, 0], r.pack_low.at[m], r.pack_high.at[m]
    wqkv, wvec, wout = r.wqkv.at[0], r.wvec.at[0], r.wout.at[0]
    write_constants(r, sz)
    xhat, scale = node_part(r, sz, own, low, high, r.norms, wqkv)
    gain = r.norms[0:1, :]
    left = r.left
    vp = r.vproj
    vp[...] = dot(left[E : E + 3 * A, :], wvec[...])
    for cg in range(CG):
        r.query_low[:, halves[cg]] = r.query[cg].astype(BF16)

    if fwd:
        r.sagg[...] = jnp.zeros_like(r.sagg)
        r.vagg[...] = jnp.zeros_like(r.vagg)
        r.uagg[...] = jnp.zeros_like(r.uagg)

        def forward_block(b, carry):
            first = first_row(b)

            def filters(part, cg, at):
                return r.silu[b, part * CG + cg, at, :]

            def keys(cg, at, cols, near_rows):
                product = r.query[cg] * r.kv[cg, near_rows, :] * filters(0, cg, at).astype(F32)
                coarse = product.astype(BF16)
                return coarse, (product - coarse.astype(F32)).astype(BF16)

            coarse, fine = stacked(sz, first, keys)
            score = dot(coarse, r.heads[...]) + dot(fine, r.heads[...])
            for cg in range(CG):
                r.score[b, cg] = score[:, halves[cg]].astype(BF16)

            def vectors(cg, at, cols, near_rows):
                value = r.kv[2 * CG + cg, near_rows, :].astype(BF16) * filters(2, cg, at)
                return [
                    r.vec[c * CG + cg, near_rows, :].astype(BF16) * value for c in range(3)
                ] + [r.kv[3 * CG + cg, near_rows, :].astype(BF16) * filters(3, cg, at)]

            moved = stacked(sz, first, vectors)
            for c in range(3):
                r.vagg[c] += dot(r.fold[...], moved[c])
            r.uagg[...] += dot(r.units[b], moved[3])

            def scalars(cg, at, cols, near_rows):
                s = r.score[b, cg, at, :]
                attention = s * (1.0 + jnp.tanh(s)) * r.cut_wide[b, at, :]
                return [
                    attention * (r.kv[CG + cg, near_rows, :].astype(BF16) * filters(1, cg, at))
                ]

            r.sagg[...] += dot(r.fold[...], *stacked(sz, first, scalars))
            return carry

        lax.fori_loop(0, NB, forward_block, 0, unroll=4)
        scalar_low = r.sagg[...].astype(BF16)
    else:
        scalar_low = r.scalar_in[...]
    left[E + 3 * A : E + 4 * A, :] = scalar_low
    out_proj = dot(scalar_low, wout[...])
    vec_dot = vector_dot(r, sz)
    if fwd:
        vector_agg = [r.vagg[c] + r.uagg[c * A : (c + 1) * A, :] for c in range(3)]
        write_layer_output(r, sz, own, out_proj, vec_dot, vector_agg)

    def incoming(index):
        if fwd:
            return r.cotangent[m, 0, index].astype(F32)
        gap = jnp.zeros((A - 2 * H, F), F32)
        edge = [r.inc_low[index, 0:H].astype(F32), gap, r.inc_high[index, 0:H].astype(F32)]
        value = r.inc[index].astype(F32) + jnp.concatenate(edge, axis=0)
        return value.astype(BF16).astype(F32)

    g_x = incoming(0)
    r.gx[0] = g_x
    g_first = jnp.zeros((A, F), F32)
    g_mid = g_x * out_proj[:, F : 2 * F]
    for c in range(3):
        g_vec = incoming(c + 1)
        r.gx[c + 1] = g_vec
        rows = slice(c * A, (c + 1) * A)
        r.gvlow[rows, :] = g_vec.astype(BF16)
        g_first = g_first + g_vec * vp[rows, 2 * F :]
        r.gvproj[rows, 0:F] = (g_mid * vp[rows, F : 2 * F]).astype(BF16)
        r.gvproj[rows, F : 2 * F] = (g_mid * vp[rows, 0:F]).astype(BF16)
        r.gvproj[rows, 2 * F :] = (g_vec * out_proj[:, 0:F]).astype(BF16)
    r.gout[:, 0:F] = g_first.astype(BF16)
    r.gout[:, F : 2 * F] = (g_x * vec_dot).astype(BF16)
    r.gout[:, 2 * F :] = g_x.astype(BF16)
    r.gs[...] = dot(r.gout[...], wout[...], 1, 1).astype(BF16)
    for total in (r.gnear, r.gq, r.gfilt):
        total[...] = jnp.zeros_like(total)

    def backward_block(b, carry):
        first = first_row(b)
        base = pl.multiple_of(first // SUBLANES * SUBLANES, SUBLANES)
        lanes = iota((W, EB), 1)
        place = jnp.where(
            lanes % A + lanes // A + (first - base) == iota((W, EB), 0), 1.0, 0.0
        ).astype(BF16)

        def collect(index, terms):
            r.gnear[index, pl.ds(base, W), :] += dot(place, terms)

        def filters(part, cg, at):
            return r.silu[b, part * CG + cg, at, :], r.slope[b, part * CG + cg, at, :]

        def weights(cg, at, cols, near_rows):
            value = r.kv[CG + cg, near_rows, :].astype(BF16)
            return [r.gs[:, cols] * (value * filters(1, cg, at)[0])]

        g_att = dot(*stacked(sz, first, weights), r.heads[...])

        def vectors(cg, at, cols, near_rows):
            f, slope = filters(2, cg, at)
            value = r.kv[2 * CG + cg, near_rows, :].astype(BF16)
            message = value * f
            moved = []
            for c in range(3):
                g_vec = r.gvlow[c * A : (c + 1) * A, cols]
                term = g_vec * r.vec[c * CG + cg, near_rows, :].astype(BF16)
                g_edge = term if c == 0 else g_edge + term
                moved.append(g_vec * message)
            return moved + [g_edge * f, g_edge * (value * slope)]

        *moved, g_value, g_pre = stacked(sz, first, vectors)
        for c in range(3):
            collect(4 + c, moved[c])
        collect(2, g_value)
        pre = [None, None, g_pre, None]
        g_third = dot(r.units[b], r.gvlow[...], 0, 0)

        def units(cg, at, cols, near_rows):
            f, slope = filters(3, cg, at)
            value = r.kv[3 * CG + cg, near_rows, :].astype(BF16)
            g_edge = g_third[at, cols].astype(BF16)
            return value * f, g_edge * f, g_edge * (value * slope)

        message, g_value, pre[3] = stacked(sz, first, units)
        collect(3, g_value)
        g_unit = dot(r.gvlow[...], message, 1, 1)
        for c in range(3):
            r.gunit[c, pl.ds(b, 1), :] = jnp.sum(
                g_unit[c * A : (c + 1) * A, :] * r.diag[...], axis=0, keepdims=True
            )

        def attention(cg, at, cols, near_rows):
            s = r.score[b, cg, at, :]
            t = jnp.tanh(s)
            up = 1.0 + t
            act = s * up
            wide = r.cut_wide[b, at, :]
            ga = g_att[at, cols].astype(BF16)
            g_score = ga * wide * (up + act * (1.0 - t))
            g_edge = r.gs[:, cols] * (act * wide)
            f, slope = filters(0, cg, at)
            key = r.kv[cg, near_rows, :].astype(BF16)
            query = r.query_low[:, cols]
            middle = g_score * f
            made = [ga * act, middle * key, middle * query, (g_score * slope) * (key * query)]
            f, slope = filters(1, cg, at)
            value = r.kv[CG + cg, near_rows, :].astype(BF16)
            return made + [g_edge * f, g_edge * (value * slope)]

        g_act, g_query, g_key, pre[0], g_value, pre[1] = stacked(sz, first, attention)
        r.gq[...] += dot(r.fold[...], g_query)
        collect(0, g_key)
        collect(1, g_value)
        g_cut = dot(jnp.ones((16, F), BF16), g_act, 1, 1)[0:1, :] * (2.0 * HEADS / F)
        g_smear = jnp.zeros((sz.basis, EB), F32)
        for part in range(4):
            cols = slice(part * F, (part + 1) * F)
            g_smear = g_smear + dot(r.wh[:, cols], pre[part], 1, 1)
            r.gfilt[:, cols] += dot(r.smear[b], pre[part])
        delta, bell = bell_of(r, sz, b)
        through = g_smear * bell
        r.gcut[pl.ds(b, 1), :] = g_cut + jnp.sum(through, axis=0, keepdims=True)
        r.gshrink[pl.ds(b, 1), :] = r.geo[CUT, pl.ds(b, 1), :] * jnp.sum(
            through * delta, axis=0, keepdims=True
        ) * (-2.0 * sharpness_of(sz.basis))
        return carry

    lax.fori_loop(0, NB, backward_block, 0)

    distance = r.geo[DISTANCE]
    g_dist = r.gcut[...] * r.geo[LIVE] * jnp.where(
        distance < CUTOFF,
        (-0.5 * math.pi / CUTOFF) * jnp.sin(math.pi * distance / CUTOFF),
        0.0,
    ) - r.gshrink[...] * r.geo[SHRINK]
    inverse = 1.0 / distance
    g_unit = [r.gunit[c] for c in range(3)]
    sep = [r.geo[c] for c in range(3)]
    along = g_unit[0] * sep[0] + g_unit[1] * sep[1] + g_unit[2] * sep[2]
    radial = (g_dist - along * inverse * inverse) * inverse
    r.gplaces[...] = jnp.zeros_like(r.gplaces)
    for c in range(3):
        g_sep = g_unit[c] * inverse + radial * sep[c]
        first, other = g_sep[:, :LANES], g_sep[:, LANES:]
        z = (
            jnp.where(lane < A, first, 0.0)
            + pltpu.roll(jnp.where(lane < A, 0.0, first), A + 1, 1)
            + pltpu.roll(jnp.where(lane < A, other, 0.0), 2, 1)
            + pltpu.roll(jnp.where(lane < A, 0.0, other), A + 3, 1)
        )
        for bit in range(3):
            z = jnp.where((row >> bit) & 1 == 1, pltpu.roll(z, GROUP * 2**bit, 1), z)
        z = jnp.where(row >= 4, pltpu.roll(z, 1, 1), z)
        total = jnp.sum(g_sep, axis=0, keepdims=True)
        mine = total[:, 0:A] + total[:, A : 2 * A] + total[:, 2 * A : 3 * A] + total[:, 3 * A :]
        mine = jnp.concatenate(
            [jnp.zeros((1, H), F32), mine, jnp.zeros((1, LANES - H - A), F32)], axis=1
        )
        r.gplaces[c : c + 1, :] = jnp.sum(z, axis=0, keepdims=True) - mine

    gproj = r.gproj
    gproj[:, 0:F] = jnp.zeros((E, F), BF16)
    gproj[H : H + A, 0:F] = r.gq[...].astype(BF16)
    for part in range(4):
        gproj[:, (part + 1) * F : (part + 2) * F] = r.gnear[part].astype(BF16)
    g_normed = dot(gproj[...], wqkv[...], 1, 1)
    u = gain * g_normed
    g_scalars = scale * (
        u
        - jnp.mean(u, axis=-1, keepdims=True)
        - xhat * jnp.mean(u * xhat, axis=-1, keepdims=True)
    )
    r.gnorm[...] = jnp.zeros_like(r.gnorm)
    r.gnorm[0:1, :] = jnp.sum(g_normed * xhat, axis=0, keepdims=True)
    r.gnorm[1:2, :] = jnp.sum(g_normed, axis=0, keepdims=True)
    vec_back = dot(r.gvproj[...], wvec[...], 1, 1)
    for index in range(4):
        if index == 0:
            whole = g_scalars
            middle = whole[H : H + A] + r.gx[0]
        else:
            c = index - 1
            whole = r.gnear[4 + c]
            middle = whole[H : H + A] + r.gx[index] + vec_back[c * A : (c + 1) * A, :]
        r.back[index] = middle
        r.back_low[index] = middle.astype(BF16)
        r.rim_low[index] = whole[0:H].astype(BF16)
        r.rim_high[index] = whole[H + A :].astype(BF16)


FACTORS = ("left", "gproj", "gvproj", "gout", "gfilt", "gnorm")
BORDERS = ("rim_low", "rim_high", "gplaces")


def call(body, arrays, outs, scratch, role=None, grant_mb=16, place=VMEM):
    arrays, outs = vars(arrays), vars(outs)
    names = list(arrays) + list(outs) + list(scratch)

    def kernel(*args):
        refs = SimpleNamespace(**dict(zip(names, args, strict=True)))
        if role is None:
            body(refs)
        else:
            pl.when(lax.axis_index("section") == role)(lambda: body(refs))

    results = pl.pallas_call(
        kernel,
        out_shape=list(outs.values()),
        in_specs=[spec for _, spec in arrays.values()],
        out_specs=[place for _ in outs],
        scratch_shapes=[
            pltpu.VMEM(*s) if isinstance(s, tuple) else s for s in scratch.values()
        ],
        compiler_params=pltpu.CompilerParams(vmem_limit_bytes=int(grant_mb * 2**20)),
    )(*[array for array, _ in arrays.values()])
    return SimpleNamespace(**dict(zip(outs, results, strict=True)))


def first_call(sz, m, fetch, sent, arrays):
    A, H, E, F = sz.atoms, sz.halo, sz.rows, sz.width
    EB, CG, NB = sz.edges, sz.halves, sz.blocks
    shape = jax.ShapeDtypeStruct
    results = dict(
        fresh=((4, A, F), BF16),
        head=((4, sent, F), BF16),
        tail=((4, sent, F), BF16),
        o_scalar=((A, F), BF16),
        score=((NB, CG, EB, LANES), BF16),
    )
    fetched = dict(
        s_own=((4, A, F), BF16),
        s_slots=((3 * sz.slots + 8, LANES), F32),
        s_norms=((16, F), F32),
        s_wqkv=((F, 5 * F), BF16),
        s_wvec=((F, 3 * F), BF16),
        s_wh=((sz.basis, 4 * F), BF16),
        s_wout=((F, 3 * F), BF16),
        sems=pltpu.SemaphoreType.DMA((10,)),
    )
    outs = SimpleNamespace(**{k: shape(*v) for k, v in results.items()})
    scratch = dict(
        left=((sz.factors, F), BF16),
        query=((CG, A, LANES), F32),
        kv=((4 * CG, E, LANES), F32),
        vec=((3 * CG, E, LANES), F32),
        vproj=((3 * A, 3 * F), F32),
        heads=((F, F), BF16),
        diag=((A, EB), F32),
        geo=((10, 8, EB), F32),
        centres=((sz.basis, EB), F32),
        smear_t=((NB, EB, sz.basis), BF16),
        cut_wide=((NB, EB, LANES), F32),
        units=((NB, 3 * A, EB), BF16),
        pack10=((EB, F), BF16),
        pack20=((EB, F), BF16),
        pack11=((EB, F), BF16),
        pack21=((EB, F), BF16),
        sagg=((CG, A, LANES), F32),
        vagg=((3 * CG, A, LANES), F32),
        third=((NB, EB, F), BF16),
    )
    if fetch:
        scratch.update(fetched)
    return call(
        lambda r: first_forward(r, sz, m, fetch), arrays, outs, scratch, FIRST, grant_mb=20
    )


def filter_call(sz, role, which, arrays):
    A, F = sz.atoms, sz.width
    EB, CG, NB = sz.edges, sz.halves, sz.blocks
    shape = jax.ShapeDtypeStruct
    outs = dict(
        geo=shape((10, 8, EB), F32),
        smear=shape((NB, sz.basis, EB), BF16),
        cut_wide=shape((NB, EB, LANES), BF16),
        units=shape((NB, 3 * A, EB), BF16),
        silu=shape((NB, 4 * CG, EB, LANES), BF16),
        slope=shape((NB, 4 * CG, EB, LANES), BF16),
    )
    scratch = dict(
        diag=((A, EB), F32),
        centres=((sz.basis, EB), F32),
        smear_t=((NB, EB, sz.basis), BF16),
    )
    made = call(
        lambda r: edge_filters(r, sz, which),
        arrays,
        SimpleNamespace(**{f"{k}{m}": v for m in which for k, v in outs.items()}),
        scratch,
        role,
        grant_mb=6,
    )
    return {m: SimpleNamespace(**{k: getattr(made, f"{k}{m}") for k in outs}) for m in which}


def both_call(sz, m, fwd, arrays, border_sets=()):
    A, H, E, F = sz.atoms, sz.halo, sz.rows, sz.width
    EB, CG, NB = sz.edges, sz.halves, sz.blocks
    shape = jax.ShapeDtypeStruct
    outs = SimpleNamespace(
        back=shape((4, A, F), F32),
        back_low=shape((4, A, F), BF16),
        rim_low=shape((4, H, F), BF16),
        rim_high=shape((4, H, F), BF16),
        gplaces=shape((8, LANES), F32),
        left=shape((sz.factors, F), BF16),
        gproj=shape((E, 5 * F), BF16),
        gvproj=shape((3 * A, 3 * F), BF16),
        gout=shape((A, 3 * F), BF16),
        gfilt=shape((sz.basis, 4 * F), F32),
        gnorm=shape((8, F), F32),
    )
    scratch = dict(
        query=((CG, A, LANES), F32),
        query_low=((A, F), BF16),
        kv=((4 * CG, E, LANES), F32),
        vec=((3 * CG, E, LANES), F32),
        vproj=((3 * A, 3 * F), F32),
        heads=((F, F), BF16),
        diag=((A, EB), F32),
        fold=((A, EB), BF16),
        centres=((sz.basis, EB), F32),
        gx=((4, A, F), F32),
        gvlow=((3 * A, F), BF16),
        gs=((A, F), BF16),
        gq=((A, F), F32),
        gnear=((7, E, F), F32),
        gunit=((3, 8, EB), F32),
        gcut=((8, EB), F32),
        gshrink=((8, EB), F32),
    )
    if fwd:
        outs.fresh = shape((4, A, F), BF16)
        scratch.update(
            score=((NB, CG, EB, LANES), BF16), sagg=((A, F), F32), vagg=((3, A, F), F32), uagg=((3 * A, F), F32)
        )
    if not border_sets:
        role = SECOND if fwd else FIRST
        return call(lambda r: both_ways(r, sz, m, fwd), arrays, outs, scratch, role)
    count = m + 1
    outs.up, outs.down = shape((count, 4, H, F), BF16), shape((count, 4, H, F), BF16)
    outs.moved = shape((count, 8, LANES), F32)
    for role, sets in enumerate(border_sets):
        for i, made in enumerate(sets):
            for name in BORDERS:
                setattr(arrays, f"{name}_{role}_{i}", (getattr(made, name), VMEM))

    def hand_on(r, role):
        for i in range(count):
            low, high, places = (
                getattr(r, f"{name}_{role}_{i}") if i < len(border_sets[role]) else getattr(r, name)
                for name in BORDERS
            )
            r.up[i] = high[...]
            r.down[i] = low[...]
            r.moved[i] = places[...]

    def body(r):
        @pl.when(lax.axis_index("section") == FIRST)
        def _():
            both_ways(r, sz, m, fwd)
            hand_on(r, FIRST)

        pl.when(lax.axis_index("section") == SECOND)(lambda: hand_on(r, SECOND))

    return call(body, arrays, outs, scratch)


def border_call(sz, features, coords):
    A, H, F = sz.atoms, sz.halo, sz.width
    count = features.shape[0]

    def body(r):
        moves = [(r.coords, r.s_coords)]
        for m in range(count):
            moves += [
                (r.features.at[m, 0, :, A - H : A, :], r.up.at[m, 0:4]),
                (r.features.at[m, 0, :, 0:H, :], r.down.at[m, 0:4]),
            ]
        copies = [
            pltpu.make_async_copy(source, target, r.sems.at[i])
            for i, (source, target) in enumerate(moves)
        ]
        for copy in copies:
            copy.start()
        copies[0].wait()
        for m in range(count):
            r.up[m, 4] = packed_places([r.s_coords[m, c][:, A - H :] for c in range(3)], F)
            r.down[m, 4] = packed_places([r.s_coords[m, c][:, :H] for c in range(3)], F)
        for copy in copies[1:]:
            copy.wait()

    shape = jax.ShapeDtypeStruct((count, 5, H, F), BF16)
    return call(
        body,
        SimpleNamespace(features=(features, HBM), coords=(coords, HBM)),
        SimpleNamespace(up=shape, down=shape),
        dict(s_coords=(coords.shape, F32), sems=pltpu.SemaphoreType.DMA((2 * count + 1,))),
        grant_mb=54,
    )


class Rooms:
    def __init__(self, sz):
        F = sz.width
        ends = [0]
        for rows in (F, F, F, 4 * sz.atoms, sz.basis):
            ends.append(ends[-1] + rows)
        self.wqkv, self.wvec, self.wout, self.own, self.wh = [
            slice(*pair) for pair in zip(ends, ends[1:])
        ]
        table = 3 * sz.slots + 8
        self.slots, self.norms = slice(0, table), slice(table, table + 8)
        self.coords = slice(table + 8, table + 16)
        self.low_shape, self.wide_shape = (20480, 5 * F), (51200, F)


def stage_call(sz, features, coords, neighbours, shifts, counts, gain, bias, filter_weight, weights):
    A, F, K = sz.atoms, sz.width, sz.slots
    count = features.shape[0]
    rooms = Rooms(sz)

    def body(r):
        moves = [(r.coords, r.s_coords), (r.counts, r.s_counts)]
        moves += [(r.gain, r.s_gain), (r.bias, r.s_bias), (r.wfilt.at[0], r.s_wfilt)]
        for m in range(count):
            moves += [
                (r.nbr.at[m, 0], r.s_slots.at[m, 0:K]),
                (r.shifts.at[m, 0, 0], r.s_slots.at[m, K : 2 * K]),
                (r.shifts.at[m, 0, 1], r.s_slots.at[m, 2 * K : 3 * K]),
            ]
        near = len(moves)
        moves += [(r.features.at[0, 0], r.s_own), (r.wqkv.at[0], r.s_wqkv)]
        moves += [(r.wvec.at[0], r.s_wvec), (r.wout.at[0], r.s_wout)]
        copies = [
            pltpu.make_async_copy(source, target, r.sems.at[i])
            for i, (source, target) in enumerate(moves)
        ]
        for copy in copies:
            copy.start()
        for copy in copies[:near]:
            copy.wait()
        r.s_wh[...] = (r.s_wfilt[...].astype(F32) * 0.5).astype(BF16)
        for m in range(count):
            r.s_table[m, 0 : 3 * K, 0:A] = r.s_slots[m].astype(F32)
            r.s_table[m, 3 * K :, 0:A] = jnp.broadcast_to(r.s_counts[m].astype(F32), (8, A))
        r.s_norms[...] = jnp.zeros_like(r.s_norms)
        r.s_norms[0:1, :] = r.s_gain[...].astype(F32)
        r.s_norms[1:2, :] = r.s_bias[...].astype(F32)
        for c in range(3):
            r.s_norms[8 + c : 9 + c, 0:A] = r.s_coords[0, c]
        for copy in copies[near:]:
            copy.wait()
        moves = [
            (r.s_table, r.slots),
            (r.s_norms.at[0:8], r.norms),
            (r.s_wh, r.wh),
            (r.s_table.at[0], r.wide.at[rooms.slots, 0:LANES]),
            (r.s_norms, r.wide.at[rooms.norms.start : rooms.coords.stop]),
            (r.s_wqkv, r.low.at[rooms.wqkv]),
            (r.s_wvec, r.low.at[rooms.wvec, 0 : 3 * F]),
            (r.s_wout, r.low.at[rooms.wout, 0 : 3 * F]),
            (r.s_wh, r.low.at[rooms.wh, 0 : 4 * F]),
        ]
        for index in range(4):
            start = rooms.own.start + index * A
            moves.append((r.s_own.at[index], r.low.at[start : start + A, 0:F]))
        later = [
            pltpu.make_async_copy(source, target, r.sems.at[len(copies) + i])
            for i, (source, target) in enumerate(moves)
        ]
        for copy in later:
            copy.start()
        for copy in later:
            copy.wait()

    shape = jax.ShapeDtypeStruct
    wqkv, wvec, wout = weights
    return call(
        body,
        SimpleNamespace(
            features=(features, HBM),
            coords=(coords, HBM),
            nbr=(neighbours, HBM),
            shifts=(shifts, HBM),
            counts=(counts, HBM),
            gain=(gain, HBM),
            bias=(bias, HBM),
            wfilt=(filter_weight, HBM),
            wqkv=(wqkv, HBM),
            wvec=(wvec, HBM),
            wout=(wout, HBM),
        ),
        SimpleNamespace(
            slots=shape((count, 3 * K + 8, LANES), F32),
            norms=shape((8, F), F32),
            wh=shape((sz.basis, 4 * F), BF16),
            low=shape(rooms.low_shape, BF16),
            wide=shape(rooms.wide_shape, F32),
        ),
        dict(
            s_coords=(coords.shape, F32),
            s_counts=(counts.shape, jnp.int32),
            s_gain=(gain.shape, BF16),
            s_bias=(bias.shape, BF16),
            s_wfilt=(filter_weight.shape[1:], BF16),
            s_slots=((count, 3 * K, A), jnp.int32),
            s_own=((4, A, F), BF16),
            s_wqkv=(wqkv.shape[1:], BF16),
            s_wvec=(wvec.shape[1:], BF16),
            s_wout=(wout.shape[1:], BF16),
            s_wh=(filter_weight.shape[1:], BF16),
            s_table=((count, 3 * K + 8, LANES), F32),
            s_norms=((16, F), F32),
            sems=pltpu.SemaphoreType.DMA((3 * count + 22,)),
        ),
        grant_mb=54,
        place=HBM,
    )


def gradient_call(sz, sets):
    A, E, F = sz.atoms, sz.rows, sz.width
    count = len(sets[0])
    w1, w2, w3 = sz.widths
    w4, w5 = 4 * F // sz.space, F // sz.space
    half = F // 2
    arrays = SimpleNamespace()
    for role in (FIRST, SECOND):
        for m in range(count):
            for name in FACTORS:
                setattr(arrays, f"{name}_{role}_{m}", (getattr(sets[role][m], name), VMEM))

    def body(r, role):
        def get(name, m):
            return getattr(r, f"{name}_{role}_{m}")

        every = range(count)
        e, a = E, A
        r.qkv[...] = sum(dot(get("gproj", m)[...], get("left", m)[0:e, :], 0, 0) for m in every)
        r.vector[...] = sum(
            dot(get("gvproj", m)[...], get("left", m)[e : e + 3 * a, :], 0, 0) for m in every
        )
        r.out[...] = sum(
            dot(get("gout", m)[...], get("left", m)[e + 3 * a : e + 4 * a, :], 0, 0) for m in every
        )
        filt = sum(get("gfilt", m)[...] for m in every) * 0.5
        norm = sum(get("gnorm", m)[...] for m in every)
        core = lax.axis_index("dp")
        for k in range(sz.space):
            spare = [filt[:, k * w4 : (k + 1) * w4]]
            if half > w4:
                spare.append(jnp.zeros((sz.basis, half - w4), F32))
            left = jnp.concatenate(spare, axis=1)
            rows = [norm[:, k * w5 : (k + 1) * w5], jnp.zeros((8, half - w5), F32)]
            right = jnp.concatenate(rows, axis=1)
            right = jnp.concatenate(
                [right, jnp.zeros((sz.packed - sz.spare - 8, half), F32)], axis=0
            )
            if sz.packed - sz.spare > sz.basis:
                gap = jnp.zeros((sz.packed - sz.spare - sz.basis, half), F32)
                left = jnp.concatenate([left, gap], axis=0)
            parts = [
                r.qkv[k * w1 : (k + 1) * w1, :],
                r.vector[k * w2 : (k + 1) * w2, :],
                r.out[k * w3 : (k + 1) * w3, :],
            ]
            first = jnp.concatenate([part[:, :half] for part in parts] + [left], axis=0)
            second = jnp.concatenate([part[:, half:] for part in parts] + [right], axis=0)
            r.send[k] = jnp.where(core == 0, second, first).astype(BF16)
            r.stay[k] = jnp.where(core == 0, first, second)

    def both(r):
        for role in (FIRST, SECOND):
            pl.when(lax.axis_index("section") == role)(lambda role=role: body(r, role))

    shape = jax.ShapeDtypeStruct
    return call(
        both,
        arrays,
        SimpleNamespace(
            send=shape((sz.space, sz.packed, half), BF16),
            stay=shape((sz.space, sz.packed, half), F32),
        ),
        dict(
            qkv=((5 * F, F), F32),
            vector=((3 * F, F), F32),
            out=((3 * F, F), F32),
        ),
    )


def border_rows(sz, m, index):
    start = sz.packed + (m * 5 + index) * 2 * sz.halo
    return [slice(start + i * sz.halo, start + (i + 1) * sz.halo) for i in range(2)]


def border_block(sz, ref, m, index):
    return jnp.concatenate([ref[rows, :] for rows in border_rows(sz, m, index)], axis=1)


def piece_call(sz, stay, recv, up, down, moved, other):
    A, H, E, F = sz.atoms, sz.halo, sz.rows, sz.width
    count = up.shape[0]
    half = F // 2

    def body(r):
        slab, space = lax.axis_index("space"), sz.space
        for hop in range(space):
            k = lax.rem(slab + hop, space)
            total = r.stay[k] + r.recv[k].astype(F32)
            target = getattr(r, f"hop{hop}")
            target[0 : sz.packed, :] = total.astype(target.dtype)
        for m in range(count):
            places = r.moved[m] + r.other[m]
            rows = [places[c : c + 1, :] for c in range(3)]
            ends = (
                (r.hop1, r.up, [row[:, H + A : E] for row in rows]),
                (getattr(r, f"hop{space - 1}"), r.down, [row[:, 0:H] for row in rows]),
            )
            for target, border, part in ends:
                blocks = [border[m, index] for index in range(4)] + [packed_places(part, F)]
                for index, block in enumerate(blocks):
                    first, second = border_rows(sz, m, index)
                    target[first, :] = block[:, :half]
                    target[second, :] = block[:, half:]
            for c in range(3):
                r.mine[m, c] = rows[c][:, H : H + A]

    shape = jax.ShapeDtypeStruct
    outs = {
        f"hop{hop}": shape(
            (sz.packed + (10 * H * count if hop in (1, sz.space - 1) else 0), half),
            BF16 if hop else F32,
        )
        for hop in range(sz.space)
    }
    outs.update(mine=shape((count, 3, 1, A), F32))
    made = call(
        body,
        SimpleNamespace(
            stay=(stay, VMEM),
            recv=(recv, VMEM),
            up=(up, VMEM),
            down=(down, VMEM),
            moved=(moved, VMEM),
            other=(other, VMEM),
        ),
        SimpleNamespace(**outs),
        {},
    )
    return [getattr(made, f"hop{hop}") for hop in range(sz.space)], made.mine


def result_call(sz, fresh, back, from_low, from_high, mine):
    A, H, F = sz.atoms, sz.halo, sz.width
    count = len(back[0])
    arrays = SimpleNamespace(
        low=(from_low, VMEM), high=(from_high, VMEM), mine=(mine, VMEM)
    )
    for role in (FIRST, SECOND):
        for m in range(count):
            setattr(arrays, f"fresh_{role}_{m}", (fresh[role][m], VMEM))
            setattr(arrays, f"back_{role}_{m}", (back[role][m], VMEM))

    def body(r, role):
        for m in range(count):
            r.outputs[0, m, 0] = getattr(r, f"fresh_{role}_{m}")[...]
            whole = getattr(r, f"back_{role}_{m}")
            for index in range(4):
                low = border_block(sz, r.low, m, index).astype(F32)
                high = border_block(sz, r.high, m, index).astype(F32)
                r.grads[0, m, 0, index, 0:H, :] = whole[index, 0:H, :] + low
                r.grads[0, m, 0, index, H : A - H, :] = whole[index, H : A - H, :]
                r.grads[0, m, 0, index, A - H :, :] = whole[index, A - H :, :] + high
            for c in range(3):
                edge = [
                    unpacked_places(border_block(sz, r.low, m, 4), c, H),
                    jnp.zeros((1, A - 2 * H), F32),
                    unpacked_places(border_block(sz, r.high, m, 4), c, H),
                ]
                r.places[m, c] = r.mine[m, c] + jnp.concatenate(edge, axis=1)

    def both(r):
        for role in (FIRST, SECOND):
            pl.when(lax.axis_index("section") == role)(lambda role=role: body(r, role))

    shape = jax.ShapeDtypeStruct
    return call(
        both,
        arrays,
        SimpleNamespace(
            outputs=shape((1, count, 1, 4, A, F), BF16),
            grads=shape((1, count, 1, 4, A, F), F32),
            places=shape((count, 3, 1, A), F32),
        ),
        {},
    )


def share_call(sz, total, other):
    F = sz.width
    w1, w2, w3 = sz.widths
    w4, w5 = 4 * F // sz.space, F // sz.space
    half = F // 2

    def body(r, first, second):
        for lanes, part in ((slice(0, half), first), (slice(half, F), second)):
            r.qkv[0, :, lanes] = part[0:w1, :]
            r.vector[0, :, lanes] = part[w1 : w1 + w2, :]
            r.out[0, :, lanes] = part[w1 + w2 : sz.spare, :]
        r.filt[0] = first[sz.spare : sz.spare + sz.basis, 0:w4]
        r.gain[...] = second[sz.spare : sz.spare + 1, 0:w5]
        r.bias[...] = second[sz.spare + 1 : sz.spare + 2, 0:w5]

    def both(r):
        pl.when(lax.axis_index("dp") == 0)(lambda: body(r, r.total, r.other))
        pl.when(lax.axis_index("dp") == 1)(lambda: body(r, r.other, r.total))

    shape = jax.ShapeDtypeStruct
    return call(
        both,
        SimpleNamespace(total=(total, VMEM), other=(other, VMEM)),
        SimpleNamespace(
            gain=shape((1, w5), F32),
            bias=shape((1, w5), F32),
            qkv=shape((1, w1, F), F32),
            vector=shape((1, w2, F), F32),
            filt=shape((1, sz.basis, w4), F32),
            out=shape((1, w3, F), F32),
        ),
        {},
    )


def on_device(
    features,
    coords,
    neighbours,
    counts,
    shifts,
    norm_gain,
    norm_bias,
    qkv_weight,
    vector_weight,
    filter_weight,
    out_weight,
    cotangent,
):
    micro_count = features.shape[0]
    space = lax.axis_size("space")
    sz = Sizes(features.shape[3], features.shape[4], filter_weight.shape[1], neighbours.shape[2], space)
    up = [(i, (i + 1) % space) for i in range(space)]
    down = [((i + 1) % space, i) for i in range(space)]

    places = jnp.transpose(coords, (0, 2, 1, 3))
    borders = border_call(sz, features, places)
    staged = stage_call(
        sz,
        features,
        places,
        neighbours,
        shifts,
        counts,
        norm_gain,
        norm_bias,
        filter_weight,
        (qkv_weight, vector_weight, out_weight),
    )
    slots, norms, half_filter = staged.slots, staged.norms, staged.wh
    pack_low = lax.ppermute(borders.up, "space", up)
    pack_high = lax.ppermute(borders.down, "space", down)
    both = ("section", "space")
    forth = [(k, space + k) for k in range(space)]
    forth_up = [(k, space + (k + 1) % space) for k in range(space)]
    forth_down = [((k + 1) % space, space + k) for k in range(space)]
    back = [(space + k, k) for k in range(space)]
    back_up = [(space + k, (k + 1) % space) for k in range(space)]
    back_down = [(space + (k + 1) % space, k) for k in range(space)]

    def geometry_inputs():
        return SimpleNamespace(
            pack_low=(pack_low, VMEM),
            pack_high=(pack_high, VMEM),
            coords=(places, VMEM),
            slots=(slots, VMEM),
            wh=(half_filter, VMEM),
        )

    firsts, sent, filters = [], [], {}
    for m in range(micro_count):
        if m == 0:
            arrays = SimpleNamespace(
                pack_low=(pack_low, VMEM),
                pack_high=(pack_high, VMEM),
                room=(staged.low, HBM),
                wide=(staged.wide, HBM),
            )
        else:
            arrays = geometry_inputs()
            arrays.features = (features, VMEM)
            arrays.norms = (norms, VMEM)
            arrays.wqkv, arrays.wvec, arrays.wout = (
                (qkv_weight, VMEM), (vector_weight, VMEM), (out_weight, VMEM)
            )
        first = first_call(sz, m, m == 0, sz.sent[m], arrays)
        firsts.append(first)
        if m == micro_count - 1:
            made = filters[SECOND] = filter_call(
                sz, SECOND, range(micro_count), geometry_inputs()
            )
            first.head, made[0].geo = lax.optimization_barrier((first.head, made[0].geo))
        sent.append((
            lax.ppermute(first.fresh, both, forth),
            lax.ppermute(first.tail, both, forth_up),
            lax.ppermute(first.head, both, forth_down),
        ))
    def both_inputs(m, role):
        made = filters[role][m]
        return SimpleNamespace(
            norms=(norms, VMEM),
            wqkv=(qkv_weight, VMEM),
            wvec=(vector_weight, VMEM),
            wh=(half_filter, VMEM),
            wout=(out_weight, VMEM),
            geo=(made.geo, VMEM),
            smear=(made.smear, VMEM),
            cut_wide=(made.cut_wide, VMEM),
            units=(made.units, VMEM),
            silu=(made.silu, VMEM),
            slope=(made.slope, VMEM),
        )

    seconds, returned = [], []
    for m in range(micro_count):
        if m == 1:
            other = filters[FIRST][0]
            other.geo, filters[SECOND][m].geo = lax.optimization_barrier(
                (other.geo, filters[SECOND][m].geo)
            )
        arrays = both_inputs(m, SECOND)
        own, low, high = sent[m]
        arrays.own, arrays.low, arrays.high = (own, VMEM), (low, VMEM), (high, VMEM)
        arrays.cotangent = (cotangent, VMEM)
        second = both_call(sz, m, True, arrays)
        seconds.append(second)
        if m == 0:
            later = geometry_inputs()
            held, second.gplaces = lax.optimization_barrier((slots, second.gplaces))
            later.slots = (held, VMEM)
            filters[FIRST] = filter_call(sz, FIRST, range(micro_count), later)
        back_low, rim_low, rim_high = second.back_low, second.rim_low, second.rim_high
        if m:
            returned[-1], back_low, rim_low, rim_high = lax.optimization_barrier(
                (returned[-1], back_low, rim_low, rim_high)
            )
        returned.append((
            lax.ppermute(back_low, both, back),
            lax.ppermute(rim_high, both, back_up),
            lax.ppermute(rim_low, both, back_down),
        ))
    thirds = []
    for m in range(micro_count):
        arrays = both_inputs(m, FIRST)
        arrays.pack_low, arrays.pack_high = (pack_low, VMEM), (pack_high, VMEM)
        arrays.features = (features, VMEM)
        arrays.scalar_in = (firsts[m].o_scalar, VMEM)
        arrays.score = (firsts[m].score, VMEM)
        inc, inc_low, inc_high = returned[m]
        arrays.inc, arrays.inc_low, arrays.inc_high = (inc, VMEM), (inc_low, VMEM), (inc_high, VMEM)
        sets = (thirds, seconds) if m == micro_count - 1 else ()
        thirds.append(both_call(sz, m, False, arrays, sets))

    last = thirds[-1]
    other = lax.ppermute(last.moved, "section", [(0, 1), (1, 0)])
    shares = gradient_call(sz, (thirds, seconds))
    recv = lax.ppermute(shares.send, "dp", [(0, 1), (1, 0)])
    (total, *pieces), mine = piece_call(sz, shares.stay, recv, last.up, last.down, last.moved, other
    )
    received = [
        lax.ppermute(piece, "space", [(i, (i + hop) % space) for i in range(space)])
        for hop, piece in enumerate(pieces, 1)
    ]
    for piece in received:
        total = total + piece[: sz.packed].astype(F32)
    results = result_call(
        sz,
        ([v.fresh for v in firsts], [v.fresh for v in seconds]),
        ([v.back for v in thirds], [v.back for v in seconds]),
        received[0],
        received[-1],
        mine,
    )
    other = lax.ppermute(total, "dp", [(0, 1), (1, 0)])
    share = share_call(sz, total, other)
    return (
        results.outputs,
        results.grads,
        share.gain,
        share.bias,
        jnp.transpose(share.qkv, (0, 2, 1)),
        jnp.transpose(share.vector, (0, 2, 1)),
        share.filt,
        jnp.transpose(share.out, (0, 2, 1)),
        jnp.transpose(results.places, (0, 2, 1, 3)),
    )


def solution(mesh):
    return jax.shard_map(
        on_device,
        mesh=mesh,
        in_specs=(
            P(None, "dp", None, "space", None),
            P(None, "dp", None, "space"),
            P(None, "dp", None, "space"),
            P(None, "dp", "space"),
            P(None, "dp", None, None, "space"),
            P("section", None),
            P("section", None),
            P("section", None, None),
            P("section", None, None),
            P("section", None, None),
            P("section", None, None),
            P(None, "dp", None, "space", None),
        ),
        out_specs=(
            P("section", None, "dp", None, "space", None),
            P("section", None, "dp", None, "space", None),
            P("section", "space"),
            P("section", "space"),
            P("section", None, "space"),
            P("section", None, "space"),
            P("section", None, "space"),
            P("section", None, "space"),
            P(None, "dp", None, "space"),
        ),
        check_vma=False,
    )
```

```python
import math
from types import SimpleNamespace

import jax
import jax.numpy as jnp
from jax import lax
from jax.experimental import pallas as pl
from jax.experimental.pallas import tpu as pltpu
from jax.sharding import PartitionSpec as P

HEADS = 8
CUTOFF = 5.0
LN_EPS = 1e-05
SOFTEN = 0.25
CROSS = 2.5
GROUP = 4
LANES = 128
SUBLANES = 8
FIRST, SECOND = 0, 1

F32 = jnp.float32
BF16 = jnp.bfloat16
VMEM = pl.BlockSpec(memory_space=pltpu.VMEM)
HBM = pl.BlockSpec(memory_space=pltpu.HBM)


def dot(left, right, left_dim=1, right_dim=0):
    return lax.dot_general(
        left, right, (((left_dim,), (right_dim,)), ((), ())), preferred_element_type=F32
    )


def iota(shape, dim):
    return lax.broadcasted_iota(jnp.int32, shape, dim)


def packed_places(rows, width):
    parts = []
    for row in rows:
        high = row.astype(BF16).astype(F32)
        rest = row - high
        middle = rest.astype(BF16).astype(F32)
        parts += [high, middle, rest - middle]
    gap = 16 - len(parts)
    whole = jnp.concatenate(parts + [jnp.zeros((gap, rows[0].shape[1]), F32)], axis=0)
    wide = [whole, jnp.zeros((16, width - whole.shape[1]), F32)]
    return jnp.concatenate(wide, axis=1).astype(BF16)


def unpacked_places(block, m, c, count):
    rows = block[:, c * count : (c + 1) * count].astype(F32)
    return rows[3 * m : 3 * m + 1] + rows[3 * m + 1 : 3 * m + 2] + rows[3 * m + 2 : 3 * m + 3]


class Sizes:
    def __init__(self, atoms, width, basis, slots, space):
        self.atoms, self.width, self.basis, self.slots, self.space = atoms, width, basis, slots, space
        self.halo = atoms // 4
        self.rows = atoms + 2 * self.halo
        self.blocks = slots // GROUP
        self.edges = GROUP * atoms
        self.halves = width // LANES
        self.window = atoms + SUBLANES
        self.sent = (self.halo, atoms)
        self.widths = (5 * width // space, 3 * width // space, 3 * width // space)
        self.spare = sum(self.widths)
        self.packed = -(-(self.spare + basis) // 16) * 16
        self.factors = -(-(self.rows + 4 * atoms) // LANES) * LANES


def halves_of(sz):
    return [slice(cg * LANES, (cg + 1) * LANES) for cg in range(sz.halves)]


def first_row(b):
    return GROUP * b + jnp.where(b >= 4, 1, 0)


def sharpness_of(basis):
    return (2.0 / basis * (1.0 - math.exp(-CUTOFF))) ** (-2)


def write_centres(ref, basis):
    low_end = math.exp(-CUTOFF)
    step = iota(ref.shape, 0).astype(F32) / (basis - 1)
    ref[...] = low_end * (1.0 - step) + step


def edge_geometry(r, sz, m, coords, slots):
    A, H, E, EB, K = sz.atoms, sz.halo, sz.rows, sz.edges, sz.slots
    lane = iota((8, LANES), 1)
    row = iota((8, LANES), 0)
    slab, last = lax.axis_index("space"), sz.space - 1
    last_block = r.pack_low.shape[0] - 1
    spot = iota((1, LANES), 1)
    length_x = sz.space * A * 4.0 / H
    places = []
    for c in range(3):
        places.append(
            jnp.concatenate(
                [
                    unpacked_places(r.pack_low[last_block], m, c, H),
                    coords[c],
                    unpacked_places(r.pack_high[last_block], m, c, H),
                    jnp.zeros((1, LANES - E), F32),
                ],
                axis=1,
            )
        )
    places.append(
        jnp.where((spot < H) & (slab == 0), -length_x, 0.0)
        + jnp.where((spot >= H + A) & (slab == last), length_x, 0.0)
    )
    near = []
    for c in range(4):
        y = jnp.broadcast_to(places[c], (8, LANES))
        for bit in range(3):
            y = jnp.where((row >> bit) & 1 == 1, pltpu.roll(y, LANES - GROUP * 2**bit, 1), y)
        y = jnp.where(row >= 4, pltpu.roll(y, LANES - 1, 1), y)
        first = jnp.where(lane < A, y, pltpu.roll(y, A - 1, 1))
        other = jnp.where(lane < A, pltpu.roll(y, LANES - 2, 1), pltpu.roll(y, A - 3, 1))
        near.append(jnp.concatenate([first, other], axis=1))
    wide_lane = iota((8, EB), 1)
    wide_row = iota((8, EB), 0)
    wanted = GROUP * wide_row + wide_lane // A + jnp.where(wide_row >= 4, 1, 0) + wide_lane % A
    table = slots[:, 0:A].astype(jnp.int32)
    alive = iota((K, A), 0) < table[3 * K : 3 * K + 1]
    code = jnp.where(alive, 16, 0) + (table[K : 2 * K] + 1) * 4 + (table[2 * K : 3 * K] + 1)
    code = jnp.concatenate([code] * GROUP, axis=1)
    named = jnp.concatenate([table[0:K]] * GROUP, axis=1)
    found = jnp.zeros((8, EB), jnp.int32)
    for n in range(K):
        found = found + jnp.where(named[n : n + 1, :] == wanted, code[n : n + 1, :], 0)
    live = (found >> 4).astype(F32)
    offsets = (
        near[3],
        (((found >> 2) & 3) - 1).astype(F32) * CROSS,
        ((found & 3) - 1).astype(F32) * CROSS,
    )
    sep = []
    for c in range(3):
        mine = coords[c]
        sep.append(near[c] - jnp.concatenate([mine] * GROUP, axis=1) + offsets[c])
    distance = jnp.sqrt(sep[0] * sep[0] + sep[1] * sep[1] + sep[2] * sep[2] + SOFTEN)
    inside = distance < CUTOFF
    cut = jnp.where(inside, 0.5 * (jnp.cos(math.pi * distance / CUTOFF) + 1.0), 0.0) * live
    for index, value in enumerate(
        sep + [distance, live, cut, jnp.exp(-distance)] + [part / distance for part in sep]
    ):
        r.geo[index] = value


DISTANCE, LIVE, CUT, SHRINK, UNIT = 3, 4, 5, 6, 7


def bell_of(r, sz, b):
    delta = r.geo[SHRINK, pl.ds(b, 1), :] - r.centres[...]
    return delta, jnp.exp(-sharpness_of(sz.basis) * delta * delta)


def write_edge_tables(r, sz, b, wide_kind):
    A, EB = sz.atoms, sz.edges
    cut = r.geo[CUT, pl.ds(b, 1), :]
    _, bell = bell_of(r, sz, b)
    smear = cut * bell
    if hasattr(r, "smear"):
        r.smear[b] = smear.astype(BF16)
    r.smear_t[b] = jnp.transpose(smear).astype(BF16)
    coarse = cut.astype(BF16).astype(F32)
    which = iota((16, EB), 0)
    pair = jnp.where(which == 0, coarse, jnp.where(which == 1, cut - coarse, 0.0)).astype(BF16)
    r.cut_wide[b] = dot(pair, jnp.ones((16, LANES), BF16), 0, 0).astype(wide_kind)
    for c in range(3):
        r.units[b, c * A : (c + 1) * A, :] = (
            r.diag[...] * r.geo[UNIT + c, pl.ds(b, 1), :]
        ).astype(BF16)


def write_constants(r, sz):
    A, EB, F = sz.atoms, sz.edges, sz.width
    if hasattr(r, "centres"):
        write_centres(r.centres, sz.basis)
    if hasattr(r, "diag"):
        r.diag[...] = jnp.where(iota((A, EB), 1) % A == iota((A, EB), 0), 1.0, 0.0)
    if hasattr(r, "fold"):
        r.fold[...] = jnp.where(iota((A, EB), 1) % A == iota((A, EB), 0), 1.0, 0.0).astype(BF16)
    if hasattr(r, "heads"):
        r.heads[...] = jnp.where(
            iota((F, F), 0) // (F // HEADS) == iota((F, F), 1) // (F // HEADS), 0.5, 0.0
        ).astype(BF16)


def node_part(r, sz, own, low, high, norms, wqkv):
    A, H, E, F, CG = sz.atoms, sz.halo, sz.rows, sz.width, sz.halves
    halves = halves_of(sz)
    scalars = jnp.concatenate([low[0, 0:H], own[0], high[0, 0:H]], axis=0).astype(F32)
    centred = scalars - jnp.mean(scalars, axis=-1, keepdims=True)
    spread = jnp.mean(centred * centred, axis=-1, keepdims=True)
    scale = lax.rsqrt(spread + LN_EPS)
    normed = (centred * scale * norms[0:1, :] + norms[1:2, :]).astype(BF16)
    left = r.left
    left[0:E, :] = normed
    left[E : E + 3 * A, :] = own[1:4].reshape(3 * A, F)
    left[E + 4 * A :, :] = jnp.zeros((sz.factors - E - 4 * A, F), BF16)
    for part in range(5):
        projected = dot(normed, wqkv[:, part * F : (part + 1) * F])
        for cg in range(CG):
            if part == 0:
                r.query[cg] = projected[H : H + A, halves[cg]]
            else:
                r.kv[(part - 1) * CG + cg] = projected[:, halves[cg]]
    for c in range(3):
        for cg in range(CG):
            r.vec[c * CG + cg, 0:H, :] = low[c + 1, 0:H, halves[cg]].astype(F32)
            r.vec[c * CG + cg, H : H + A, :] = own[c + 1][:, halves[cg]].astype(F32)
            r.vec[c * CG + cg, H + A : E, :] = high[c + 1, 0:H, halves[cg]].astype(F32)
    return centred * scale, scale


def buffers(r, sz, which):
    end = str(which)
    return SimpleNamespace(**{k[:-1]: v for k, v in vars(r).items() if k.endswith(end)})


def tiles(sz, first):
    A = sz.atoms
    for kk in range(GROUP):
        for cg in range(sz.halves):
            yield (
                cg,
                slice(kk * A, (kk + 1) * A),
                slice(cg * LANES, (cg + 1) * LANES),
                pl.ds(first + kk, A),
            )


def stacked(sz, first, tile):
    made = [tile(*where) for where in tiles(sz, first)]
    CG = sz.halves
    wholes = []
    for index in range(len(made[0])):
        lines = [
            jnp.concatenate([made[kk * CG + cg][index] for cg in range(CG)], axis=1)
            for kk in range(GROUP)
        ]
        wholes.append(jnp.concatenate(lines, axis=0))
    return wholes


def vector_dot(r, sz):
    A, F, vp = sz.atoms, sz.width, r.vproj
    return sum(
        vp[c * A : (c + 1) * A, 0:F] * vp[c * A : (c + 1) * A, F : 2 * F] for c in range(3)
    )


def write_layer_output(r, sz, own, out_proj, vec_dot, vector_agg):
    A, H, F, vp = sz.atoms, sz.halo, sz.width, r.vproj
    for index in range(4):
        if index == 0:
            fresh = vec_dot * out_proj[:, F : 2 * F] + out_proj[:, 2 * F :]
        else:
            rows = slice((index - 1) * A, index * A)
            fresh = vp[rows, 2 * F :] * out_proj[:, 0:F] + vector_agg[index - 1]
        fresh = (own[index].astype(F32) + fresh).astype(BF16)
        r.fresh[index] = fresh
        if hasattr(r, "head"):
            r.head[index, 0:H, :] = fresh[:H]
            r.tail[index, 0:H, :] = fresh[A - H :]


def first_forward(r, sz, m, fetch):
    A, H, E, F, EB = sz.atoms, sz.halo, sz.rows, sz.width, sz.edges
    CG = sz.halves
    r.s_low, r.s_high = r.pack_low.at[4 * m : 4 * m + 4], r.pack_high.at[4 * m : 4 * m + 4]
    copies = early = []
    if fetch:
        rooms = Rooms(sz)
        early = [
            (r.wide.at[rooms.slots, 0:LANES], r.s_slots),
            (r.wide.at[rooms.norms.start : rooms.coords.stop], r.s_norms),
            (r.room.at[rooms.wqkv], r.s_wqkv),
        ]
        for index in range(4):
            start = rooms.own.start + index * A
            early.append((r.room.at[start : start + A, 0:F], r.s_own.at[index]))
        late = [
            (r.room.at[rooms.wh, 0 : 4 * F], r.s_wh),
            (r.room.at[rooms.wvec, 0 : 3 * F], r.s_wvec),
            (r.room.at[rooms.wout, 0 : 3 * F], r.s_wout),
        ]
        copies = [
            pltpu.make_async_copy(source, target, r.sems.at[i])
            for i, (source, target) in enumerate(early + late)
        ]
        for copy in copies:
            copy.start()
    else:
        r.s_slots, r.s_norms, r.s_wh = r.slots.at[m], r.norms, r.wh
        r.s_own, r.s_wqkv = r.features.at[m, 0], r.wqkv.at[0]
        r.s_wvec, r.s_wout = r.wvec.at[0], r.wout.at[0]
    write_constants(r, sz)
    r.sagg[...] = jnp.zeros_like(r.sagg)
    r.vagg[...] = jnp.zeros_like(r.vagg)
    for copy in copies[: len(early)]:
        copy.wait()
    coords = [r.s_norms[8 + c : 9 + c, 0:A] if fetch else r.coords[m, c] for c in range(3)]
    edge_geometry(r, sz, m, coords, r.s_slots)

    def tables(b, carry):
        write_edge_tables(r, sz, b, F32)
        return carry

    lax.fori_loop(0, sz.blocks, tables, 0, unroll=2)
    own = r.s_own
    xhat, scale = node_part(r, sz, own, r.s_low, r.s_high, r.s_norms, r.s_wqkv)
    r.xhat[...] = xhat
    r.scale[...] = jnp.broadcast_to(scale, r.scale.shape)
    for cg in range(CG):
        r.query_low[:, cg * LANES : (cg + 1) * LANES] = r.query[cg].astype(BF16)
    for copy in copies[len(early) :]:
        copy.wait()
    r.vproj[...] = dot(r.left[E : E + 3 * A, :], r.s_wvec[...])

    def filter_part(b, part):
        return dot(r.smear_t[b], r.s_wh[:, part * F : (part + 1) * F])

    def block(b, w):
        first = first_row(b)
        half = filter_part(b, 0)
        for cg, at, cols, near_rows in tiles(sz, first):
            h = half[at, cols]
            product = r.query[cg] * r.kv[cg, near_rows, :] * (h + h * jnp.tanh(h))
            coarse = product.astype(BF16)
            w.pack1[at, cols] = coarse
            w.pack2[at, cols] = (product - coarse.astype(F32)).astype(BF16)
        score = dot(w.pack1[...], r.heads[...]) + dot(w.pack2[...], r.heads[...])
        for cg in range(CG):
            r.score[b, cg] = score[:, cg * LANES : (cg + 1) * LANES].astype(BF16)
        half = filter_part(b, 2)
        for cg, at, cols, near_rows in tiles(sz, first):
            h = half[at, cols]
            value = r.kv[2 * CG + cg, near_rows, :] * (h + h * jnp.tanh(h))
            for c in range(3):
                r.vagg[c * CG + cg] += r.vec[c * CG + cg, near_rows, :] * value
        half = filter_part(b, 3)
        for cg, at, cols, near_rows in tiles(sz, first):
            h = half[at, cols]
            value = r.kv[3 * CG + cg, near_rows, :] * (h + h * jnp.tanh(h))
            r.third[b, at, cols] = value.astype(BF16)
        half = filter_part(b, 1)
        for cg, at, cols, near_rows in tiles(sz, first):
            h = half[at, cols]
            s = score[at, cols]
            attention = (s + s * jnp.tanh(s)) * r.cut_wide[b, at, :]
            r.sagg[cg] += attention * (r.kv[CG + cg, near_rows, :] * (h + h * jnp.tanh(h)))

    def pair(i, carry):
        for which in range(2):
            block(2 * i + which, buffers(r, sz, which))
        return carry

    lax.fori_loop(0, sz.blocks // 2, pair, 0)
    third = sum(dot(r.units[b], r.third[b]) for b in range(sz.blocks))
    scalar_low = jnp.concatenate([r.sagg[cg] for cg in range(CG)], axis=1).astype(BF16)
    r.left[E + 3 * A : E + 4 * A, :] = scalar_low
    out_proj = dot(scalar_low, r.s_wout[...])
    vec_dot = vector_dot(r, sz)
    r.out_proj[...] = out_proj
    r.vec_dot[...] = vec_dot
    vector_agg = [
        jnp.concatenate([r.vagg[c * CG + cg] for cg in range(CG)], axis=1)
        + third[c * A : (c + 1) * A, :]
        for c in range(3)
    ]
    write_layer_output(r, sz, own, out_proj, vec_dot, vector_agg)


def edge_filters(r, sz, which):
    F = sz.width
    write_constants(r, sz)
    for m in which:
        w = SimpleNamespace(**vars(r))
        vars(w).update(vars(buffers(r, sz, m)))
        edge_geometry(w, sz, m, r.coords.at[m], r.slots.at[m])

        def block(b, carry, w=w):
            write_edge_tables(w, sz, b, BF16)
            for part in range(4):
                cols = slice(part * F, (part + 1) * F)
                h = dot(r.smear_t[b], r.wh[:, cols])
                if part:
                    h = h.astype(BF16)
                up = 1.0 + jnp.tanh(h)
                f = h * up
                for cg in range(sz.halves):
                    if part == 0 and hasattr(w, "key"):
                        w.key[b, cg] = f[:, cg * LANES : (cg + 1) * LANES]
                f, up = f.astype(BF16), up.astype(BF16)
                slope = up + f * (2.0 - up)
                for cg in range(sz.halves):
                    half = slice(cg * LANES, (cg + 1) * LANES)
                    w.silu[b, part * sz.halves + cg] = f[:, half]
                    w.slope[b, part * sz.halves + cg] = slope[:, half]
            return carry

        lax.fori_loop(0, sz.blocks, block, 0, unroll=2)


def both_ways(r, sz, m, fwd):
    A, H, E, F = sz.atoms, sz.halo, sz.rows, sz.width
    EB, CG, NB, W = sz.edges, sz.halves, sz.blocks, sz.window
    lane = iota((8, LANES), 1)
    row = iota((8, LANES), 0)
    halves = halves_of(sz)
    wqkv, wvec, wout = r.wqkv.at[0], r.wvec.at[0], r.wout.at[0]
    write_constants(r, sz)
    gain = r.norms[0:1, :]
    vp = r.vproj
    if fwd:
        own, left = r.own, r.left
        xhat, scale = node_part(r, sz, own, r.low, r.high, r.norms, wqkv)
        vp[...] = dot(left[E : E + 3 * A, :], wvec[...])
        for cg in range(CG):
            r.query_low[:, halves[cg]] = r.query[cg].astype(BF16)
    else:
        xhat, scale = r.xhat[...], r.scale[:, 0:1]

    if fwd:
        r.sagg[...] = jnp.zeros_like(r.sagg)
        r.vagg[...] = jnp.zeros_like(r.vagg)
        r.uagg[...] = jnp.zeros_like(r.uagg)

        def forward_block(b, carry):
            first = first_row(b)

            def filters(part, cg, at):
                return r.silu[b, part * CG + cg, at, :]

            def keys(cg, at, cols, near_rows):
                product = r.query[cg] * r.kv[cg, near_rows, :] * r.key[b, cg, at, :]
                return [product.astype(BF16)]

            score = dot(*stacked(sz, first, keys), r.heads[...])
            for cg in range(CG):
                r.score[b, cg] = score[:, halves[cg]].astype(BF16)

            def vectors(cg, at, cols, near_rows):
                value = r.kv[2 * CG + cg, near_rows, :].astype(BF16) * filters(2, cg, at)
                return [
                    r.vec[c * CG + cg, near_rows, :].astype(BF16) * value for c in range(3)
                ] + [r.kv[3 * CG + cg, near_rows, :].astype(BF16) * filters(3, cg, at)]

            moved = stacked(sz, first, vectors)
            for c in range(3):
                r.vagg[c] += dot(r.fold[...], moved[c])
            r.uagg[...] += dot(r.units[b], moved[3])

            def scalars(cg, at, cols, near_rows):
                s = r.score[b, cg, at, :]
                attention = s * (1.0 + jnp.tanh(s)) * r.cut_wide[b, at, :]
                return [
                    attention * (r.kv[CG + cg, near_rows, :].astype(BF16) * filters(1, cg, at))
                ]

            r.sagg[...] += dot(r.fold[...], *stacked(sz, first, scalars))
            return carry

        lax.fori_loop(0, NB, forward_block, 0, unroll=8)
        scalar_low = r.sagg[...].astype(BF16)
        left[E + 3 * A : E + 4 * A, :] = scalar_low
        out_proj = dot(scalar_low, wout[...])
        vec_dot = vector_dot(r, sz)
    else:
        out_proj, vec_dot = r.out_proj, r.vec_dot[...]
    if fwd:
        vector_agg = [r.vagg[c] + r.uagg[c * A : (c + 1) * A, :] for c in range(3)]
        write_layer_output(r, sz, own, out_proj, vec_dot, vector_agg)

    def incoming(index):
        if fwd:
            return r.cotangent[m, 0, index].astype(F32)
        gap = jnp.zeros((A - 2 * H, F), F32)
        edge = [r.inc_low[index, 0:H].astype(F32), gap, r.inc_high[index, 0:H].astype(F32)]
        value = r.inc[index].astype(F32) + jnp.concatenate(edge, axis=0)
        return value.astype(BF16).astype(F32)

    g_x = incoming(0)
    r.gx[0] = g_x
    g_first = jnp.zeros((A, F), F32)
    g_mid = g_x * out_proj[:, F : 2 * F]
    for c in range(3):
        g_vec = incoming(c + 1)
        r.gx[c + 1] = g_vec
        rows = slice(c * A, (c + 1) * A)
        r.gvlow[rows, :] = g_vec.astype(BF16)
        g_first = g_first + g_vec * vp[rows, 2 * F :]
        r.gvproj[rows, 0:F] = (g_mid * vp[rows, F : 2 * F]).astype(BF16)
        r.gvproj[rows, F : 2 * F] = (g_mid * vp[rows, 0:F]).astype(BF16)
        r.gvproj[rows, 2 * F :] = (g_vec * out_proj[:, 0:F]).astype(BF16)
    r.gout[:, 0:F] = g_first.astype(BF16)
    r.gout[:, F : 2 * F] = (g_x * vec_dot).astype(BF16)
    r.gout[:, 2 * F :] = g_x.astype(BF16)
    r.gs[...] = dot(r.gout[...], wout[...], 1, 1).astype(BF16)
    for total in (r.gnear, r.gq, r.gfilt):
        total[...] = jnp.zeros_like(total)

    scores = r.score if fwd else r.score_here
    if not fwd:
        scores[...] = r.score[...]

    def backward_block(b, carry):
        first = first_row(b)
        base = pl.multiple_of(first // SUBLANES * SUBLANES, SUBLANES)
        lanes = iota((W, EB), 1)
        place = jnp.where(
            lanes % A + lanes // A + (first - base) == iota((W, EB), 0), 1.0, 0.0
        ).astype(BF16)

        def collect(index, terms):
            r.gnear[index, pl.ds(base, W), :] += dot(place, terms)

        def filters(part, cg, at):
            return r.silu[b, part * CG + cg, at, :], r.slope[b, part * CG + cg, at, :]

        def weights(cg, at, cols, near_rows):
            value = r.kv[CG + cg, near_rows, :].astype(BF16)
            return [r.gs[:, cols] * (value * filters(1, cg, at)[0])]

        g_att = dot(*stacked(sz, first, weights), r.heads[...])

        def vectors(cg, at, cols, near_rows):
            f, slope = filters(2, cg, at)
            value = r.kv[2 * CG + cg, near_rows, :].astype(BF16)
            message = value * f
            moved = []
            for c in range(3):
                g_vec = r.gvlow[c * A : (c + 1) * A, cols]
                term = g_vec * r.vec[c * CG + cg, near_rows, :].astype(BF16)
                g_edge = term if c == 0 else g_edge + term
                moved.append(g_vec * message)
            return moved + [g_edge * f, g_edge * (value * slope)]

        *moved, g_value, g_pre = stacked(sz, first, vectors)
        for c in range(3):
            collect(4 + c, moved[c])
        collect(2, g_value)
        pre = [None, None, g_pre, None]
        g_third = dot(r.units[b], r.gvlow[...], 0, 0)

        def units(cg, at, cols, near_rows):
            f, slope = filters(3, cg, at)
            value = r.kv[3 * CG + cg, near_rows, :].astype(BF16)
            g_edge = g_third[at, cols].astype(BF16)
            return value * f, g_edge * f, g_edge * (value * slope)

        message, g_value, pre[3] = stacked(sz, first, units)
        collect(3, g_value)
        g_unit = dot(r.gvlow[...], message, 1, 1)
        for c in range(3):
            r.gunit[c, pl.ds(b, 1), :] = jnp.sum(
                g_unit[c * A : (c + 1) * A, :] * r.diag[...], axis=0, keepdims=True
            )

        def attention(cg, at, cols, near_rows):
            s = scores[b, cg, at, :]
            t = jnp.tanh(s)
            up = 1.0 + t
            act = s * up
            wide = r.cut_wide[b, at, :]
            ga = g_att[at, cols].astype(BF16)
            g_score = ga * wide * (up + act * (1.0 - t))
            g_edge = r.gs[:, cols] * (act * wide)
            f, slope = filters(0, cg, at)
            key = r.kv[cg, near_rows, :].astype(BF16)
            query = r.query_low[:, cols]
            middle = g_score * f
            made = [ga * act, middle * key, middle * query, (g_score * slope) * (key * query)]
            f, slope = filters(1, cg, at)
            value = r.kv[CG + cg, near_rows, :].astype(BF16)
            return made + [g_edge * f, g_edge * (value * slope)]

        g_act, g_query, g_key, pre[0], g_value, pre[1] = stacked(sz, first, attention)
        collect(1, g_value)
        collect(0, g_key)
        r.gq[...] += dot(r.fold[...], g_query)
        g_cut = dot(jnp.ones((16, F), BF16), g_act, 1, 1)[0:1, :] * (2.0 * HEADS / F)
        g_smear = jnp.zeros((sz.basis, EB), F32)
        for part in range(4):
            cols = slice(part * F, (part + 1) * F)
            g_smear = g_smear + dot(r.wh[:, cols], pre[part], 1, 1)
            r.gfilt[:, cols] += dot(r.smear[b], pre[part])
        delta, bell = bell_of(r, sz, b)
        through = g_smear * bell
        r.gcut[pl.ds(b, 1), :] = g_cut + jnp.sum(through, axis=0, keepdims=True)
        r.gshrink[pl.ds(b, 1), :] = r.geo[CUT, pl.ds(b, 1), :] * jnp.sum(
            through * delta, axis=0, keepdims=True
        ) * (-2.0 * sharpness_of(sz.basis))
        return carry

    lax.fori_loop(0, NB, backward_block, 0)

    distance = r.geo[DISTANCE]
    g_dist = r.gcut[...] * r.geo[LIVE] * jnp.where(
        distance < CUTOFF,
        (-0.5 * math.pi / CUTOFF) * jnp.sin(math.pi * distance / CUTOFF),
        0.0,
    ) - r.gshrink[...] * r.geo[SHRINK]
    inverse = 1.0 / distance
    g_unit = [r.gunit[c] for c in range(3)]
    sep = [r.geo[c] for c in range(3)]
    along = g_unit[0] * sep[0] + g_unit[1] * sep[1] + g_unit[2] * sep[2]
    radial = (g_dist - along * inverse * inverse) * inverse
    r.gplaces[...] = jnp.zeros_like(r.gplaces)
    for c in range(3):
        g_sep = g_unit[c] * inverse + radial * sep[c]
        first, other = g_sep[:, :LANES], g_sep[:, LANES:]
        z = (
            jnp.where(lane < A, first, 0.0)
            + pltpu.roll(jnp.where(lane < A, 0.0, first), A + 1, 1)
            + pltpu.roll(jnp.where(lane < A, other, 0.0), 2, 1)
            + pltpu.roll(jnp.where(lane < A, 0.0, other), A + 3, 1)
        )
        for bit in range(3):
            z = jnp.where((row >> bit) & 1 == 1, pltpu.roll(z, GROUP * 2**bit, 1), z)
        z = jnp.where(row >= 4, pltpu.roll(z, 1, 1), z)
        total = jnp.sum(g_sep, axis=0, keepdims=True)
        mine = total[:, 0:A] + total[:, A : 2 * A] + total[:, 2 * A : 3 * A] + total[:, 3 * A :]
        mine = jnp.concatenate(
            [jnp.zeros((1, H), F32), mine, jnp.zeros((1, LANES - H - A), F32)], axis=1
        )
        r.gplaces[c : c + 1, :] = jnp.sum(z, axis=0, keepdims=True) - mine

    gproj = r.gproj
    gproj[:, 0:F] = jnp.zeros((E, F), BF16)
    gproj[H : H + A, 0:F] = r.gq[...].astype(BF16)
    for part in range(4):
        gproj[:, (part + 1) * F : (part + 2) * F] = r.gnear[part].astype(BF16)
    g_normed = dot(gproj[...], wqkv[...], 1, 1)
    u = gain * g_normed
    g_scalars = scale * (
        u
        - jnp.mean(u, axis=-1, keepdims=True)
        - xhat * jnp.mean(u * xhat, axis=-1, keepdims=True)
    )
    r.gnorm[...] = jnp.zeros_like(r.gnorm)
    r.gnorm[0:1, :] = jnp.sum(g_normed * xhat, axis=0, keepdims=True)
    r.gnorm[1:2, :] = jnp.sum(g_normed, axis=0, keepdims=True)
    vec_back = dot(r.gvproj[...], wvec[...], 1, 1)
    for index in range(4):
        if index == 0:
            whole = g_scalars
            middle = whole[H : H + A] + r.gx[0]
        else:
            c = index - 1
            whole = r.gnear[4 + c]
            middle = whole[H : H + A] + r.gx[index] + vec_back[c * A : (c + 1) * A, :]
        r.back[index] = middle
        r.back_low[index] = middle.astype(BF16)
        r.rim_low[index] = whole[0:H].astype(BF16)
        r.rim_high[index] = whole[H + A :].astype(BF16)


FACTORS = ("left", "gproj", "gvproj", "gout", "gfilt", "gnorm")
HANDED = (
    "query_low", "kv", "vec", "vproj", "xhat", "scale", "out_proj", "vec_dot", "score"
)
BORDERS = ("rim_low", "rim_high", "gplaces")


def call(body, arrays, outs, scratch, role=None, grant_mb=16, place=VMEM):
    arrays, outs = vars(arrays), vars(outs)
    names = list(arrays) + list(outs) + list(scratch)

    def kernel(*args):
        refs = SimpleNamespace(**dict(zip(names, args, strict=True)))
        if role is None:
            body(refs)
        else:
            pl.when(lax.axis_index("section") == role)(lambda: body(refs))

    results = pl.pallas_call(
        kernel,
        out_shape=list(outs.values()),
        in_specs=[spec for _, spec in arrays.values()],
        out_specs=[place for _ in outs],
        scratch_shapes=[
            pltpu.VMEM(*s) if isinstance(s, tuple) else s for s in scratch.values()
        ],
        compiler_params=pltpu.CompilerParams(vmem_limit_bytes=int(grant_mb * 2**20)),
    )(*[array for array, _ in arrays.values()])
    return SimpleNamespace(**dict(zip(outs, results, strict=True)))


def first_call(sz, m, fetch, sent, arrays):
    A, H, E, F = sz.atoms, sz.halo, sz.rows, sz.width
    EB, CG, NB = sz.edges, sz.halves, sz.blocks
    shape = jax.ShapeDtypeStruct
    results = dict(
        fresh=((4, A, F), BF16),
        head=((4, sent, F), BF16),
        tail=((4, sent, F), BF16),
        left=((sz.factors, F), BF16),
        query_low=((A, F), BF16),
        kv=((4 * CG, E, LANES), F32),
        vec=((3 * CG, E, LANES), F32),
        vproj=((3 * A, 3 * F), F32),
        xhat=((E, F), F32),
        scale=((E, LANES), F32),
        out_proj=((A, 3 * F), F32),
        vec_dot=((A, F), F32),
        score=((NB, CG, EB, LANES), BF16),
    )
    fetched = dict(
        s_own=((4, A, F), BF16),
        s_slots=((3 * sz.slots + 8, LANES), F32),
        s_norms=((16, F), F32),
        s_wqkv=((F, 5 * F), BF16),
        s_wvec=((F, 3 * F), BF16),
        s_wh=((sz.basis, 4 * F), BF16),
        s_wout=((F, 3 * F), BF16),
        sems=pltpu.SemaphoreType.DMA((10,)),
    )
    outs = SimpleNamespace(**{k: shape(*v) for k, v in results.items()})
    scratch = dict(
        query=((CG, A, LANES), F32),
        heads=((F, F), BF16),
        diag=((A, EB), F32),
        geo=((10, 8, EB), F32),
        centres=((sz.basis, EB), F32),
        smear_t=((NB, EB, sz.basis), BF16),
        cut_wide=((NB, EB, LANES), F32),
        units=((NB, 3 * A, EB), BF16),
        pack10=((EB, F), BF16),
        pack20=((EB, F), BF16),
        pack11=((EB, F), BF16),
        pack21=((EB, F), BF16),
        sagg=((CG, A, LANES), F32),
        vagg=((3 * CG, A, LANES), F32),
        third=((NB, EB, F), BF16),
    )
    if fetch:
        scratch.update(fetched)
    return call(
        lambda r: first_forward(r, sz, m, fetch), arrays, outs, scratch, FIRST, grant_mb=20
    )


def filter_call(sz, role, which, arrays):
    A, F = sz.atoms, sz.width
    EB, CG, NB = sz.edges, sz.halves, sz.blocks
    shape = jax.ShapeDtypeStruct
    outs = dict(
        geo=shape((10, 8, EB), F32),
        smear=shape((NB, sz.basis, EB), BF16),
        cut_wide=shape((NB, EB, LANES), BF16),
        units=shape((NB, 3 * A, EB), BF16),
        silu=shape((NB, 4 * CG, EB, LANES), BF16),
        slope=shape((NB, 4 * CG, EB, LANES), BF16),
    )
    if role == SECOND:
        outs.update(key=shape((NB, CG, EB, LANES), F32))
    scratch = dict(
        diag=((A, EB), F32),
        centres=((sz.basis, EB), F32),
        smear_t=((NB, EB, sz.basis), BF16),
    )
    made = call(
        lambda r: edge_filters(r, sz, which),
        arrays,
        SimpleNamespace(**{f"{k}{m}": v for m in which for k, v in outs.items()}),
        scratch,
        role,
        grant_mb=6,
    )
    return {m: SimpleNamespace(**{k: getattr(made, f"{k}{m}") for k in outs}) for m in which}


def both_call(sz, m, fwd, arrays, border_sets=()):
    A, H, E, F = sz.atoms, sz.halo, sz.rows, sz.width
    EB, CG, NB = sz.edges, sz.halves, sz.blocks
    shape = jax.ShapeDtypeStruct
    outs = SimpleNamespace(
        back=shape((4, A, F), F32),
        back_low=shape((4, A, F), BF16),
        rim_low=shape((4, H, F), BF16),
        rim_high=shape((4, H, F), BF16),
        gplaces=shape((8, LANES), F32),
        gproj=shape((E, 5 * F), BF16),
        gvproj=shape((3 * A, 3 * F), BF16),
        gout=shape((A, 3 * F), BF16),
        gfilt=shape((sz.basis, 4 * F), F32),
        gnorm=shape((8, F), F32),
    )
    scratch = dict(
        heads=((F, F), BF16),
        diag=((A, EB), F32),
        fold=((A, EB), BF16),
        centres=((sz.basis, EB), F32),
        gx=((4, A, F), F32),
        gvlow=((3 * A, F), BF16),
        gs=((A, F), BF16),
        gq=((A, F), F32),
        gnear=((7, E, F), F32),
        gunit=((3, 8, EB), F32),
        gcut=((8, EB), F32),
        gshrink=((8, EB), F32),
    )
    if not fwd:
        scratch.update(score_here=((NB, CG, EB, LANES), BF16))
    if fwd:
        outs.fresh = shape((4, A, F), BF16)
        outs.left = shape((sz.factors, F), BF16)
        scratch.update(
            query=((CG, A, LANES), F32),
            query_low=((A, F), BF16),
            kv=((4 * CG, E, LANES), F32),
            vec=((3 * CG, E, LANES), F32),
            vproj=((3 * A, 3 * F), F32),
            score=((NB, CG, EB, LANES), BF16), sagg=((A, F), F32), vagg=((3, A, F), F32), uagg=((3 * A, F), F32)
        )
    if fwd and m:
        outs.all_places = shape((m + 1, 8, LANES), F32)
        for i, made in enumerate(border_sets):
            setattr(arrays, f"gplaces_{i}", (made.gplaces, VMEM))

        def layer(r):
            both_ways(r, sz, m, fwd)
            for i in range(m):
                r.all_places[i] = getattr(r, f"gplaces_{i}")[...]
            r.all_places[m] = r.gplaces[...]

        return call(layer, arrays, outs, scratch, SECOND)
    if not border_sets:
        role = SECOND if fwd else FIRST
        return call(lambda r: both_ways(r, sz, m, fwd), arrays, outs, scratch, role)
    count = m + 1
    outs.up, outs.down = shape((count, 4, H, F), BF16), shape((count, 4, H, F), BF16)
    outs.moved = shape((count, 8, LANES), F32)
    outs.total = shape((count, 8, LANES), F32)
    for role, sets in enumerate(border_sets):
        for i, made in enumerate(sets):
            for name in BORDERS:
                setattr(arrays, f"{name}_{role}_{i}", (getattr(made, name), VMEM))

    def hand_on(r, role):
        for i in range(count):
            low, high, places = (
                getattr(r, f"{name}_{role}_{i}") if i < len(border_sets[role]) else getattr(r, name)
                for name in BORDERS
            )
            r.up[i] = high[...]
            r.down[i] = low[...]
            r.moved[i] = places[...]
            r.total[i] = places[...] + r.early[i] if role == FIRST else places[...]

    def body(r):
        @pl.when(lax.axis_index("section") == FIRST)
        def _():
            both_ways(r, sz, m, fwd)
            hand_on(r, FIRST)

        pl.when(lax.axis_index("section") == SECOND)(lambda: hand_on(r, SECOND))

    return call(body, arrays, outs, scratch)


def border_call(sz, features, coords):
    A, H, F = sz.atoms, sz.halo, sz.width
    count = features.shape[0]

    def body(r):
        moves = [(r.coords, r.s_coords)]
        for m in range(count):
            moves += [
                (r.features.at[m, 0, :, A - H : A, :], r.up.at[4 * m : 4 * m + 4]),
                (r.features.at[m, 0, :, 0:H, :], r.down.at[4 * m : 4 * m + 4]),
            ]
        copies = [
            pltpu.make_async_copy(source, target, r.sems.at[i])
            for i, (source, target) in enumerate(moves)
        ]
        for copy in copies:
            copy.start()
        copies[0].wait()
        for target, ends in ((r.up, slice(A - H, A)), (r.down, slice(0, H))):
            rows = []
            for m in range(count):
                parts = [r.s_coords[m, c][:, ends] for c in range(3)]
                rows.append(jnp.concatenate(parts, axis=1))
            target[4 * count] = packed_places(rows, F)
        for copy in copies[1:]:
            copy.wait()

    shape = jax.ShapeDtypeStruct((4 * count + 1, H, F), BF16)
    return call(
        body,
        SimpleNamespace(features=(features, HBM), coords=(coords, HBM)),
        SimpleNamespace(up=shape, down=shape),
        dict(s_coords=(coords.shape, F32), sems=pltpu.SemaphoreType.DMA((2 * count + 1,))),
        grant_mb=54,
    )


class Rooms:
    def __init__(self, sz):
        F = sz.width
        ends = [0]
        for rows in (F, F, F, 4 * sz.atoms, sz.basis):
            ends.append(ends[-1] + rows)
        self.wqkv, self.wvec, self.wout, self.own, self.wh = [
            slice(*pair) for pair in zip(ends, ends[1:])
        ]
        table = 3 * sz.slots + 8
        self.slots, self.norms = slice(0, table), slice(table, table + 8)
        self.coords = slice(table + 8, table + 16)
        self.low_shape, self.wide_shape = (20480, 5 * F), (51200, F)


def stage_call(sz, features, coords, neighbours, shifts, counts, gain, bias, filter_weight, weights):
    A, F, K = sz.atoms, sz.width, sz.slots
    count = features.shape[0]
    rooms = Rooms(sz)

    def body(r):
        moves = [(r.coords, r.s_coords), (r.counts, r.s_counts)]
        moves += [(r.gain, r.s_gain), (r.bias, r.s_bias), (r.wfilt.at[0], r.s_wfilt)]
        for m in range(count):
            moves += [
                (r.nbr.at[m, 0], r.s_slots.at[m, 0:K]),
                (r.shifts.at[m, 0, 0], r.s_slots.at[m, K : 2 * K]),
                (r.shifts.at[m, 0, 1], r.s_slots.at[m, 2 * K : 3 * K]),
            ]
        near = len(moves)
        moves += [(r.features.at[0, 0], r.s_own), (r.wqkv.at[0], r.s_wqkv)]
        moves += [(r.wvec.at[0], r.s_wvec), (r.wout.at[0], r.s_wout)]
        copies = [
            pltpu.make_async_copy(source, target, r.sems.at[i])
            for i, (source, target) in enumerate(moves)
        ]
        for copy in copies:
            copy.start()
        for copy in copies[:near]:
            copy.wait()
        r.s_wh[...] = (r.s_wfilt[...].astype(F32) * 0.5).astype(BF16)
        for m in range(count):
            r.s_table[m, 0 : 3 * K, 0:A] = r.s_slots[m].astype(F32)
            r.s_table[m, 3 * K :, 0:A] = jnp.broadcast_to(r.s_counts[m].astype(F32), (8, A))
        r.s_norms[...] = jnp.zeros_like(r.s_norms)
        r.s_norms[0:1, :] = r.s_gain[...].astype(F32)
        r.s_norms[1:2, :] = r.s_bias[...].astype(F32)
        for c in range(3):
            r.s_norms[8 + c : 9 + c, 0:A] = r.s_coords[0, c]
        for copy in copies[near:]:
            copy.wait()
        moves = [
            (r.s_table, r.slots),
            (r.s_norms.at[0:8], r.norms),
            (r.s_wh, r.wh),
            (r.s_table.at[0], r.wide.at[rooms.slots, 0:LANES]),
            (r.s_norms, r.wide.at[rooms.norms.start : rooms.coords.stop]),
            (r.s_wqkv, r.low.at[rooms.wqkv]),
            (r.s_wvec, r.low.at[rooms.wvec, 0 : 3 * F]),
            (r.s_wout, r.low.at[rooms.wout, 0 : 3 * F]),
            (r.s_wh, r.low.at[rooms.wh, 0 : 4 * F]),
        ]
        for index in range(4):
            start = rooms.own.start + index * A
            moves.append((r.s_own.at[index], r.low.at[start : start + A, 0:F]))
        later = [
            pltpu.make_async_copy(source, target, r.sems.at[len(copies) + i])
            for i, (source, target) in enumerate(moves)
        ]
        for copy in later:
            copy.start()
        for copy in later:
            copy.wait()

    shape = jax.ShapeDtypeStruct
    wqkv, wvec, wout = weights
    return call(
        body,
        SimpleNamespace(
            features=(features, HBM),
            coords=(coords, HBM),
            nbr=(neighbours, HBM),
            shifts=(shifts, HBM),
            counts=(counts, HBM),
            gain=(gain, HBM),
            bias=(bias, HBM),
            wfilt=(filter_weight, HBM),
            wqkv=(wqkv, HBM),
            wvec=(wvec, HBM),
            wout=(wout, HBM),
        ),
        SimpleNamespace(
            slots=shape((count, 3 * K + 8, LANES), F32),
            norms=shape((8, F), F32),
            wh=shape((sz.basis, 4 * F), BF16),
            low=shape(rooms.low_shape, BF16),
            wide=shape(rooms.wide_shape, F32),
        ),
        dict(
            s_coords=(coords.shape, F32),
            s_counts=(counts.shape, jnp.int32),
            s_gain=(gain.shape, BF16),
            s_bias=(bias.shape, BF16),
            s_wfilt=(filter_weight.shape[1:], BF16),
            s_slots=((count, 3 * K, A), jnp.int32),
            s_own=((4, A, F), BF16),
            s_wqkv=(wqkv.shape[1:], BF16),
            s_wvec=(wvec.shape[1:], BF16),
            s_wout=(wout.shape[1:], BF16),
            s_wh=(filter_weight.shape[1:], BF16),
            s_table=((count, 3 * K + 8, LANES), F32),
            s_norms=((16, F), F32),
            sems=pltpu.SemaphoreType.DMA((3 * count + 22,)),
        ),
        grant_mb=54,
        place=HBM,
    )


def gradient_call(sz, sets):
    A, E, F = sz.atoms, sz.rows, sz.width
    count = len(sets[0])
    w1, w2, w3 = sz.widths
    w4, w5 = 4 * F // sz.space, F // sz.space
    half = F // 2
    arrays = SimpleNamespace()
    for role in (FIRST, SECOND):
        for m in range(count):
            for name in FACTORS:
                setattr(arrays, f"{name}_{role}_{m}", (getattr(sets[role][m], name), VMEM))

    def body(r, role):
        def get(name, m):
            return getattr(r, f"{name}_{role}_{m}")

        every = range(count)
        e, a = E, A
        r.qkv[...] = sum(dot(get("gproj", m)[...], get("left", m)[0:e, :], 0, 0) for m in every)
        r.vector[...] = sum(
            dot(get("gvproj", m)[...], get("left", m)[e : e + 3 * a, :], 0, 0) for m in every
        )
        r.out[...] = sum(
            dot(get("gout", m)[...], get("left", m)[e + 3 * a : e + 4 * a, :], 0, 0) for m in every
        )
        filt = sum(get("gfilt", m)[...] for m in every) * 0.5
        norm = sum(get("gnorm", m)[...] for m in every)
        core = lax.axis_index("dp")
        for k in range(sz.space):
            spare = [filt[:, k * w4 : (k + 1) * w4]]
            if half > w4:
                spare.append(jnp.zeros((sz.basis, half - w4), F32))
            left = jnp.concatenate(spare, axis=1)
            rows = [norm[:, k * w5 : (k + 1) * w5], jnp.zeros((8, half - w5), F32)]
            right = jnp.concatenate(rows, axis=1)
            right = jnp.concatenate(
                [right, jnp.zeros((sz.packed - sz.spare - 8, half), F32)], axis=0
            )
            if sz.packed - sz.spare > sz.basis:
                gap = jnp.zeros((sz.packed - sz.spare - sz.basis, half), F32)
                left = jnp.concatenate([left, gap], axis=0)
            parts = [
                r.qkv[k * w1 : (k + 1) * w1, :],
                r.vector[k * w2 : (k + 1) * w2, :],
                r.out[k * w3 : (k + 1) * w3, :],
            ]
            first = jnp.concatenate([part[:, :half] for part in parts] + [left], axis=0)
            second = jnp.concatenate([part[:, half:] for part in parts] + [right], axis=0)
            r.send[k] = jnp.where(core == 0, second, first).astype(BF16)
            r.stay[k] = jnp.where(core == 0, first, second)

    def both(r):
        for role in (FIRST, SECOND):
            pl.when(lax.axis_index("section") == role)(lambda role=role: body(r, role))

    shape = jax.ShapeDtypeStruct
    return call(
        both,
        arrays,
        SimpleNamespace(
            send=shape((sz.space, sz.packed, half), BF16),
            stay=shape((sz.space, sz.packed, half), F32),
        ),
        dict(
            qkv=((5 * F, F), F32),
            vector=((3 * F, F), F32),
            out=((3 * F, F), F32),
        ),
    )


def border_rows(sz, index):
    start = sz.packed + index * 2 * sz.halo
    return [slice(start + i * sz.halo, start + (i + 1) * sz.halo) for i in range(2)]


def border_block(sz, ref, index):
    return jnp.concatenate([ref[rows, :] for rows in border_rows(sz, index)], axis=1)


def piece_call(sz, stay, recv, up, down, total, late):
    A, H, E, F = sz.atoms, sz.halo, sz.rows, sz.width
    count = up.shape[0]
    half = F // 2

    def body(r):
        slab, space = lax.axis_index("space"), sz.space
        for hop in range(space):
            k = lax.rem(slab + hop, space)
            share = r.stay[k] + r.recv[k].astype(F32)
            target = getattr(r, f"hop{hop}")
            target[0 : sz.packed, :] = share.astype(target.dtype)
        places = [r.total[m] + r.late[m] for m in range(count)]
        ends = (
            (r.hop1, r.up, slice(H + A, E)),
            (getattr(r, f"hop{space - 1}"), r.down, slice(0, H)),
        )
        for target, border, lanes in ends:
            rows = []
            for m in range(count):
                parts = [places[m][c : c + 1, lanes] for c in range(3)]
                rows.append(jnp.concatenate(parts, axis=1))
            blocks = [border[m, index] for m in range(count) for index in range(4)]
            for index, block in enumerate(blocks + [packed_places(rows, F)]):
                first, second = border_rows(sz, index)
                target[first, :] = block[:, :half]
                target[second, :] = block[:, half:]
        for m in range(count):
            for c in range(3):
                r.mine[m, c] = places[m][c : c + 1, H : H + A]

    shape = jax.ShapeDtypeStruct
    outs = {
        f"hop{hop}": shape(
            (sz.packed + ((8 * count + 2) * H if hop in (1, sz.space - 1) else 0), half),
            BF16 if hop else F32,
        )
        for hop in range(sz.space)
    }
    outs.update(mine=shape((count, 3, 1, A), F32))
    made = call(
        body,
        SimpleNamespace(
            stay=(stay, VMEM),
            recv=(recv, VMEM),
            up=(up, VMEM),
            down=(down, VMEM),
            total=(total, VMEM),
            late=(late, VMEM),
        ),
        SimpleNamespace(**outs),
        {},
    )
    return [getattr(made, f"hop{hop}") for hop in range(sz.space)], made.mine


def result_call(sz, fresh, back, from_low, from_high, mine):
    A, H, F = sz.atoms, sz.halo, sz.width
    count = len(back[0])
    arrays = SimpleNamespace(
        low=(from_low, VMEM), high=(from_high, VMEM), mine=(mine, VMEM)
    )
    for role in (FIRST, SECOND):
        for m in range(count):
            setattr(arrays, f"fresh_{role}_{m}", (fresh[role][m], VMEM))
            setattr(arrays, f"back_{role}_{m}", (back[role][m], VMEM))

    def body(r, role):
        for m in range(count):
            r.outputs[0, m, 0] = getattr(r, f"fresh_{role}_{m}")[...]
            whole = getattr(r, f"back_{role}_{m}")
            for index in range(4):
                low = border_block(sz, r.low, 4 * m + index).astype(F32)
                high = border_block(sz, r.high, 4 * m + index).astype(F32)
                r.grads[0, m, 0, index, 0:H, :] = whole[index, 0:H, :] + low
                r.grads[0, m, 0, index, H : A - H, :] = whole[index, H : A - H, :]
                r.grads[0, m, 0, index, A - H :, :] = whole[index, A - H :, :] + high
            for c in range(3):
                edge = [
                    unpacked_places(border_block(sz, r.low, 4 * count), m, c, H),
                    jnp.zeros((1, A - 2 * H), F32),
                    unpacked_places(border_block(sz, r.high, 4 * count), m, c, H),
                ]
                r.places[m, c] = r.mine[m, c] + jnp.concatenate(edge, axis=1)

    def both(r):
        for role in (FIRST, SECOND):
            pl.when(lax.axis_index("section") == role)(lambda role=role: body(r, role))

    shape = jax.ShapeDtypeStruct
    return call(
        both,
        arrays,
        SimpleNamespace(
            outputs=shape((1, count, 1, 4, A, F), BF16),
            grads=shape((1, count, 1, 4, A, F), F32),
            places=shape((count, 3, 1, A), F32),
        ),
        {},
    )


def share_call(sz, total, other):
    F = sz.width
    w1, w2, w3 = sz.widths
    w4, w5 = 4 * F // sz.space, F // sz.space
    half = F // 2

    def body(r, first, second):
        for lanes, part in ((slice(0, half), first), (slice(half, F), second)):
            r.qkv[0, :, lanes] = part[0:w1, :]
            r.vector[0, :, lanes] = part[w1 : w1 + w2, :]
            r.out[0, :, lanes] = part[w1 + w2 : sz.spare, :]
        r.filt[0] = first[sz.spare : sz.spare + sz.basis, 0:w4]
        r.gain[...] = second[sz.spare : sz.spare + 1, 0:w5]
        r.bias[...] = second[sz.spare + 1 : sz.spare + 2, 0:w5]

    def both(r):
        pl.when(lax.axis_index("dp") == 0)(lambda: body(r, r.total, r.other))
        pl.when(lax.axis_index("dp") == 1)(lambda: body(r, r.other, r.total))

    shape = jax.ShapeDtypeStruct
    return call(
        both,
        SimpleNamespace(total=(total, VMEM), other=(other, VMEM)),
        SimpleNamespace(
            gain=shape((1, w5), F32),
            bias=shape((1, w5), F32),
            qkv=shape((1, w1, F), F32),
            vector=shape((1, w2, F), F32),
            filt=shape((1, sz.basis, w4), F32),
            out=shape((1, w3, F), F32),
        ),
        {},
    )


def on_device(
    features,
    coords,
    neighbours,
    counts,
    shifts,
    norm_gain,
    norm_bias,
    qkv_weight,
    vector_weight,
    filter_weight,
    out_weight,
    cotangent,
):
    micro_count = features.shape[0]
    space = lax.axis_size("space")
    sz = Sizes(features.shape[3], features.shape[4], filter_weight.shape[1], neighbours.shape[2], space)
    up = [(i, (i + 1) % space) for i in range(space)]
    down = [((i + 1) % space, i) for i in range(space)]

    places = jnp.transpose(coords, (0, 2, 1, 3))
    borders = border_call(sz, features, places)
    staged = stage_call(
        sz,
        features,
        places,
        neighbours,
        shifts,
        counts,
        norm_gain,
        norm_bias,
        filter_weight,
        (qkv_weight, vector_weight, out_weight),
    )
    slots, norms, half_filter = staged.slots, staged.norms, staged.wh
    pack_low = lax.ppermute(borders.up, "space", up)
    pack_high = lax.ppermute(borders.down, "space", down)
    both = ("section", "space")
    forth = [(k, space + k) for k in range(space)]
    forth_up = [(k, space + (k + 1) % space) for k in range(space)]
    forth_down = [((k + 1) % space, space + k) for k in range(space)]
    back = [(space + k, k) for k in range(space)]
    back_up = [(space + k, (k + 1) % space) for k in range(space)]
    back_down = [(space + (k + 1) % space, k) for k in range(space)]

    def geometry_inputs():
        return SimpleNamespace(
            pack_low=(pack_low, VMEM),
            pack_high=(pack_high, VMEM),
            coords=(places, VMEM),
            slots=(slots, VMEM),
            wh=(half_filter, VMEM),
        )

    firsts, sent, filters = [], [], {}
    for m in range(micro_count):
        if m == 0:
            arrays = SimpleNamespace(
                pack_low=(pack_low, VMEM),
                pack_high=(pack_high, VMEM),
                room=(staged.low, HBM),
                wide=(staged.wide, HBM),
            )
        else:
            arrays = geometry_inputs()
            arrays.features = (features, VMEM)
            arrays.norms = (norms, VMEM)
            arrays.wqkv, arrays.wvec, arrays.wout = (
                (qkv_weight, VMEM), (vector_weight, VMEM), (out_weight, VMEM)
            )
        first = first_call(sz, m, m == 0, sz.sent[m], arrays)
        firsts.append(first)
        if m == micro_count - 1:
            made = filters[SECOND] = filter_call(
                sz, SECOND, range(micro_count), geometry_inputs()
            )
            first.head, made[0].geo = lax.optimization_barrier((first.head, made[0].geo))
        sent.append((
            lax.ppermute(first.fresh, both, forth),
            lax.ppermute(first.tail, both, forth_up),
            lax.ppermute(first.head, both, forth_down),
        ))
    def both_inputs(m, role):
        made = filters[role][m]
        return SimpleNamespace(
            norms=(norms, VMEM),
            wqkv=(qkv_weight, VMEM),
            wvec=(vector_weight, VMEM),
            wh=(half_filter, VMEM),
            wout=(out_weight, VMEM),
            geo=(made.geo, VMEM),
            smear=(made.smear, VMEM),
            cut_wide=(made.cut_wide, VMEM),
            units=(made.units, VMEM),
            silu=(made.silu, VMEM),
            slope=(made.slope, VMEM),
        )

    seconds, returned = [], []
    for m in range(micro_count):
        if m == 1:
            other = filters[FIRST][0]
            other.geo, filters[SECOND][m].geo = lax.optimization_barrier(
                (other.geo, filters[SECOND][m].geo)
            )
        arrays = both_inputs(m, SECOND)
        arrays.key = (filters[SECOND][m].key, VMEM)
        own, low, high = sent[m]
        arrays.own, arrays.low, arrays.high = (own, VMEM), (low, VMEM), (high, VMEM)
        arrays.cotangent = (cotangent, VMEM)
        second = both_call(sz, m, True, arrays, seconds)
        seconds.append(second)
        if m == 0:
            later = geometry_inputs()
            held, second.gplaces = lax.optimization_barrier((slots, second.gplaces))
            later.slots = (held, VMEM)
            filters[FIRST] = filter_call(sz, FIRST, range(micro_count), later)
        back_low, rim_low, rim_high = second.back_low, second.rim_low, second.rim_high
        if m:
            returned[-1], back_low, rim_low, rim_high = lax.optimization_barrier(
                (returned[-1], back_low, rim_low, rim_high)
            )
        returned.append((
            lax.ppermute(back_low, both, back),
            lax.ppermute(rim_high, both, back_up),
            lax.ppermute(rim_low, both, back_down),
        ))
    thirds = []
    for m in range(micro_count):
        arrays = both_inputs(m, FIRST)
        for name in HANDED:
            setattr(arrays, name, (getattr(firsts[m], name), VMEM))
        inc, inc_low, inc_high = returned[m]
        arrays.inc, arrays.inc_low, arrays.inc_high = (inc, VMEM), (inc_low, VMEM), (inc_high, VMEM)
        sets = (thirds, seconds) if m == micro_count - 1 else ()
        if sets:
            arrays.early = (lax.ppermute(seconds[-1].all_places, both, back), VMEM)
        third = both_call(sz, m, False, arrays, sets)
        third.left = firsts[m].left
        thirds.append(third)

    last = thirds[-1]
    late = lax.ppermute(last.moved, both, forth)
    shares = gradient_call(sz, (thirds, seconds))
    recv = lax.ppermute(shares.send, "dp", [(0, 1), (1, 0)])
    (total, *pieces), mine = piece_call(sz, shares.stay, recv, last.up, last.down, last.total, late
    )
    received = [
        lax.ppermute(piece, "space", [(i, (i + hop) % space) for i in range(space)])
        for hop, piece in enumerate(pieces, 1)
    ]
    for piece in received:
        total = total + piece[: sz.packed].astype(F32)
    results = result_call(
        sz,
        ([v.fresh for v in firsts], [v.fresh for v in seconds]),
        ([v.back for v in thirds], [v.back for v in seconds]),
        received[0],
        received[-1],
        mine,
    )
    other = lax.ppermute(total, "dp", [(0, 1), (1, 0)])
    share = share_call(sz, total, other)
    return (
        results.outputs,
        results.grads,
        share.gain,
        share.bias,
        jnp.transpose(share.qkv, (0, 2, 1)),
        jnp.transpose(share.vector, (0, 2, 1)),
        share.filt,
        jnp.transpose(share.out, (0, 2, 1)),
        jnp.transpose(results.places, (0, 2, 1, 3)),
    )


def solution(mesh):
    return jax.shard_map(
        on_device,
        mesh=mesh,
        in_specs=(
            P(None, "dp", None, "space", None),
            P(None, "dp", None, "space"),
            P(None, "dp", None, "space"),
            P(None, "dp", "space"),
            P(None, "dp", None, None, "space"),
            P("section", None),
            P("section", None),
            P("section", None, None),
            P("section", None, None),
            P("section", None, None),
            P("section", None, None),
            P(None, "dp", None, "space", None),
        ),
        out_specs=(
            P("section", None, "dp", None, "space", None),
            P("section", None, "dp", None, "space", None),
            P("section", "space"),
            P("section", "space"),
            P("section", None, "space"),
            P("section", None, "space"),
            P("section", None, "space"),
            P("section", None, "space"),
            P(None, "dp", None, "space"),
        ),
        check_vma=False,
    )
```

```python
import math
from types import SimpleNamespace

import jax
import jax.numpy as jnp
from jax import lax
from jax.experimental import pallas as pl
from jax.experimental.pallas import tpu as pltpu
from jax.sharding import PartitionSpec as P

HEADS = 8
CUTOFF = 5.0
LN_EPS = 1e-05
SOFTEN = 0.25
CROSS = 2.5
GROUP = 4
LANES = 128
SUBLANES = 8
FIRST, SECOND = 0, 1

F32 = jnp.float32
BF16 = jnp.bfloat16
VMEM = pl.BlockSpec(memory_space=pltpu.VMEM)
HBM = pl.BlockSpec(memory_space=pltpu.HBM)


def dot(left, right, left_dim=1, right_dim=0):
    return lax.dot_general(
        left, right, (((left_dim,), (right_dim,)), ((), ())), preferred_element_type=F32
    )


def iota(shape, dim):
    return lax.broadcasted_iota(jnp.int32, shape, dim)


def packed_places(rows, width):
    parts = []
    for row in rows:
        high = row.astype(BF16).astype(F32)
        rest = row - high
        middle = rest.astype(BF16).astype(F32)
        parts += [high, middle, rest - middle]
    gap = 16 - len(parts)
    whole = jnp.concatenate(parts + [jnp.zeros((gap, rows[0].shape[1]), F32)], axis=0)
    wide = [whole, jnp.zeros((16, width - whole.shape[1]), F32)]
    return jnp.concatenate(wide, axis=1).astype(BF16)


def unpacked_places(block, m, c, count):
    rows = block[:, c * count : (c + 1) * count].astype(F32)
    return rows[3 * m : 3 * m + 1] + rows[3 * m + 1 : 3 * m + 2] + rows[3 * m + 2 : 3 * m + 3]


class Sizes:
    def __init__(self, atoms, width, basis, slots, space):
        self.atoms, self.width, self.basis, self.slots, self.space = atoms, width, basis, slots, space
        self.halo = atoms // 4
        self.rows = atoms + 2 * self.halo
        self.blocks = slots // GROUP
        self.edges = GROUP * atoms
        self.halves = width // LANES
        self.window = atoms + SUBLANES
        self.sent = (self.halo, atoms)
        self.widths = (5 * width // space, 3 * width // space, 3 * width // space)
        self.spare = sum(self.widths)
        self.packed = -(-(self.spare + basis) // 16) * 16
        self.factors = -(-(self.rows + 4 * atoms) // LANES) * LANES


def halves_of(sz):
    return [slice(cg * LANES, (cg + 1) * LANES) for cg in range(sz.halves)]


def first_row(b):
    return GROUP * b + jnp.where(b >= 4, 1, 0)


def sharpness_of(basis):
    return (2.0 / basis * (1.0 - math.exp(-CUTOFF))) ** (-2)


def write_centres(ref, basis):
    low_end = math.exp(-CUTOFF)
    step = iota(ref.shape, 0).astype(F32) / (basis - 1)
    ref[...] = low_end * (1.0 - step) + step


def edge_geometry(r, sz, m, coords, slots):
    A, H, E, EB, K = sz.atoms, sz.halo, sz.rows, sz.edges, sz.slots
    lane = iota((8, LANES), 1)
    row = iota((8, LANES), 0)
    slab, last = lax.axis_index("space"), sz.space - 1
    last_block = r.pack_low.shape[0] - 1
    spot = iota((1, LANES), 1)
    length_x = sz.space * A * 4.0 / H
    places = []
    for c in range(3):
        places.append(
            jnp.concatenate(
                [
                    unpacked_places(r.pack_low[last_block], m, c, H),
                    coords[c],
                    unpacked_places(r.pack_high[last_block], m, c, H),
                    jnp.zeros((1, LANES - E), F32),
                ],
                axis=1,
            )
        )
    places.append(
        jnp.where((spot < H) & (slab == 0), -length_x, 0.0)
        + jnp.where((spot >= H + A) & (slab == last), length_x, 0.0)
    )
    near = []
    for c in range(4):
        y = jnp.broadcast_to(places[c], (8, LANES))
        for bit in range(3):
            y = jnp.where((row >> bit) & 1 == 1, pltpu.roll(y, LANES - GROUP * 2**bit, 1), y)
        y = jnp.where(row >= 4, pltpu.roll(y, LANES - 1, 1), y)
        first = jnp.where(lane < A, y, pltpu.roll(y, A - 1, 1))
        other = jnp.where(lane < A, pltpu.roll(y, LANES - 2, 1), pltpu.roll(y, A - 3, 1))
        near.append(jnp.concatenate([first, other], axis=1))
    wide_lane = iota((8, EB), 1)
    wide_row = iota((8, EB), 0)
    wanted = GROUP * wide_row + wide_lane // A + jnp.where(wide_row >= 4, 1, 0) + wide_lane % A
    table = slots[:, 0:A].astype(jnp.int32)
    alive = iota((K, A), 0) < table[3 * K : 3 * K + 1]
    code = jnp.where(alive, 16, 0) + (table[K : 2 * K] + 1) * 4 + (table[2 * K : 3 * K] + 1)
    code = jnp.concatenate([code] * GROUP, axis=1)
    named = jnp.concatenate([table[0:K]] * GROUP, axis=1)
    found = jnp.zeros((8, EB), jnp.int32)
    for n in range(K):
        found = found + jnp.where(named[n : n + 1, :] == wanted, code[n : n + 1, :], 0)
    live = (found >> 4).astype(F32)
    offsets = (
        near[3],
        (((found >> 2) & 3) - 1).astype(F32) * CROSS,
        ((found & 3) - 1).astype(F32) * CROSS,
    )
    sep = []
    for c in range(3):
        mine = coords[c]
        sep.append(near[c] - jnp.concatenate([mine] * GROUP, axis=1) + offsets[c])
    distance = jnp.sqrt(sep[0] * sep[0] + sep[1] * sep[1] + sep[2] * sep[2] + SOFTEN)
    inside = distance < CUTOFF
    cut = jnp.where(inside, 0.5 * (jnp.cos(math.pi * distance / CUTOFF) + 1.0), 0.0) * live
    for index, value in enumerate(
        sep + [distance, live, cut, jnp.exp(-distance)] + [part / distance for part in sep]
    ):
        r.geo[index] = value


DISTANCE, LIVE, CUT, SHRINK, UNIT = 3, 4, 5, 6, 7


def bell_of(r, sz, b):
    delta = r.geo[SHRINK, pl.ds(b, 1), :] - r.centres[...]
    return delta, jnp.exp(-sharpness_of(sz.basis) * delta * delta)


def write_edge_tables(r, sz, b, wide_kind):
    A, EB = sz.atoms, sz.edges
    cut = r.geo[CUT, pl.ds(b, 1), :]
    _, bell = bell_of(r, sz, b)
    smear = cut * bell
    if hasattr(r, "smear"):
        r.smear[b] = smear.astype(BF16)
    r.smear_t[b] = jnp.transpose(smear).astype(BF16)
    coarse = cut.astype(BF16).astype(F32)
    which = iota((16, EB), 0)
    pair = jnp.where(which == 0, coarse, jnp.where(which == 1, cut - coarse, 0.0)).astype(BF16)
    r.cut_wide[b] = dot(pair, jnp.ones((16, LANES), BF16), 0, 0).astype(wide_kind)
    for c in range(3):
        r.units[b, c * A : (c + 1) * A, :] = (
            r.diag[...] * r.geo[UNIT + c, pl.ds(b, 1), :]
        ).astype(BF16)


def write_constants(r, sz):
    A, EB, F = sz.atoms, sz.edges, sz.width
    if hasattr(r, "centres"):
        write_centres(r.centres, sz.basis)
    if hasattr(r, "diag"):
        r.diag[...] = jnp.where(iota((A, EB), 1) % A == iota((A, EB), 0), 1.0, 0.0)
    if hasattr(r, "fold"):
        r.fold[...] = jnp.where(iota((A, EB), 1) % A == iota((A, EB), 0), 1.0, 0.0).astype(BF16)
    if hasattr(r, "heads"):
        r.heads[...] = jnp.where(
            iota((F, F), 0) // (F // HEADS) == iota((F, F), 1) // (F // HEADS), 0.5, 0.0
        ).astype(BF16)


def node_part(r, sz, own, low, high, norms, wqkv):
    A, H, E, F, CG = sz.atoms, sz.halo, sz.rows, sz.width, sz.halves
    halves = halves_of(sz)
    scalars = jnp.concatenate([low[0, 0:H], own[0], high[0, 0:H]], axis=0).astype(F32)
    centred = scalars - jnp.mean(scalars, axis=-1, keepdims=True)
    spread = jnp.mean(centred * centred, axis=-1, keepdims=True)
    scale = lax.rsqrt(spread + LN_EPS)
    normed = (centred * scale * norms[0:1, :] + norms[1:2, :]).astype(BF16)
    left = r.left
    left[0:E, :] = normed
    left[E : E + 3 * A, :] = own[1:4].reshape(3 * A, F)
    left[E + 4 * A :, :] = jnp.zeros((sz.factors - E - 4 * A, F), BF16)
    for part in range(5):
        projected = dot(normed, wqkv[:, part * F : (part + 1) * F])
        for cg in range(CG):
            if part == 0:
                r.query[cg] = projected[H : H + A, halves[cg]]
            else:
                r.kv[(part - 1) * CG + cg] = projected[:, halves[cg]]
    for c in range(3):
        for cg in range(CG):
            r.vec[c * CG + cg, 0:H, :] = low[c + 1, 0:H, halves[cg]].astype(F32)
            r.vec[c * CG + cg, H : H + A, :] = own[c + 1][:, halves[cg]].astype(F32)
            r.vec[c * CG + cg, H + A : E, :] = high[c + 1, 0:H, halves[cg]].astype(F32)
    return centred * scale, scale


def buffers(r, sz, which):
    end = str(which)
    return SimpleNamespace(**{k[:-1]: v for k, v in vars(r).items() if k.endswith(end)})


def tiles(sz, first):
    A = sz.atoms
    for kk in range(GROUP):
        for cg in range(sz.halves):
            yield (
                cg,
                slice(kk * A, (kk + 1) * A),
                slice(cg * LANES, (cg + 1) * LANES),
                pl.ds(first + kk, A),
            )


def stacked(sz, first, tile):
    made = [tile(*where) for where in tiles(sz, first)]
    CG = sz.halves
    wholes = []
    for index in range(len(made[0])):
        lines = [
            jnp.concatenate([made[kk * CG + cg][index] for cg in range(CG)], axis=1)
            for kk in range(GROUP)
        ]
        wholes.append(jnp.concatenate(lines, axis=0))
    return wholes


def vector_dot(r, sz):
    A, F, vp = sz.atoms, sz.width, r.vproj
    return sum(
        vp[c * A : (c + 1) * A, 0:F] * vp[c * A : (c + 1) * A, F : 2 * F] for c in range(3)
    )


def write_layer_output(r, sz, own, out_proj, vec_dot, vector_agg):
    A, H, F, vp = sz.atoms, sz.halo, sz.width, r.vproj
    for index in range(4):
        if index == 0:
            fresh = vec_dot * out_proj[:, F : 2 * F] + out_proj[:, 2 * F :]
        else:
            rows = slice((index - 1) * A, index * A)
            fresh = vp[rows, 2 * F :] * out_proj[:, 0:F] + vector_agg[index - 1]
        fresh = (own[index].astype(F32) + fresh).astype(BF16)
        r.fresh[index] = fresh
        if hasattr(r, "head"):
            r.head[index, 0:H, :] = fresh[:H]
            r.tail[index, 0:H, :] = fresh[A - H :]


def first_forward(r, sz, m, fetch):
    A, H, E, F, EB = sz.atoms, sz.halo, sz.rows, sz.width, sz.edges
    CG = sz.halves
    r.s_low, r.s_high = r.pack_low.at[4 * m : 4 * m + 4], r.pack_high.at[4 * m : 4 * m + 4]
    copies = early = []
    if fetch:
        rooms = Rooms(sz)
        early = [
            (r.wide.at[rooms.slots, 0:LANES], r.s_slots),
            (r.wide.at[rooms.norms.start : rooms.coords.stop], r.s_norms),
            (r.room.at[rooms.wqkv], r.s_wqkv),
        ]
        for index in range(4):
            start = rooms.own.start + index * A
            early.append((r.room.at[start : start + A, 0:F], r.s_own.at[index]))
        late = [
            (r.room.at[rooms.wh, 0 : 4 * F], r.s_wh),
            (r.room.at[rooms.wvec, 0 : 3 * F], r.s_wvec),
            (r.room.at[rooms.wout, 0 : 3 * F], r.s_wout),
        ]
        copies = [
            pltpu.make_async_copy(source, target, r.sems.at[i])
            for i, (source, target) in enumerate(early + late)
        ]
        for copy in copies:
            copy.start()
    else:
        r.s_slots, r.s_norms, r.s_wh = r.slots.at[m], r.norms, r.wh
        r.s_own, r.s_wqkv = r.features.at[m, 0], r.wqkv.at[0]
        r.s_wvec, r.s_wout = r.wvec.at[0], r.wout.at[0]
    write_constants(r, sz)
    r.sagg[...] = jnp.zeros_like(r.sagg)
    r.vagg[...] = jnp.zeros_like(r.vagg)
    for copy in copies[: len(early)]:
        copy.wait()
    coords = [r.s_norms[8 + c : 9 + c, 0:A] if fetch else r.coords[m, c] for c in range(3)]
    edge_geometry(r, sz, m, coords, r.s_slots)

    def tables(b, carry):
        write_edge_tables(r, sz, b, F32)
        return carry

    lax.fori_loop(0, sz.blocks, tables, 0, unroll=4)
    own = r.s_own
    xhat, scale = node_part(r, sz, own, r.s_low, r.s_high, r.s_norms, r.s_wqkv)
    r.xhat[...] = xhat
    r.scale[...] = jnp.broadcast_to(scale, r.scale.shape)
    for cg in range(CG):
        r.query_low[:, cg * LANES : (cg + 1) * LANES] = r.query[cg].astype(BF16)
    for copy in copies[len(early) :]:
        copy.wait()
    r.vproj[...] = dot(r.left[E : E + 3 * A, :], r.s_wvec[...])

    def filter_part(b, part):
        return dot(r.smear_t[b], r.s_wh[:, part * F : (part + 1) * F])

    def block(b, w):
        first = first_row(b)
        half = filter_part(b, 0)
        for cg, at, cols, near_rows in tiles(sz, first):
            h = half[at, cols]
            product = r.query[cg] * r.kv[cg, near_rows, :] * (h + h * jnp.tanh(h))
            coarse = product.astype(BF16)
            w.pack1[at, cols] = coarse
            w.pack2[at, cols] = (product - coarse.astype(F32)).astype(BF16)
        score = dot(w.pack1[...], r.heads[...]) + dot(w.pack2[...], r.heads[...])
        for cg in range(CG):
            r.score[b, cg] = score[:, cg * LANES : (cg + 1) * LANES].astype(BF16)
        half = filter_part(b, 2)
        for cg, at, cols, near_rows in tiles(sz, first):
            h = half[at, cols]
            value = r.kv[2 * CG + cg, near_rows, :] * (h + h * jnp.tanh(h))
            for c in range(3):
                r.vagg[c * CG + cg] += r.vec[c * CG + cg, near_rows, :] * value
        half = filter_part(b, 3)
        for cg, at, cols, near_rows in tiles(sz, first):
            h = half[at, cols]
            value = r.kv[3 * CG + cg, near_rows, :] * (h + h * jnp.tanh(h))
            r.third[b, at, cols] = value.astype(BF16)
        half = filter_part(b, 1)
        for cg, at, cols, near_rows in tiles(sz, first):
            h = half[at, cols]
            s = score[at, cols]
            attention = (s + s * jnp.tanh(s)) * r.cut_wide[b, at, :]
            r.sagg[cg] += attention * (r.kv[CG + cg, near_rows, :] * (h + h * jnp.tanh(h)))

    def pair(i, carry):
        for which in range(2):
            block(2 * i + which, buffers(r, sz, which))
        return carry

    lax.fori_loop(0, sz.blocks // 2, pair, 0, unroll=2)
    third = sum(dot(r.units[b], r.third[b]) for b in range(sz.blocks))
    scalar_low = jnp.concatenate([r.sagg[cg] for cg in range(CG)], axis=1).astype(BF16)
    r.left[E + 3 * A : E + 4 * A, :] = scalar_low
    out_proj = dot(scalar_low, r.s_wout[...])
    vec_dot = vector_dot(r, sz)
    r.out_proj[...] = out_proj
    r.vec_dot[...] = vec_dot
    vector_agg = [
        jnp.concatenate([r.vagg[c * CG + cg] for cg in range(CG)], axis=1)
        + third[c * A : (c + 1) * A, :]
        for c in range(3)
    ]
    write_layer_output(r, sz, own, out_proj, vec_dot, vector_agg)


def edge_filters(r, sz, which):
    F = sz.width
    write_constants(r, sz)
    for m in which:
        w = SimpleNamespace(**vars(r))
        vars(w).update(vars(buffers(r, sz, m)))
        edge_geometry(w, sz, m, r.coords.at[m], r.slots.at[m])

        def block(b, carry, w=w):
            write_edge_tables(w, sz, b, BF16)
            for part in range(4):
                cols = slice(part * F, (part + 1) * F)
                h = dot(r.smear_t[b], r.wh[:, cols])
                if part:
                    h = h.astype(BF16)
                up = 1.0 + jnp.tanh(h)
                f = h * up
                for cg in range(sz.halves):
                    if part == 0 and hasattr(w, "key"):
                        w.key[b, cg] = f[:, cg * LANES : (cg + 1) * LANES]
                f, up = f.astype(BF16), up.astype(BF16)
                slope = up + f * (2.0 - up)
                for cg in range(sz.halves):
                    half = slice(cg * LANES, (cg + 1) * LANES)
                    w.silu[b, part * sz.halves + cg] = f[:, half]
                    w.slope[b, part * sz.halves + cg] = slope[:, half]
            return carry

        lax.fori_loop(0, sz.blocks, block, 0, unroll=2)


def both_ways(r, sz, m, fwd):
    A, H, E, F = sz.atoms, sz.halo, sz.rows, sz.width
    EB, CG, NB, W = sz.edges, sz.halves, sz.blocks, sz.window
    lane = iota((8, LANES), 1)
    row = iota((8, LANES), 0)
    halves = halves_of(sz)
    wqkv, wvec, wout = r.wqkv.at[0], r.wvec.at[0], r.wout.at[0]
    write_constants(r, sz)
    gain = r.norms[0:1, :]
    vp = r.vproj
    if fwd:
        own, left = r.own, r.left
        xhat, scale = node_part(r, sz, own, r.low, r.high, r.norms, wqkv)
        vp[...] = dot(left[E : E + 3 * A, :], wvec[...])
        for cg in range(CG):
            r.query_low[:, halves[cg]] = r.query[cg].astype(BF16)
    else:
        xhat, scale = r.xhat[...], r.scale[:, 0:1]

    if fwd:
        r.sagg[...] = jnp.zeros_like(r.sagg)
        r.vagg[...] = jnp.zeros_like(r.vagg)
        r.uagg[...] = jnp.zeros_like(r.uagg)

        def forward_block(b, carry):
            first = first_row(b)

            def filters(part, cg, at):
                return r.silu[b, part * CG + cg, at, :]

            def keys(cg, at, cols, near_rows):
                product = r.query[cg] * r.kv[cg, near_rows, :] * r.key[b, cg, at, :]
                return [product.astype(BF16)]

            score = dot(*stacked(sz, first, keys), r.heads[...])
            for cg in range(CG):
                r.score[b, cg] = score[:, halves[cg]].astype(BF16)

            def vectors(cg, at, cols, near_rows):
                value = r.kv[2 * CG + cg, near_rows, :].astype(BF16) * filters(2, cg, at)
                return [
                    r.vec[c * CG + cg, near_rows, :].astype(BF16) * value for c in range(3)
                ] + [r.kv[3 * CG + cg, near_rows, :].astype(BF16) * filters(3, cg, at)]

            moved = stacked(sz, first, vectors)
            for c in range(3):
                r.vagg[c] += dot(r.fold[...], moved[c])
            r.uagg[...] += dot(r.units[b], moved[3])

            def scalars(cg, at, cols, near_rows):
                s = r.score[b, cg, at, :]
                attention = s * (1.0 + jnp.tanh(s)) * r.cut_wide[b, at, :]
                return [
                    attention * (r.kv[CG + cg, near_rows, :].astype(BF16) * filters(1, cg, at))
                ]

            r.sagg[...] += dot(r.fold[...], *stacked(sz, first, scalars))
            return carry

        lax.fori_loop(0, NB, forward_block, 0, unroll=8)
        scalar_low = r.sagg[...].astype(BF16)
        left[E + 3 * A : E + 4 * A, :] = scalar_low
        out_proj = dot(scalar_low, wout[...])
        vec_dot = vector_dot(r, sz)
    else:
        out_proj, vec_dot = r.out_proj, r.vec_dot[...]
    if fwd:
        vector_agg = [r.vagg[c] + r.uagg[c * A : (c + 1) * A, :] for c in range(3)]
        write_layer_output(r, sz, own, out_proj, vec_dot, vector_agg)

    def incoming(index):
        if fwd:
            return r.cotangent[m, 0, index].astype(F32)
        gap = jnp.zeros((A - 2 * H, F), F32)
        edge = [r.inc_low[index, 0:H].astype(F32), gap, r.inc_high[index, 0:H].astype(F32)]
        value = r.inc[index].astype(F32) + jnp.concatenate(edge, axis=0)
        return value.astype(BF16).astype(F32)

    g_x = incoming(0)
    r.gx[0] = g_x
    g_first = jnp.zeros((A, F), F32)
    g_mid = g_x * out_proj[:, F : 2 * F]
    for c in range(3):
        g_vec = incoming(c + 1)
        r.gx[c + 1] = g_vec
        rows = slice(c * A, (c + 1) * A)
        r.gvlow[rows, :] = g_vec.astype(BF16)
        g_first = g_first + g_vec * vp[rows, 2 * F :]
        r.gvproj[rows, 0:F] = (g_mid * vp[rows, F : 2 * F]).astype(BF16)
        r.gvproj[rows, F : 2 * F] = (g_mid * vp[rows, 0:F]).astype(BF16)
        r.gvproj[rows, 2 * F :] = (g_vec * out_proj[:, 0:F]).astype(BF16)
    r.gout[:, 0:F] = g_first.astype(BF16)
    r.gout[:, F : 2 * F] = (g_x * vec_dot).astype(BF16)
    r.gout[:, 2 * F :] = g_x.astype(BF16)
    r.gs[...] = dot(r.gout[...], wout[...], 1, 1).astype(BF16)
    for total in (r.gnear, r.gq, r.gfilt):
        total[...] = jnp.zeros_like(total)

    scores = r.score if fwd else r.score_here
    if not fwd:
        scores[...] = r.score[...]

    def backward_block(b, carry):
        first = first_row(b)
        base = pl.multiple_of(first // SUBLANES * SUBLANES, SUBLANES)
        lanes = iota((W, EB), 1)
        place = jnp.where(
            lanes % A + lanes // A + (first - base) == iota((W, EB), 0), 1.0, 0.0
        ).astype(BF16)

        def collect(index, terms):
            r.gnear[index, pl.ds(base, W), :] += dot(place, terms)

        def filters(part, cg, at):
            return r.silu[b, part * CG + cg, at, :], r.slope[b, part * CG + cg, at, :]

        def weights(cg, at, cols, near_rows):
            value = r.kv[CG + cg, near_rows, :].astype(BF16)
            return [r.gs[:, cols] * (value * filters(1, cg, at)[0])]

        g_att = dot(*stacked(sz, first, weights), r.heads[...])

        def vectors(cg, at, cols, near_rows):
            f, slope = filters(2, cg, at)
            value = r.kv[2 * CG + cg, near_rows, :].astype(BF16)
            message = value * f
            moved = []
            for c in range(3):
                g_vec = r.gvlow[c * A : (c + 1) * A, cols]
                term = g_vec * r.vec[c * CG + cg, near_rows, :].astype(BF16)
                g_edge = term if c == 0 else g_edge + term
                moved.append(g_vec * message)
            return moved + [g_edge * f, g_edge * (value * slope)]

        *moved, g_value, g_pre = stacked(sz, first, vectors)
        for c in range(3):
            collect(4 + c, moved[c])
        collect(2, g_value)
        pre = [None, None, g_pre, None]
        g_third = dot(r.units[b], r.gvlow[...], 0, 0)

        def units(cg, at, cols, near_rows):
            f, slope = filters(3, cg, at)
            value = r.kv[3 * CG + cg, near_rows, :].astype(BF16)
            g_edge = g_third[at, cols].astype(BF16)
            return value * f, g_edge * f, g_edge * (value * slope)

        message, g_value, pre[3] = stacked(sz, first, units)
        collect(3, g_value)
        g_unit = dot(r.gvlow[...], message, 1, 1)
        for c in range(3):
            r.gunit[c, pl.ds(b, 1), :] = jnp.sum(
                g_unit[c * A : (c + 1) * A, :] * r.diag[...], axis=0, keepdims=True
            )

        def attention(cg, at, cols, near_rows):
            s = scores[b, cg, at, :]
            t = jnp.tanh(s)
            up = 1.0 + t
            act = s * up
            wide = r.cut_wide[b, at, :]
            ga = g_att[at, cols].astype(BF16)
            g_score = ga * wide * (up + act * (1.0 - t))
            g_edge = r.gs[:, cols] * (act * wide)
            f, slope = filters(0, cg, at)
            key = r.kv[cg, near_rows, :].astype(BF16)
            query = r.query_low[:, cols]
            middle = g_score * f
            made = [ga * act, middle * key, middle * query, (g_score * slope) * (key * query)]
            f, slope = filters(1, cg, at)
            value = r.kv[CG + cg, near_rows, :].astype(BF16)
            return made + [g_edge * f, g_edge * (value * slope)]

        g_act, g_query, g_key, pre[0], g_value, pre[1] = stacked(sz, first, attention)
        collect(1, g_value)
        collect(0, g_key)
        r.gq[...] += dot(r.fold[...], g_query)
        g_cut = dot(jnp.ones((16, F), BF16), g_act, 1, 1)[0:1, :] * (2.0 * HEADS / F)
        g_smear = jnp.zeros((sz.basis, EB), F32)
        for part in range(4):
            cols = slice(part * F, (part + 1) * F)
            g_smear = g_smear + dot(r.wh[:, cols], pre[part], 1, 1)
            r.gfilt[:, cols] += dot(r.smear[b], pre[part])
        delta, bell = bell_of(r, sz, b)
        through = g_smear * bell
        r.gcut[pl.ds(b, 1), :] = g_cut + jnp.sum(through, axis=0, keepdims=True)
        r.gshrink[pl.ds(b, 1), :] = r.geo[CUT, pl.ds(b, 1), :] * jnp.sum(
            through * delta, axis=0, keepdims=True
        ) * (-2.0 * sharpness_of(sz.basis))
        return carry

    lax.fori_loop(0, NB, backward_block, 0)

    distance = r.geo[DISTANCE]
    g_dist = r.gcut[...] * r.geo[LIVE] * jnp.where(
        distance < CUTOFF,
        (-0.5 * math.pi / CUTOFF) * jnp.sin(math.pi * distance / CUTOFF),
        0.0,
    ) - r.gshrink[...] * r.geo[SHRINK]
    inverse = 1.0 / distance
    g_unit = [r.gunit[c] for c in range(3)]
    sep = [r.geo[c] for c in range(3)]
    along = g_unit[0] * sep[0] + g_unit[1] * sep[1] + g_unit[2] * sep[2]
    radial = (g_dist - along * inverse * inverse) * inverse
    r.gplaces[...] = jnp.zeros_like(r.gplaces)
    for c in range(3):
        g_sep = g_unit[c] * inverse + radial * sep[c]
        first, other = g_sep[:, :LANES], g_sep[:, LANES:]
        z = (
            jnp.where(lane < A, first, 0.0)
            + pltpu.roll(jnp.where(lane < A, 0.0, first), A + 1, 1)
            + pltpu.roll(jnp.where(lane < A, other, 0.0), 2, 1)
            + pltpu.roll(jnp.where(lane < A, 0.0, other), A + 3, 1)
        )
        for bit in range(3):
            z = jnp.where((row >> bit) & 1 == 1, pltpu.roll(z, GROUP * 2**bit, 1), z)
        z = jnp.where(row >= 4, pltpu.roll(z, 1, 1), z)
        total = jnp.sum(g_sep, axis=0, keepdims=True)
        mine = total[:, 0:A] + total[:, A : 2 * A] + total[:, 2 * A : 3 * A] + total[:, 3 * A :]
        mine = jnp.concatenate(
            [jnp.zeros((1, H), F32), mine, jnp.zeros((1, LANES - H - A), F32)], axis=1
        )
        r.gplaces[c : c + 1, :] = jnp.sum(z, axis=0, keepdims=True) - mine

    gproj = r.gproj
    gproj[:, 0:F] = jnp.zeros((E, F), BF16)
    gproj[H : H + A, 0:F] = r.gq[...].astype(BF16)
    for part in range(4):
        gproj[:, (part + 1) * F : (part + 2) * F] = r.gnear[part].astype(BF16)
    g_normed = dot(gproj[...], wqkv[...], 1, 1)
    u = gain * g_normed
    g_scalars = scale * (
        u
        - jnp.mean(u, axis=-1, keepdims=True)
        - xhat * jnp.mean(u * xhat, axis=-1, keepdims=True)
    )
    r.gnorm[...] = jnp.zeros_like(r.gnorm)
    r.gnorm[0:1, :] = jnp.sum(g_normed * xhat, axis=0, keepdims=True)
    r.gnorm[1:2, :] = jnp.sum(g_normed, axis=0, keepdims=True)
    vec_back = dot(r.gvproj[...], wvec[...], 1, 1)
    for index in range(4):
        if index == 0:
            whole = g_scalars
            middle = whole[H : H + A] + r.gx[0]
        else:
            c = index - 1
            whole = r.gnear[4 + c]
            middle = whole[H : H + A] + r.gx[index] + vec_back[c * A : (c + 1) * A, :]
        r.back[index] = middle
        r.back_low[index] = middle.astype(BF16)
        r.rim_low[index] = whole[0:H].astype(BF16)
        r.rim_high[index] = whole[H + A :].astype(BF16)


FACTORS = ("left", "gproj", "gvproj", "gout", "gfilt", "gnorm")
HANDED = (
    "query_low", "kv", "vec", "vproj", "xhat", "scale", "out_proj", "vec_dot", "score"
)
BORDERS = ("rim_low", "rim_high", "gplaces")


def call(body, arrays, outs, scratch, role=None, grant_mb=16, place=VMEM):
    arrays, outs = vars(arrays), vars(outs)
    names = list(arrays) + list(outs) + list(scratch)

    def kernel(*args):
        refs = SimpleNamespace(**dict(zip(names, args, strict=True)))
        if role is None:
            body(refs)
        else:
            pl.when(lax.axis_index("section") == role)(lambda: body(refs))

    results = pl.pallas_call(
        kernel,
        out_shape=list(outs.values()),
        in_specs=[spec for _, spec in arrays.values()],
        out_specs=[place for _ in outs],
        scratch_shapes=[
            pltpu.VMEM(*s) if isinstance(s, tuple) else s for s in scratch.values()
        ],
        compiler_params=pltpu.CompilerParams(vmem_limit_bytes=int(grant_mb * 2**20)),
    )(*[array for array, _ in arrays.values()])
    return SimpleNamespace(**dict(zip(outs, results, strict=True)))


def first_call(sz, m, fetch, sent, arrays):
    A, H, E, F = sz.atoms, sz.halo, sz.rows, sz.width
    EB, CG, NB = sz.edges, sz.halves, sz.blocks
    shape = jax.ShapeDtypeStruct
    results = dict(
        fresh=((4, A, F), BF16),
        head=((4, sent, F), BF16),
        tail=((4, sent, F), BF16),
        left=((sz.factors, F), BF16),
        query_low=((A, F), BF16),
        kv=((4 * CG, E, LANES), F32),
        vec=((3 * CG, E, LANES), F32),
        vproj=((3 * A, 3 * F), F32),
        xhat=((E, F), F32),
        scale=((E, LANES), F32),
        out_proj=((A, 3 * F), F32),
        vec_dot=((A, F), F32),
        score=((NB, CG, EB, LANES), BF16),
    )
    fetched = dict(
        s_own=((4, A, F), BF16),
        s_slots=((3 * sz.slots + 8, LANES), F32),
        s_norms=((16, F), F32),
        s_wqkv=((F, 5 * F), BF16),
        s_wvec=((F, 3 * F), BF16),
        s_wh=((sz.basis, 4 * F), BF16),
        s_wout=((F, 3 * F), BF16),
        sems=pltpu.SemaphoreType.DMA((10,)),
    )
    outs = SimpleNamespace(**{k: shape(*v) for k, v in results.items()})
    scratch = dict(
        query=((CG, A, LANES), F32),
        heads=((F, F), BF16),
        diag=((A, EB), F32),
        geo=((10, 8, EB), F32),
        centres=((sz.basis, EB), F32),
        smear_t=((NB, EB, sz.basis), BF16),
        cut_wide=((NB, EB, LANES), F32),
        units=((NB, 3 * A, EB), BF16),
        pack10=((EB, F), BF16),
        pack20=((EB, F), BF16),
        pack11=((EB, F), BF16),
        pack21=((EB, F), BF16),
        sagg=((CG, A, LANES), F32),
        vagg=((3 * CG, A, LANES), F32),
        third=((NB, EB, F), BF16),
    )
    if fetch:
        scratch.update(fetched)
    return call(
        lambda r: first_forward(r, sz, m, fetch), arrays, outs, scratch, FIRST, grant_mb=20
    )


def filter_call(sz, role, which, arrays):
    A, F = sz.atoms, sz.width
    EB, CG, NB = sz.edges, sz.halves, sz.blocks
    shape = jax.ShapeDtypeStruct
    outs = dict(
        geo=shape((10, 8, EB), F32),
        smear=shape((NB, sz.basis, EB), BF16),
        cut_wide=shape((NB, EB, LANES), BF16),
        units=shape((NB, 3 * A, EB), BF16),
        silu=shape((NB, 4 * CG, EB, LANES), BF16),
        slope=shape((NB, 4 * CG, EB, LANES), BF16),
    )
    if role == SECOND:
        outs.update(key=shape((NB, CG, EB, LANES), F32))
    scratch = dict(
        diag=((A, EB), F32),
        centres=((sz.basis, EB), F32),
        smear_t=((NB, EB, sz.basis), BF16),
    )
    made = call(
        lambda r: edge_filters(r, sz, which),
        arrays,
        SimpleNamespace(**{f"{k}{m}": v for m in which for k, v in outs.items()}),
        scratch,
        role,
        grant_mb=6,
    )
    return {m: SimpleNamespace(**{k: getattr(made, f"{k}{m}") for k in outs}) for m in which}


def both_call(sz, m, fwd, arrays, border_sets=()):
    A, H, E, F = sz.atoms, sz.halo, sz.rows, sz.width
    EB, CG, NB = sz.edges, sz.halves, sz.blocks
    shape = jax.ShapeDtypeStruct
    outs = SimpleNamespace(
        back=shape((4, A, F), F32),
        back_low=shape((4, A, F), BF16),
        rim_low=shape((4, H, F), BF16),
        rim_high=shape((4, H, F), BF16),
        gplaces=shape((8, LANES), F32),
        gproj=shape((E, 5 * F), BF16),
        gvproj=shape((3 * A, 3 * F), BF16),
        gout=shape((A, 3 * F), BF16),
        gfilt=shape((sz.basis, 4 * F), F32),
        gnorm=shape((8, F), F32),
    )
    scratch = dict(
        heads=((F, F), BF16),
        diag=((A, EB), F32),
        fold=((A, EB), BF16),
        centres=((sz.basis, EB), F32),
        gx=((4, A, F), F32),
        gvlow=((3 * A, F), BF16),
        gs=((A, F), BF16),
        gq=((A, F), F32),
        gnear=((7, E, F), F32),
        gunit=((3, 8, EB), F32),
        gcut=((8, EB), F32),
        gshrink=((8, EB), F32),
    )
    if not fwd:
        scratch.update(score_here=((NB, CG, EB, LANES), BF16))
    if fwd:
        outs.fresh = shape((4, A, F), BF16)
        outs.left = shape((sz.factors, F), BF16)
        scratch.update(
            query=((CG, A, LANES), F32),
            query_low=((A, F), BF16),
            kv=((4 * CG, E, LANES), F32),
            vec=((3 * CG, E, LANES), F32),
            vproj=((3 * A, 3 * F), F32),
            score=((NB, CG, EB, LANES), BF16), sagg=((A, F), F32), vagg=((3, A, F), F32), uagg=((3 * A, F), F32)
        )
    if fwd and m:
        outs.all_places = shape((m + 1, 8, LANES), F32)
        for i, made in enumerate(border_sets):
            setattr(arrays, f"gplaces_{i}", (made.gplaces, VMEM))

        def layer(r):
            both_ways(r, sz, m, fwd)
            for i in range(m):
                r.all_places[i] = getattr(r, f"gplaces_{i}")[...]
            r.all_places[m] = r.gplaces[...]

        return call(layer, arrays, outs, scratch, SECOND)
    if not border_sets:
        role = SECOND if fwd else FIRST
        return call(lambda r: both_ways(r, sz, m, fwd), arrays, outs, scratch, role)
    count = m + 1
    outs.up, outs.down = shape((count, 4, H, F), BF16), shape((count, 4, H, F), BF16)
    outs.moved = shape((count, 8, LANES), F32)
    outs.total = shape((count, 8, LANES), F32)
    for role, sets in enumerate(border_sets):
        for i, made in enumerate(sets):
            for name in BORDERS:
                setattr(arrays, f"{name}_{role}_{i}", (getattr(made, name), VMEM))

    def hand_on(r, role):
        for i in range(count):
            low, high, places = (
                getattr(r, f"{name}_{role}_{i}") if i < len(border_sets[role]) else getattr(r, name)
                for name in BORDERS
            )
            r.up[i] = high[...]
            r.down[i] = low[...]
            r.moved[i] = places[...]
            r.total[i] = places[...] + r.early[i] if role == FIRST else places[...]

    def body(r):
        @pl.when(lax.axis_index("section") == FIRST)
        def _():
            both_ways(r, sz, m, fwd)
            hand_on(r, FIRST)

        pl.when(lax.axis_index("section") == SECOND)(lambda: hand_on(r, SECOND))

    return call(body, arrays, outs, scratch)


def border_call(sz, features, coords):
    A, H, F = sz.atoms, sz.halo, sz.width
    count = features.shape[0]

    def body(r):
        moves = [(r.coords, r.s_coords)]
        for m in range(count):
            moves += [
                (r.features.at[m, 0, :, A - H : A, :], r.up.at[4 * m : 4 * m + 4]),
                (r.features.at[m, 0, :, 0:H, :], r.down.at[4 * m : 4 * m + 4]),
            ]
        copies = [
            pltpu.make_async_copy(source, target, r.sems.at[i])
            for i, (source, target) in enumerate(moves)
        ]
        for copy in copies:
            copy.start()
        copies[0].wait()
        for target, ends in ((r.up, slice(A - H, A)), (r.down, slice(0, H))):
            rows = []
            for m in range(count):
                parts = [r.s_coords[m, c][:, ends] for c in range(3)]
                rows.append(jnp.concatenate(parts, axis=1))
            target[4 * count] = packed_places(rows, F)
        for copy in copies[1:]:
            copy.wait()

    shape = jax.ShapeDtypeStruct((4 * count + 1, H, F), BF16)
    return call(
        body,
        SimpleNamespace(features=(features, HBM), coords=(coords, HBM)),
        SimpleNamespace(up=shape, down=shape),
        dict(s_coords=(coords.shape, F32), sems=pltpu.SemaphoreType.DMA((2 * count + 1,))),
        grant_mb=54,
    )


class Rooms:
    def __init__(self, sz):
        F = sz.width
        ends = [0]
        for rows in (F, F, F, 4 * sz.atoms, sz.basis):
            ends.append(ends[-1] + rows)
        self.wqkv, self.wvec, self.wout, self.own, self.wh = [
            slice(*pair) for pair in zip(ends, ends[1:])
        ]
        table = 3 * sz.slots + 8
        self.slots, self.norms = slice(0, table), slice(table, table + 8)
        self.coords = slice(table + 8, table + 16)
        self.low_shape, self.wide_shape = (20480, 5 * F), (51200, F)


def stage_call(sz, features, coords, neighbours, shifts, counts, gain, bias, filter_weight, weights):
    A, F, K = sz.atoms, sz.width, sz.slots
    count = features.shape[0]
    rooms = Rooms(sz)

    def body(r):
        moves = [(r.coords, r.s_coords), (r.counts, r.s_counts)]
        moves += [(r.gain, r.s_gain), (r.bias, r.s_bias), (r.wfilt.at[0], r.s_wfilt)]
        for m in range(count):
            moves += [
                (r.nbr.at[m, 0], r.s_slots.at[m, 0:K]),
                (r.shifts.at[m, 0, 0], r.s_slots.at[m, K : 2 * K]),
                (r.shifts.at[m, 0, 1], r.s_slots.at[m, 2 * K : 3 * K]),
            ]
        near = len(moves)
        moves += [(r.features.at[0, 0], r.s_own), (r.wqkv.at[0], r.s_wqkv)]
        moves += [(r.wvec.at[0], r.s_wvec), (r.wout.at[0], r.s_wout)]
        copies = [
            pltpu.make_async_copy(source, target, r.sems.at[i])
            for i, (source, target) in enumerate(moves)
        ]
        for copy in copies:
            copy.start()
        for copy in copies[:near]:
            copy.wait()
        r.s_wh[...] = (r.s_wfilt[...].astype(F32) * 0.5).astype(BF16)
        for m in range(count):
            r.s_table[m, 0 : 3 * K, 0:A] = r.s_slots[m].astype(F32)
            r.s_table[m, 3 * K :, 0:A] = jnp.broadcast_to(r.s_counts[m].astype(F32), (8, A))
        r.s_norms[...] = jnp.zeros_like(r.s_norms)
        r.s_norms[0:1, :] = r.s_gain[...].astype(F32)
        r.s_norms[1:2, :] = r.s_bias[...].astype(F32)
        for c in range(3):
            r.s_norms[8 + c : 9 + c, 0:A] = r.s_coords[0, c]
        for copy in copies[near:]:
            copy.wait()
        moves = [
            (r.s_table, r.slots),
            (r.s_norms.at[0:8], r.norms),
            (r.s_wh, r.wh),
            (r.s_table.at[0], r.wide.at[rooms.slots, 0:LANES]),
            (r.s_norms, r.wide.at[rooms.norms.start : rooms.coords.stop]),
            (r.s_wqkv, r.low.at[rooms.wqkv]),
            (r.s_wvec, r.low.at[rooms.wvec, 0 : 3 * F]),
            (r.s_wout, r.low.at[rooms.wout, 0 : 3 * F]),
            (r.s_wh, r.low.at[rooms.wh, 0 : 4 * F]),
        ]
        for index in range(4):
            start = rooms.own.start + index * A
            moves.append((r.s_own.at[index], r.low.at[start : start + A, 0:F]))
        later = [
            pltpu.make_async_copy(source, target, r.sems.at[len(copies) + i])
            for i, (source, target) in enumerate(moves)
        ]
        for copy in later:
            copy.start()
        for copy in later:
            copy.wait()

    shape = jax.ShapeDtypeStruct
    wqkv, wvec, wout = weights
    return call(
        body,
        SimpleNamespace(
            features=(features, HBM),
            coords=(coords, HBM),
            nbr=(neighbours, HBM),
            shifts=(shifts, HBM),
            counts=(counts, HBM),
            gain=(gain, HBM),
            bias=(bias, HBM),
            wfilt=(filter_weight, HBM),
            wqkv=(wqkv, HBM),
            wvec=(wvec, HBM),
            wout=(wout, HBM),
        ),
        SimpleNamespace(
            slots=shape((count, 3 * K + 8, LANES), F32),
            norms=shape((8, F), F32),
            wh=shape((sz.basis, 4 * F), BF16),
            low=shape(rooms.low_shape, BF16),
            wide=shape(rooms.wide_shape, F32),
        ),
        dict(
            s_coords=(coords.shape, F32),
            s_counts=(counts.shape, jnp.int32),
            s_gain=(gain.shape, BF16),
            s_bias=(bias.shape, BF16),
            s_wfilt=(filter_weight.shape[1:], BF16),
            s_slots=((count, 3 * K, A), jnp.int32),
            s_own=((4, A, F), BF16),
            s_wqkv=(wqkv.shape[1:], BF16),
            s_wvec=(wvec.shape[1:], BF16),
            s_wout=(wout.shape[1:], BF16),
            s_wh=(filter_weight.shape[1:], BF16),
            s_table=((count, 3 * K + 8, LANES), F32),
            s_norms=((16, F), F32),
            sems=pltpu.SemaphoreType.DMA((3 * count + 22,)),
        ),
        grant_mb=54,
        place=HBM,
    )


def gradient_call(sz, sets):
    A, E, F = sz.atoms, sz.rows, sz.width
    count = len(sets[0])
    w1, w2, w3 = sz.widths
    w4, w5 = 4 * F // sz.space, F // sz.space
    half = F // 2
    arrays = SimpleNamespace()
    for role in (FIRST, SECOND):
        for m in range(count):
            for name in FACTORS:
                setattr(arrays, f"{name}_{role}_{m}", (getattr(sets[role][m], name), VMEM))

    def body(r, role):
        def get(name, m):
            return getattr(r, f"{name}_{role}_{m}")

        every = range(count)
        e, a = E, A
        r.qkv[...] = sum(dot(get("gproj", m)[...], get("left", m)[0:e, :], 0, 0) for m in every)
        r.vector[...] = sum(
            dot(get("gvproj", m)[...], get("left", m)[e : e + 3 * a, :], 0, 0) for m in every
        )
        r.out[...] = sum(
            dot(get("gout", m)[...], get("left", m)[e + 3 * a : e + 4 * a, :], 0, 0) for m in every
        )
        filt = sum(get("gfilt", m)[...] for m in every) * 0.5
        norm = sum(get("gnorm", m)[...] for m in every)
        core = lax.axis_index("dp")
        for k in range(sz.space):
            spare = [filt[:, k * w4 : (k + 1) * w4]]
            if half > w4:
                spare.append(jnp.zeros((sz.basis, half - w4), F32))
            left = jnp.concatenate(spare, axis=1)
            rows = [norm[:, k * w5 : (k + 1) * w5], jnp.zeros((8, half - w5), F32)]
            right = jnp.concatenate(rows, axis=1)
            right = jnp.concatenate(
                [right, jnp.zeros((sz.packed - sz.spare - 8, half), F32)], axis=0
            )
            if sz.packed - sz.spare > sz.basis:
                gap = jnp.zeros((sz.packed - sz.spare - sz.basis, half), F32)
                left = jnp.concatenate([left, gap], axis=0)
            parts = [
                r.qkv[k * w1 : (k + 1) * w1, :],
                r.vector[k * w2 : (k + 1) * w2, :],
                r.out[k * w3 : (k + 1) * w3, :],
            ]
            first = jnp.concatenate([part[:, :half] for part in parts] + [left], axis=0)
            second = jnp.concatenate([part[:, half:] for part in parts] + [right], axis=0)
            r.send[k] = jnp.where(core == 0, second, first).astype(BF16)
            r.stay[k] = jnp.where(core == 0, first, second)

    def both(r):
        for role in (FIRST, SECOND):
            pl.when(lax.axis_index("section") == role)(lambda role=role: body(r, role))

    shape = jax.ShapeDtypeStruct
    return call(
        both,
        arrays,
        SimpleNamespace(
            send=shape((sz.space, sz.packed, half), BF16),
            stay=shape((sz.space, sz.packed, half), F32),
        ),
        dict(
            qkv=((5 * F, F), F32),
            vector=((3 * F, F), F32),
            out=((3 * F, F), F32),
        ),
    )


def border_rows(sz, index):
    start = sz.packed + index * 2 * sz.halo
    return [slice(start + i * sz.halo, start + (i + 1) * sz.halo) for i in range(2)]


def border_block(sz, ref, index):
    return jnp.concatenate([ref[rows, :] for rows in border_rows(sz, index)], axis=1)


def piece_call(sz, stay, recv, up, down, total, late):
    A, H, E, F = sz.atoms, sz.halo, sz.rows, sz.width
    count = up.shape[0]
    half = F // 2

    def body(r):
        slab, space = lax.axis_index("space"), sz.space
        for hop in range(space):
            k = lax.rem(slab + hop, space)
            share = r.stay[k] + r.recv[k].astype(F32)
            target = getattr(r, f"hop{hop}")
            target[0 : sz.packed, :] = share.astype(target.dtype)
        places = [r.total[m] + r.late[m] for m in range(count)]
        ends = (
            (r.hop1, r.up, slice(H + A, E)),
            (getattr(r, f"hop{space - 1}"), r.down, slice(0, H)),
        )
        for target, border, lanes in ends:
            rows = []
            for m in range(count):
                parts = [places[m][c : c + 1, lanes] for c in range(3)]
                rows.append(jnp.concatenate(parts, axis=1))
            blocks = [border[m, index] for m in range(count) for index in range(4)]
            for index, block in enumerate(blocks + [packed_places(rows, F)]):
                first, second = border_rows(sz, index)
                target[first, :] = block[:, :half]
                target[second, :] = block[:, half:]
        for m in range(count):
            for c in range(3):
                r.mine[m, c] = places[m][c : c + 1, H : H + A]

    shape = jax.ShapeDtypeStruct
    outs = {
        f"hop{hop}": shape(
            (sz.packed + ((8 * count + 2) * H if hop in (1, sz.space - 1) else 0), half),
            BF16 if hop else F32,
        )
        for hop in range(sz.space)
    }
    outs.update(mine=shape((count, 3, 1, A), F32))
    made = call(
        body,
        SimpleNamespace(
            stay=(stay, VMEM),
            recv=(recv, VMEM),
            up=(up, VMEM),
            down=(down, VMEM),
            total=(total, VMEM),
            late=(late, VMEM),
        ),
        SimpleNamespace(**outs),
        {},
    )
    return [getattr(made, f"hop{hop}") for hop in range(sz.space)], made.mine


def result_call(sz, fresh, back, from_low, from_high, mine):
    A, H, F = sz.atoms, sz.halo, sz.width
    count = len(back[0])
    arrays = SimpleNamespace(
        low=(from_low, VMEM), high=(from_high, VMEM), mine=(mine, VMEM)
    )
    for role in (FIRST, SECOND):
        for m in range(count):
            setattr(arrays, f"fresh_{role}_{m}", (fresh[role][m], VMEM))
            setattr(arrays, f"back_{role}_{m}", (back[role][m], VMEM))

    def body(r, role):
        for m in range(count):
            r.outputs[0, m, 0] = getattr(r, f"fresh_{role}_{m}")[...]
            whole = getattr(r, f"back_{role}_{m}")
            for index in range(4):
                low = border_block(sz, r.low, 4 * m + index).astype(F32)
                high = border_block(sz, r.high, 4 * m + index).astype(F32)
                r.grads[0, m, 0, index, 0:H, :] = whole[index, 0:H, :] + low
                r.grads[0, m, 0, index, H : A - H, :] = whole[index, H : A - H, :]
                r.grads[0, m, 0, index, A - H :, :] = whole[index, A - H :, :] + high
            for c in range(3):
                edge = [
                    unpacked_places(border_block(sz, r.low, 4 * count), m, c, H),
                    jnp.zeros((1, A - 2 * H), F32),
                    unpacked_places(border_block(sz, r.high, 4 * count), m, c, H),
                ]
                r.places[m, c] = r.mine[m, c] + jnp.concatenate(edge, axis=1)

    def both(r):
        for role in (FIRST, SECOND):
            pl.when(lax.axis_index("section") == role)(lambda role=role: body(r, role))

    shape = jax.ShapeDtypeStruct
    return call(
        both,
        arrays,
        SimpleNamespace(
            outputs=shape((1, count, 1, 4, A, F), BF16),
            grads=shape((1, count, 1, 4, A, F), F32),
            places=shape((count, 3, 1, A), F32),
        ),
        {},
    )


def share_call(sz, total, other):
    F = sz.width
    w1, w2, w3 = sz.widths
    w4, w5 = 4 * F // sz.space, F // sz.space
    half = F // 2

    def body(r, first, second):
        for lanes, part in ((slice(0, half), first), (slice(half, F), second)):
            r.qkv[0, :, lanes] = part[0:w1, :]
            r.vector[0, :, lanes] = part[w1 : w1 + w2, :]
            r.out[0, :, lanes] = part[w1 + w2 : sz.spare, :]
        r.filt[0] = first[sz.spare : sz.spare + sz.basis, 0:w4]
        r.gain[...] = second[sz.spare : sz.spare + 1, 0:w5]
        r.bias[...] = second[sz.spare + 1 : sz.spare + 2, 0:w5]

    def both(r):
        pl.when(lax.axis_index("dp") == 0)(lambda: body(r, r.total, r.other))
        pl.when(lax.axis_index("dp") == 1)(lambda: body(r, r.other, r.total))

    shape = jax.ShapeDtypeStruct
    return call(
        both,
        SimpleNamespace(total=(total, VMEM), other=(other, VMEM)),
        SimpleNamespace(
            gain=shape((1, w5), F32),
            bias=shape((1, w5), F32),
            qkv=shape((1, w1, F), F32),
            vector=shape((1, w2, F), F32),
            filt=shape((1, sz.basis, w4), F32),
            out=shape((1, w3, F), F32),
        ),
        {},
    )


def on_device(
    features,
    coords,
    neighbours,
    counts,
    shifts,
    norm_gain,
    norm_bias,
    qkv_weight,
    vector_weight,
    filter_weight,
    out_weight,
    cotangent,
):
    micro_count = features.shape[0]
    space = lax.axis_size("space")
    sz = Sizes(features.shape[3], features.shape[4], filter_weight.shape[1], neighbours.shape[2], space)
    up = [(i, (i + 1) % space) for i in range(space)]
    down = [((i + 1) % space, i) for i in range(space)]

    places = jnp.transpose(coords, (0, 2, 1, 3))
    borders = border_call(sz, features, places)
    staged = stage_call(
        sz,
        features,
        places,
        neighbours,
        shifts,
        counts,
        norm_gain,
        norm_bias,
        filter_weight,
        (qkv_weight, vector_weight, out_weight),
    )
    slots, norms, half_filter = staged.slots, staged.norms, staged.wh
    pack_low = lax.ppermute(borders.up, "space", up)
    pack_high = lax.ppermute(borders.down, "space", down)
    both = ("section", "space")
    forth = [(k, space + k) for k in range(space)]
    forth_up = [(k, space + (k + 1) % space) for k in range(space)]
    forth_down = [((k + 1) % space, space + k) for k in range(space)]
    back = [(space + k, k) for k in range(space)]
    back_up = [(space + k, (k + 1) % space) for k in range(space)]
    back_down = [(space + (k + 1) % space, k) for k in range(space)]

    def geometry_inputs():
        return SimpleNamespace(
            pack_low=(pack_low, VMEM),
            pack_high=(pack_high, VMEM),
            coords=(places, VMEM),
            slots=(slots, VMEM),
            wh=(half_filter, VMEM),
        )

    firsts, sent, filters = [], [], {}
    for m in range(micro_count):
        if m == 0:
            arrays = SimpleNamespace(
                pack_low=(pack_low, VMEM),
                pack_high=(pack_high, VMEM),
                room=(staged.low, HBM),
                wide=(staged.wide, HBM),
            )
        else:
            arrays = geometry_inputs()
            arrays.features = (features, VMEM)
            arrays.norms = (norms, VMEM)
            arrays.wqkv, arrays.wvec, arrays.wout = (
                (qkv_weight, VMEM), (vector_weight, VMEM), (out_weight, VMEM)
            )
        first = first_call(sz, m, m == 0, sz.sent[m], arrays)
        firsts.append(first)
        if m == micro_count - 1:
            made = filters[SECOND] = filter_call(
                sz, SECOND, range(micro_count), geometry_inputs()
            )
            own, *rest = sent[0]
            first.head, made[0].geo, own = lax.optimization_barrier(
                (first.head, made[0].geo, own)
            )
            sent[0] = (own, *rest)
        sent.append((
            lax.ppermute(first.fresh, both, forth),
            lax.ppermute(first.tail, both, forth_up),
            lax.ppermute(first.head, both, forth_down),
        ))
    def both_inputs(m, role):
        made = filters[role][m]
        return SimpleNamespace(
            norms=(norms, VMEM),
            wqkv=(qkv_weight, VMEM),
            wvec=(vector_weight, VMEM),
            wh=(half_filter, VMEM),
            wout=(out_weight, VMEM),
            geo=(made.geo, VMEM),
            smear=(made.smear, VMEM),
            cut_wide=(made.cut_wide, VMEM),
            units=(made.units, VMEM),
            silu=(made.silu, VMEM),
            slope=(made.slope, VMEM),
        )

    seconds, returned = [], []
    for m in range(micro_count):
        if m == 1:
            other = filters[FIRST][0]
            other.geo, filters[SECOND][m].geo = lax.optimization_barrier(
                (other.geo, filters[SECOND][m].geo)
            )
        arrays = both_inputs(m, SECOND)
        arrays.key = (filters[SECOND][m].key, VMEM)
        own, low, high = sent[m]
        arrays.own, arrays.low, arrays.high = (own, VMEM), (low, VMEM), (high, VMEM)
        arrays.cotangent = (cotangent, VMEM)
        second = both_call(sz, m, True, arrays, seconds)
        seconds.append(second)
        if m == 0:
            later = geometry_inputs()
            held, second.gplaces = lax.optimization_barrier((slots, second.gplaces))
            later.slots = (held, VMEM)
            filters[FIRST] = filter_call(sz, FIRST, range(micro_count), later)
        back_low, rim_low, rim_high = second.back_low, second.rim_low, second.rim_high
        if m:
            returned[-1], back_low, rim_low, rim_high = lax.optimization_barrier(
                (returned[-1], back_low, rim_low, rim_high)
            )
        returned.append((
            lax.ppermute(back_low, both, back),
            lax.ppermute(rim_high, both, back_up),
            lax.ppermute(rim_low, both, back_down),
        ))
    thirds = []
    for m in range(micro_count):
        arrays = both_inputs(m, FIRST)
        for name in HANDED:
            setattr(arrays, name, (getattr(firsts[m], name), VMEM))
        inc, inc_low, inc_high = returned[m]
        arrays.inc, arrays.inc_low, arrays.inc_high = (inc, VMEM), (inc_low, VMEM), (inc_high, VMEM)
        sets = (thirds, seconds) if m == micro_count - 1 else ()
        if sets:
            arrays.early = (lax.ppermute(seconds[-1].all_places, both, back), VMEM)
        third = both_call(sz, m, False, arrays, sets)
        third.left = firsts[m].left
        thirds.append(third)

    last = thirds[-1]
    late = lax.ppermute(last.moved, both, forth)
    shares = gradient_call(sz, (thirds, seconds))
    recv = lax.ppermute(shares.send, "dp", [(0, 1), (1, 0)])
    (total, *pieces), mine = piece_call(sz, shares.stay, recv, last.up, last.down, last.total, late
    )
    received = [
        lax.ppermute(piece, "space", [(i, (i + hop) % space) for i in range(space)])
        for hop, piece in enumerate(pieces, 1)
    ]
    for piece in received:
        total = total + piece[: sz.packed].astype(F32)
    results = result_call(
        sz,
        ([v.fresh for v in firsts], [v.fresh for v in seconds]),
        ([v.back for v in thirds], [v.back for v in seconds]),
        received[0],
        received[-1],
        mine,
    )
    other = lax.ppermute(total, "dp", [(0, 1), (1, 0)])
    share = share_call(sz, total, other)
    return (
        results.outputs,
        results.grads,
        share.gain,
        share.bias,
        jnp.transpose(share.qkv, (0, 2, 1)),
        jnp.transpose(share.vector, (0, 2, 1)),
        share.filt,
        jnp.transpose(share.out, (0, 2, 1)),
        jnp.transpose(results.places, (0, 2, 1, 3)),
    )


def solution(mesh):
    return jax.shard_map(
        on_device,
        mesh=mesh,
        in_specs=(
            P(None, "dp", None, "space", None),
            P(None, "dp", None, "space"),
            P(None, "dp", None, "space"),
            P(None, "dp", "space"),
            P(None, "dp", None, None, "space"),
            P("section", None),
            P("section", None),
            P("section", None, None),
            P("section", None, None),
            P("section", None, None),
            P("section", None, None),
            P(None, "dp", None, "space", None),
        ),
        out_specs=(
            P("section", None, "dp", None, "space", None),
            P("section", None, "dp", None, "space", None),
            P("section", "space"),
            P("section", "space"),
            P("section", None, "space"),
            P("section", None, "space"),
            P("section", None, "space"),
            P("section", None, "space"),
            P(None, "dp", None, "space"),
        ),
        check_vma=False,
    )
```

```python
import math
from types import SimpleNamespace

import jax
import jax.numpy as jnp
from jax import lax
from jax.experimental import pallas as pl
from jax.experimental.pallas import tpu as pltpu
from jax.sharding import PartitionSpec as P

HEADS = 8
CUTOFF = 5.0
LN_EPS = 1e-05
SOFTEN = 0.25
CROSS = 2.5
GROUP = 4
LANES = 128
SUBLANES = 8
FIRST, SECOND = 0, 1

F32 = jnp.float32
BF16 = jnp.bfloat16
VMEM = pl.BlockSpec(memory_space=pltpu.VMEM)
HBM = pl.BlockSpec(memory_space=pltpu.HBM)


def dot(left, right, left_dim=1, right_dim=0):
    return lax.dot_general(
        left, right, (((left_dim,), (right_dim,)), ((), ())), preferred_element_type=F32
    )


def iota(shape, dim):
    return lax.broadcasted_iota(jnp.int32, shape, dim)


def packed_places(rows, width):
    parts = []
    for row in rows:
        high = row.astype(BF16).astype(F32)
        rest = row - high
        middle = rest.astype(BF16).astype(F32)
        parts += [high, middle, rest - middle]
    gap = 16 - len(parts)
    whole = jnp.concatenate(parts + [jnp.zeros((gap, rows[0].shape[1]), F32)], axis=0)
    wide = [whole, jnp.zeros((16, width - whole.shape[1]), F32)]
    return jnp.concatenate(wide, axis=1).astype(BF16)


def unpacked_places(block, m, c, count):
    rows = block[:, c * count : (c + 1) * count].astype(F32)
    return rows[3 * m : 3 * m + 1] + rows[3 * m + 1 : 3 * m + 2] + rows[3 * m + 2 : 3 * m + 3]


class Sizes:
    def __init__(self, atoms, width, basis, slots, space):
        self.atoms, self.width, self.basis, self.slots, self.space = atoms, width, basis, slots, space
        self.halo = atoms // 4
        self.rows = atoms + 2 * self.halo
        self.blocks = slots // GROUP
        self.edges = GROUP * atoms
        self.halves = width // LANES
        self.window = atoms + SUBLANES
        self.sent = (self.halo, atoms)
        self.widths = (5 * width // space, 3 * width // space, 3 * width // space)
        self.spare = sum(self.widths)
        self.packed = -(-(self.spare + basis) // 16) * 16
        self.factors = -(-(self.rows + 4 * atoms) // LANES) * LANES


def halves_of(sz):
    return [slice(cg * LANES, (cg + 1) * LANES) for cg in range(sz.halves)]


def first_row(b):
    return GROUP * b + jnp.where(b >= 4, 1, 0)


def sharpness_of(basis):
    return (2.0 / basis * (1.0 - math.exp(-CUTOFF))) ** (-2)


def write_centres(ref, basis):
    low_end = math.exp(-CUTOFF)
    step = iota(ref.shape, 0).astype(F32) / (basis - 1)
    ref[...] = low_end * (1.0 - step) + step


def edge_geometry(r, sz, m, coords, slots):
    A, H, E, EB, K = sz.atoms, sz.halo, sz.rows, sz.edges, sz.slots
    lane = iota((8, LANES), 1)
    row = iota((8, LANES), 0)
    slab, last = lax.axis_index("space"), sz.space - 1
    last_block = r.pack_low.shape[0] - 1
    spot = iota((1, LANES), 1)
    length_x = sz.space * A * 4.0 / H
    places = []
    for c in range(3):
        places.append(
            jnp.concatenate(
                [
                    unpacked_places(r.pack_low[last_block], m, c, H),
                    coords[c],
                    unpacked_places(r.pack_high[last_block], m, c, H),
                    jnp.zeros((1, LANES - E), F32),
                ],
                axis=1,
            )
        )
    places.append(
        jnp.where((spot < H) & (slab == 0), -length_x, 0.0)
        + jnp.where((spot >= H + A) & (slab == last), length_x, 0.0)
    )
    near = []
    for c in range(4):
        y = jnp.broadcast_to(places[c], (8, LANES))
        for bit in range(3):
            y = jnp.where((row >> bit) & 1 == 1, pltpu.roll(y, LANES - GROUP * 2**bit, 1), y)
        y = jnp.where(row >= 4, pltpu.roll(y, LANES - 1, 1), y)
        first = jnp.where(lane < A, y, pltpu.roll(y, A - 1, 1))
        other = jnp.where(lane < A, pltpu.roll(y, LANES - 2, 1), pltpu.roll(y, A - 3, 1))
        near.append(jnp.concatenate([first, other], axis=1))
    wide_lane = iota((8, EB), 1)
    wide_row = iota((8, EB), 0)
    wanted = GROUP * wide_row + wide_lane // A + jnp.where(wide_row >= 4, 1, 0) + wide_lane % A
    table = slots[:, 0:A].astype(jnp.int32)
    alive = iota((K, A), 0) < table[3 * K : 3 * K + 1]
    code = jnp.where(alive, 16, 0) + (table[K : 2 * K] + 1) * 4 + (table[2 * K : 3 * K] + 1)
    code = jnp.concatenate([code] * GROUP, axis=1)
    named = jnp.concatenate([table[0:K]] * GROUP, axis=1)
    found = jnp.zeros((8, EB), jnp.int32)
    for n in range(K):
        found = found + jnp.where(named[n : n + 1, :] == wanted, code[n : n + 1, :], 0)
    live = (found >> 4).astype(F32)
    offsets = (
        near[3],
        (((found >> 2) & 3) - 1).astype(F32) * CROSS,
        ((found & 3) - 1).astype(F32) * CROSS,
    )
    sep = []
    for c in range(3):
        mine = coords[c]
        sep.append(near[c] - jnp.concatenate([mine] * GROUP, axis=1) + offsets[c])
    distance = jnp.sqrt(sep[0] * sep[0] + sep[1] * sep[1] + sep[2] * sep[2] + SOFTEN)
    inside = distance < CUTOFF
    cut = jnp.where(inside, 0.5 * (jnp.cos(math.pi * distance / CUTOFF) + 1.0), 0.0) * live
    for index, value in enumerate(
        sep + [distance, live, cut, jnp.exp(-distance)] + [part / distance for part in sep]
    ):
        r.geo[index] = value


DISTANCE, LIVE, CUT, SHRINK, UNIT = 3, 4, 5, 6, 7


def bell_of(r, sz, b):
    delta = r.geo[SHRINK, pl.ds(b, 1), :] - r.centres[...]
    return delta, jnp.exp(-sharpness_of(sz.basis) * delta * delta)


def write_edge_tables(r, sz, b, wide_kind):
    A, EB = sz.atoms, sz.edges
    cut = r.geo[CUT, pl.ds(b, 1), :]
    _, bell = bell_of(r, sz, b)
    smear = cut * bell
    if hasattr(r, "smear"):
        r.smear[b] = smear.astype(BF16)
    r.smear_t[b] = jnp.transpose(smear).astype(BF16)
    coarse = cut.astype(BF16).astype(F32)
    which = iota((16, EB), 0)
    pair = jnp.where(which == 0, coarse, jnp.where(which == 1, cut - coarse, 0.0)).astype(BF16)
    r.cut_wide[b] = dot(pair, jnp.ones((16, LANES), BF16), 0, 0).astype(wide_kind)
    for c in range(3):
        r.units[b, c * A : (c + 1) * A, :] = (
            r.diag[...] * r.geo[UNIT + c, pl.ds(b, 1), :]
        ).astype(BF16)


def write_constants(r, sz):
    A, EB, F = sz.atoms, sz.edges, sz.width
    if hasattr(r, "centres"):
        write_centres(r.centres, sz.basis)
    if hasattr(r, "diag"):
        r.diag[...] = jnp.where(iota((A, EB), 1) % A == iota((A, EB), 0), 1.0, 0.0)
    if hasattr(r, "fold"):
        r.fold[...] = jnp.where(iota((A, EB), 1) % A == iota((A, EB), 0), 1.0, 0.0).astype(BF16)
    if hasattr(r, "heads"):
        r.heads[...] = jnp.where(
            iota((F, F), 0) // (F // HEADS) == iota((F, F), 1) // (F // HEADS), 0.5, 0.0
        ).astype(BF16)


def node_part(r, sz, own, low, high, norms, wqkv):
    A, H, E, F, CG = sz.atoms, sz.halo, sz.rows, sz.width, sz.halves
    halves = halves_of(sz)
    scalars = jnp.concatenate([low[0, 0:H], own[0], high[0, 0:H]], axis=0).astype(F32)
    centred = scalars - jnp.mean(scalars, axis=-1, keepdims=True)
    spread = jnp.mean(centred * centred, axis=-1, keepdims=True)
    scale = lax.rsqrt(spread + LN_EPS)
    normed = (centred * scale * norms[0:1, :] + norms[1:2, :]).astype(BF16)
    left = r.left
    left[0:E, :] = normed
    left[E : E + 3 * A, :] = own[1:4].reshape(3 * A, F)
    left[E + 4 * A :, :] = jnp.zeros((sz.factors - E - 4 * A, F), BF16)
    for part in range(5):
        projected = dot(normed, wqkv[:, part * F : (part + 1) * F])
        for cg in range(CG):
            if part == 0:
                r.query[cg] = projected[H : H + A, halves[cg]]
            else:
                r.kv[(part - 1) * CG + cg] = projected[:, halves[cg]]
    for c in range(3):
        for cg in range(CG):
            r.vec[c * CG + cg, 0:H, :] = low[c + 1, 0:H, halves[cg]].astype(F32)
            r.vec[c * CG + cg, H : H + A, :] = own[c + 1][:, halves[cg]].astype(F32)
            r.vec[c * CG + cg, H + A : E, :] = high[c + 1, 0:H, halves[cg]].astype(F32)
    return centred * scale, scale


def buffers(r, sz, which):
    end = str(which)
    return SimpleNamespace(**{k[:-1]: v for k, v in vars(r).items() if k.endswith(end)})


def tiles(sz, first):
    A = sz.atoms
    for kk in range(GROUP):
        for cg in range(sz.halves):
            yield (
                cg,
                slice(kk * A, (kk + 1) * A),
                slice(cg * LANES, (cg + 1) * LANES),
                pl.ds(first + kk, A),
            )


def stacked(sz, first, tile):
    made = [tile(*where) for where in tiles(sz, first)]
    CG = sz.halves
    wholes = []
    for index in range(len(made[0])):
        lines = [
            jnp.concatenate([made[kk * CG + cg][index] for cg in range(CG)], axis=1)
            for kk in range(GROUP)
        ]
        wholes.append(jnp.concatenate(lines, axis=0))
    return wholes


def vector_dot(r, sz):
    A, F, vp = sz.atoms, sz.width, r.vproj
    return sum(
        vp[c * A : (c + 1) * A, 0:F] * vp[c * A : (c + 1) * A, F : 2 * F] for c in range(3)
    )


def write_layer_output(r, sz, own, out_proj, vec_dot, vector_agg):
    A, H, F, vp = sz.atoms, sz.halo, sz.width, r.vproj
    for index in range(4):
        if index == 0:
            fresh = vec_dot * out_proj[:, F : 2 * F] + out_proj[:, 2 * F :]
        else:
            rows = slice((index - 1) * A, index * A)
            fresh = vp[rows, 2 * F :] * out_proj[:, 0:F] + vector_agg[index - 1]
        fresh = (own[index].astype(F32) + fresh).astype(BF16)
        r.fresh[index] = fresh
        if hasattr(r, "head"):
            r.head[index, 0:H, :] = fresh[:H]
            r.tail[index, 0:H, :] = fresh[A - H :]


def first_forward(r, sz, m, fetch):
    A, H, E, F, EB = sz.atoms, sz.halo, sz.rows, sz.width, sz.edges
    CG = sz.halves
    r.s_low, r.s_high = r.pack_low.at[4 * m : 4 * m + 4], r.pack_high.at[4 * m : 4 * m + 4]
    copies = early = []
    if fetch:
        rooms = Rooms(sz)
        early = [
            (r.wide.at[rooms.slots, 0:LANES], r.s_slots),
            (r.wide.at[rooms.norms.start : rooms.coords.stop], r.s_norms),
            (r.room.at[rooms.wqkv], r.s_wqkv),
        ]
        for index in range(4):
            start = rooms.own.start + index * A
            early.append((r.room.at[start : start + A, 0:F], r.s_own.at[index]))
        late = [
            (r.room.at[rooms.wh, 0 : 4 * F], r.s_wh),
            (r.room.at[rooms.wvec, 0 : 3 * F], r.s_wvec),
            (r.room.at[rooms.wout, 0 : 3 * F], r.s_wout),
        ]
        copies = [
            pltpu.make_async_copy(source, target, r.sems.at[i])
            for i, (source, target) in enumerate(early + late)
        ]
        for copy in copies:
            copy.start()
    else:
        r.s_slots, r.s_norms, r.s_wh = r.slots.at[m], r.norms, r.wh
        r.s_own, r.s_wqkv = r.features.at[m, 0], r.wqkv.at[0]
        r.s_wvec, r.s_wout = r.wvec.at[0], r.wout.at[0]
    write_constants(r, sz)
    r.sagg[...] = jnp.zeros_like(r.sagg)
    r.vagg[...] = jnp.zeros_like(r.vagg)
    for copy in copies[: len(early)]:
        copy.wait()
    coords = [r.s_norms[8 + c : 9 + c, 0:A] if fetch else r.coords[m, c] for c in range(3)]
    edge_geometry(r, sz, m, coords, r.s_slots)

    def tables(b, carry):
        write_edge_tables(r, sz, b, F32)
        return carry

    lax.fori_loop(0, sz.blocks, tables, 0, unroll=4)
    own = r.s_own
    xhat, scale = node_part(r, sz, own, r.s_low, r.s_high, r.s_norms, r.s_wqkv)
    r.xhat[...] = xhat
    r.scale[...] = jnp.broadcast_to(scale, r.scale.shape)
    for cg in range(CG):
        r.query_low[:, cg * LANES : (cg + 1) * LANES] = r.query[cg].astype(BF16)
    for copy in copies[len(early) :]:
        copy.wait()
    r.vproj[...] = dot(r.left[E : E + 3 * A, :], r.s_wvec[...])

    def filter_part(b, part):
        return dot(r.smear_t[b], r.s_wh[:, part * F : (part + 1) * F])

    def block(b, w):
        first = first_row(b)
        half = filter_part(b, 0)
        for cg, at, cols, near_rows in tiles(sz, first):
            h = half[at, cols]
            product = r.query[cg] * r.kv[cg, near_rows, :] * (h + h * jnp.tanh(h))
            coarse = product.astype(BF16)
            w.pack1[at, cols] = coarse
            w.pack2[at, cols] = (product - coarse.astype(F32)).astype(BF16)
        score = dot(w.pack1[...], r.heads[...]) + dot(w.pack2[...], r.heads[...])
        for cg in range(CG):
            r.score[b, cg] = score[:, cg * LANES : (cg + 1) * LANES].astype(BF16)
        half = filter_part(b, 2)
        for cg, at, cols, near_rows in tiles(sz, first):
            h = half[at, cols]
            value = r.kv[2 * CG + cg, near_rows, :] * (h + h * jnp.tanh(h))
            for c in range(3):
                r.vagg[c * CG + cg] += r.vec[c * CG + cg, near_rows, :] * value
        half = filter_part(b, 3)
        for cg, at, cols, near_rows in tiles(sz, first):
            h = half[at, cols]
            value = r.kv[3 * CG + cg, near_rows, :] * (h + h * jnp.tanh(h))
            r.third[b, at, cols] = value.astype(BF16)
        half = filter_part(b, 1)
        for cg, at, cols, near_rows in tiles(sz, first):
            h = half[at, cols]
            s = score[at, cols]
            attention = (s + s * jnp.tanh(s)) * r.cut_wide[b, at, :]
            r.sagg[cg] += attention * (r.kv[CG + cg, near_rows, :] * (h + h * jnp.tanh(h)))

    def pair(i, carry):
        for which in range(2):
            block(2 * i + which, buffers(r, sz, which))
        return carry

    lax.fori_loop(0, sz.blocks // 2, pair, 0, unroll=2)
    third = sum(dot(r.units[b], r.third[b]) for b in range(sz.blocks))
    scalar_low = jnp.concatenate([r.sagg[cg] for cg in range(CG)], axis=1).astype(BF16)
    r.left[E + 3 * A : E + 4 * A, :] = scalar_low
    out_proj = dot(scalar_low, r.s_wout[...])
    vec_dot = vector_dot(r, sz)
    r.out_proj[...] = out_proj
    r.vec_dot[...] = vec_dot
    vector_agg = [
        jnp.concatenate([r.vagg[c * CG + cg] for cg in range(CG)], axis=1)
        + third[c * A : (c + 1) * A, :]
        for c in range(3)
    ]
    write_layer_output(r, sz, own, out_proj, vec_dot, vector_agg)


def edge_filters(r, sz, which):
    F = sz.width
    write_constants(r, sz)
    for m in which:
        w = SimpleNamespace(**vars(r))
        vars(w).update(vars(buffers(r, sz, m)))
        edge_geometry(w, sz, m, r.coords.at[m], r.slots.at[m])

        def block(b, carry, w=w):
            write_edge_tables(w, sz, b, BF16)
            for part in range(4):
                cols = slice(part * F, (part + 1) * F)
                h = dot(r.smear_t[b], r.wh[:, cols])
                if part:
                    h = h.astype(BF16)
                up = 1.0 + jnp.tanh(h)
                f = h * up
                for cg in range(sz.halves):
                    if part == 0 and hasattr(w, "key"):
                        w.key[b, cg] = f[:, cg * LANES : (cg + 1) * LANES]
                f, up = f.astype(BF16), up.astype(BF16)
                slope = up + f * (2.0 - up)
                for cg in range(sz.halves):
                    half = slice(cg * LANES, (cg + 1) * LANES)
                    w.silu[b, part * sz.halves + cg] = f[:, half]
                    w.slope[b, part * sz.halves + cg] = slope[:, half]
            return carry

        lax.fori_loop(0, sz.blocks, block, 0, unroll=4)


def both_ways(r, sz, m, fwd):
    A, H, E, F = sz.atoms, sz.halo, sz.rows, sz.width
    EB, CG, NB, W = sz.edges, sz.halves, sz.blocks, sz.window
    lane = iota((8, LANES), 1)
    row = iota((8, LANES), 0)
    halves = halves_of(sz)
    wqkv, wvec, wout = r.wqkv.at[0], r.wvec.at[0], r.wout.at[0]
    write_constants(r, sz)
    gain = r.norms[0:1, :]
    vp = r.vproj
    if fwd:
        own, left = r.own, r.left
        xhat, scale = node_part(r, sz, own, r.low, r.high, r.norms, wqkv)
        vp[...] = dot(left[E : E + 3 * A, :], wvec[...])
        for cg in range(CG):
            r.query_low[:, halves[cg]] = r.query[cg].astype(BF16)
    else:
        xhat, scale = r.xhat[...], r.scale[:, 0:1]

    if fwd:
        r.sagg[...] = jnp.zeros_like(r.sagg)
        r.vagg[...] = jnp.zeros_like(r.vagg)
        r.uagg[...] = jnp.zeros_like(r.uagg)

        def forward_block(b, carry):
            first = first_row(b)

            def filters(part, cg, at):
                return r.silu[b, part * CG + cg, at, :]

            def keys(cg, at, cols, near_rows):
                product = r.query[cg] * r.kv[cg, near_rows, :] * r.key[b, cg, at, :]
                return [product.astype(BF16)]

            score = dot(*stacked(sz, first, keys), r.heads[...])
            for cg in range(CG):
                r.score[b, cg] = score[:, halves[cg]].astype(BF16)

            def vectors(cg, at, cols, near_rows):
                value = r.kv[2 * CG + cg, near_rows, :].astype(BF16) * filters(2, cg, at)
                return [
                    r.vec[c * CG + cg, near_rows, :].astype(BF16) * value for c in range(3)
                ] + [r.kv[3 * CG + cg, near_rows, :].astype(BF16) * filters(3, cg, at)]

            moved = stacked(sz, first, vectors)
            for c in range(3):
                r.vagg[c] += dot(r.fold[...], moved[c])
            r.uagg[...] += dot(r.units[b], moved[3])

            def scalars(cg, at, cols, near_rows):
                s = r.score[b, cg, at, :]
                attention = s * (1.0 + jnp.tanh(s)) * r.cut_wide[b, at, :]
                return [
                    attention * (r.kv[CG + cg, near_rows, :].astype(BF16) * filters(1, cg, at))
                ]

            r.sagg[...] += dot(r.fold[...], *stacked(sz, first, scalars))
            return carry

        lax.fori_loop(0, NB, forward_block, 0, unroll=8)
        scalar_low = r.sagg[...].astype(BF16)
        left[E + 3 * A : E + 4 * A, :] = scalar_low
        out_proj = dot(scalar_low, wout[...])
        vec_dot = vector_dot(r, sz)
    else:
        out_proj, vec_dot = r.out_proj, r.vec_dot[...]
    if fwd:
        vector_agg = [r.vagg[c] + r.uagg[c * A : (c + 1) * A, :] for c in range(3)]
        write_layer_output(r, sz, own, out_proj, vec_dot, vector_agg)

    def incoming(index):
        if fwd:
            return r.cotangent[m, 0, index].astype(F32)
        gap = jnp.zeros((A - 2 * H, F), F32)
        edge = [r.inc_low[index, 0:H].astype(F32), gap, r.inc_high[index, 0:H].astype(F32)]
        value = r.inc[index].astype(F32) + jnp.concatenate(edge, axis=0)
        return value.astype(BF16).astype(F32)

    g_x = incoming(0)
    r.gx[0] = g_x
    g_first = jnp.zeros((A, F), F32)
    g_mid = g_x * out_proj[:, F : 2 * F]
    for c in range(3):
        g_vec = incoming(c + 1)
        r.gx[c + 1] = g_vec
        rows = slice(c * A, (c + 1) * A)
        r.gvlow[rows, :] = g_vec.astype(BF16)
        g_first = g_first + g_vec * vp[rows, 2 * F :]
        r.gvproj[rows, 0:F] = (g_mid * vp[rows, F : 2 * F]).astype(BF16)
        r.gvproj[rows, F : 2 * F] = (g_mid * vp[rows, 0:F]).astype(BF16)
        r.gvproj[rows, 2 * F :] = (g_vec * out_proj[:, 0:F]).astype(BF16)
    r.gout[:, 0:F] = g_first.astype(BF16)
    r.gout[:, F : 2 * F] = (g_x * vec_dot).astype(BF16)
    r.gout[:, 2 * F :] = g_x.astype(BF16)
    r.gs[...] = dot(r.gout[...], wout[...], 1, 1).astype(BF16)
    for total in (r.gnear, r.gq, r.gfilt):
        total[...] = jnp.zeros_like(total)

    scores = r.score if fwd else r.score_here
    if not fwd:
        scores[...] = r.score[...]

    def backward_block(b, carry):
        first = first_row(b)
        base = pl.multiple_of(first // SUBLANES * SUBLANES, SUBLANES)
        lanes = iota((W, EB), 1)
        place = jnp.where(
            lanes % A + lanes // A + (first - base) == iota((W, EB), 0), 1.0, 0.0
        ).astype(BF16)

        def collect(index, terms):
            r.gnear[index, pl.ds(base, W), :] += dot(place, terms)

        def filters(part, cg, at):
            return r.silu[b, part * CG + cg, at, :], r.slope[b, part * CG + cg, at, :]

        def weights(cg, at, cols, near_rows):
            value = r.kv[CG + cg, near_rows, :].astype(BF16)
            return [r.gs[:, cols] * (value * filters(1, cg, at)[0])]

        g_att = dot(*stacked(sz, first, weights), r.heads[...])

        def vectors(cg, at, cols, near_rows):
            f, slope = filters(2, cg, at)
            value = r.kv[2 * CG + cg, near_rows, :].astype(BF16)
            message = value * f
            moved = []
            for c in range(3):
                g_vec = r.gvlow[c * A : (c + 1) * A, cols]
                term = g_vec * r.vec[c * CG + cg, near_rows, :].astype(BF16)
                g_edge = term if c == 0 else g_edge + term
                moved.append(g_vec * message)
            return moved + [g_edge * f, g_edge * (value * slope)]

        *moved, g_value, g_pre = stacked(sz, first, vectors)
        for c in range(3):
            collect(4 + c, moved[c])
        collect(2, g_value)
        pre = [None, None, g_pre, None]
        g_third = dot(r.units[b], r.gvlow[...], 0, 0)

        def units(cg, at, cols, near_rows):
            f, slope = filters(3, cg, at)
            value = r.kv[3 * CG + cg, near_rows, :].astype(BF16)
            g_edge = g_third[at, cols].astype(BF16)
            return value * f, g_edge * f, g_edge * (value * slope)

        message, g_value, pre[3] = stacked(sz, first, units)
        collect(3, g_value)
        g_unit = dot(r.gvlow[...], message, 1, 1)
        for c in range(3):
            r.gunit[c, pl.ds(b, 1), :] = jnp.sum(
                g_unit[c * A : (c + 1) * A, :] * r.diag[...], axis=0, keepdims=True
            )

        def attention(cg, at, cols, near_rows):
            s = scores[b, cg, at, :]
            t = jnp.tanh(s)
            up = 1.0 + t
            act = s * up
            wide = r.cut_wide[b, at, :]
            ga = g_att[at, cols].astype(BF16)
            g_score = ga * wide * (up + act * (1.0 - t))
            g_edge = r.gs[:, cols] * (act * wide)
            f, slope = filters(0, cg, at)
            key = r.kv[cg, near_rows, :].astype(BF16)
            query = r.query_low[:, cols]
            middle = g_score * f
            made = [ga * act, middle * key, middle * query, (g_score * slope) * (key * query)]
            f, slope = filters(1, cg, at)
            value = r.kv[CG + cg, near_rows, :].astype(BF16)
            return made + [g_edge * f, g_edge * (value * slope)]

        g_act, g_query, g_key, pre[0], g_value, pre[1] = stacked(sz, first, attention)
        collect(1, g_value)
        collect(0, g_key)
        r.gq[...] += dot(r.fold[...], g_query)
        g_cut = dot(jnp.ones((16, F), BF16), g_act, 1, 1)[0:1, :] * (2.0 * HEADS / F)
        g_smear = jnp.zeros((sz.basis, EB), F32)
        for part in range(4):
            cols = slice(part * F, (part + 1) * F)
            g_smear = g_smear + dot(r.wh[:, cols], pre[part], 1, 1)
            r.gfilt[:, cols] += dot(r.smear[b], pre[part])
        delta, bell = bell_of(r, sz, b)
        through = g_smear * bell
        r.gcut[pl.ds(b, 1), :] = g_cut + jnp.sum(through, axis=0, keepdims=True)
        r.gshrink[pl.ds(b, 1), :] = r.geo[CUT, pl.ds(b, 1), :] * jnp.sum(
            through * delta, axis=0, keepdims=True
        ) * (-2.0 * sharpness_of(sz.basis))
        return carry

    lax.fori_loop(0, NB, backward_block, 0)

    distance = r.geo[DISTANCE]
    g_dist = r.gcut[...] * r.geo[LIVE] * jnp.where(
        distance < CUTOFF,
        (-0.5 * math.pi / CUTOFF) * jnp.sin(math.pi * distance / CUTOFF),
        0.0,
    ) - r.gshrink[...] * r.geo[SHRINK]
    inverse = 1.0 / distance
    g_unit = [r.gunit[c] for c in range(3)]
    sep = [r.geo[c] for c in range(3)]
    along = g_unit[0] * sep[0] + g_unit[1] * sep[1] + g_unit[2] * sep[2]
    radial = (g_dist - along * inverse * inverse) * inverse
    r.gplaces[...] = jnp.zeros_like(r.gplaces)
    for c in range(3):
        g_sep = g_unit[c] * inverse + radial * sep[c]
        first, other = g_sep[:, :LANES], g_sep[:, LANES:]
        z = (
            jnp.where(lane < A, first, 0.0)
            + pltpu.roll(jnp.where(lane < A, 0.0, first), A + 1, 1)
            + pltpu.roll(jnp.where(lane < A, other, 0.0), 2, 1)
            + pltpu.roll(jnp.where(lane < A, 0.0, other), A + 3, 1)
        )
        for bit in range(3):
            z = jnp.where((row >> bit) & 1 == 1, pltpu.roll(z, GROUP * 2**bit, 1), z)
        z = jnp.where(row >= 4, pltpu.roll(z, 1, 1), z)
        total = jnp.sum(g_sep, axis=0, keepdims=True)
        mine = total[:, 0:A] + total[:, A : 2 * A] + total[:, 2 * A : 3 * A] + total[:, 3 * A :]
        mine = jnp.concatenate(
            [jnp.zeros((1, H), F32), mine, jnp.zeros((1, LANES - H - A), F32)], axis=1
        )
        r.gplaces[c : c + 1, :] = jnp.sum(z, axis=0, keepdims=True) - mine

    gproj = r.gproj
    gproj[:, 0:F] = jnp.zeros((E, F), BF16)
    gproj[H : H + A, 0:F] = r.gq[...].astype(BF16)
    for part in range(4):
        gproj[:, (part + 1) * F : (part + 2) * F] = r.gnear[part].astype(BF16)
    g_normed = dot(gproj[...], wqkv[...], 1, 1)
    u = gain * g_normed
    g_scalars = scale * (
        u
        - jnp.mean(u, axis=-1, keepdims=True)
        - xhat * jnp.mean(u * xhat, axis=-1, keepdims=True)
    )
    r.gnorm[...] = jnp.zeros_like(r.gnorm)
    r.gnorm[0:1, :] = jnp.sum(g_normed * xhat, axis=0, keepdims=True)
    r.gnorm[1:2, :] = jnp.sum(g_normed, axis=0, keepdims=True)
    vec_back = dot(r.gvproj[...], wvec[...], 1, 1)
    for index in range(4):
        if index == 0:
            whole = g_scalars
            middle = whole[H : H + A] + r.gx[0]
        else:
            c = index - 1
            whole = r.gnear[4 + c]
            middle = whole[H : H + A] + r.gx[index] + vec_back[c * A : (c + 1) * A, :]
        r.back[index] = middle
        r.back_low[index] = middle.astype(BF16)
        r.rim_low[index] = whole[0:H].astype(BF16)
        r.rim_high[index] = whole[H + A :].astype(BF16)


FACTORS = ("left", "gproj", "gvproj", "gout", "gfilt", "gnorm")
HANDED = (
    "query_low", "kv", "vec", "vproj", "xhat", "scale", "out_proj", "vec_dot", "score"
)
BORDERS = ("rim_low", "rim_high", "gplaces")


def call(body, arrays, outs, scratch, role=None, grant_mb=16, place=VMEM):
    arrays, outs = vars(arrays), vars(outs)
    names = list(arrays) + list(outs) + list(scratch)

    def kernel(*args):
        refs = SimpleNamespace(**dict(zip(names, args, strict=True)))
        if role is None:
            body(refs)
        else:
            pl.when(lax.axis_index("section") == role)(lambda: body(refs))

    results = pl.pallas_call(
        kernel,
        out_shape=list(outs.values()),
        in_specs=[spec for _, spec in arrays.values()],
        out_specs=[place for _ in outs],
        scratch_shapes=[
            pltpu.VMEM(*s) if isinstance(s, tuple) else s for s in scratch.values()
        ],
        compiler_params=pltpu.CompilerParams(vmem_limit_bytes=int(grant_mb * 2**20)),
    )(*[array for array, _ in arrays.values()])
    return SimpleNamespace(**dict(zip(outs, results, strict=True)))


def first_call(sz, m, fetch, sent, arrays):
    A, H, E, F = sz.atoms, sz.halo, sz.rows, sz.width
    EB, CG, NB = sz.edges, sz.halves, sz.blocks
    shape = jax.ShapeDtypeStruct
    results = dict(
        fresh=((4, A, F), BF16),
        head=((4, sent, F), BF16),
        tail=((4, sent, F), BF16),
        left=((sz.factors, F), BF16),
        query_low=((A, F), BF16),
        kv=((4 * CG, E, LANES), F32),
        vec=((3 * CG, E, LANES), F32),
        vproj=((3 * A, 3 * F), F32),
        xhat=((E, F), F32),
        scale=((E, LANES), F32),
        out_proj=((A, 3 * F), F32),
        vec_dot=((A, F), F32),
        score=((NB, CG, EB, LANES), BF16),
    )
    fetched = dict(
        s_own=((4, A, F), BF16),
        s_slots=((3 * sz.slots + 8, LANES), F32),
        s_norms=((16, F), F32),
        s_wqkv=((F, 5 * F), BF16),
        s_wvec=((F, 3 * F), BF16),
        s_wh=((sz.basis, 4 * F), BF16),
        s_wout=((F, 3 * F), BF16),
        sems=pltpu.SemaphoreType.DMA((10,)),
    )
    outs = SimpleNamespace(**{k: shape(*v) for k, v in results.items()})
    scratch = dict(
        query=((CG, A, LANES), F32),
        heads=((F, F), BF16),
        diag=((A, EB), F32),
        geo=((10, 8, EB), F32),
        centres=((sz.basis, EB), F32),
        smear_t=((NB, EB, sz.basis), BF16),
        cut_wide=((NB, EB, LANES), F32),
        units=((NB, 3 * A, EB), BF16),
        pack10=((EB, F), BF16),
        pack20=((EB, F), BF16),
        pack11=((EB, F), BF16),
        pack21=((EB, F), BF16),
        sagg=((CG, A, LANES), F32),
        vagg=((3 * CG, A, LANES), F32),
        third=((NB, EB, F), BF16),
    )
    if fetch:
        scratch.update(fetched)
    return call(
        lambda r: first_forward(r, sz, m, fetch), arrays, outs, scratch, FIRST, grant_mb=20
    )


def filter_call(sz, role, which, arrays):
    A, F = sz.atoms, sz.width
    EB, CG, NB = sz.edges, sz.halves, sz.blocks
    shape = jax.ShapeDtypeStruct
    outs = dict(
        geo=shape((10, 8, EB), F32),
        smear=shape((NB, sz.basis, EB), BF16),
        cut_wide=shape((NB, EB, LANES), BF16),
        units=shape((NB, 3 * A, EB), BF16),
        silu=shape((NB, 4 * CG, EB, LANES), BF16),
        slope=shape((NB, 4 * CG, EB, LANES), BF16),
    )
    if role == SECOND:
        outs.update(key=shape((NB, CG, EB, LANES), F32))
    scratch = dict(
        diag=((A, EB), F32),
        centres=((sz.basis, EB), F32),
        smear_t=((NB, EB, sz.basis), BF16),
    )
    made = call(
        lambda r: edge_filters(r, sz, which),
        arrays,
        SimpleNamespace(**{f"{k}{m}": v for m in which for k, v in outs.items()}),
        scratch,
        role,
        grant_mb=6,
    )
    return {m: SimpleNamespace(**{k: getattr(made, f"{k}{m}") for k in outs}) for m in which}


def both_call(sz, m, fwd, arrays, border_sets=()):
    A, H, E, F = sz.atoms, sz.halo, sz.rows, sz.width
    EB, CG, NB = sz.edges, sz.halves, sz.blocks
    shape = jax.ShapeDtypeStruct
    outs = SimpleNamespace(
        back=shape((4, A, F), F32),
        back_low=shape((5 if fwd and m else 4, A, F), BF16),
        rim_low=shape((4, H, F), BF16),
        rim_high=shape((4, H, F), BF16),
        gplaces=shape((8, LANES), F32),
        gproj=shape((E, 5 * F), BF16),
        gvproj=shape((3 * A, 3 * F), BF16),
        gout=shape((A, 3 * F), BF16),
        gfilt=shape((sz.basis, 4 * F), F32),
        gnorm=shape((8, F), F32),
    )
    scratch = dict(
        heads=((F, F), BF16),
        diag=((A, EB), F32),
        fold=((A, EB), BF16),
        centres=((sz.basis, EB), F32),
        gx=((4, A, F), F32),
        gvlow=((3 * A, F), BF16),
        gs=((A, F), BF16),
        gq=((A, F), F32),
        gnear=((7, E, F), F32),
        gunit=((3, 8, EB), F32),
        gcut=((8, EB), F32),
        gshrink=((8, EB), F32),
    )
    if not fwd:
        scratch.update(score_here=((NB, CG, EB, LANES), BF16))
    if fwd:
        outs.fresh = shape((4, A, F), BF16)
        outs.left = shape((sz.factors, F), BF16)
        scratch.update(
            query=((CG, A, LANES), F32),
            query_low=((A, F), BF16),
            kv=((4 * CG, E, LANES), F32),
            vec=((3 * CG, E, LANES), F32),
            vproj=((3 * A, 3 * F), F32),
            score=((NB, CG, EB, LANES), BF16), sagg=((A, F), F32), vagg=((3, A, F), F32), uagg=((3 * A, F), F32)
        )
    if fwd and m:
        for i, made in enumerate(border_sets):
            setattr(arrays, f"gplaces_{i}", (made.gplaces, VMEM))

        def layer(r):
            both_ways(r, sz, m, fwd)
            for i in range(m + 1):
                places = r.gplaces if i == m else getattr(r, f"gplaces_{i}")
                rows = [places[c : c + 1, :] for c in range(3)]
                r.back_low[4, 16 * i : 16 * i + 16, :] = packed_places(rows, F)

        return call(layer, arrays, outs, scratch, SECOND)
    if not border_sets:
        role = SECOND if fwd else FIRST
        return call(lambda r: both_ways(r, sz, m, fwd), arrays, outs, scratch, role)
    count = m + 1
    outs.up, outs.down = shape((count, 4, H, F), BF16), shape((count, 4, H, F), BF16)
    outs.moved = shape((count, 8, LANES), F32)
    outs.total = shape((count, 8, LANES), F32)
    for role, sets in enumerate(border_sets):
        for i, made in enumerate(sets):
            for name in BORDERS:
                setattr(arrays, f"{name}_{role}_{i}", (getattr(made, name), VMEM))

    def hand_on(r, role):
        for i in range(count):
            low, high, places = (
                getattr(r, f"{name}_{role}_{i}") if i < len(border_sets[role]) else getattr(r, name)
                for name in BORDERS
            )
            r.up[i] = high[...]
            r.down[i] = low[...]
            r.moved[i] = places[...]
            r.total[i] = places[...]
            if role == FIRST:
                block = r.inc[4, 16 * i : 16 * i + 16, :]
                for c in range(3):
                    r.total[i, c : c + 1, :] += unpacked_places(block, c, 0, LANES)

    def body(r):
        @pl.when(lax.axis_index("section") == FIRST)
        def _():
            both_ways(r, sz, m, fwd)
            hand_on(r, FIRST)

        pl.when(lax.axis_index("section") == SECOND)(lambda: hand_on(r, SECOND))

    return call(body, arrays, outs, scratch)


def border_call(sz, features, coords):
    A, H, F = sz.atoms, sz.halo, sz.width
    count = features.shape[0]

    def body(r):
        moves = [(r.coords, r.s_coords)]
        for m in range(count):
            moves += [
                (r.features.at[m, 0, :, A - H : A, :], r.up.at[4 * m : 4 * m + 4]),
                (r.features.at[m, 0, :, 0:H, :], r.down.at[4 * m : 4 * m + 4]),
            ]
        copies = [
            pltpu.make_async_copy(source, target, r.sems.at[i])
            for i, (source, target) in enumerate(moves)
        ]
        for copy in copies:
            copy.start()
        copies[0].wait()
        for target, ends in ((r.up, slice(A - H, A)), (r.down, slice(0, H))):
            rows = []
            for m in range(count):
                parts = [r.s_coords[m, c][:, ends] for c in range(3)]
                rows.append(jnp.concatenate(parts, axis=1))
            target[4 * count] = packed_places(rows, F)
        for copy in copies[1:]:
            copy.wait()

    shape = jax.ShapeDtypeStruct((4 * count + 1, H, F), BF16)
    return call(
        body,
        SimpleNamespace(features=(features, HBM), coords=(coords, HBM)),
        SimpleNamespace(up=shape, down=shape),
        dict(s_coords=(coords.shape, F32), sems=pltpu.SemaphoreType.DMA((2 * count + 1,))),
        grant_mb=54,
    )


class Rooms:
    def __init__(self, sz):
        F = sz.width
        ends = [0]
        for rows in (F, F, F, 4 * sz.atoms, sz.basis):
            ends.append(ends[-1] + rows)
        self.wqkv, self.wvec, self.wout, self.own, self.wh = [
            slice(*pair) for pair in zip(ends, ends[1:])
        ]
        table = 3 * sz.slots + 8
        self.slots, self.norms = slice(0, table), slice(table, table + 8)
        self.coords = slice(table + 8, table + 16)
        self.low_shape, self.wide_shape = (20480, 5 * F), (51200, F)


def stage_call(sz, features, coords, neighbours, shifts, counts, gain, bias, filter_weight, weights):
    A, F, K = sz.atoms, sz.width, sz.slots
    count = features.shape[0]
    rooms = Rooms(sz)

    def body(r):
        moves = [(r.coords, r.s_coords), (r.counts, r.s_counts)]
        moves += [(r.gain, r.s_gain), (r.bias, r.s_bias), (r.wfilt.at[0], r.s_wfilt)]
        for m in range(count):
            moves += [
                (r.nbr.at[m, 0], r.s_slots.at[m, 0:K]),
                (r.shifts.at[m, 0, 0], r.s_slots.at[m, K : 2 * K]),
                (r.shifts.at[m, 0, 1], r.s_slots.at[m, 2 * K : 3 * K]),
            ]
        near = len(moves)
        moves += [(r.features.at[0, 0], r.s_own), (r.wqkv.at[0], r.s_wqkv)]
        moves += [(r.wvec.at[0], r.s_wvec), (r.wout.at[0], r.s_wout)]
        copies = [
            pltpu.make_async_copy(source, target, r.sems.at[i])
            for i, (source, target) in enumerate(moves)
        ]
        for copy in copies:
            copy.start()
        for copy in copies[:near]:
            copy.wait()
        r.s_wh[...] = (r.s_wfilt[...].astype(F32) * 0.5).astype(BF16)
        for m in range(count):
            r.s_table[m, 0 : 3 * K, 0:A] = r.s_slots[m].astype(F32)
            r.s_table[m, 3 * K :, 0:A] = jnp.broadcast_to(r.s_counts[m].astype(F32), (8, A))
        r.s_norms[...] = jnp.zeros_like(r.s_norms)
        r.s_norms[0:1, :] = r.s_gain[...].astype(F32)
        r.s_norms[1:2, :] = r.s_bias[...].astype(F32)
        for c in range(3):
            r.s_norms[8 + c : 9 + c, 0:A] = r.s_coords[0, c]
        for copy in copies[near:]:
            copy.wait()
        moves = [
            (r.s_table, r.slots),
            (r.s_norms.at[0:8], r.norms),
            (r.s_wh, r.wh),
            (r.s_table.at[0], r.wide.at[rooms.slots, 0:LANES]),
            (r.s_norms, r.wide.at[rooms.norms.start : rooms.coords.stop]),
            (r.s_wqkv, r.low.at[rooms.wqkv]),
            (r.s_wvec, r.low.at[rooms.wvec, 0 : 3 * F]),
            (r.s_wout, r.low.at[rooms.wout, 0 : 3 * F]),
            (r.s_wh, r.low.at[rooms.wh, 0 : 4 * F]),
        ]
        for index in range(4):
            start = rooms.own.start + index * A
            moves.append((r.s_own.at[index], r.low.at[start : start + A, 0:F]))
        later = [
            pltpu.make_async_copy(source, target, r.sems.at[len(copies) + i])
            for i, (source, target) in enumerate(moves)
        ]
        for copy in later:
            copy.start()
        for copy in later:
            copy.wait()

    shape = jax.ShapeDtypeStruct
    wqkv, wvec, wout = weights
    return call(
        body,
        SimpleNamespace(
            features=(features, HBM),
            coords=(coords, HBM),
            nbr=(neighbours, HBM),
            shifts=(shifts, HBM),
            counts=(counts, HBM),
            gain=(gain, HBM),
            bias=(bias, HBM),
            wfilt=(filter_weight, HBM),
            wqkv=(wqkv, HBM),
            wvec=(wvec, HBM),
            wout=(wout, HBM),
        ),
        SimpleNamespace(
            slots=shape((count, 3 * K + 8, LANES), F32),
            norms=shape((8, F), F32),
            wh=shape((sz.basis, 4 * F), BF16),
            low=shape(rooms.low_shape, BF16),
            wide=shape(rooms.wide_shape, F32),
        ),
        dict(
            s_coords=(coords.shape, F32),
            s_counts=(counts.shape, jnp.int32),
            s_gain=(gain.shape, BF16),
            s_bias=(bias.shape, BF16),
            s_wfilt=(filter_weight.shape[1:], BF16),
            s_slots=((count, 3 * K, A), jnp.int32),
            s_own=((4, A, F), BF16),
            s_wqkv=(wqkv.shape[1:], BF16),
            s_wvec=(wvec.shape[1:], BF16),
            s_wout=(wout.shape[1:], BF16),
            s_wh=(filter_weight.shape[1:], BF16),
            s_table=((count, 3 * K + 8, LANES), F32),
            s_norms=((16, F), F32),
            sems=pltpu.SemaphoreType.DMA((3 * count + 22,)),
        ),
        grant_mb=54,
        place=HBM,
    )


def gradient_call(sz, sets):
    A, E, F = sz.atoms, sz.rows, sz.width
    count = len(sets[0])
    w1, w2, w3 = sz.widths
    w4, w5 = 4 * F // sz.space, F // sz.space
    half = F // 2
    arrays = SimpleNamespace()
    for role in (FIRST, SECOND):
        for m in range(count):
            for name in FACTORS:
                setattr(arrays, f"{name}_{role}_{m}", (getattr(sets[role][m], name), VMEM))

    def body(r, role):
        def get(name, m):
            return getattr(r, f"{name}_{role}_{m}")

        every = range(count)
        e, a = E, A
        r.qkv[...] = sum(dot(get("gproj", m)[...], get("left", m)[0:e, :], 0, 0) for m in every)
        r.vector[...] = sum(
            dot(get("gvproj", m)[...], get("left", m)[e : e + 3 * a, :], 0, 0) for m in every
        )
        r.out[...] = sum(
            dot(get("gout", m)[...], get("left", m)[e + 3 * a : e + 4 * a, :], 0, 0) for m in every
        )
        filt = sum(get("gfilt", m)[...] for m in every) * 0.5
        norm = sum(get("gnorm", m)[...] for m in every)
        core = lax.axis_index("dp")
        for k in range(sz.space):
            spare = [filt[:, k * w4 : (k + 1) * w4]]
            if half > w4:
                spare.append(jnp.zeros((sz.basis, half - w4), F32))
            left = jnp.concatenate(spare, axis=1)
            rows = [norm[:, k * w5 : (k + 1) * w5], jnp.zeros((8, half - w5), F32)]
            right = jnp.concatenate(rows, axis=1)
            right = jnp.concatenate(
                [right, jnp.zeros((sz.packed - sz.spare - 8, half), F32)], axis=0
            )
            if sz.packed - sz.spare > sz.basis:
                gap = jnp.zeros((sz.packed - sz.spare - sz.basis, half), F32)
                left = jnp.concatenate([left, gap], axis=0)
            parts = [
                r.qkv[k * w1 : (k + 1) * w1, :],
                r.vector[k * w2 : (k + 1) * w2, :],
                r.out[k * w3 : (k + 1) * w3, :],
            ]
            first = jnp.concatenate([part[:, :half] for part in parts] + [left], axis=0)
            second = jnp.concatenate([part[:, half:] for part in parts] + [right], axis=0)
            r.send[k] = jnp.where(core == 0, second, first).astype(BF16)
            r.stay[k] = jnp.where(core == 0, first, second)

    def both(r):
        for role in (FIRST, SECOND):
            pl.when(lax.axis_index("section") == role)(lambda role=role: body(r, role))

    shape = jax.ShapeDtypeStruct
    return call(
        both,
        arrays,
        SimpleNamespace(
            send=shape((sz.space, sz.packed, half), BF16),
            stay=shape((sz.space, sz.packed, half), F32),
        ),
        dict(
            qkv=((5 * F, F), F32),
            vector=((3 * F, F), F32),
            out=((3 * F, F), F32),
        ),
    )


def border_rows(sz, index):
    start = sz.packed + index * 2 * sz.halo
    return [slice(start + i * sz.halo, start + (i + 1) * sz.halo) for i in range(2)]


def border_block(sz, ref, index):
    return jnp.concatenate([ref[rows, :] for rows in border_rows(sz, index)], axis=1)


def piece_call(sz, stay, recv, up, down, total, late):
    A, H, E, F = sz.atoms, sz.halo, sz.rows, sz.width
    count = up.shape[0]
    half = F // 2

    def body(r):
        slab, space = lax.axis_index("space"), sz.space
        for hop in range(space):
            k = lax.rem(slab + hop, space)
            share = r.stay[k] + r.recv[k].astype(F32)
            target = getattr(r, f"hop{hop}")
            target[0 : sz.packed, :] = share.astype(target.dtype)
        places = [r.total[m] + r.late[m] for m in range(count)]
        ends = (
            (r.hop1, r.up, slice(H + A, E)),
            (getattr(r, f"hop{space - 1}"), r.down, slice(0, H)),
        )
        for target, border, lanes in ends:
            rows = []
            for m in range(count):
                parts = [places[m][c : c + 1, lanes] for c in range(3)]
                rows.append(jnp.concatenate(parts, axis=1))
            blocks = [border[m, index] for m in range(count) for index in range(4)]
            for index, block in enumerate(blocks + [packed_places(rows, F)]):
                first, second = border_rows(sz, index)
                target[first, :] = block[:, :half]
                target[second, :] = block[:, half:]
        for m in range(count):
            for c in range(3):
                r.mine[m, c] = places[m][c : c + 1, H : H + A]

    shape = jax.ShapeDtypeStruct
    outs = {
        f"hop{hop}": shape(
            (sz.packed + ((8 * count + 2) * H if hop in (1, sz.space - 1) else 0), half),
            BF16 if hop else F32,
        )
        for hop in range(sz.space)
    }
    outs.update(mine=shape((count, 3, 1, A), F32))
    made = call(
        body,
        SimpleNamespace(
            stay=(stay, VMEM),
            recv=(recv, VMEM),
            up=(up, VMEM),
            down=(down, VMEM),
            total=(total, VMEM),
            late=(late, VMEM),
        ),
        SimpleNamespace(**outs),
        {},
    )
    return [getattr(made, f"hop{hop}") for hop in range(sz.space)], made.mine


def result_call(sz, fresh, back, from_low, from_high, mine):
    A, H, F = sz.atoms, sz.halo, sz.width
    count = len(back[0])
    arrays = SimpleNamespace(
        low=(from_low, VMEM), high=(from_high, VMEM), mine=(mine, VMEM)
    )
    for role in (FIRST, SECOND):
        for m in range(count):
            setattr(arrays, f"fresh_{role}_{m}", (fresh[role][m], VMEM))
            setattr(arrays, f"back_{role}_{m}", (back[role][m], VMEM))

    def body(r, role):
        for m in range(count):
            r.outputs[0, m, 0] = getattr(r, f"fresh_{role}_{m}")[...]
            whole = getattr(r, f"back_{role}_{m}")
            for index in range(4):
                low = border_block(sz, r.low, 4 * m + index).astype(F32)
                high = border_block(sz, r.high, 4 * m + index).astype(F32)
                r.grads[0, m, 0, index, 0:H, :] = whole[index, 0:H, :] + low
                r.grads[0, m, 0, index, H : A - H, :] = whole[index, H : A - H, :]
                r.grads[0, m, 0, index, A - H :, :] = whole[index, A - H :, :] + high
            for c in range(3):
                edge = [
                    unpacked_places(border_block(sz, r.low, 4 * count), m, c, H),
                    jnp.zeros((1, A - 2 * H), F32),
                    unpacked_places(border_block(sz, r.high, 4 * count), m, c, H),
                ]
                r.places[m, c] = r.mine[m, c] + jnp.concatenate(edge, axis=1)

    def both(r):
        for role in (FIRST, SECOND):
            pl.when(lax.axis_index("section") == role)(lambda role=role: body(r, role))

    shape = jax.ShapeDtypeStruct
    return call(
        both,
        arrays,
        SimpleNamespace(
            outputs=shape((1, count, 1, 4, A, F), BF16),
            grads=shape((1, count, 1, 4, A, F), F32),
            places=shape((count, 3, 1, A), F32),
        ),
        {},
    )


def share_call(sz, total, other):
    F = sz.width
    w1, w2, w3 = sz.widths
    w4, w5 = 4 * F // sz.space, F // sz.space
    half = F // 2

    def body(r, first, second):
        for lanes, part in ((slice(0, half), first), (slice(half, F), second)):
            r.qkv[0, :, lanes] = part[0:w1, :]
            r.vector[0, :, lanes] = part[w1 : w1 + w2, :]
            r.out[0, :, lanes] = part[w1 + w2 : sz.spare, :]
        r.filt[0] = first[sz.spare : sz.spare + sz.basis, 0:w4]
        r.gain[...] = second[sz.spare : sz.spare + 1, 0:w5]
        r.bias[...] = second[sz.spare + 1 : sz.spare + 2, 0:w5]

    def both(r):
        pl.when(lax.axis_index("dp") == 0)(lambda: body(r, r.total, r.other))
        pl.when(lax.axis_index("dp") == 1)(lambda: body(r, r.other, r.total))

    shape = jax.ShapeDtypeStruct
    return call(
        both,
        SimpleNamespace(total=(total, VMEM), other=(other, VMEM)),
        SimpleNamespace(
            gain=shape((1, w5), F32),
            bias=shape((1, w5), F32),
            qkv=shape((1, w1, F), F32),
            vector=shape((1, w2, F), F32),
            filt=shape((1, sz.basis, w4), F32),
            out=shape((1, w3, F), F32),
        ),
        {},
    )


def on_device(
    features,
    coords,
    neighbours,
    counts,
    shifts,
    norm_gain,
    norm_bias,
    qkv_weight,
    vector_weight,
    filter_weight,
    out_weight,
    cotangent,
):
    micro_count = features.shape[0]
    space = lax.axis_size("space")
    sz = Sizes(features.shape[3], features.shape[4], filter_weight.shape[1], neighbours.shape[2], space)
    up = [(i, (i + 1) % space) for i in range(space)]
    down = [((i + 1) % space, i) for i in range(space)]

    places = jnp.transpose(coords, (0, 2, 1, 3))
    borders = border_call(sz, features, places)
    staged = stage_call(
        sz,
        features,
        places,
        neighbours,
        shifts,
        counts,
        norm_gain,
        norm_bias,
        filter_weight,
        (qkv_weight, vector_weight, out_weight),
    )
    slots, norms, half_filter = staged.slots, staged.norms, staged.wh
    pack_low = lax.ppermute(borders.up, "space", up)
    pack_high = lax.ppermute(borders.down, "space", down)
    both = ("section", "space")
    forth = [(k, space + k) for k in range(space)]
    forth_up = [(k, space + (k + 1) % space) for k in range(space)]
    forth_down = [((k + 1) % space, space + k) for k in range(space)]
    back = [(space + k, k) for k in range(space)]
    back_up = [(space + k, (k + 1) % space) for k in range(space)]
    back_down = [(space + (k + 1) % space, k) for k in range(space)]

    def geometry_inputs():
        return SimpleNamespace(
            pack_low=(pack_low, VMEM),
            pack_high=(pack_high, VMEM),
            coords=(places, VMEM),
            slots=(slots, VMEM),
            wh=(half_filter, VMEM),
        )

    firsts, sent, filters = [], [], {}
    for m in range(micro_count):
        if m == 0:
            arrays = SimpleNamespace(
                pack_low=(pack_low, VMEM),
                pack_high=(pack_high, VMEM),
                room=(staged.low, HBM),
                wide=(staged.wide, HBM),
            )
        else:
            arrays = geometry_inputs()
            arrays.features = (features, VMEM)
            arrays.norms = (norms, VMEM)
            arrays.wqkv, arrays.wvec, arrays.wout = (
                (qkv_weight, VMEM), (vector_weight, VMEM), (out_weight, VMEM)
            )
        first = first_call(sz, m, m == 0, sz.sent[m], arrays)
        firsts.append(first)
        if m == micro_count - 1:
            made = filters[SECOND] = filter_call(
                sz, SECOND, range(micro_count), geometry_inputs()
            )
            own, *rest = sent[0]
            first.head, made[0].geo, own = lax.optimization_barrier(
                (first.head, made[0].geo, own)
            )
            sent[0] = (own, *rest)
        sent.append((
            lax.ppermute(first.fresh, both, forth),
            lax.ppermute(first.tail, both, forth_up),
            lax.ppermute(first.head, both, forth_down),
        ))
    def both_inputs(m, role):
        made = filters[role][m]
        return SimpleNamespace(
            norms=(norms, VMEM),
            wqkv=(qkv_weight, VMEM),
            wvec=(vector_weight, VMEM),
            wh=(half_filter, VMEM),
            wout=(out_weight, VMEM),
            geo=(made.geo, VMEM),
            smear=(made.smear, VMEM),
            cut_wide=(made.cut_wide, VMEM),
            units=(made.units, VMEM),
            silu=(made.silu, VMEM),
            slope=(made.slope, VMEM),
        )

    seconds, returned = [], []
    for m in range(micro_count):
        if m == 1:
            other = filters[FIRST][0]
            other.geo, filters[SECOND][m].geo = lax.optimization_barrier(
                (other.geo, filters[SECOND][m].geo)
            )
        arrays = both_inputs(m, SECOND)
        arrays.key = (filters[SECOND][m].key, VMEM)
        own, low, high = sent[m]
        arrays.own, arrays.low, arrays.high = (own, VMEM), (low, VMEM), (high, VMEM)
        arrays.cotangent = (cotangent, VMEM)
        second = both_call(sz, m, True, arrays, seconds)
        seconds.append(second)
        if m == 0:
            later = geometry_inputs()
            held, second.gplaces = lax.optimization_barrier((slots, second.gplaces))
            later.slots = (held, VMEM)
            filters[FIRST] = filter_call(sz, FIRST, range(micro_count), later)
        back_low, rim_low, rim_high = second.back_low, second.rim_low, second.rim_high
        if m:
            returned[-1], back_low, rim_low, rim_high = lax.optimization_barrier(
                (returned[-1], back_low, rim_low, rim_high)
            )
        returned.append((
            lax.ppermute(back_low, both, back),
            lax.ppermute(rim_high, both, back_up),
            lax.ppermute(rim_low, both, back_down),
        ))
    thirds = []
    for m in range(micro_count):
        arrays = both_inputs(m, FIRST)
        for name in HANDED:
            setattr(arrays, name, (getattr(firsts[m], name), VMEM))
        inc, inc_low, inc_high = returned[m]
        arrays.inc, arrays.inc_low, arrays.inc_high = (inc, VMEM), (inc_low, VMEM), (inc_high, VMEM)
        sets = (thirds, seconds) if m == micro_count - 1 else ()
        third = both_call(sz, m, False, arrays, sets)
        third.left = firsts[m].left
        thirds.append(third)

    last = thirds[-1]
    late = lax.ppermute(last.moved, both, forth)
    shares = gradient_call(sz, (thirds, seconds))
    recv = lax.ppermute(shares.send, "dp", [(0, 1), (1, 0)])
    (total, *pieces), mine = piece_call(sz, shares.stay, recv, last.up, last.down, last.total, late
    )
    received = [
        lax.ppermute(piece, "space", [(i, (i + hop) % space) for i in range(space)])
        for hop, piece in enumerate(pieces, 1)
    ]
    for piece in received:
        total = total + piece[: sz.packed].astype(F32)
    results = result_call(
        sz,
        ([v.fresh for v in firsts], [v.fresh for v in seconds]),
        ([v.back for v in thirds], [v.back for v in seconds]),
        received[0],
        received[-1],
        mine,
    )
    other = lax.ppermute(total, "dp", [(0, 1), (1, 0)])
    share = share_call(sz, total, other)
    return (
        results.outputs,
        results.grads,
        share.gain,
        share.bias,
        jnp.transpose(share.qkv, (0, 2, 1)),
        jnp.transpose(share.vector, (0, 2, 1)),
        share.filt,
        jnp.transpose(share.out, (0, 2, 1)),
        jnp.transpose(results.places, (0, 2, 1, 3)),
    )


def solution(mesh):
    return jax.shard_map(
        on_device,
        mesh=mesh,
        in_specs=(
            P(None, "dp", None, "space", None),
            P(None, "dp", None, "space"),
            P(None, "dp", None, "space"),
            P(None, "dp", "space"),
            P(None, "dp", None, None, "space"),
            P("section", None),
            P("section", None),
            P("section", None, None),
            P("section", None, None),
            P("section", None, None),
            P("section", None, None),
            P(None, "dp", None, "space", None),
        ),
        out_specs=(
            P("section", None, "dp", None, "space", None),
            P("section", None, "dp", None, "space", None),
            P("section", "space"),
            P("section", "space"),
            P("section", None, "space"),
            P("section", None, "space"),
            P("section", None, "space"),
            P("section", None, "space"),
            P(None, "dp", None, "space"),
        ),
        check_vma=False,
    )
```

```python
import math
from types import SimpleNamespace

import jax
import jax.numpy as jnp
from jax import lax
from jax.experimental import pallas as pl
from jax.experimental.pallas import tpu as pltpu
from jax.sharding import PartitionSpec as P

HEADS = 8
CUTOFF = 5.0
LN_EPS = 1e-05
SOFTEN = 0.25
CROSS = 2.5
GROUP = 4
LANES = 128
SUBLANES = 8
FIRST, SECOND = 0, 1

F32 = jnp.float32
BF16 = jnp.bfloat16
VMEM = pl.BlockSpec(memory_space=pltpu.VMEM)
HBM = pl.BlockSpec(memory_space=pltpu.HBM)


def dot(left, right, left_dim=1, right_dim=0):
    return lax.dot_general(
        left, right, (((left_dim,), (right_dim,)), ((), ())), preferred_element_type=F32
    )


def iota(shape, dim):
    return lax.broadcasted_iota(jnp.int32, shape, dim)


def packed_places(rows, width):
    parts = []
    for row in rows:
        high = row.astype(BF16).astype(F32)
        rest = row - high
        middle = rest.astype(BF16).astype(F32)
        parts += [high, middle, rest - middle]
    gap = 16 - len(parts)
    whole = jnp.concatenate(parts + [jnp.zeros((gap, rows[0].shape[1]), F32)], axis=0)
    wide = [whole, jnp.zeros((16, width - whole.shape[1]), F32)]
    return jnp.concatenate(wide, axis=1).astype(BF16)


def unpacked_places(block, m, c, count):
    rows = block[:, c * count : (c + 1) * count].astype(F32)
    return rows[3 * m : 3 * m + 1] + rows[3 * m + 1 : 3 * m + 2] + rows[3 * m + 2 : 3 * m + 3]


class Sizes:
    def __init__(self, atoms, width, basis, slots, space):
        self.atoms, self.width, self.basis, self.slots, self.space = atoms, width, basis, slots, space
        self.halo = atoms // 4
        self.rows = atoms + 2 * self.halo
        self.blocks = slots // GROUP
        self.edges = GROUP * atoms
        self.halves = width // LANES
        self.window = atoms + SUBLANES
        self.sent = (self.halo, atoms)
        self.widths = (5 * width // space, 3 * width // space, 3 * width // space)
        self.spare = sum(self.widths)
        self.packed = -(-(self.spare + basis) // 16) * 16
        self.factors = -(-(self.rows + 4 * atoms) // LANES) * LANES


def halves_of(sz):
    return [slice(cg * LANES, (cg + 1) * LANES) for cg in range(sz.halves)]


def first_row(b):
    return GROUP * b + jnp.where(b >= 4, 1, 0)


def sharpness_of(basis):
    return (2.0 / basis * (1.0 - math.exp(-CUTOFF))) ** (-2)


def write_centres(ref, basis):
    low_end = math.exp(-CUTOFF)
    step = iota(ref.shape, 0).astype(F32) / (basis - 1)
    ref[...] = low_end * (1.0 - step) + step


def edge_geometry(r, sz, m, coords, slots):
    A, H, E, EB, K = sz.atoms, sz.halo, sz.rows, sz.edges, sz.slots
    lane = iota((8, LANES), 1)
    row = iota((8, LANES), 0)
    slab, last = lax.axis_index("space"), sz.space - 1
    last_block = r.pack_low.shape[0] - 1
    spot = iota((1, LANES), 1)
    length_x = sz.space * A * 4.0 / H
    places = []
    for c in range(3):
        places.append(
            jnp.concatenate(
                [
                    unpacked_places(r.pack_low[last_block], m, c, H),
                    coords[c],
                    unpacked_places(r.pack_high[last_block], m, c, H),
                    jnp.zeros((1, LANES - E), F32),
                ],
                axis=1,
            )
        )
    places.append(
        jnp.where((spot < H) & (slab == 0), -length_x, 0.0)
        + jnp.where((spot >= H + A) & (slab == last), length_x, 0.0)
    )
    near = []
    for c in range(4):
        y = jnp.broadcast_to(places[c], (8, LANES))
        for bit in range(3):
            y = jnp.where((row >> bit) & 1 == 1, pltpu.roll(y, LANES - GROUP * 2**bit, 1), y)
        y = jnp.where(row >= 4, pltpu.roll(y, LANES - 1, 1), y)
        first = jnp.where(lane < A, y, pltpu.roll(y, A - 1, 1))
        other = jnp.where(lane < A, pltpu.roll(y, LANES - 2, 1), pltpu.roll(y, A - 3, 1))
        near.append(jnp.concatenate([first, other], axis=1))
    wide_lane = iota((8, EB), 1)
    wide_row = iota((8, EB), 0)
    wanted = GROUP * wide_row + wide_lane // A + jnp.where(wide_row >= 4, 1, 0) + wide_lane % A
    table = slots[:, 0:A].astype(jnp.int32)
    alive = iota((K, A), 0) < table[3 * K : 3 * K + 1]
    code = jnp.where(alive, 16, 0) + (table[K : 2 * K] + 1) * 4 + (table[2 * K : 3 * K] + 1)
    code = jnp.concatenate([code] * GROUP, axis=1)
    named = jnp.concatenate([table[0:K]] * GROUP, axis=1)
    found = jnp.zeros((8, EB), jnp.int32)
    for n in range(K):
        found = found + jnp.where(named[n : n + 1, :] == wanted, code[n : n + 1, :], 0)
    live = (found >> 4).astype(F32)
    offsets = (
        near[3],
        (((found >> 2) & 3) - 1).astype(F32) * CROSS,
        ((found & 3) - 1).astype(F32) * CROSS,
    )
    sep = []
    for c in range(3):
        mine = coords[c]
        sep.append(near[c] - jnp.concatenate([mine] * GROUP, axis=1) + offsets[c])
    distance = jnp.sqrt(sep[0] * sep[0] + sep[1] * sep[1] + sep[2] * sep[2] + SOFTEN)
    inside = distance < CUTOFF
    cut = jnp.where(inside, 0.5 * (jnp.cos(math.pi * distance / CUTOFF) + 1.0), 0.0) * live
    for index, value in enumerate(
        sep + [distance, live, cut, jnp.exp(-distance)] + [part / distance for part in sep]
    ):
        r.geo[index] = value


DISTANCE, LIVE, CUT, SHRINK, UNIT = 3, 4, 5, 6, 7


def bell_of(r, sz, b):
    delta = r.geo[SHRINK, pl.ds(b, 1), :] - r.centres[...]
    return delta, jnp.exp(-sharpness_of(sz.basis) * delta * delta)


def write_edge_tables(r, sz, b, wide_kind):
    A, EB = sz.atoms, sz.edges
    cut = r.geo[CUT, pl.ds(b, 1), :]
    _, bell = bell_of(r, sz, b)
    smear = cut * bell
    if hasattr(r, "smear"):
        r.smear[b] = smear.astype(BF16)
    r.smear_t[b] = jnp.transpose(smear).astype(BF16)
    coarse = cut.astype(BF16).astype(F32)
    which = iota((16, EB), 0)
    pair = jnp.where(which == 0, coarse, jnp.where(which == 1, cut - coarse, 0.0)).astype(BF16)
    r.cut_wide[b] = dot(pair, jnp.ones((16, LANES), BF16), 0, 0).astype(wide_kind)
    for c in range(3):
        r.units[b, c * A : (c + 1) * A, :] = (
            r.diag[...] * r.geo[UNIT + c, pl.ds(b, 1), :]
        ).astype(BF16)


def write_constants(r, sz):
    A, EB, F = sz.atoms, sz.edges, sz.width
    if hasattr(r, "centres"):
        write_centres(r.centres, sz.basis)
    if hasattr(r, "diag"):
        r.diag[...] = jnp.where(iota((A, EB), 1) % A == iota((A, EB), 0), 1.0, 0.0)
    if hasattr(r, "fold"):
        r.fold[...] = jnp.where(iota((A, EB), 1) % A == iota((A, EB), 0), 1.0, 0.0).astype(BF16)
    if hasattr(r, "heads"):
        r.heads[...] = jnp.where(
            iota((F, F), 0) // (F // HEADS) == iota((F, F), 1) // (F // HEADS), 0.5, 0.0
        ).astype(BF16)


def node_part(r, sz, own, low, high, norms, wqkv):
    A, H, E, F, CG = sz.atoms, sz.halo, sz.rows, sz.width, sz.halves
    halves = halves_of(sz)
    scalars = jnp.concatenate([low[0, 0:H], own[0], high[0, 0:H]], axis=0).astype(F32)
    centred = scalars - jnp.mean(scalars, axis=-1, keepdims=True)
    spread = jnp.mean(centred * centred, axis=-1, keepdims=True)
    scale = lax.rsqrt(spread + LN_EPS)
    normed = (centred * scale * norms[0:1, :] + norms[1:2, :]).astype(BF16)
    left = r.left
    left[0:E, :] = normed
    left[E : E + 3 * A, :] = own[1:4].reshape(3 * A, F)
    left[E + 4 * A :, :] = jnp.zeros((sz.factors - E - 4 * A, F), BF16)
    for part in range(5):
        projected = dot(normed, wqkv[:, part * F : (part + 1) * F])
        for cg in range(CG):
            if part == 0:
                r.query[cg] = projected[H : H + A, halves[cg]]
            else:
                r.kv[(part - 1) * CG + cg] = projected[:, halves[cg]]
    for c in range(3):
        for cg in range(CG):
            r.vec[c * CG + cg, 0:H, :] = low[c + 1, 0:H, halves[cg]].astype(F32)
            r.vec[c * CG + cg, H : H + A, :] = own[c + 1][:, halves[cg]].astype(F32)
            r.vec[c * CG + cg, H + A : E, :] = high[c + 1, 0:H, halves[cg]].astype(F32)
    return centred * scale, scale


def buffers(r, sz, which):
    end = str(which)
    return SimpleNamespace(**{k[:-1]: v for k, v in vars(r).items() if k.endswith(end)})


def tiles(sz, first):
    A = sz.atoms
    for kk in range(GROUP):
        for cg in range(sz.halves):
            yield (
                cg,
                slice(kk * A, (kk + 1) * A),
                slice(cg * LANES, (cg + 1) * LANES),
                pl.ds(first + kk, A),
            )


def stacked(sz, first, tile):
    made = [tile(*where) for where in tiles(sz, first)]
    CG = sz.halves
    wholes = []
    for index in range(len(made[0])):
        lines = [
            jnp.concatenate([made[kk * CG + cg][index] for cg in range(CG)], axis=1)
            for kk in range(GROUP)
        ]
        wholes.append(jnp.concatenate(lines, axis=0))
    return wholes


def vector_dot(r, sz):
    A, F, vp = sz.atoms, sz.width, r.vproj
    return sum(
        vp[c * A : (c + 1) * A, 0:F] * vp[c * A : (c + 1) * A, F : 2 * F] for c in range(3)
    )


def write_layer_output(r, sz, own, out_proj, vec_dot, vector_agg):
    A, H, F, vp = sz.atoms, sz.halo, sz.width, r.vproj
    for index in range(4):
        if index == 0:
            fresh = vec_dot * out_proj[:, F : 2 * F] + out_proj[:, 2 * F :]
        else:
            rows = slice((index - 1) * A, index * A)
            fresh = vp[rows, 2 * F :] * out_proj[:, 0:F] + vector_agg[index - 1]
        fresh = (own[index].astype(F32) + fresh).astype(BF16)
        r.fresh[index] = fresh
        if hasattr(r, "head"):
            r.head[index, 0:H, :] = fresh[:H]
            r.tail[index, 0:H, :] = fresh[A - H :]


def first_forward(r, sz, m, fetch):
    A, H, E, F, EB = sz.atoms, sz.halo, sz.rows, sz.width, sz.edges
    CG = sz.halves
    r.s_low, r.s_high = r.pack_low.at[4 * m : 4 * m + 4], r.pack_high.at[4 * m : 4 * m + 4]
    copies = early = []
    if fetch:
        rooms = Rooms(sz)
        early = [
            (r.wide.at[rooms.slots, 0:LANES], r.s_slots),
            (r.wide.at[rooms.norms.start : rooms.coords.stop], r.s_norms),
            (r.room.at[rooms.wqkv], r.s_wqkv),
        ]
        for index in range(4):
            start = rooms.own.start + index * A
            early.append((r.room.at[start : start + A, 0:F], r.s_own.at[index]))
        late = [
            (r.room.at[rooms.wh, 0 : 4 * F], r.s_wh),
            (r.room.at[rooms.wvec, 0 : 3 * F], r.s_wvec),
            (r.room.at[rooms.wout, 0 : 3 * F], r.s_wout),
        ]
        copies = [
            pltpu.make_async_copy(source, target, r.sems.at[i])
            for i, (source, target) in enumerate(early + late)
        ]
        for copy in copies:
            copy.start()
    else:
        r.s_slots, r.s_norms, r.s_wh = r.slots.at[m], r.norms, r.wh
        r.s_own, r.s_wqkv = r.features.at[m, 0], r.wqkv.at[0]
        r.s_wvec, r.s_wout = r.wvec.at[0], r.wout.at[0]
    write_constants(r, sz)
    r.sagg[...] = jnp.zeros_like(r.sagg)
    r.vagg[...] = jnp.zeros_like(r.vagg)
    for copy in copies[: len(early)]:
        copy.wait()
    coords = [r.s_norms[8 + c : 9 + c, 0:A] if fetch else r.coords[m, c] for c in range(3)]
    edge_geometry(r, sz, m, coords, r.s_slots)

    def tables(b, carry):
        write_edge_tables(r, sz, b, F32)
        return carry

    lax.fori_loop(0, sz.blocks, tables, 0, unroll=4)
    own = r.s_own
    xhat, scale = node_part(r, sz, own, r.s_low, r.s_high, r.s_norms, r.s_wqkv)
    r.xhat[...] = xhat
    r.scale[...] = jnp.broadcast_to(scale, r.scale.shape)
    for cg in range(CG):
        r.query_low[:, cg * LANES : (cg + 1) * LANES] = r.query[cg].astype(BF16)
    for copy in copies[len(early) :]:
        copy.wait()
    r.vproj[...] = dot(r.left[E : E + 3 * A, :], r.s_wvec[...])

    def filter_part(b, part):
        return dot(r.smear_t[b], r.s_wh[:, part * F : (part + 1) * F])

    def block(b, w):
        first = first_row(b)
        half = filter_part(b, 0)
        for cg, at, cols, near_rows in tiles(sz, first):
            h = half[at, cols]
            product = r.query[cg] * r.kv[cg, near_rows, :] * (h + h * jnp.tanh(h))
            coarse = product.astype(BF16)
            w.pack1[at, cols] = coarse
            w.pack2[at, cols] = (product - coarse.astype(F32)).astype(BF16)
        score = dot(w.pack1[...], r.heads[...]) + dot(w.pack2[...], r.heads[...])
        for cg in range(CG):
            r.score[b, cg] = score[:, cg * LANES : (cg + 1) * LANES].astype(BF16)
        half = filter_part(b, 2)
        for cg, at, cols, near_rows in tiles(sz, first):
            h = half[at, cols]
            value = r.kv[2 * CG + cg, near_rows, :] * (h + h * jnp.tanh(h))
            for c in range(3):
                r.vagg[c * CG + cg] += r.vec[c * CG + cg, near_rows, :] * value
        half = filter_part(b, 3)
        for cg, at, cols, near_rows in tiles(sz, first):
            h = half[at, cols]
            value = r.kv[3 * CG + cg, near_rows, :] * (h + h * jnp.tanh(h))
            r.third[b, at, cols] = value.astype(BF16)
        half = filter_part(b, 1)
        for cg, at, cols, near_rows in tiles(sz, first):
            h = half[at, cols]
            s = score[at, cols]
            attention = (s + s * jnp.tanh(s)) * r.cut_wide[b, at, :]
            r.sagg[cg] += attention * (r.kv[CG + cg, near_rows, :] * (h + h * jnp.tanh(h)))

    def pair(i, carry):
        for which in range(2):
            block(2 * i + which, buffers(r, sz, which))
        return carry

    lax.fori_loop(0, sz.blocks // 2, pair, 0, unroll=2)
    third = sum(dot(r.units[b], r.third[b]) for b in range(sz.blocks))
    scalar_low = jnp.concatenate([r.sagg[cg] for cg in range(CG)], axis=1).astype(BF16)
    r.left[E + 3 * A : E + 4 * A, :] = scalar_low
    out_proj = dot(scalar_low, r.s_wout[...])
    vec_dot = vector_dot(r, sz)
    r.out_proj[...] = out_proj
    r.vec_dot[...] = vec_dot
    vector_agg = [
        jnp.concatenate([r.vagg[c * CG + cg] for cg in range(CG)], axis=1)
        + third[c * A : (c + 1) * A, :]
        for c in range(3)
    ]
    write_layer_output(r, sz, own, out_proj, vec_dot, vector_agg)


def edge_filters(r, sz, which):
    F = sz.width
    write_constants(r, sz)
    for m in which:
        w = SimpleNamespace(**vars(r))
        vars(w).update(vars(buffers(r, sz, m)))
        edge_geometry(w, sz, m, r.coords.at[m], r.slots.at[m])

        def block(b, carry, w=w):
            write_edge_tables(w, sz, b, BF16)
            for part in range(4):
                cols = slice(part * F, (part + 1) * F)
                h = dot(r.smear_t[b], r.wh[:, cols])
                if part:
                    h = h.astype(BF16)
                up = 1.0 + jnp.tanh(h)
                f = h * up
                for cg in range(sz.halves):
                    if part == 0 and hasattr(w, "key"):
                        w.key[b, cg] = f[:, cg * LANES : (cg + 1) * LANES]
                f, up = f.astype(BF16), up.astype(BF16)
                slope = up + f * (2.0 - up)
                for cg in range(sz.halves):
                    half = slice(cg * LANES, (cg + 1) * LANES)
                    w.silu[b, part * sz.halves + cg] = f[:, half]
                    w.slope[b, part * sz.halves + cg] = slope[:, half]
            return carry

        lax.fori_loop(0, sz.blocks, block, 0, unroll=4)


def both_ways(r, sz, m, fwd):
    A, H, E, F = sz.atoms, sz.halo, sz.rows, sz.width
    EB, CG, NB, W = sz.edges, sz.halves, sz.blocks, sz.window
    lane = iota((8, LANES), 1)
    row = iota((8, LANES), 0)
    halves = halves_of(sz)
    wqkv, wvec, wout = r.wqkv.at[0], r.wvec.at[0], r.wout.at[0]
    write_constants(r, sz)
    gain = r.norms[0:1, :]
    vp = r.vproj
    if fwd:
        own, left = r.own, r.left
        xhat, scale = node_part(r, sz, own, r.low, r.high, r.norms, wqkv)
        vp[...] = dot(left[E : E + 3 * A, :], wvec[...])
        for cg in range(CG):
            r.query_low[:, halves[cg]] = r.query[cg].astype(BF16)
    else:
        xhat, scale = r.xhat[...], r.scale[:, 0:1]

    if fwd:
        r.sagg[...] = jnp.zeros_like(r.sagg)
        r.vagg[...] = jnp.zeros_like(r.vagg)
        r.uagg[...] = jnp.zeros_like(r.uagg)

        def forward_block(b, carry):
            first = first_row(b)

            def filters(part, cg, at):
                return r.silu[b, part * CG + cg, at, :]

            def keys(cg, at, cols, near_rows):
                product = r.query[cg] * r.kv[cg, near_rows, :] * r.key[b, cg, at, :]
                return [product.astype(BF16)]

            score = dot(*stacked(sz, first, keys), r.heads[...])
            for cg in range(CG):
                r.score[b, cg] = score[:, halves[cg]].astype(BF16)

            def vectors(cg, at, cols, near_rows):
                value = r.kv[2 * CG + cg, near_rows, :].astype(BF16) * filters(2, cg, at)
                return [
                    r.vec[c * CG + cg, near_rows, :].astype(BF16) * value for c in range(3)
                ] + [r.kv[3 * CG + cg, near_rows, :].astype(BF16) * filters(3, cg, at)]

            moved = stacked(sz, first, vectors)
            for c in range(3):
                r.vagg[c] += dot(r.fold[...], moved[c])
            r.uagg[...] += dot(r.units[b], moved[3])

            def scalars(cg, at, cols, near_rows):
                s = r.score[b, cg, at, :]
                attention = s * (1.0 + jnp.tanh(s)) * r.cut_wide[b, at, :]
                return [
                    attention * (r.kv[CG + cg, near_rows, :].astype(BF16) * filters(1, cg, at))
                ]

            r.sagg[...] += dot(r.fold[...], *stacked(sz, first, scalars))
            return carry

        lax.fori_loop(0, NB, forward_block, 0, unroll=8)
        scalar_low = r.sagg[...].astype(BF16)
        left[E + 3 * A : E + 4 * A, :] = scalar_low
        out_proj = dot(scalar_low, wout[...])
        vec_dot = vector_dot(r, sz)
    else:
        out_proj, vec_dot = r.out_proj, r.vec_dot[...]
    if fwd:
        vector_agg = [r.vagg[c] + r.uagg[c * A : (c + 1) * A, :] for c in range(3)]
        write_layer_output(r, sz, own, out_proj, vec_dot, vector_agg)

    def incoming(index):
        if fwd:
            return r.cotangent[m, 0, index].astype(F32)
        gap = jnp.zeros((A - 2 * H, F), F32)
        edge = [r.inc_low[index, 0:H].astype(F32), gap, r.inc_high[index, 0:H].astype(F32)]
        value = r.inc[index].astype(F32) + jnp.concatenate(edge, axis=0)
        return value.astype(BF16).astype(F32)

    g_x = incoming(0)
    r.gx[0] = g_x
    g_first = jnp.zeros((A, F), F32)
    g_mid = g_x * out_proj[:, F : 2 * F]
    for c in range(3):
        g_vec = incoming(c + 1)
        r.gx[c + 1] = g_vec
        rows = slice(c * A, (c + 1) * A)
        r.gvlow[rows, :] = g_vec.astype(BF16)
        g_first = g_first + g_vec * vp[rows, 2 * F :]
        r.gvproj[rows, 0:F] = (g_mid * vp[rows, F : 2 * F]).astype(BF16)
        r.gvproj[rows, F : 2 * F] = (g_mid * vp[rows, 0:F]).astype(BF16)
        r.gvproj[rows, 2 * F :] = (g_vec * out_proj[:, 0:F]).astype(BF16)
    r.gout[:, 0:F] = g_first.astype(BF16)
    r.gout[:, F : 2 * F] = (g_x * vec_dot).astype(BF16)
    r.gout[:, 2 * F :] = g_x.astype(BF16)
    r.gs[...] = dot(r.gout[...], wout[...], 1, 1).astype(BF16)
    for total in (r.gnear, r.gq, r.gfilt):
        total[...] = jnp.zeros_like(total)

    scores = r.score if fwd else r.score_here
    if not fwd:
        scores[...] = r.score[...]

    def backward_block(b, carry):
        first = first_row(b)
        base = pl.multiple_of(first // SUBLANES * SUBLANES, SUBLANES)
        lanes = iota((W, EB), 1)
        place = jnp.where(
            lanes % A + lanes // A + (first - base) == iota((W, EB), 0), 1.0, 0.0
        ).astype(BF16)

        def collect(index, terms):
            r.gnear[index, pl.ds(base, W), :] += dot(place, terms)

        def filters(part, cg, at):
            return r.silu[b, part * CG + cg, at, :], r.slope[b, part * CG + cg, at, :]

        def weights(cg, at, cols, near_rows):
            value = r.kv[CG + cg, near_rows, :].astype(BF16)
            return [r.gs[:, cols] * (value * filters(1, cg, at)[0])]

        g_att = dot(*stacked(sz, first, weights), r.heads[...])

        def vectors(cg, at, cols, near_rows):
            f, slope = filters(2, cg, at)
            value = r.kv[2 * CG + cg, near_rows, :].astype(BF16)
            message = value * f
            moved = []
            for c in range(3):
                g_vec = r.gvlow[c * A : (c + 1) * A, cols]
                term = g_vec * r.vec[c * CG + cg, near_rows, :].astype(BF16)
                g_edge = term if c == 0 else g_edge + term
                moved.append(g_vec * message)
            return moved + [g_edge * f, g_edge * (value * slope)]

        *moved, g_value, g_pre = stacked(sz, first, vectors)
        for c in range(3):
            collect(4 + c, moved[c])
        collect(2, g_value)
        pre = [None, None, g_pre, None]
        g_third = dot(r.units[b], r.gvlow[...], 0, 0)

        def units(cg, at, cols, near_rows):
            f, slope = filters(3, cg, at)
            value = r.kv[3 * CG + cg, near_rows, :].astype(BF16)
            g_edge = g_third[at, cols].astype(BF16)
            return value * f, g_edge * f, g_edge * (value * slope)

        message, g_value, pre[3] = stacked(sz, first, units)
        collect(3, g_value)
        g_unit = dot(r.gvlow[...], message, 1, 1)
        for c in range(3):
            r.gunit[c, pl.ds(b, 1), :] = jnp.sum(
                g_unit[c * A : (c + 1) * A, :] * r.diag[...], axis=0, keepdims=True
            )

        def attention(cg, at, cols, near_rows):
            s = scores[b, cg, at, :]
            t = jnp.tanh(s)
            up = 1.0 + t
            act = s * up
            wide = r.cut_wide[b, at, :]
            ga = g_att[at, cols].astype(BF16)
            g_score = ga * wide * (up + act * (1.0 - t))
            g_edge = r.gs[:, cols] * (act * wide)
            f, slope = filters(0, cg, at)
            key = r.kv[cg, near_rows, :].astype(BF16)
            query = r.query_low[:, cols]
            middle = g_score * f
            made = [ga * act, middle * key, middle * query, (g_score * slope) * (key * query)]
            f, slope = filters(1, cg, at)
            value = r.kv[CG + cg, near_rows, :].astype(BF16)
            return made + [g_edge * f, g_edge * (value * slope)]

        g_act, g_query, g_key, pre[0], g_value, pre[1] = stacked(sz, first, attention)
        collect(1, g_value)
        collect(0, g_key)
        r.gq[...] += dot(r.fold[...], g_query)
        g_cut = dot(jnp.ones((16, F), BF16), g_act, 1, 1)[0:1, :] * (2.0 * HEADS / F)
        g_smear = jnp.zeros((sz.basis, EB), F32)
        for part in range(4):
            cols = slice(part * F, (part + 1) * F)
            g_smear = g_smear + dot(r.wh[:, cols], pre[part], 1, 1)
            r.gfilt[:, cols] += dot(r.smear[b], pre[part])
        delta, bell = bell_of(r, sz, b)
        through = g_smear * bell
        r.gcut[pl.ds(b, 1), :] = g_cut + jnp.sum(through, axis=0, keepdims=True)
        r.gshrink[pl.ds(b, 1), :] = r.geo[CUT, pl.ds(b, 1), :] * jnp.sum(
            through * delta, axis=0, keepdims=True
        ) * (-2.0 * sharpness_of(sz.basis))
        return carry

    lax.fori_loop(0, NB, backward_block, 0)

    distance = r.geo[DISTANCE]
    g_dist = r.gcut[...] * r.geo[LIVE] * jnp.where(
        distance < CUTOFF,
        (-0.5 * math.pi / CUTOFF) * jnp.sin(math.pi * distance / CUTOFF),
        0.0,
    ) - r.gshrink[...] * r.geo[SHRINK]
    inverse = 1.0 / distance
    g_unit = [r.gunit[c] for c in range(3)]
    sep = [r.geo[c] for c in range(3)]
    along = g_unit[0] * sep[0] + g_unit[1] * sep[1] + g_unit[2] * sep[2]
    radial = (g_dist - along * inverse * inverse) * inverse
    r.gplaces[...] = jnp.zeros_like(r.gplaces)
    for c in range(3):
        g_sep = g_unit[c] * inverse + radial * sep[c]
        first, other = g_sep[:, :LANES], g_sep[:, LANES:]
        z = (
            jnp.where(lane < A, first, 0.0)
            + pltpu.roll(jnp.where(lane < A, 0.0, first), A + 1, 1)
            + pltpu.roll(jnp.where(lane < A, other, 0.0), 2, 1)
            + pltpu.roll(jnp.where(lane < A, 0.0, other), A + 3, 1)
        )
        for bit in range(3):
            z = jnp.where((row >> bit) & 1 == 1, pltpu.roll(z, GROUP * 2**bit, 1), z)
        z = jnp.where(row >= 4, pltpu.roll(z, 1, 1), z)
        total = jnp.sum(g_sep, axis=0, keepdims=True)
        mine = total[:, 0:A] + total[:, A : 2 * A] + total[:, 2 * A : 3 * A] + total[:, 3 * A :]
        mine = jnp.concatenate(
            [jnp.zeros((1, H), F32), mine, jnp.zeros((1, LANES - H - A), F32)], axis=1
        )
        r.gplaces[c : c + 1, :] = jnp.sum(z, axis=0, keepdims=True) - mine

    gproj = r.gproj
    gproj[:, 0:F] = jnp.zeros((E, F), BF16)
    gproj[H : H + A, 0:F] = r.gq[...].astype(BF16)
    for part in range(4):
        gproj[:, (part + 1) * F : (part + 2) * F] = r.gnear[part].astype(BF16)
    g_normed = dot(gproj[...], wqkv[...], 1, 1)
    u = gain * g_normed
    g_scalars = scale * (
        u
        - jnp.mean(u, axis=-1, keepdims=True)
        - xhat * jnp.mean(u * xhat, axis=-1, keepdims=True)
    )
    r.gnorm[...] = jnp.zeros_like(r.gnorm)
    r.gnorm[0:1, :] = jnp.sum(g_normed * xhat, axis=0, keepdims=True)
    r.gnorm[1:2, :] = jnp.sum(g_normed, axis=0, keepdims=True)
    vec_back = dot(r.gvproj[...], wvec[...], 1, 1)
    for index in range(4):
        if index == 0:
            whole = g_scalars
            middle = whole[H : H + A] + r.gx[0]
        else:
            c = index - 1
            whole = r.gnear[4 + c]
            middle = whole[H : H + A] + r.gx[index] + vec_back[c * A : (c + 1) * A, :]
        r.back[index] = middle
        r.back_low[index] = middle.astype(BF16)
        r.rim_low[index] = whole[0:H].astype(BF16)
        r.rim_high[index] = whole[H + A :].astype(BF16)


FACTORS = ("left", "gproj", "gvproj", "gout", "gfilt", "gnorm")
HANDED = (
    "query_low", "kv", "vec", "vproj", "xhat", "scale", "out_proj", "vec_dot", "score"
)
BORDERS = ("rim_low", "rim_high", "gplaces")


def call(body, arrays, outs, scratch, role=None, grant_mb=14, place=VMEM):
    arrays, outs = vars(arrays), vars(outs)
    names = list(arrays) + list(outs) + list(scratch)

    def kernel(*args):
        refs = SimpleNamespace(**dict(zip(names, args, strict=True)))
        if role is None:
            body(refs)
        else:
            pl.when(lax.axis_index("section") == role)(lambda: body(refs))

    results = pl.pallas_call(
        kernel,
        out_shape=list(outs.values()),
        in_specs=[spec for _, spec in arrays.values()],
        out_specs=[place for _ in outs],
        scratch_shapes=[
            pltpu.VMEM(*s) if isinstance(s, tuple) else s for s in scratch.values()
        ],
        compiler_params=pltpu.CompilerParams(vmem_limit_bytes=int(grant_mb * 2**20)),
    )(*[array for array, _ in arrays.values()])
    return SimpleNamespace(**dict(zip(outs, results, strict=True)))


def first_call(sz, m, fetch, sent, arrays):
    A, H, E, F = sz.atoms, sz.halo, sz.rows, sz.width
    EB, CG, NB = sz.edges, sz.halves, sz.blocks
    shape = jax.ShapeDtypeStruct
    results = dict(
        fresh=((4, A, F), BF16),
        head=((4, sent, F), BF16),
        tail=((4, sent, F), BF16),
        left=((sz.factors, F), BF16),
        query_low=((A, F), BF16),
        kv=((4 * CG, E, LANES), F32),
        vec=((3 * CG, E, LANES), F32),
        vproj=((3 * A, 3 * F), F32),
        xhat=((E, F), F32),
        scale=((E, LANES), F32),
        out_proj=((A, 3 * F), F32),
        vec_dot=((A, F), F32),
        score=((NB, CG, EB, LANES), BF16),
    )
    fetched = dict(
        s_own=((4, A, F), BF16),
        s_slots=((3 * sz.slots + 8, LANES), F32),
        s_norms=((16, F), F32),
        s_wqkv=((F, 5 * F), BF16),
        s_wvec=((F, 3 * F), BF16),
        s_wh=((sz.basis, 4 * F), BF16),
        s_wout=((F, 3 * F), BF16),
        sems=pltpu.SemaphoreType.DMA((10,)),
    )
    outs = SimpleNamespace(**{k: shape(*v) for k, v in results.items()})
    scratch = dict(
        query=((CG, A, LANES), F32),
        heads=((F, F), BF16),
        diag=((A, EB), F32),
        geo=((10, 8, EB), F32),
        centres=((sz.basis, EB), F32),
        smear_t=((NB, EB, sz.basis), BF16),
        cut_wide=((NB, EB, LANES), F32),
        units=((NB, 3 * A, EB), BF16),
        pack10=((EB, F), BF16),
        pack20=((EB, F), BF16),
        pack11=((EB, F), BF16),
        pack21=((EB, F), BF16),
        sagg=((CG, A, LANES), F32),
        vagg=((3 * CG, A, LANES), F32),
        third=((NB, EB, F), BF16),
    )
    if fetch:
        scratch.update(fetched)
    return call(
        lambda r: first_forward(r, sz, m, fetch), arrays, outs, scratch, FIRST, grant_mb=20
    )


def filter_call(sz, role, which, arrays):
    A, F = sz.atoms, sz.width
    EB, CG, NB = sz.edges, sz.halves, sz.blocks
    shape = jax.ShapeDtypeStruct
    outs = dict(
        geo=shape((10, 8, EB), F32),
        smear=shape((NB, sz.basis, EB), BF16),
        cut_wide=shape((NB, EB, LANES), BF16),
        units=shape((NB, 3 * A, EB), BF16),
        silu=shape((NB, 4 * CG, EB, LANES), BF16),
        slope=shape((NB, 4 * CG, EB, LANES), BF16),
    )
    if role == SECOND:
        outs.update(key=shape((NB, CG, EB, LANES), F32))
    scratch = dict(
        diag=((A, EB), F32),
        centres=((sz.basis, EB), F32),
        smear_t=((NB, EB, sz.basis), BF16),
    )
    made = call(
        lambda r: edge_filters(r, sz, which),
        arrays,
        SimpleNamespace(**{f"{k}{m}": v for m in which for k, v in outs.items()}),
        scratch,
        role,
        grant_mb=6,
    )
    return {m: SimpleNamespace(**{k: getattr(made, f"{k}{m}") for k in outs}) for m in which}


def both_call(sz, m, fwd, arrays, border_sets=()):
    A, H, E, F = sz.atoms, sz.halo, sz.rows, sz.width
    EB, CG, NB = sz.edges, sz.halves, sz.blocks
    shape = jax.ShapeDtypeStruct
    outs = SimpleNamespace(
        back=shape((4, A, F), F32),
        back_low=shape((5 if fwd and m else 4, A, F), BF16),
        rim_low=shape((4, H, F), BF16),
        rim_high=shape((4, H, F), BF16),
        gplaces=shape((8, LANES), F32),
        gproj=shape((E, 5 * F), BF16),
        gvproj=shape((3 * A, 3 * F), BF16),
        gout=shape((A, 3 * F), BF16),
        gfilt=shape((sz.basis, 4 * F), F32),
        gnorm=shape((8, F), F32),
    )
    scratch = dict(
        heads=((F, F), BF16),
        diag=((A, EB), F32),
        fold=((A, EB), BF16),
        centres=((sz.basis, EB), F32),
        gx=((4, A, F), F32),
        gvlow=((3 * A, F), BF16),
        gs=((A, F), BF16),
        gq=((A, F), F32),
        gnear=((7, E, F), F32),
        gunit=((3, 8, EB), F32),
        gcut=((8, EB), F32),
        gshrink=((8, EB), F32),
    )
    if not fwd:
        scratch.update(score_here=((NB, CG, EB, LANES), BF16))
    if fwd:
        outs.fresh = shape((4, A, F), BF16)
        outs.left = shape((sz.factors, F), BF16)
        scratch.update(
            query=((CG, A, LANES), F32),
            query_low=((A, F), BF16),
            kv=((4 * CG, E, LANES), F32),
            vec=((3 * CG, E, LANES), F32),
            vproj=((3 * A, 3 * F), F32),
            score=((NB, CG, EB, LANES), BF16), sagg=((A, F), F32), vagg=((3, A, F), F32), uagg=((3 * A, F), F32)
        )
    if fwd and m:
        for i, made in enumerate(border_sets):
            setattr(arrays, f"gplaces_{i}", (made.gplaces, VMEM))

        def layer(r):
            both_ways(r, sz, m, fwd)
            for i in range(m + 1):
                places = r.gplaces if i == m else getattr(r, f"gplaces_{i}")
                rows = [places[c : c + 1, :] for c in range(3)]
                r.back_low[4, 16 * i : 16 * i + 16, :] = packed_places(rows, F)

        return call(layer, arrays, outs, scratch, SECOND)
    if not border_sets:
        role = SECOND if fwd else FIRST
        return call(lambda r: both_ways(r, sz, m, fwd), arrays, outs, scratch, role)
    count = m + 1
    outs.up, outs.down = shape((count, 4, H, F), BF16), shape((count, 4, H, F), BF16)
    outs.moved = shape((count, 8, LANES), F32)
    outs.total = shape((count, 8, LANES), F32)
    for role, sets in enumerate(border_sets):
        for i, made in enumerate(sets):
            for name in BORDERS:
                setattr(arrays, f"{name}_{role}_{i}", (getattr(made, name), VMEM))

    def hand_on(r, role):
        for i in range(count):
            low, high, places = (
                getattr(r, f"{name}_{role}_{i}") if i < len(border_sets[role]) else getattr(r, name)
                for name in BORDERS
            )
            r.up[i] = high[...]
            r.down[i] = low[...]
            r.moved[i] = places[...]
            r.total[i] = places[...]
            if role == FIRST:
                block = r.inc[4, 16 * i : 16 * i + 16, :]
                for c in range(3):
                    r.total[i, c : c + 1, :] += unpacked_places(block, c, 0, LANES)

    def body(r):
        @pl.when(lax.axis_index("section") == FIRST)
        def _():
            both_ways(r, sz, m, fwd)
            hand_on(r, FIRST)

        pl.when(lax.axis_index("section") == SECOND)(lambda: hand_on(r, SECOND))

    return call(body, arrays, outs, scratch)


def border_call(sz, features, coords):
    A, H, F = sz.atoms, sz.halo, sz.width
    count = features.shape[0]

    def body(r):
        moves = [(r.coords, r.s_coords)]
        for m in range(count):
            moves += [
                (r.features.at[m, 0, :, A - H : A, :], r.up.at[4 * m : 4 * m + 4]),
                (r.features.at[m, 0, :, 0:H, :], r.down.at[4 * m : 4 * m + 4]),
            ]
        copies = [
            pltpu.make_async_copy(source, target, r.sems.at[i])
            for i, (source, target) in enumerate(moves)
        ]
        for copy in copies:
            copy.start()
        copies[0].wait()
        for target, ends in ((r.up, slice(A - H, A)), (r.down, slice(0, H))):
            rows = []
            for m in range(count):
                parts = [r.s_coords[m, c][:, ends] for c in range(3)]
                rows.append(jnp.concatenate(parts, axis=1))
            target[4 * count] = packed_places(rows, F)
        for copy in copies[1:]:
            copy.wait()

    shape = jax.ShapeDtypeStruct((4 * count + 1, H, F), BF16)
    return call(
        body,
        SimpleNamespace(features=(features, HBM), coords=(coords, HBM)),
        SimpleNamespace(up=shape, down=shape),
        dict(s_coords=(coords.shape, F32), sems=pltpu.SemaphoreType.DMA((2 * count + 1,))),
        grant_mb=54,
    )


class Rooms:
    def __init__(self, sz):
        F = sz.width
        ends = [0]
        for rows in (F, F, F, 4 * sz.atoms, sz.basis):
            ends.append(ends[-1] + rows)
        self.wqkv, self.wvec, self.wout, self.own, self.wh = [
            slice(*pair) for pair in zip(ends, ends[1:])
        ]
        table = 3 * sz.slots + 8
        self.slots, self.norms = slice(0, table), slice(table, table + 8)
        self.coords = slice(table + 8, table + 16)
        self.low_shape, self.wide_shape = (20480, 5 * F), (51200, F)


def stage_call(sz, features, coords, neighbours, shifts, counts, gain, bias, filter_weight, weights):
    A, F, K = sz.atoms, sz.width, sz.slots
    count = features.shape[0]
    rooms = Rooms(sz)

    def body(r):
        moves = [(r.coords, r.s_coords), (r.counts, r.s_counts)]
        moves += [(r.gain, r.s_gain), (r.bias, r.s_bias), (r.wfilt.at[0], r.s_wfilt)]
        for m in range(count):
            moves += [
                (r.nbr.at[m, 0], r.s_slots.at[m, 0:K]),
                (r.shifts.at[m, 0, 0], r.s_slots.at[m, K : 2 * K]),
                (r.shifts.at[m, 0, 1], r.s_slots.at[m, 2 * K : 3 * K]),
            ]
        near = len(moves)
        moves += [(r.features.at[0, 0], r.s_own), (r.wqkv.at[0], r.s_wqkv)]
        moves += [(r.wvec.at[0], r.s_wvec), (r.wout.at[0], r.s_wout)]
        copies = [
            pltpu.make_async_copy(source, target, r.sems.at[i])
            for i, (source, target) in enumerate(moves)
        ]
        for copy in copies:
            copy.start()
        for copy in copies[:near]:
            copy.wait()
        r.s_wh[...] = (r.s_wfilt[...].astype(F32) * 0.5).astype(BF16)
        for m in range(count):
            r.s_table[m, 0 : 3 * K, 0:A] = r.s_slots[m].astype(F32)
            r.s_table[m, 3 * K :, 0:A] = jnp.broadcast_to(r.s_counts[m].astype(F32), (8, A))
        r.s_norms[...] = jnp.zeros_like(r.s_norms)
        r.s_norms[0:1, :] = r.s_gain[...].astype(F32)
        r.s_norms[1:2, :] = r.s_bias[...].astype(F32)
        for c in range(3):
            r.s_norms[8 + c : 9 + c, 0:A] = r.s_coords[0, c]
        for copy in copies[near:]:
            copy.wait()
        moves = [
            (r.s_table, r.slots),
            (r.s_norms.at[0:8], r.norms),
            (r.s_wh, r.wh),
            (r.s_table.at[0], r.wide.at[rooms.slots, 0:LANES]),
            (r.s_norms, r.wide.at[rooms.norms.start : rooms.coords.stop]),
            (r.s_wqkv, r.low.at[rooms.wqkv]),
            (r.s_wvec, r.low.at[rooms.wvec, 0 : 3 * F]),
            (r.s_wout, r.low.at[rooms.wout, 0 : 3 * F]),
            (r.s_wh, r.low.at[rooms.wh, 0 : 4 * F]),
        ]
        for index in range(4):
            start = rooms.own.start + index * A
            moves.append((r.s_own.at[index], r.low.at[start : start + A, 0:F]))
        later = [
            pltpu.make_async_copy(source, target, r.sems.at[len(copies) + i])
            for i, (source, target) in enumerate(moves)
        ]
        for copy in later:
            copy.start()
        for copy in later:
            copy.wait()

    shape = jax.ShapeDtypeStruct
    wqkv, wvec, wout = weights
    return call(
        body,
        SimpleNamespace(
            features=(features, HBM),
            coords=(coords, HBM),
            nbr=(neighbours, HBM),
            shifts=(shifts, HBM),
            counts=(counts, HBM),
            gain=(gain, HBM),
            bias=(bias, HBM),
            wfilt=(filter_weight, HBM),
            wqkv=(wqkv, HBM),
            wvec=(wvec, HBM),
            wout=(wout, HBM),
        ),
        SimpleNamespace(
            slots=shape((count, 3 * K + 8, LANES), F32),
            norms=shape((8, F), F32),
            wh=shape((sz.basis, 4 * F), BF16),
            low=shape(rooms.low_shape, BF16),
            wide=shape(rooms.wide_shape, F32),
        ),
        dict(
            s_coords=(coords.shape, F32),
            s_counts=(counts.shape, jnp.int32),
            s_gain=(gain.shape, BF16),
            s_bias=(bias.shape, BF16),
            s_wfilt=(filter_weight.shape[1:], BF16),
            s_slots=((count, 3 * K, A), jnp.int32),
            s_own=((4, A, F), BF16),
            s_wqkv=(wqkv.shape[1:], BF16),
            s_wvec=(wvec.shape[1:], BF16),
            s_wout=(wout.shape[1:], BF16),
            s_wh=(filter_weight.shape[1:], BF16),
            s_table=((count, 3 * K + 8, LANES), F32),
            s_norms=((16, F), F32),
            sems=pltpu.SemaphoreType.DMA((3 * count + 22,)),
        ),
        grant_mb=54,
        place=HBM,
    )


def gradient_call(sz, sets):
    A, E, F = sz.atoms, sz.rows, sz.width
    count = len(sets[0])
    w1, w2, w3 = sz.widths
    w4, w5 = 4 * F // sz.space, F // sz.space
    half = F // 2
    arrays = SimpleNamespace()
    for role in (FIRST, SECOND):
        for m in range(count):
            for name in FACTORS:
                setattr(arrays, f"{name}_{role}_{m}", (getattr(sets[role][m], name), VMEM))

    def body(r, role):
        def get(name, m):
            return getattr(r, f"{name}_{role}_{m}")

        every = range(count)
        e, a = E, A
        r.qkv[...] = sum(dot(get("gproj", m)[...], get("left", m)[0:e, :], 0, 0) for m in every)
        r.vector[...] = sum(
            dot(get("gvproj", m)[...], get("left", m)[e : e + 3 * a, :], 0, 0) for m in every
        )
        r.out[...] = sum(
            dot(get("gout", m)[...], get("left", m)[e + 3 * a : e + 4 * a, :], 0, 0) for m in every
        )
        filt = sum(get("gfilt", m)[...] for m in every) * 0.5
        norm = sum(get("gnorm", m)[...] for m in every)
        core = lax.axis_index("dp")
        for k in range(sz.space):
            spare = [filt[:, k * w4 : (k + 1) * w4]]
            if half > w4:
                spare.append(jnp.zeros((sz.basis, half - w4), F32))
            left = jnp.concatenate(spare, axis=1)
            rows = [norm[:, k * w5 : (k + 1) * w5], jnp.zeros((8, half - w5), F32)]
            right = jnp.concatenate(rows, axis=1)
            right = jnp.concatenate(
                [right, jnp.zeros((sz.packed - sz.spare - 8, half), F32)], axis=0
            )
            if sz.packed - sz.spare > sz.basis:
                gap = jnp.zeros((sz.packed - sz.spare - sz.basis, half), F32)
                left = jnp.concatenate([left, gap], axis=0)
            parts = [
                r.qkv[k * w1 : (k + 1) * w1, :],
                r.vector[k * w2 : (k + 1) * w2, :],
                r.out[k * w3 : (k + 1) * w3, :],
            ]
            first = jnp.concatenate([part[:, :half] for part in parts] + [left], axis=0)
            second = jnp.concatenate([part[:, half:] for part in parts] + [right], axis=0)
            r.send[k] = jnp.where(core == 0, second, first).astype(BF16)
            r.stay[k] = jnp.where(core == 0, first, second)

    def both(r):
        for role in (FIRST, SECOND):
            pl.when(lax.axis_index("section") == role)(lambda role=role: body(r, role))

    shape = jax.ShapeDtypeStruct
    return call(
        both,
        arrays,
        SimpleNamespace(
            send=shape((sz.space, sz.packed, half), BF16),
            stay=shape((sz.space, sz.packed, half), F32),
        ),
        dict(
            qkv=((5 * F, F), F32),
            vector=((3 * F, F), F32),
            out=((3 * F, F), F32),
        ),
    )


def border_rows(sz, index):
    start = sz.packed + index * 2 * sz.halo
    return [slice(start + i * sz.halo, start + (i + 1) * sz.halo) for i in range(2)]


def border_block(sz, ref, index):
    return jnp.concatenate([ref[rows, :] for rows in border_rows(sz, index)], axis=1)


def piece_call(sz, stay, recv, up, down, total, late):
    A, H, E, F = sz.atoms, sz.halo, sz.rows, sz.width
    count = up.shape[0]
    half = F // 2

    def body(r):
        slab, space = lax.axis_index("space"), sz.space
        for hop in range(space):
            k = lax.rem(slab + hop, space)
            share = r.stay[k] + r.recv[k].astype(F32)
            target = getattr(r, f"hop{hop}")
            target[0 : sz.packed, :] = share.astype(target.dtype)
        places = [r.total[m] + r.late[m] for m in range(count)]
        ends = (
            (r.hop1, r.up, slice(H + A, E)),
            (getattr(r, f"hop{space - 1}"), r.down, slice(0, H)),
        )
        for target, border, lanes in ends:
            rows = []
            for m in range(count):
                parts = [places[m][c : c + 1, lanes] for c in range(3)]
                rows.append(jnp.concatenate(parts, axis=1))
            blocks = [border[m, index] for m in range(count) for index in range(4)]
            for index, block in enumerate(blocks + [packed_places(rows, F)]):
                first, second = border_rows(sz, index)
                target[first, :] = block[:, :half]
                target[second, :] = block[:, half:]
        for m in range(count):
            for c in range(3):
                r.mine[m, c] = places[m][c : c + 1, H : H + A]

    shape = jax.ShapeDtypeStruct
    outs = {
        f"hop{hop}": shape(
            (sz.packed + ((8 * count + 2) * H if hop in (1, sz.space - 1) else 0), half),
            BF16 if hop else F32,
        )
        for hop in range(sz.space)
    }
    outs.update(mine=shape((count, 3, 1, A), F32))
    made = call(
        body,
        SimpleNamespace(
            stay=(stay, VMEM),
            recv=(recv, VMEM),
            up=(up, VMEM),
            down=(down, VMEM),
            total=(total, VMEM),
            late=(late, VMEM),
        ),
        SimpleNamespace(**outs),
        {},
    )
    return [getattr(made, f"hop{hop}") for hop in range(sz.space)], made.mine


def result_call(sz, fresh, back, from_low, from_high, mine):
    A, H, F = sz.atoms, sz.halo, sz.width
    count = len(back[0])
    arrays = SimpleNamespace(
        low=(from_low, VMEM), high=(from_high, VMEM), mine=(mine, VMEM)
    )
    for role in (FIRST, SECOND):
        for m in range(count):
            setattr(arrays, f"fresh_{role}_{m}", (fresh[role][m], VMEM))
            setattr(arrays, f"back_{role}_{m}", (back[role][m], VMEM))

    def body(r, role):
        for m in range(count):
            r.outputs[0, m, 0] = getattr(r, f"fresh_{role}_{m}")[...]
            whole = getattr(r, f"back_{role}_{m}")
            for index in range(4):
                low = border_block(sz, r.low, 4 * m + index).astype(F32)
                high = border_block(sz, r.high, 4 * m + index).astype(F32)
                r.grads[0, m, 0, index, 0:H, :] = whole[index, 0:H, :] + low
                r.grads[0, m, 0, index, H : A - H, :] = whole[index, H : A - H, :]
                r.grads[0, m, 0, index, A - H :, :] = whole[index, A - H :, :] + high
            for c in range(3):
                edge = [
                    unpacked_places(border_block(sz, r.low, 4 * count), m, c, H),
                    jnp.zeros((1, A - 2 * H), F32),
                    unpacked_places(border_block(sz, r.high, 4 * count), m, c, H),
                ]
                r.places[m, c] = r.mine[m, c] + jnp.concatenate(edge, axis=1)

    def both(r):
        for role in (FIRST, SECOND):
            pl.when(lax.axis_index("section") == role)(lambda role=role: body(r, role))

    shape = jax.ShapeDtypeStruct
    return call(
        both,
        arrays,
        SimpleNamespace(
            outputs=shape((1, count, 1, 4, A, F), BF16),
            grads=shape((1, count, 1, 4, A, F), F32),
            places=shape((count, 3, 1, A), F32),
        ),
        {},
    )


def share_call(sz, total, other):
    F = sz.width
    w1, w2, w3 = sz.widths
    w4, w5 = 4 * F // sz.space, F // sz.space
    half = F // 2

    def body(r, first, second):
        for lanes, part in ((slice(0, half), first), (slice(half, F), second)):
            r.qkv[0, :, lanes] = part[0:w1, :]
            r.vector[0, :, lanes] = part[w1 : w1 + w2, :]
            r.out[0, :, lanes] = part[w1 + w2 : sz.spare, :]
        r.filt[0] = first[sz.spare : sz.spare + sz.basis, 0:w4]
        r.gain[...] = second[sz.spare : sz.spare + 1, 0:w5]
        r.bias[...] = second[sz.spare + 1 : sz.spare + 2, 0:w5]

    def both(r):
        pl.when(lax.axis_index("dp") == 0)(lambda: body(r, r.total, r.other))
        pl.when(lax.axis_index("dp") == 1)(lambda: body(r, r.other, r.total))

    shape = jax.ShapeDtypeStruct
    return call(
        both,
        SimpleNamespace(total=(total, VMEM), other=(other, VMEM)),
        SimpleNamespace(
            gain=shape((1, w5), F32),
            bias=shape((1, w5), F32),
            qkv=shape((1, w1, F), F32),
            vector=shape((1, w2, F), F32),
            filt=shape((1, sz.basis, w4), F32),
            out=shape((1, w3, F), F32),
        ),
        {},
    )


def on_device(
    features,
    coords,
    neighbours,
    counts,
    shifts,
    norm_gain,
    norm_bias,
    qkv_weight,
    vector_weight,
    filter_weight,
    out_weight,
    cotangent,
):
    micro_count = features.shape[0]
    space = lax.axis_size("space")
    sz = Sizes(features.shape[3], features.shape[4], filter_weight.shape[1], neighbours.shape[2], space)
    up = [(i, (i + 1) % space) for i in range(space)]
    down = [((i + 1) % space, i) for i in range(space)]

    places = jnp.transpose(coords, (0, 2, 1, 3))
    borders = border_call(sz, features, places)
    staged = stage_call(
        sz,
        features,
        places,
        neighbours,
        shifts,
        counts,
        norm_gain,
        norm_bias,
        filter_weight,
        (qkv_weight, vector_weight, out_weight),
    )
    slots, norms, half_filter = staged.slots, staged.norms, staged.wh
    pack_low = lax.ppermute(borders.up, "space", up)
    pack_high = lax.ppermute(borders.down, "space", down)
    both = ("section", "space")
    forth = [(k, space + k) for k in range(space)]
    forth_up = [(k, space + (k + 1) % space) for k in range(space)]
    forth_down = [((k + 1) % space, space + k) for k in range(space)]
    back = [(space + k, k) for k in range(space)]
    back_up = [(space + k, (k + 1) % space) for k in range(space)]
    back_down = [(space + (k + 1) % space, k) for k in range(space)]

    def geometry_inputs():
        return SimpleNamespace(
            pack_low=(pack_low, VMEM),
            pack_high=(pack_high, VMEM),
            coords=(places, VMEM),
            slots=(slots, VMEM),
            wh=(half_filter, VMEM),
        )

    firsts, sent, filters = [], [], {}
    for m in range(micro_count):
        if m == 0:
            arrays = SimpleNamespace(
                pack_low=(pack_low, VMEM),
                pack_high=(pack_high, VMEM),
                room=(staged.low, HBM),
                wide=(staged.wide, HBM),
            )
        else:
            arrays = geometry_inputs()
            arrays.features = (features, VMEM)
            arrays.norms = (norms, VMEM)
            arrays.wqkv, arrays.wvec, arrays.wout = (
                (qkv_weight, VMEM), (vector_weight, VMEM), (out_weight, VMEM)
            )
        first = first_call(sz, m, m == 0, sz.sent[m], arrays)
        firsts.append(first)
        if m == micro_count - 1:
            made = filters[SECOND] = filter_call(
                sz, SECOND, range(micro_count), geometry_inputs()
            )
            own, *rest = sent[0]
            first.head, made[0].geo, own = lax.optimization_barrier(
                (first.head, made[0].geo, own)
            )
            sent[0] = (own, *rest)
        sent.append((
            lax.ppermute(first.fresh, both, forth),
            lax.ppermute(first.tail, both, forth_up),
            lax.ppermute(first.head, both, forth_down),
        ))
    def both_inputs(m, role):
        made = filters[role][m]
        return SimpleNamespace(
            norms=(norms, VMEM),
            wqkv=(qkv_weight, VMEM),
            wvec=(vector_weight, VMEM),
            wh=(half_filter, VMEM),
            wout=(out_weight, VMEM),
            geo=(made.geo, VMEM),
            smear=(made.smear, VMEM),
            cut_wide=(made.cut_wide, VMEM),
            units=(made.units, VMEM),
            silu=(made.silu, VMEM),
            slope=(made.slope, VMEM),
        )

    seconds, returned = [], []
    for m in range(micro_count):
        if m == 1:
            other = filters[FIRST][0]
            other.geo, filters[SECOND][m].geo = lax.optimization_barrier(
                (other.geo, filters[SECOND][m].geo)
            )
        arrays = both_inputs(m, SECOND)
        arrays.key = (filters[SECOND][m].key, VMEM)
        own, low, high = sent[m]
        arrays.own, arrays.low, arrays.high = (own, VMEM), (low, VMEM), (high, VMEM)
        arrays.cotangent = (cotangent, VMEM)
        second = both_call(sz, m, True, arrays, seconds)
        seconds.append(second)
        if m == 0:
            later = geometry_inputs()
            held, second.gplaces = lax.optimization_barrier((slots, second.gplaces))
            later.slots = (held, VMEM)
            filters[FIRST] = filter_call(sz, FIRST, range(micro_count), later)
        back_low, rim_low, rim_high = second.back_low, second.rim_low, second.rim_high
        if m:
            returned[-1], back_low, rim_low, rim_high = lax.optimization_barrier(
                (returned[-1], back_low, rim_low, rim_high)
            )
        returned.append((
            lax.ppermute(back_low, both, back),
            lax.ppermute(rim_high, both, back_up),
            lax.ppermute(rim_low, both, back_down),
        ))
    thirds = []
    for m in range(micro_count):
        arrays = both_inputs(m, FIRST)
        for name in HANDED:
            setattr(arrays, name, (getattr(firsts[m], name), VMEM))
        inc, inc_low, inc_high = returned[m]
        arrays.inc, arrays.inc_low, arrays.inc_high = (inc, VMEM), (inc_low, VMEM), (inc_high, VMEM)
        sets = (thirds, seconds) if m == micro_count - 1 else ()
        third = both_call(sz, m, False, arrays, sets)
        third.left = firsts[m].left
        thirds.append(third)

    last = thirds[-1]
    late = lax.ppermute(last.moved, both, forth)
    shares = gradient_call(sz, (thirds, seconds))
    recv = lax.ppermute(shares.send, "dp", [(0, 1), (1, 0)])
    (total, *pieces), mine = piece_call(sz, shares.stay, recv, last.up, last.down, last.total, late
    )
    received = [
        lax.ppermute(piece, "space", [(i, (i + hop) % space) for i in range(space)])
        for hop, piece in enumerate(pieces, 1)
    ]
    for piece in received:
        total = total + piece[: sz.packed].astype(F32)
    results = result_call(
        sz,
        ([v.fresh for v in firsts], [v.fresh for v in seconds]),
        ([v.back for v in thirds], [v.back for v in seconds]),
        received[0],
        received[-1],
        mine,
    )
    other = lax.ppermute(total, "dp", [(0, 1), (1, 0)])
    share = share_call(sz, total, other)
    return (
        results.outputs,
        results.grads,
        share.gain,
        share.bias,
        jnp.transpose(share.qkv, (0, 2, 1)),
        jnp.transpose(share.vector, (0, 2, 1)),
        share.filt,
        jnp.transpose(share.out, (0, 2, 1)),
        jnp.transpose(results.places, (0, 2, 1, 3)),
    )


def solution(mesh):
    return jax.shard_map(
        on_device,
        mesh=mesh,
        in_specs=(
            P(None, "dp", None, "space", None),
            P(None, "dp", None, "space"),
            P(None, "dp", None, "space"),
            P(None, "dp", "space"),
            P(None, "dp", None, None, "space"),
            P("section", None),
            P("section", None),
            P("section", None, None),
            P("section", None, None),
            P("section", None, None),
            P("section", None, None),
            P(None, "dp", None, "space", None),
        ),
        out_specs=(
            P("section", None, "dp", None, "space", None),
            P("section", None, "dp", None, "space", None),
            P("section", "space"),
            P("section", "space"),
            P("section", None, "space"),
            P("section", None, "space"),
            P("section", None, "space"),
            P("section", None, "space"),
            P(None, "dp", None, "space"),
        ),
        check_vma=False,
    )
```
